32 devices in a mesh: section: 2 (over core), row: 4 (over y, x), col: 4 (over z).
Axes of the slice: x: 2, y: 2, z: 4, core: 2. Of those that a mesh axis runs over, the one named last changes fastest.
Arguments:
- hidden_in: bfloat16 [2, 2048, 1024], P(None, 'row', 'col'), may hold values from -6 to 6
- cotangent: bfloat16 [2, 2048, 1024], P(None, 'row', 'col'), may hold values from -6 to 6
- lengths: int32 [2, 3], replicated, may hold values from 320 to 1280, as said below
- norm_gains: float32 [2, 2, 1024], P('section', None, 'col'), may hold values from 0.25 to 1.75
- norm_biases: float32 [2, 2, 1024], P('section', None, 'col'), may hold values from -3 to 3
- w_qkv: bfloat16 [2, 3, 1024, 1024], P('section', None, 'row', 'col'), may hold values from -0.1875 to 0.1875
- b_qkv: float32 [2, 3, 1024], P('section', None, 'col'), may hold values from -3 to 3
- w_out: bfloat16 [2, 1024, 1024], P('section', 'col', 'row'), may hold values from -3 to 3
- w_fc: bfloat16 [2, 1024, 4096], P('section', 'row', 'col'), may hold values from -0.1875 to 0.1875
- b_fc: float32 [2, 4096], P('section', 'col'), may hold values from -3 to 3
- w_proj: bfloat16 [2, 4096, 1024], P('section', 'col', 'row'), may hold values from -0.09375 to 0.09375
- b_out: float32 [2, 1024], P('section', 'col'), may hold values from -3 to 3
Outputs:
- layer_out: bfloat16 [2, 2, 2048, 1024], P('section', None, 'row', 'col')
- input_grad: bfloat16 [2, 2, 2048, 1024], P('section', None, 'row', 'col')
- grad_norm_gains: float32 [2, 2, 1024], P('section', None, 'col')
- grad_norm_biases: float32 [2, 2, 1024], P('section', None, 'col')
- grad_w_qkv: float32 [2, 3, 1024, 1024], P('section', None, 'row', 'col')
- grad_b_qkv: float32 [2, 3, 1024], P('section', None, 'col')
- grad_w_out: float32 [2, 1024, 1024], P('section', 'col', 'row')
- grad_w_fc: float32 [2, 1024, 4096], P('section', 'row', 'col')
- grad_b_fc: float32 [2, 4096], P('section', 'col')
- grad_w_proj: float32 [2, 4096, 1024], P('section', 'col', 'row')
- grad_b_out: float32 [2, 1024], P('section', 'col')
The draws below stay inside these ranges and needn't reach their ends.
Inputs may be any that keep to these rules, and one draw needn't show every extreme that they name: `lengths`: each row sums to 2048; the prompt has between 768 and 1280 tokens, each continuation between 320 and 704.
All inputs are finite; a program needn't handle non-finite values.
Results may differ from the reference program's by a relative error of at most 0.02.
Values may be sent and summed in bfloat16 or wider, within the bound.
A program may use at most 192 MiB of HBM per device.

```python
import math
import jax
import jax.numpy as jnp
from jax import lax

MODEL_WIDTH = 1024
HEADS = 16
FF = 4096
HEAD_DIM = 64
ROT = 16
MICRO = 2
CONTS = 2
MB = 2048


def draw_lengths(key, part):
    key = jax.random.fold_in(key, 7)
    prompt_key, cont_key = jax.random.split(key)
    prompt_shift = jax.random.randint(prompt_key, (MICRO, 1), -(MB // 8), MB // 8 + 1)
    prompt_shift = prompt_shift.at[0, 0].set(MB // 8)
    prompt = MB // 2 + prompt_shift
    remain = MB - prompt
    base_len = remain // CONTS
    wobble = jax.random.randint(cont_key, (MICRO, CONTS - 1), -(MB // 32), MB // 32 + 1)
    wobble = wobble.at[0, 0].set(-(MB // 32))
    leading = base_len + wobble
    closing = remain - jnp.sum(leading, axis=1, keepdims=True)
    return jnp.concatenate([prompt, leading, closing], axis=1).astype(jnp.int32)


def shard_levels(own_key, dims, pieces, low, largest):
    factor_of, own = 1.0, jax.random.fold_in(own_key, 6)
    for dim, parts in pieces:
        draws = jnp.exp(jax.random.uniform(jax.random.fold_in(own, dim), (parts,), jnp.float32, low / len(pieces), largest / len(pieces)))
        factor_of = factor_of * jnp.repeat(draws, dims[dim] // parts).reshape([-1 if axis == dim else 1 for axis in range(len(dims))])
    return factor_of


def bell_draw(key, shape, scale, reach, shards=(), kind=jnp.bfloat16):
    level = shard_levels(key, shape, shards, -0.22, 0.18) if shards else 1.0
    entries = jax.random.normal(key, shape, jnp.float32) * scale * level
    return jnp.minimum(jnp.maximum(entries, -reach), reach).astype(kind)


def setup_inputs(seed: int = 0) -> dict:
    streams_of = jax.random.split(jax.random.key(seed), 13)
    return {
        "hidden_in": bell_draw(streams_of[0], (MICRO, MB, MODEL_WIDTH), 1.0, 6.0, ((1, 4), (2, 4))),
        "cotangent": bell_draw(streams_of[1], (MICRO, MB, MODEL_WIDTH), 1.0, 6.0, ((1, 4), (2, 4))),
        "lengths": draw_lengths(jax.random.fold_in(streams_of[12], 71), 0),
        "norm_gains": jnp.clip(1.0 + 0.15 * jax.random.normal(streams_of[3], (2, 2, MODEL_WIDTH), jnp.float32), 0.25, 1.75),
        "norm_biases": bell_draw(streams_of[4], (2, 2, MODEL_WIDTH), 0.3, 3.0, ((0, 2), (2, 4)), jnp.float32),
        "w_qkv": bell_draw(streams_of[5], (2, 3, MODEL_WIDTH, MODEL_WIDTH), MODEL_WIDTH ** -0.5, 0.1875, ((0, 2), (2, 4), (3, 4))),
        "b_qkv": bell_draw(streams_of[6], (2, 3, MODEL_WIDTH), 0.3, 3.0, ((0, 2), (2, 4)), jnp.float32),
        "w_out": bell_draw(streams_of[7], (2, MODEL_WIDTH, MODEL_WIDTH), (max(MODEL_WIDTH // 256, 1)) ** -0.5, 3.0, ((0, 2), (1, 4), (2, 4))),
        "w_fc": bell_draw(streams_of[8], (2, MODEL_WIDTH, FF), MODEL_WIDTH ** -0.5, 0.1875, ((0, 2), (1, 4), (2, 4))),
        "b_fc": bell_draw(streams_of[9], (2, FF), 0.5, 3.0, ((0, 2), (1, 4)), jnp.float32),
        "w_proj": bell_draw(streams_of[10], (2, FF, MODEL_WIDTH), FF ** -0.5, 0.09375, ((0, 2), (1, 4), (2, 4))),
        "b_out": bell_draw(streams_of[11], (2, MODEL_WIDTH), 0.3, 3.0, ((0, 2), (1, 4)), jnp.float32),
    }


EPS = 1e-05
NEG = -1e+30

@jax.custom_vjp
def low(v):
    return lax.optimization_barrier(v.astype(jnp.bfloat16)).astype(jnp.float32)

@jax.custom_vjp
def low_back(v):
    return v

def low_keep(v):
    return (low(v), None)

def low_pass(kept, grad):
    return (grad,)

def back_keep(v):
    return (v, None)

def back_low(kept, grad):
    return (low(grad),)
low.defvjp(low_keep, low_pass)
low_back.defvjp(back_keep, back_low)

def segment_of(token_ids, starts):
    return lax.optimization_barrier(jnp.sum((token_ids[:, None] >= starts[None, 1:]).astype(jnp.int32), axis=1)).astype(jnp.int32)

def token_layout(lengths_row, token_ids):
    starts = (jnp.cumsum(lengths_row) - lengths_row).astype(jnp.int32)
    segment = segment_of(token_ids, starts)
    labels = jnp.arange(1, lengths_row.shape[0], dtype=jnp.int32)
    seg_begin = lax.optimization_barrier(jnp.sum(jnp.where(segment[:, None] == labels[None, :], starts[None, 1:], 0), axis=1)).astype(jnp.int32)
    position = jnp.where(segment == 0, token_ids, lengths_row[0] + token_ids - seg_begin).astype(jnp.int32)
    return (starts, segment, position)

def rotary_tables(position, turned):
    half_rot = turned // 2
    freqs = 10000.0 ** (-(2.0 * jnp.arange(half_rot, dtype=jnp.float32)) / turned)
    angles = position.astype(jnp.float32)[:, None] * freqs[None, :]
    return (jnp.cos(angles), jnp.sin(angles))

def rotate(values, cos_table, sin_table, direction):
    half_rot = cos_table.shape[-1]
    lower = values[..., :half_rot]
    upper = values[..., half_rot:2 * half_rot]
    cos_cast = cos_table[:, None, :]
    sin_cast = direction * sin_table[:, None, :]
    return jnp.concatenate([lower * cos_cast - upper * sin_cast, upper * cos_cast + lower * sin_cast, values[..., 2 * half_rot:]], axis=-1)

def permitted(query_seg, query_tok, key_seg, key_tok):
    from_prompt = (key_seg[None, :] == 0) & (query_seg[:, None] > 0)
    same_causal = (key_seg[None, :] == query_seg[:, None]) & (key_tok[None, :] <= query_tok[:, None])
    return from_prompt | same_causal

def layer_norm(values, gain_row, shift_row):
    centre = lax.optimization_barrier(jnp.mean(values, axis=-1, keepdims=True))
    centred_rows = values - centre
    spread = lax.optimization_barrier(jnp.mean(centred_rows * centred_rows, axis=-1, keepdims=True))
    return centred_rows * lax.rsqrt(spread + EPS) * gain_row + shift_row

def section_layer(inputs, params, cos_table, sin_table, segment, token_ids):
    norm_gain, shifts, w_query, b_query, w_output, w_hidden, b_hidden, w_project, b_output = params
    highest = lax.Precision.HIGHEST
    attention_normed_rows = low(layer_norm(inputs, norm_gain[0], shifts[0]))
    feedforward_normed_rows = low(layer_norm(inputs, norm_gain[1], shifts[1]))
    projected = low_back(jnp.einsum('td,cde->cte', attention_normed_rows, w_query, precision=highest) + b_query[:, None, :])
    shaped = (MB, HEADS, HEAD_DIM)
    queries = low(rotate(projected[0].reshape(shaped), cos_table, sin_table, 1.0))
    key_vals = low(rotate(projected[1].reshape(shaped), cos_table, sin_table, 1.0))
    value_vals = low(projected[2].reshape(shaped))
    query_block = min(512, MB)

    def attend_block(blocks):
        query_part, seg_part, tok_part = blocks
        scores = low_back(jnp.einsum('qhd,khd->hqk', query_part, key_vals, precision=highest) / math.sqrt(HEAD_DIM))
        allowed = permitted(seg_part, tok_part, segment, token_ids)[None]
        weights = low(jax.nn.softmax(jnp.where(allowed, scores, NEG), axis=-1))
        return jnp.einsum('hqk,khd->qhd', weights, value_vals, precision=highest)
    mixing = lax.map(jax.checkpoint(attend_block), (queries.reshape(MB // query_block, query_block, HEADS, HEAD_DIM), segment.reshape(MB // query_block, query_block), token_ids.reshape(MB // query_block, query_block)))
    attention = low(low_back(mixing.reshape(MB, MODEL_WIDTH)))
    hidden_pre = low_back(jnp.dot(feedforward_normed_rows, w_hidden, precision=highest) + b_hidden)
    hidden = low(jax.nn.gelu(hidden_pre, approximate=False))
    summed = inputs + jnp.dot(attention, w_output, precision=highest) + jnp.dot(hidden, w_project, precision=highest) + b_output
    return low(low_back(summed))

def reference(hidden_in, cotangent, lengths, norm_gains, norm_biases, w_qkv, b_qkv, w_out, w_fc, b_fc, w_proj, b_out):
    token_ids = jnp.arange(MB, dtype=jnp.int32)
    params = (norm_gains.astype(jnp.float32), norm_biases.astype(jnp.float32), w_qkv.astype(jnp.float32), b_qkv.astype(jnp.float32), w_out.astype(jnp.float32), w_fc.astype(jnp.float32), b_fc.astype(jnp.float32), w_proj.astype(jnp.float32), b_out.astype(jnp.float32))

    def forward(inputs, probes, weights):
        section_zero = tuple((stacked[0] for stacked in weights))
        section_one = tuple((stacked[1] for stacked in weights))

        def one_batch(unused, batch):
            x_batch, probe_batch, lengths_row = batch
            starts, segment, position = token_layout(lengths_row, token_ids)
            cos_table, sin_table = rotary_tables(position, ROT)
            first_out = section_layer(x_batch, section_zero, cos_table, sin_table, segment, token_ids)
            second_out = section_layer(first_out + probe_batch, section_one, cos_table, sin_table, segment, token_ids)
            return (unused, (first_out, second_out))
        unused, outputs = lax.scan(one_batch, jnp.zeros((), jnp.float32), (inputs, probes, lengths))
        return jnp.stack([outputs[0], outputs[1]])
    inputs = hidden_in.astype(jnp.float32)
    probes = jnp.zeros_like(inputs)
    layer_out, pullback = jax.vjp(forward, inputs, probes, params)
    cotangents = jnp.stack([jnp.zeros_like(inputs), cotangent.astype(jnp.float32)])
    grad_in, grad_probe, grads = pullback(cotangents)
    input_grad = jnp.stack([grad_in, grad_probe]).astype(jnp.bfloat16)
    return (layer_out.astype(jnp.bfloat16), input_grad, grads[0], grads[1], grads[2], grads[3], grads[4], grads[5], grads[6], grads[7], grads[8])
```

```python
from functools import partial
import math

import jax
import jax.numpy as jnp
from jax import lax
from jax.experimental import pallas as pl
from jax.experimental.pallas import tpu as pltpu
from jax.sharding import PartitionSpec as P

MODEL_WIDTH = 1024
HEAD_DIM = 64
ROT = 16


EPS = 1e-05
NEG = -1e30


def from_partner(value, axis, apart):
    mask = 2**apart
    pairs = [(source, source ^ mask) for source in range(lax.axis_size(axis))]
    return lax.ppermute(value, axis, pairs)


def segment_of(token_ids, starts):
    return jnp.sum((token_ids[:, None] >= starts[None, 1:]).astype(jnp.int32), axis=1)


def token_layout(lengths_row, token_ids):
    starts = jnp.cumsum(lengths_row) - lengths_row
    segment = segment_of(token_ids, starts)
    labels = jnp.arange(1, lengths_row.shape[0], dtype=jnp.int32)
    seg_begin = jnp.sum(jnp.where(segment[:, None] == labels[None, :], starts[None, 1:], 0), axis=1)
    position = jnp.where(segment == 0, token_ids, lengths_row[0] + token_ids - seg_begin)
    return (starts, segment, position)


def rotary_tables(position, turned):
    half_rot = turned // 2
    freqs = 10000.0 ** (-(2.0 * jnp.arange(half_rot, dtype=jnp.float32)) / turned)
    angles = position.astype(jnp.float32)[:, None] * freqs[None, :]
    return (jnp.cos(angles), jnp.sin(angles))


def rotate(values, cos_table, sin_table, direction):
    half_rot = cos_table.shape[-1]
    lower = values[..., :half_rot]
    upper = values[..., half_rot : 2 * half_rot]
    cos_cast = cos_table[:, None, :]
    sin_cast = direction * sin_table[:, None, :]
    return jnp.concatenate(
        [
            lower * cos_cast - upper * sin_cast,
            upper * cos_cast + lower * sin_cast,
            values[..., 2 * half_rot :],
        ],
        axis=-1,
    )


def permitted(query_seg, query_tok, key_seg, key_tok):
    from_prompt = (key_seg[None, :] == 0) & (query_seg[:, None] > 0)
    same_causal = (key_seg[None, :] == query_seg[:, None]) & (
        key_tok[None, :] <= query_tok[:, None]
    )
    return from_prompt | same_causal


def attend(running, key_piece, value_piece, query3, layout):
    run_max, run_sum, totals = running
    piece_len = key_piece.shape[0]
    key3 = key_piece.reshape(piece_len, query3.shape[1], query3.shape[2])
    value3 = value_piece.reshape(piece_len, query3.shape[1], query3.shape[2])
    key_tok = jnp.arange(piece_len, dtype=jnp.int32)
    key_seg = segment_of(key_tok, layout["starts"])
    allowed = permitted(layout["segment"], layout["tokens"], key_seg, key_tok)[None]
    scores = jnp.einsum("qhd,khd->hqk", query3, key3, preferred_element_type=jnp.float32) * (
        1.0 / math.sqrt(query3.shape[2])
    )
    masked = jnp.where(allowed, scores, NEG)
    new_max = jnp.maximum(run_max, jnp.max(masked, axis=-1))
    weights = jnp.where(allowed, jnp.exp(masked - new_max[..., None]), 0.0)
    run_sum = jnp.sum(weights, axis=-1)
    totals = jnp.einsum(
        "hqk,khd->hqd", weights.astype(jnp.bfloat16), value3, preferred_element_type=jnp.float32
    )
    return (new_max, run_sum, totals)


def layer_forward(x, full, weights, layout, complete_gains, complete_shifts):
    w_query, b_query, w_output, w_hidden, b_hidden, w_project, b_output = weights
    row_tokens, local_width = x.shape
    heads_local = local_width // HEAD_DIM
    shaped = (row_tokens, heads_local, HEAD_DIM)
    as_float = full.astype(jnp.float32)
    row_mean = jnp.mean(as_float, axis=1, keepdims=True)
    centred = as_float - row_mean
    rstd = lax.rsqrt(jnp.mean(centred * centred, axis=1, keepdims=True) + EPS)
    unit = centred * rstd
    normed_a = (unit * complete_gains[0] + complete_shifts[0]).astype(jnp.bfloat16)
    normed_m = (unit * complete_gains[1] + complete_shifts[1]).astype(jnp.bfloat16)
    projected = (
        jnp.einsum("td,cde->cte", normed_a, w_query, preferred_element_type=jnp.float32)
        + b_query[:, None, :]
    )
    cos_table, sin_table = layout["cos_table"], layout["sin_table"]
    query3 = rotate(projected[0].reshape(shaped), cos_table, sin_table, 1.0).astype(jnp.bfloat16)
    key_flat = (
        rotate(projected[1].reshape(shaped), cos_table, sin_table, 1.0)
        .reshape(row_tokens, local_width)
        .astype(jnp.bfloat16)
    )
    value_flat = projected[2].astype(jnp.bfloat16)
    key_full = lax.all_gather(key_flat, "row", axis=0, tiled=True)
    value_full = lax.all_gather(value_flat, "row", axis=0, tiled=True)
    initial = (
        jnp.full((heads_local, row_tokens), NEG, jnp.float32),
        jnp.zeros((heads_local, row_tokens), jnp.float32),
        jnp.zeros((heads_local, row_tokens, HEAD_DIM), jnp.float32),
    )
    run_max, run_sum, totals = attend(initial, key_full, value_full, query3, layout)
    out_exact = totals / run_sum[..., None]
    log_sum = run_max + jnp.log(run_sum)
    attn_flat = (
        jnp.transpose(out_exact, (1, 0, 2)).reshape(row_tokens, local_width).astype(jnp.bfloat16)
    )
    hidden_pre = jnp.dot(normed_m, w_hidden, preferred_element_type=jnp.float32) + b_hidden
    hidden = jax.nn.gelu(hidden_pre, approximate=False).astype(jnp.bfloat16)
    branch = jnp.dot(attn_flat, w_output, preferred_element_type=jnp.float32) + jnp.dot(
        hidden, w_project, preferred_element_type=jnp.float32
    )
    summed = lax.psum_scatter(
        branch.astype(jnp.bfloat16), "col", scatter_dimension=1, tiled=True
    ).astype(jnp.float32)
    output = (x.astype(jnp.float32) + summed + b_output).astype(jnp.bfloat16)
    state = dict(
        unit=unit, rstd=rstd, normed_a=normed_a, normed_m=normed_m, query3=query3,
        key_full=key_full, value_full=value_full, attn_flat=attn_flat, out_exact=out_exact,
        log_sum=log_sum, hidden_pre=hidden_pre, hidden=hidden,
    )
    return output, state


def layer_backward(state, grad_in, grad_full, weights, layout, complete_gains, scatter_tokens):
    w_query, b_query, w_output, w_hidden, b_hidden, w_project, b_output = weights
    row_tokens = state["normed_a"].shape[0]
    local_width = w_output.shape[0]
    heads_local = local_width // HEAD_DIM
    shaped = (row_tokens, heads_local, HEAD_DIM)
    score_scale = 1.0 / math.sqrt(HEAD_DIM)
    total_tokens = state["key_full"].shape[0]
    key_block = min(512, total_tokens)
    grad_wout = jnp.einsum(
        "te,td->ed", state["attn_flat"], grad_full, preferred_element_type=jnp.float32
    )
    grad_wproj = jnp.einsum(
        "tf,td->fd", state["hidden"], grad_full, preferred_element_type=jnp.float32
    )
    grad_bout = jnp.sum(grad_in.astype(jnp.float32), axis=0)
    grad_attn = jnp.einsum(
        "td,ed->te", grad_full, w_output, preferred_element_type=jnp.float32
    ).astype(jnp.bfloat16)
    grad_hidden = jnp.einsum("td,fd->tf", grad_full, w_project, preferred_element_type=jnp.float32)
    gelu_value, gelu_back = jax.vjp(partial(jax.nn.gelu, approximate=False), state["hidden_pre"])
    grad_hpre = gelu_back(grad_hidden)[0].astype(jnp.bfloat16)
    grad_wfc = jnp.einsum(
        "td,tf->df", state["normed_m"], grad_hpre, preferred_element_type=jnp.float32
    )
    grad_bfc = jnp.sum(grad_hpre.astype(jnp.float32), axis=0)
    grad_normed_m = jnp.einsum("tf,df->td", grad_hpre, w_hidden, preferred_element_type=jnp.float32)
    grad_out3 = grad_attn.reshape(shaped)
    query3 = state["query3"]
    delta = jnp.sum(
        jnp.transpose(grad_out3.astype(jnp.float32), (1, 0, 2)) * state["out_exact"], axis=-1
    )
    grad_query = jnp.zeros(shaped, jnp.float32)
    key_terms = []
    value_terms = []
    for block_no in range(total_tokens // key_block):
        begin_at = block_no * key_block
        key_part = state["key_full"][begin_at : begin_at + key_block].reshape(
            key_block, heads_local, HEAD_DIM
        )
        value_part = state["value_full"][begin_at : begin_at + key_block].reshape(
            key_block, heads_local, HEAD_DIM
        )
        key_tok = begin_at + jnp.arange(key_block, dtype=jnp.int32)
        key_seg = segment_of(key_tok, layout["starts"])
        allowed = permitted(layout["segment"], layout["tokens"], key_seg, key_tok)[None]
        scores = (
            jnp.einsum("qhd,khd->hqk", query3, key_part, preferred_element_type=jnp.float32)
            * score_scale
        )
        probs = jnp.where(
            allowed,
            jnp.exp(jnp.where(allowed, scores, NEG) - state["log_sum"][..., None]),
            0.0,
        )
        grad_probs = jnp.einsum(
            "qhd,khd->hqk", grad_out3, value_part, preferred_element_type=jnp.float32
        )
        grad_scores = (probs * (grad_probs - delta[..., None])).astype(jnp.bfloat16)
        grad_query = grad_query + jnp.einsum(
            "hqk,khd->qhd", grad_scores, key_part, preferred_element_type=jnp.float32
        )
        key_terms.append(
            jnp.einsum(
                "hqk,qhd->khd", grad_scores, query3, preferred_element_type=jnp.float32
            ).reshape(key_block, local_width)
            * score_scale
        )
        value_terms.append(
            jnp.einsum(
                "hqk,qhd->khd",
                probs.astype(jnp.bfloat16),
                grad_out3,
                preferred_element_type=jnp.float32,
            ).reshape(key_block, local_width)
        )
    grad_query = grad_query * score_scale
    kv_terms = jnp.concatenate(
        [jnp.concatenate(key_terms, axis=0), jnp.concatenate(value_terms, axis=0)], axis=1
    )
    kv_grads = lax.psum_scatter(
        kv_terms.astype(jnp.bfloat16), "row", scatter_dimension=0, tiled=True
    ).astype(jnp.float32)
    grad_key = kv_grads[:, :local_width].reshape(shaped)
    grad_value = kv_grads[:, local_width:]
    cos_table, sin_table = layout["cos_table"], layout["sin_table"]
    grad_pre = jnp.stack(
        [
            rotate(grad_query, cos_table, sin_table, -1.0).reshape(row_tokens, local_width),
            rotate(grad_key, cos_table, sin_table, -1.0).reshape(row_tokens, local_width),
            grad_value,
        ]
    ).astype(jnp.bfloat16)
    grad_wqkv = jnp.einsum(
        "td,cte->cde", state["normed_a"], grad_pre, preferred_element_type=jnp.float32
    )
    grad_bqkv = jnp.sum(grad_pre.astype(jnp.float32), axis=1)
    grad_normed_a = jnp.einsum("cte,cde->td", grad_pre, w_query, preferred_element_type=jnp.float32)
    unit = state["unit"]
    grad_gains = jnp.stack(
        [jnp.sum(grad_normed_a * unit, axis=0), jnp.sum(grad_normed_m * unit, axis=0)]
    )
    grad_shifts = jnp.stack([jnp.sum(grad_normed_a, axis=0), jnp.sum(grad_normed_m, axis=0)])
    grad_unit = grad_normed_a * complete_gains[0] + grad_normed_m * complete_gains[1]
    big = (grad_wqkv, grad_wout, grad_wfc, grad_wproj)
    big = tuple(member.astype(jnp.bfloat16) for member in big)
    shared = (grad_gains, grad_shifts)
    local = (grad_bqkv, grad_bfc, grad_bout)
    if scatter_tokens:
        piece = lax.psum_scatter(
            grad_unit.astype(jnp.bfloat16), "col", scatter_dimension=0, tiled=True
        ).astype(jnp.float32)
        rows = piece.shape[0]
        start = lax.axis_index("col") * rows
        unit_part = lax.dynamic_slice_in_dim(unit, start, rows, 0)
        rstd_part = lax.dynamic_slice_in_dim(state["rstd"], start, rows, 0)
        grad_part = lax.dynamic_slice_in_dim(grad_full, start, rows, 0).astype(jnp.float32)
        moved = (
            piece
            - jnp.mean(piece, axis=1, keepdims=True)
            - unit_part * jnp.mean(piece * unit_part, axis=1, keepdims=True)
        )
        grad_input = (grad_part + rstd_part * moved).astype(jnp.bfloat16)
    else:
        sums = lax.psum(
            jnp.stack([jnp.sum(grad_unit, axis=1), jnp.sum(grad_unit * unit, axis=1)]), "col"
        )
        piece = lax.psum_scatter(
            grad_unit.astype(jnp.bfloat16), "col", scatter_dimension=1, tiled=True
        ).astype(jnp.float32)
        width = piece.shape[1]
        unit_part = lax.dynamic_slice_in_dim(unit, lax.axis_index("col") * width, width, 1)
        moved = (
            piece
            - sums[0][:, None] / MODEL_WIDTH
            - unit_part * (sums[1][:, None] / MODEL_WIDTH)
        )
        grad_input = (grad_in.astype(jnp.float32) + state["rstd"] * moved).astype(jnp.bfloat16)
    return grad_input, big, shared, local


def body(
    hidden_in,
    cotangent,
    lengths,
    norm_gains,
    norm_biases,
    w_qkv,
    b_qkv,
    w_out,
    w_fc,
    b_fc,
    w_proj,
    b_out,
):
    row_tokens = hidden_in.shape[1]
    local_width = hidden_in.shape[2]
    section = lax.axis_index("section")
    is_first = section == 0
    my_tokens = lax.axis_index("row") * row_tokens + jnp.arange(row_tokens, dtype=jnp.int32)
    x0 = lax.dynamic_index_in_dim(hidden_in, section, 0, keepdims=False)
    cot = lax.dynamic_index_in_dim(cotangent, section, 0, keepdims=False)
    lengths_row = lax.dynamic_index_in_dim(lengths, section, 0, keepdims=False)
    starts, segment, position = token_layout(lengths_row, my_tokens)
    cos_table, sin_table = rotary_tables(position, ROT)
    layout = {
        "starts": starts,
        "segment": segment,
        "tokens": my_tokens,
        "cos_table": cos_table,
        "sin_table": sin_table,
    }
    both = ("section", "row")
    gains = lax.all_gather(norm_gains[0], ("section", "col"), axis=0)
    shifts = lax.all_gather(norm_biases[0], ("section", "col"), axis=0)
    cols = lax.axis_size("col")

    def whole(vectors):
        split = vectors.reshape(2, cols, 2, local_width)
        return jnp.transpose(split, (0, 2, 1, 3)).reshape(2, 2, cols * local_width)

    gains, shifts = whole(gains), whole(shifts)
    biases = [lax.all_gather(member[0], "section", axis=0) for member in (b_qkv, b_fc, b_out)]
    x0_full = lax.all_gather(x0, "col", axis=1, tiled=True)
    rows = lax.axis_size("row")

    def unite(member, axis):
        gathered = lax.all_gather(member[0], both, axis=0)
        pieces = gathered.reshape((2, rows) + gathered.shape[1:])
        return [
            jnp.concatenate([pieces[layer, row] for row in range(rows)], axis=axis)
            for layer in range(2)
        ]

    w_query, w_hidden = unite(w_qkv, 1), unite(w_fc, 0)
    w_output, w_project = unite(w_out, 1), unite(w_proj, 1)
    weights = [
        (
            w_query[layer],
            biases[0][layer],
            w_output[layer],
            w_hidden[layer],
            biases[1][layer],
            w_project[layer],
            biases[2][layer],
        )
        for layer in range(2)
    ]
    out0, state0 = layer_forward(x0, x0_full, weights[0], layout, gains[0], shifts[0])
    x1_full = lax.all_gather(out0, "col", axis=1, tiled=True)
    cot_full = lax.all_gather(cot, "col", axis=1, tiled=True)
    out1, state1 = layer_forward(out0, x1_full, weights[1], layout, gains[1], shifts[1])
    grad1_part, big1, shared1, local1 = layer_backward(
        state1, cot, cot_full, weights[1], layout, gains[1], True
    )
    grad1_full = lax.all_gather(grad1_part, "col", axis=0, tiled=True)
    grad1 = lax.dynamic_slice_in_dim(
        grad1_full, lax.axis_index("col") * local_width, local_width, 1
    )
    grad0, big0, shared0, local0 = layer_backward(
        state0, grad1, grad1_full, weights[0], layout, gains[0], False
    )

    def swap(first, second):
        mine = jnp.where(is_first, first, second)
        theirs = from_partner(jnp.where(is_first, second, first), "section", 0)
        return jnp.where(is_first, jnp.stack([mine, theirs]), jnp.stack([theirs, mine]))[None]

    out_rows = swap(out0, out1)
    grad_rows = swap(grad0, grad1)

    def scatter(first, second, axis):
        length = first.shape[axis] // rows
        pieces = jnp.stack(
            [
                lax.slice_in_dim(member, row * length, (row + 1) * length, axis=axis)
                for member in (first, second)
                for row in range(rows)
            ]
        )
        return lax.psum_scatter(pieces, both, scatter_dimension=0, tiled=True).astype(jnp.float32)

    large = [scatter(a, b, axis) for a, b, axis in zip(big0, big1, (1, 1, 0, 1))]
    shared_sums = lax.psum(
        tuple(jnp.stack([a, b]) for a, b in zip(shared0, shared1)), ("section", "row", "col")
    )
    shared_mine = [
        lax.dynamic_slice(
            member,
            (section, 0, lax.axis_index("col") * local_width),
            (1, 2, local_width),
        )
        for member in shared_sums
    ]
    local_sums = lax.psum(tuple(jnp.stack([a, b]) for a, b in zip(local0, local1)), both)
    local_mine = [lax.dynamic_index_in_dim(member, section, 0) for member in local_sums]
    return (
        out_rows,
        grad_rows,
        shared_mine[0],
        shared_mine[1],
        large[0],
        local_mine[0],
        large[1],
        large[2],
        local_mine[1],
        large[3],
        local_mine[2],
    )


BF = jnp.bfloat16
F32 = jnp.float32
BY_MESH = pl.DeviceIdType.MESH
VMEM_LIMIT = 60 * 2**20
ATTENTION_BLOCK = 256
PARTS = 2


def dot(a, b, contract=((1,), (0,))):
    return lax.dot_general(a, b, (contract, ((), ())), preferred_element_type=F32)


def rcopy(src, dst, ssem, rsem, **device):
    return pltpu.make_async_remote_copy(
        src_ref=src,
        dst_ref=dst,
        send_sem=ssem,
        recv_sem=rsem,
        device_id=device,
        device_id_type=BY_MESH,
    )


class Place:
    def __init__(self, rows, cols):
        self.rows, self.cols = rows, cols
        self.s = lax.axis_index("section")
        self.r = lax.axis_index("row")
        self.c = lax.axis_index("col")

    def row_to(self, step):
        return lax.rem(self.r + step, self.rows)

    def row_from(self, step):
        return lax.rem(self.r + self.rows - step, self.rows)

    def col_to(self, step):
        return lax.rem(self.c + step, self.cols)

    def col_from(self, step):
        return lax.rem(self.c + self.cols - step, self.cols)

    def greet(self, rows=False, cols=False, partner=False, cross_cols=False, cross_rows=False):
        barrier = pltpu.get_barrier_semaphore()
        count = 0

        def signal(**device):
            pl.semaphore_signal(barrier, inc=1, device_id=device, device_id_type=BY_MESH)

        if rows:
            for step in range(1, self.rows):
                signal(row=self.row_to(step))
                count += 1
        if cols:
            for step in range(1, self.cols):
                signal(col=self.col_to(step))
                count += 1
        if partner:
            signal(section=1 - self.s)
            count += 1
        if cross_cols:
            for step in range(1, self.cols):
                signal(section=1 - self.s, col=self.col_to(step))
                count += 1
        if cross_rows:
            for step in range(1, self.rows):
                signal(section=1 - self.s, row=self.row_to(step))
                count += 1
        pl.semaphore_wait(barrier, count)


class LineGather:
    def __init__(self, place, view, send_right, send_left, recv, lane=0):
        self.place, self.view, self.lane = place, view, lane
        self.send_right, self.send_left, self.recv = send_right, send_left, recv

    def right(self, block):
        return rcopy(
            self.view(block), self.view(block), self.send_right.at[self.lane, block],
            self.recv.at[self.lane, block],
            col=lax.rem(self.place.c + 1, self.place.cols),
        )

    def left(self, block):
        cols = self.place.cols
        return rcopy(
            self.view(block), self.view(block), self.send_left.at[self.lane, block],
            self.recv.at[self.lane, block],
            col=lax.rem(self.place.c + cols - 1, cols),
        )

    def hop(self, distance):
        c, cols = self.place.c, self.place.cols

        @pl.when(c >= distance)
        def _():
            block = lax.rem(c + cols - distance, cols)
            if distance:
                self.right(block).wait_recv()

            @pl.when(c < cols - 1)
            def _():
                self.right(block).start()

        @pl.when(c + distance < cols)
        def _():
            block = lax.rem(c + distance, cols)
            if distance:
                self.left(block).wait_recv()

            @pl.when(c > 0)
            def _():
                self.left(block).start()

    def finish(self):
        c, cols = self.place.c, self.place.cols
        for distance in range(cols):

            @pl.when((c >= distance) & (c < cols - 1))
            def _():
                self.right(lax.rem(c + cols - distance, cols)).wait_send()

            @pl.when((c + distance < cols) & (c > 0))
            def _():
                self.left(lax.rem(c + distance, cols)).wait_send()


class WeightGather:
    def __init__(self, place, layer, own, full, send, recv, pass_on, local):
        self.place, self.layer, self.own, self.full = place, layer, own, full
        self.send, self.recv, self.pass_on, self.local = send, recv, pass_on, local

    def view(self, kind, block):
        length = self.own[kind].shape[-2 if kind in (0, 1) else -1]
        piece = pl.ds(pl.multiple_of(block * length, length), length)
        if kind == 0:
            return self.full[0].at[:, piece, :]
        if kind == 1:
            return self.full[1].at[piece, :]
        return self.full[kind].at[:, piece]

    def over_row(self, kind, step):
        place = self.place
        return rcopy(
            self.own[kind], self.view(kind, place.r), self.send.at[kind, step],
            self.recv.at[kind, step], row=place.row_to(step),
        )

    def arriving(self, kind, step):
        block = self.view(kind, self.place.row_from(step))
        return rcopy(
            block, block, self.send.at[kind, step], self.recv.at[kind, step],
            row=self.place.row_to(step),
        )

    def to_partner(self, kind, step):
        place = self.place
        block = self.view(kind, place.row_from(step))
        return rcopy(
            self.own[kind] if step == 0 else block, block, self.pass_on.at[kind, step],
            self.recv.at[kind, step], section=1 - place.s,
        )

    def keep(self, kind):
        return pltpu.make_async_copy(
            self.own[kind], self.view(kind, self.place.r), self.local.at[kind]
        )

    def start(self, kind):
        @pl.when(self.place.s == self.layer)
        def _():
            for step in range(1, self.place.rows):
                self.over_row(kind, step).start()
            self.keep(kind).start()
            self.to_partner(kind, 0).start()

    def forward(self, kind):
        @pl.when(self.place.s == self.layer)
        def _():
            for step in range(1, self.place.rows):
                self.arriving(kind, step).wait_recv()
                self.to_partner(kind, step).start()
            self.keep(kind).wait()

    def ready(self, kind):
        @pl.when(self.place.s != self.layer)
        def _():
            for step in range(self.place.rows):
                self.to_partner(kind, step).wait_recv()

    def finish(self, kind):
        @pl.when(self.place.s == self.layer)
        def _():
            for step in range(1, self.place.rows):
                self.over_row(kind, step).wait_send()
            for step in range(self.place.rows):
                self.to_partner(kind, step).wait_send()


class RowExchange:
    def __init__(self, place, piece_for, slot_of, send, recv, local):
        self.place, self.piece_for, self.slot_of = place, piece_for, slot_of
        self.send, self.recv, self.local = send, recv, local

    def out(self, step):
        place = self.place
        target = place.row_to(step)
        return rcopy(
            self.piece_for(target), self.slot_of(place.r), self.send.at[step], self.recv.at[step],
            row=target,
        )

    def into(self, step):
        slot = self.slot_of(self.place.row_from(step))
        return rcopy(
            slot, slot, self.send.at[step], self.recv.at[step], row=self.place.row_to(step)
        )

    def keep(self):
        return pltpu.make_async_copy(
            self.piece_for(self.place.r), self.slot_of(self.place.r), self.local
        )

    def start(self):
        for step in range(1, self.place.rows):
            self.out(step).start()
        self.keep().start()

    def arrive(self):
        for step in range(1, self.place.rows):
            self.into(step).wait_recv()
        self.keep().wait()

    def finish(self):
        for step in range(1, self.place.rows):
            self.out(step).wait_send()


def norm_rows(source, gains_a, shifts_a, gains_m, shifts_m, normed_a, normed_m):
    tokens = source.shape[0]
    tile = min(128, tokens)

    @pl.loop(0, tokens // tile)
    def _(index):
        rows = pl.ds(pl.multiple_of(index * tile, tile), tile)
        values = source[rows, :].astype(F32)
        centred = values - jnp.mean(values, axis=1, keepdims=True)
        unit = centred * lax.rsqrt(jnp.mean(centred * centred, axis=1, keepdims=True) + EPS)
        normed_a[rows, :] = (unit * gains_a + shifts_a).astype(BF)
        normed_m[rows, :] = (unit * gains_m + shifts_m).astype(BF)


def turn(block, cos, sin, direction):
    half = cos.shape[0]
    lower, upper, rest = block[:half], block[half : 2 * half], block[2 * half :]
    return jnp.concatenate(
        [
            lower * cos - upper * (direction * sin),
            upper * cos + lower * (direction * sin),
            rest,
        ],
        axis=0,
    )


def project_heads(normed_a, w_query, bias_rows, cos, sin, pieces, heads):
    for kind in range(3):
        values = dot(normed_a[...], w_query[kind]) + bias_rows(kind)
        flipped = values.T
        for head in range(heads):
            block = flipped[head * HEAD_DIM : (head + 1) * HEAD_DIM]
            if kind < 2:
                block = turn(block, cos[...], sin[...], 1.0)
            pieces[head, kind * HEAD_DIM : (kind + 1) * HEAD_DIM, :] = block.astype(BF)


def feed_forward(normed_m, w_hidden, bias_of, hidden, slope):
    tile = min(256, w_hidden.shape[1])

    @pl.loop(0, w_hidden.shape[1] // tile)
    def _(index):
        cols = pl.ds(pl.multiple_of(index * tile, tile), tile)
        pre = dot(normed_m[...], w_hidden[:, cols]) + bias_of(index)
        phi = 0.5 * (1.0 + lax.erf(pre * math.sqrt(0.5)))
        hidden[:, cols] = (pre * phi).astype(BF)
        slope[:, cols] = phi + pre * (jnp.exp(-0.5 * pre * pre) * (1.0 / math.sqrt(2.0 * math.pi)))


def times_tiles(left, right, out, convert=None, contract=((1,), (0,))):
    tile = min(256, out.shape[1])

    @pl.loop(0, out.shape[1] // tile)
    def _(index):
        cols = pl.ds(pl.multiple_of(index * tile, tile), tile)
        piece = right[:, cols] if contract[1] == (0,) else right[cols, :]
        value = dot(left[...], piece, contract)
        out[:, cols] = value if convert is None else convert(value, cols)


def opening_kernel(
    rows, cols,
    hidden_in, cotangent, vectors, wq, wf, wo, wp, cos, sin,
    x_full, cot_full, vec_all, wq_all, wf_all, wo_all, wp_all, normed_a, normed_m, qkv, hidden, slope, branch,
    pieces,
    xr, xl, xv, cr, cl, cv, vs, vr, ws, wr, wpas, wloc, as_, ar, local,
):
    place = Place(rows, cols)
    s, c = place.s, place.c
    width = hidden_in.shape[2]

    def cols_of(ref):
        return lambda block: ref.at[:, pl.ds(pl.multiple_of(block * width, width), width)]

    def vec_slot(section, col):
        return vec_all.at[section, :, pl.ds(pl.multiple_of(col * width, width), width)]

    def vec_copy(ds, dc):
        index = ds * cols + dc
        return rcopy(
            vectors, vec_slot(s, c), vs.at[index], vr.at[index],
            section=lax.rem(s + ds, 2), col=place.col_to(dc),
        )

    def vec_into(ds, dc):
        index = ds * cols + dc
        slot = vec_slot(lax.rem(s + ds, 2), place.col_from(dc))
        return rcopy(
            slot, slot, vs.at[index], vr.at[index],
            section=lax.rem(s + ds, 2), col=place.col_to(dc),
        )

    others = [(ds, dc) for ds in range(2) for dc in range(cols) if ds or dc]
    x_own = pltpu.make_async_copy(hidden_in.at[s], cols_of(x_full)(c), local.at[0])
    c_own = pltpu.make_async_copy(cotangent.at[s], cols_of(cot_full)(c), local.at[1])
    v_own = pltpu.make_async_copy(vectors, vec_slot(s, c), local.at[2])
    for copy in (x_own, c_own, v_own):
        copy.start()
    place.greet(rows=True, cols=True, partner=True, cross_cols=True)
    weights = WeightGather(
        place, 0, (wq, wf, wo, wp), (wq_all, wf_all, wo_all, wp_all), ws, wr, wpas, wloc
    )
    x_gather = LineGather(place, cols_of(x_full), xr, xl, xv)
    c_gather = LineGather(place, cols_of(cot_full), cr, cl, cv)
    x_own.wait()
    x_gather.hop(0)
    for ds, dc in others:
        vec_copy(ds, dc).start()
    weights.start(0)
    x_gather.hop(1)
    weights.forward(0)
    weights.start(1)
    for distance in range(2, cols):
        x_gather.hop(distance)
    c_own.wait()
    c_gather.hop(0)
    v_own.wait()
    for ds, dc in others:
        vec_into(ds, dc).wait_recv()

    def row(index):
        return vec_all[0, index : index + 1, :]

    own = pl.ds(pl.multiple_of(c * width, width), width)
    norm_rows(x_full, row(0), row(2), row(1), row(3), normed_a, normed_m)
    weights.ready(0)
    project_heads(
        normed_a, wq_all, lambda kind: vec_all[0, 4 + kind : 5 + kind, own], cos, sin, pieces, rows
    )
    tokens = normed_a.shape[0]
    exchange = RowExchange(
        place,
        lambda target: pieces.at[target],
        lambda source: qkv.at[:, pl.ds(pl.multiple_of(source * tokens, tokens), tokens)],
        as_, ar, local.at[3],
    )
    exchange.start()
    weights.forward(1)
    weights.start(3)
    weights.start(2)
    c_gather.hop(1)
    weights.ready(1)
    feed_forward(
        normed_m, wf_all, lambda index: vec_all[0, pl.ds(8 + index, 1), own], hidden, slope
    )
    for distance in range(2, cols):
        c_gather.hop(distance)
    exchange.arrive()
    weights.forward(3)
    weights.forward(2)
    weights.ready(3)
    times_tiles(hidden, wp_all, branch)
    weights.ready(2)
    x_gather.finish()
    c_gather.finish()
    exchange.finish()
    for ds, dc in others:
        vec_copy(ds, dc).wait_send()
    for kind in range(4):
        weights.finish(kind)


def kernel_call(kernel, collective_id, outs, scratch, *args, cost=None):
    vmem = pl.BlockSpec(memory_space=pltpu.VMEM)
    return pl.pallas_call(
        kernel,
        out_shape=[jax.ShapeDtypeStruct(shape, dtype) for shape, dtype in outs],
        in_specs=[vmem] * len(args),
        out_specs=[vmem] * len(outs),
        scratch_shapes=scratch,
        compiler_params=pltpu.CompilerParams(
            collective_id=collective_id, has_side_effects=True, vmem_limit_bytes=VMEM_LIMIT
        ),
    )(*args)


def dma(*shape):
    return pltpu.SemaphoreType.DMA(shape)


def opening(rows, cols, hidden_in, cotangent, vectors, wq, wf, wo, wp, cos, sin):
    tokens, width = hidden_in.shape[1:]
    full = cols * width
    units = wf.shape[1]
    outs = [
        ((tokens, full), BF),
        ((tokens, full), BF),
        ((2,) + vectors.shape[:1] + (full,), F32),
        ((3, full, width), BF),
        ((full, units), BF),
        ((width, full), BF),
        ((units, full), BF),
        ((tokens, full), BF),
        ((tokens, full), BF),
        ((3 * HEAD_DIM, rows * tokens), BF),
        ((tokens, units), BF),
        ((tokens, units), F32),
        ((tokens, full), F32),
    ]
    scratch = (
        [pltpu.VMEM((rows, 3 * HEAD_DIM, tokens), BF)]
        + [dma(1, cols)] * 6
        + [dma(2 * cols)] * 2
        + [dma(4, rows)] * 3
        + [dma(4)]
        + [dma(rows)] * 2
        + [dma(4)]
    )
    return kernel_call(
        partial(opening_kernel, rows, cols), 1, outs, scratch,
        hidden_in, cotangent, vectors, wq, wf, wo, wp, cos, sin,
    )


def key_mask(prompt, first_ref, cols, key_at, query_at, keys, queries):
    key = lax.broadcasted_iota(jnp.int32, (keys, queries), 0) + key_at
    query = lax.broadcasted_iota(jnp.int32, (keys, queries), 1) + query_at
    return ((key < prompt) | (key >= first_ref[:, cols])) & (key <= query)


def forward_pass(block, prompt, first, qkv, key_rows, out, out_low, log_sum):
    total = qkv.shape[1]

    @pl.loop(0, total // block)
    def _(j):
        query_at = pl.multiple_of(j * block, block)
        cols = pl.ds(query_at, block)
        query = qkv[:HEAD_DIM, cols]

        def step(i, carry):
            top, weight, totals = carry
            key_at = pl.multiple_of(i * block, block)
            scores = dot(key_rows[pl.ds(key_at, block), :], query) * (1.0 / math.sqrt(HEAD_DIM))
            allowed = key_mask(prompt, first, cols, key_at, query_at, block, block)
            scores = jnp.where(allowed, scores, NEG)
            new_top = jnp.maximum(top, jnp.max(scores, axis=0, keepdims=True))
            probs = jnp.exp(scores - new_top)
            fade = jnp.exp(top - new_top)
            weight = weight * fade + jnp.sum(probs, axis=0, keepdims=True)
            value = qkv[2 * HEAD_DIM : 3 * HEAD_DIM, pl.ds(key_at, block)]
            totals = totals * fade + dot(value, probs.astype(BF))
            return new_top, weight, totals

        top, weight, totals = lax.fori_loop(
            0,
            j + 1,
            step,
            (
                jnp.full((1, block), NEG, F32),
                jnp.zeros((1, block), F32),
                jnp.zeros((HEAD_DIM, block), F32),
            ),
        )
        exact = totals / weight
        out[:, cols] = exact
        out_low[:HEAD_DIM, cols] = exact.astype(BF)
        log_sum[:, cols] = top + jnp.log(weight)


def backward_pass(block, prompt, first, qkv, d_out, out, log_sum, key_rows, value_rows, key_acc, value_acc, grads, at):
    total = qkv.shape[1]
    scale = 1.0 / math.sqrt(HEAD_DIM)
    key_acc[...] = jnp.zeros_like(key_acc)
    value_acc[...] = jnp.zeros_like(value_acc)

    @pl.loop(0, total // block)
    def _(j):
        query_at = pl.multiple_of(j * block, block)
        cols = pl.ds(query_at, block)
        query = qkv[:HEAD_DIM, cols]
        d_query = d_out[:, cols]
        delta = jnp.sum(d_query.astype(F32) * out[:, cols], axis=0, keepdims=True)
        log_row = log_sum[:, cols]

        def step(i, d_sum):
            key_at = pl.multiple_of(i * block, block)
            keys = pl.ds(key_at, block)
            scores = dot(key_rows[keys, :], query) * scale
            allowed = key_mask(prompt, first, cols, key_at, query_at, block, block)
            probs = jnp.exp(jnp.where(allowed, scores, NEG) - log_row)
            d_probs = dot(value_rows[keys, :], d_query)
            d_scores = (probs * (d_probs - delta)).astype(BF)
            probs_low = probs.astype(BF)
            key_acc[:, keys] += dot(query, d_scores, ((1,), (1,)))
            value_acc[:, keys] += dot(d_query, probs_low, ((1,), (1,)))
            return d_sum + dot(qkv[HEAD_DIM : 2 * HEAD_DIM, keys], d_scores)

        d_sum = lax.fori_loop(0, j + 1, step, jnp.zeros((HEAD_DIM, block), F32))
        grads[at : at + HEAD_DIM, cols] = (d_sum * scale).astype(BF)

    grads[at + HEAD_DIM : at + 2 * HEAD_DIM, :] = (key_acc[...] * scale).astype(BF)
    grads[at + 2 * HEAD_DIM : at + 3 * HEAD_DIM, :] = value_acc[...].astype(BF)


def rows_of_keys(qkv, at, rows):
    rows[...] = qkv[at : at + HEAD_DIM, :].astype(F32).T.astype(BF)


def attention_forward_kernel(block, lengths, first, qkv, out, out_low, log_sum, key_rows):
    rows_of_keys(qkv, HEAD_DIM, key_rows)
    forward_pass(block, lengths[0], first, qkv, key_rows, out, out_low, log_sum)


def attention_backward_kernel(
    block, lengths, first, qkv, d_out, out, log_sum, grads, key_rows, value_rows, key_acc, value_acc
):
    rows_of_keys(qkv, HEAD_DIM, key_rows)
    rows_of_keys(qkv, 2 * HEAD_DIM, value_rows)
    backward_pass(
        block, lengths[0], first, qkv, d_out, out, log_sum, key_rows, value_rows, key_acc,
        value_acc, grads, 0,
    )


def attention_both_kernel(
    block, lengths, first, qkvd, result, out, log_sum, key_rows, value_rows, key_acc, value_acc
):
    rows_of_keys(qkvd, HEAD_DIM, key_rows)
    rows_of_keys(qkvd, 2 * HEAD_DIM, value_rows)
    forward_pass(block, lengths[0], first, qkvd, key_rows, out, result, log_sum)
    backward_pass(
        block, lengths[0], first, qkvd, qkvd.at[3 * HEAD_DIM :], out, log_sum, key_rows,
        value_rows, key_acc, value_acc, result, HEAD_DIM,
    )


def attention_call(kernel, outs, scratch, lengths, *args):
    vmem = pl.BlockSpec(memory_space=pltpu.VMEM)
    total = args[0].shape[1]
    return pl.pallas_call(
        partial(kernel, min(ATTENTION_BLOCK, total)),
        out_shape=[jax.ShapeDtypeStruct(shape, dtype) for shape, dtype in outs],
        in_specs=[pl.BlockSpec(memory_space=pltpu.SMEM)] + [vmem] * len(args),
        out_specs=[vmem] * len(outs),
        scratch_shapes=[pltpu.VMEM(shape, dtype) for shape, dtype in scratch],
        compiler_params=pltpu.CompilerParams(vmem_limit_bytes=VMEM_LIMIT),
    )(lengths, *args)


def attention_forward(lengths, first, qkv):
    total = qkv.shape[1]
    outs = [((HEAD_DIM, total), F32), ((HEAD_DIM, total), BF), ((1, total), F32)]
    scratch = [((total, HEAD_DIM), BF)]
    return attention_call(attention_forward_kernel, outs, scratch, lengths, first, qkv)


def attention_backward(lengths, first, qkv, d_out, out, log_sum):
    total = qkv.shape[1]
    outs = [((3 * HEAD_DIM, total), BF)]
    scratch = [((total, HEAD_DIM), BF)] * 2 + [((HEAD_DIM, total), F32)] * 2
    return attention_call(
        attention_backward_kernel, outs, scratch, lengths, first, qkv, d_out, out, log_sum
    )[0]


def attention_both(lengths, first, qkvd):
    total = qkvd.shape[1]
    outs = [((4 * HEAD_DIM, total), BF)]
    scratch = (
        [((HEAD_DIM, total), F32), ((1, total), F32)]
        + [((total, HEAD_DIM), BF)] * 2
        + [((HEAD_DIM, total), F32)] * 2
    )
    return attention_call(attention_both_kernel, outs, scratch, lengths, first, qkvd)[0]


class LineReduce:
    def __init__(self, place, total, low, from_left, from_right, view, sems, lane=0):
        self.place, self.total, self.low, self.view, self.lane = place, total, low, view, lane
        self.from_left, self.from_right = from_left, from_right
        self.send_right, self.send_left, self.recv_left, self.recv_right = sems

    def right(self, owner):
        return rcopy(
            self.low.at[self.view(owner)], self.from_left.at[self.view(owner)],
            self.send_right.at[self.lane, owner], self.recv_left.at[self.lane, owner],
            col=lax.rem(self.place.c + 1, self.place.cols),
        )

    def left(self, owner):
        cols = self.place.cols
        return rcopy(
            self.low.at[self.view(owner)], self.from_right.at[self.view(owner)],
            self.send_left.at[self.lane, owner], self.recv_right.at[self.lane, owner],
            col=lax.rem(self.place.c + cols - 1, cols),
        )

    def add_in(self, owner, arrived):
        view = self.view(owner)
        self.low[view] = (self.total[view] + arrived[view].astype(F32)).astype(BF)

    def step(self, time):
        c, cols = self.place.c, self.place.cols

        @pl.when(c <= time)
        def _():
            owner = cols - 1 - time + c

            @pl.when(c > 0)
            def _():
                self.right(owner).wait_recv()
                self.add_in(owner, self.from_left)

            self.right(owner).start()

        @pl.when(c >= cols - 1 - time)
        def _():
            owner = time + c - (cols - 1)

            @pl.when(c < cols - 1)
            def _():
                self.left(owner).wait_recv()
                self.add_in(owner, self.from_right)

            self.left(owner).start()

    def own(self):
        c, cols = self.place.c, self.place.cols
        view = self.view(c)

        @pl.when(c > 0)
        def _():
            self.right(c).wait_recv()

        @pl.when(c == 0)
        def _():
            self.from_left[view] = jnp.zeros_like(self.from_left[view])

        @pl.when(c < cols - 1)
        def _():
            self.left(c).wait_recv()

        @pl.when(c == cols - 1)
        def _():
            self.from_right[view] = jnp.zeros_like(self.from_right[view])

        return (
            self.total[view] + self.from_left[view].astype(F32) + self.from_right[view].astype(F32)
        )

    def finish(self):
        c, cols = self.place.c, self.place.cols
        for time in range(cols - 1):

            @pl.when(c <= time)
            def _():
                self.right(cols - 1 - time + c).wait_send()

            @pl.when(c >= cols - 1 - time)
            def _():
                self.left(time + c - (cols - 1)).wait_send()


def line_sum(place, total, low, from_left, from_right, full, sems, gather_sems, parts, produce, work):
    cols = place.cols
    length = total.shape[0] // cols
    piece = length // parts

    def rows(owner, lane):
        return pl.ds(pl.multiple_of(owner * length + lane * piece, piece), piece)

    reduces = [
        LineReduce(
            place, total, low, from_left, from_right,
            lambda owner, lane=lane: (rows(owner, lane), slice(None)), sems, lane,
        )
        for lane in range(parts)
    ]
    gathers = [
        LineGather(
            place, lambda block, lane=lane: full.at[rows(block, lane), :], *gather_sems, lane=lane
        )
        for lane in range(parts)
    ]
    for time in range(parts * (cols - 1) + cols):
        for lane in reversed(range(parts)):
            phase = time - lane * (cols - 1)
            if 0 <= phase < cols - 1:
                reduces[lane].step(phase)
            elif phase == cols - 1:
                mine = rows(place.c, lane)
                full[mine, :] = produce(reduces[lane].own(), mine)
                gathers[lane].hop(0)
            elif cols - 1 < phase <= 2 * (cols - 1):
                gathers[lane].hop(phase - (cols - 1))
        work(time)
    for lane in range(parts):
        reduces[lane].finish()
        gathers[lane].finish()


class GradExchange:
    def __init__(self, place, layer, mine, theirs, inbox, hand, hand_recv, send, recv):
        self.place, self.layer, self.mine, self.theirs, self.inbox = place, layer, mine, theirs, inbox
        self.hands, self.hand_recv, self.send, self.recv = hand, hand_recv, send, recv
        self.order = tuple(range(1, place.rows)) + (0,)

    def view(self, kind, block):
        length = self.inbox[kind].shape[-2 if kind in (0, 1) else -1]
        piece = pl.ds(pl.multiple_of(block * length, length), length)
        return {
            0: (slice(None), piece, slice(None)),
            1: (piece, slice(None)),
            2: (slice(None), piece),
            3: (slice(None), piece),
        }[kind]

    def passing(self, kind, step):
        view = self.view(kind, self.place.row_to(step))
        return rcopy(
            self.mine[kind].at[view], self.theirs[kind].at[view], self.hands.at[kind, step],
            self.hand_recv.at[kind, step], section=1 - self.place.s,
        )

    def sending(self, kind, step):
        view = self.view(kind, self.place.row_to(step))
        return rcopy(
            self.mine[kind].at[view], self.inbox[kind].at[step], self.send.at[kind, step],
            self.recv.at[kind, step], row=self.place.row_to(step),
        )

    def hand(self, kind):
        @pl.when(self.place.s != self.layer)
        def _():
            for step in self.order:
                self.passing(kind, step).start()

    def merge(self, kind):
        @pl.when(self.place.s == self.layer)
        def _():
            for step in self.order[:-1]:
                self.passing(kind, step).wait_recv()
                view = self.view(kind, self.place.row_to(step))
                self.mine[kind][view] = (
                    self.mine[kind][view].astype(F32) + self.theirs[kind][view].astype(F32)
                ).astype(BF)
                self.sending(kind, step).start()

    def take(self, kind, out):
        @pl.when(self.place.s == self.layer)
        def _():
            self.passing(kind, 0).wait_recv()
            view = self.view(kind, self.place.r)
            total = self.mine[kind][view].astype(F32) + self.theirs[kind][view].astype(F32)
            for step in self.order[:-1]:
                self.sending(kind, step).wait_recv()
                total = total + self.inbox[kind][step].astype(F32)
            out[...] = total

    def finish(self, kind):
        @pl.when(self.place.s == self.layer)
        def _():
            for step in self.order[:-1]:
                self.sending(kind, step).wait_send()

        @pl.when(self.place.s != self.layer)
        def _():
            for step in self.order:
                self.passing(kind, step).wait_send()


def unit_rows(values):
    centred = values - jnp.mean(values, axis=1, keepdims=True)
    rstd = lax.rsqrt(jnp.mean(centred * centred, axis=1, keepdims=True) + EPS)
    return centred * rstd, rstd


def middle_kernel(
    rows, cols,
    attn, wo0, branch0, x_full, vec_all, wq, wf, wo, wp, cot_full, cos, sin,
    attn_t, x1_full, wq_all, wf_all, wo_all, wp_all, normed_a, normed_m, qkvd, hidden, d_pre, branch, d_normed,
    total, low, from_left, from_right, pieces, slope,
    back_s, back_r, rs_a, rs_b, rs_c, rs_d, ag_a, ag_b, ag_c, ws, wr, wpas, wloc, as_, ar, local,
):
    place = Place(rows, cols)
    c = place.c
    tokens, full = x_full.shape
    width = full // cols
    place.greet(rows=True, cols=True, partner=True)
    back = RowExchange(
        place,
        lambda target: attn.at[:, pl.ds(pl.multiple_of(target * tokens, tokens), tokens)],
        lambda source: attn_t.at[pl.ds(pl.multiple_of(source * HEAD_DIM, HEAD_DIM), HEAD_DIM), :],
        back_s, back_r, local.at[0],
    )
    back.start()
    weights = WeightGather(
        place, 1, (wq, wf, wo, wp), (wq_all, wf_all, wo_all, wp_all), ws, wr, wpas, wloc
    )
    back.arrive()
    weights.start(0)
    weights.start(2)
    attn_rows = attn_t[...].astype(F32).T.astype(BF)
    tile = min(256, full)
    for at in range(0, full, tile):
        value = branch0[:, at : at + tile] + dot(attn_rows, wo0[:, at : at + tile])
        total[:, at : at + tile] = value
        low[:, at : at + tile] = value.astype(BF)

    def produce(summed, mine):
        return (x_full[mine, :].astype(F32) + summed + vec_all[0, 7:8, :]).astype(BF)

    def work(time):
        if time == 2:
            weights.start(1)
        if time == 4:
            weights.forward(0)
            weights.forward(2)
            weights.start(3)
        if time == 6:
            weights.ready(2)
            flipped = dot(cot_full[...], wo_all[...], ((1,), (1,))).T
            for head in range(rows):
                pieces[head, 3 * HEAD_DIM :, :] = flipped[
                    head * HEAD_DIM : (head + 1) * HEAD_DIM
                ].astype(BF)
        if time == 7:
            weights.forward(1)

    line_sum(
        place, total, low, from_left, from_right, x1_full, (rs_a, rs_b, rs_c, rs_d),
        (ag_a, ag_b, ag_c), PARTS, produce, work,
    )

    def row(index):
        return vec_all[1, index : index + 1, :]

    own = pl.ds(pl.multiple_of(c * width, width), width)
    norm_rows(x1_full, row(0), row(2), row(1), row(3), normed_a, normed_m)
    weights.ready(0)
    project_heads(
        normed_a, wq_all, lambda kind: vec_all[1, 4 + kind : 5 + kind, own], cos, sin, pieces, rows
    )
    exchange = RowExchange(
        place,
        lambda target: pieces.at[target],
        lambda source: qkvd.at[:, pl.ds(pl.multiple_of(source * tokens, tokens), tokens)],
        as_, ar, local.at[1],
    )
    exchange.start()
    weights.ready(1)
    feed_forward(
        normed_m, wf_all, lambda index: vec_all[1, pl.ds(8 + index, 1), own], hidden, slope
    )
    weights.forward(3)
    weights.ready(3)

    def times_slope(value, where):
        return (value * slope[:, where]).astype(BF)

    times_tiles(cot_full, wp_all, d_pre, times_slope, ((1,), (1,)))
    times_tiles(hidden, wp_all, branch)
    times_tiles(d_pre, wf_all, d_normed, None, ((1,), (1,)))
    exchange.arrive()
    exchange.finish()
    back.finish()
    for kind in range(4):
        weights.finish(kind)


def middle(rows, cols, attn, wo0, branch0, x_full, vec_all, wq, wf, wo, wp, cot_full, cos, sin):
    tokens, full = x_full.shape
    width, units = full // cols, wf.shape[1]
    outs = [
        ((width, tokens), BF),
        ((tokens, full), BF),
        ((3, full, width), BF),
        ((full, units), BF),
        ((width, full), BF),
        ((units, full), BF),
        ((tokens, full), BF),
        ((tokens, full), BF),
        ((4 * HEAD_DIM, rows * tokens), BF),
        ((tokens, units), BF),
        ((tokens, units), BF),
        ((tokens, full), F32),
        ((tokens, full), F32),
    ]
    scratch = (
        [
            pltpu.VMEM((tokens, full), F32),
            pltpu.VMEM((tokens, full), BF),
            pltpu.VMEM((tokens, full), BF),
            pltpu.VMEM((tokens, full), BF),
            pltpu.VMEM((rows, 4 * HEAD_DIM, tokens), BF),
            pltpu.VMEM((tokens, units), F32),
        ]
        + [dma(rows)] * 2
        + [dma(PARTS, cols)] * 7
        + [dma(4, rows)] * 3
        + [dma(4)]
        + [dma(rows)] * 2
        + [dma(2)]
    )
    return kernel_call(
        partial(middle_kernel, rows, cols), 2, outs, scratch,
        attn, wo0, branch0, x_full, vec_all, wq, wf, wo, wp, cot_full, cos, sin,
    )


def d_projection(inbox, at, cos, sin, rows, d_pre, small):
    width = rows * HEAD_DIM
    for kind in range(3):
        parts = []
        for head in range(rows):
            start = at + kind * HEAD_DIM
            block = inbox[head, start : start + HEAD_DIM, :].astype(F32)
            parts.append(turn(block, cos[...], sin[...], -1.0) if kind < 2 else block)
        values = jnp.concatenate(parts, axis=0).T.astype(BF)
        d_pre[:, kind * width : (kind + 1) * width] = values
        small[8 + kind : 9 + kind, :] = jnp.sum(values.astype(F32), axis=0, keepdims=True)


def d_norms(source, d_pre, wq, d_normed, gain_a, gain_m, total, low, sums, after=None):
    tokens = source.shape[0]
    width = wq.shape[2]
    tile = min(128, tokens)
    sums[...] = jnp.zeros_like(sums)

    @pl.loop(0, tokens // tile)
    def _(index):
        rows = pl.ds(pl.multiple_of(index * tile, tile), tile)
        d_a = dot(d_pre[rows, :width], wq[0], ((1,), (1,)))
        for kind in range(1, 3):
            d_a += dot(d_pre[rows, kind * width : (kind + 1) * width], wq[kind], ((1,), (1,)))
        d_m = d_normed[rows, :]
        unit, _ = unit_rows(source[rows, :].astype(F32))
        sums[0:1, :] += jnp.sum(d_a * unit, axis=0, keepdims=True)
        sums[1:2, :] += jnp.sum(d_m * unit, axis=0, keepdims=True)
        sums[2:3, :] += jnp.sum(d_a, axis=0, keepdims=True)
        sums[3:4, :] += jnp.sum(d_m, axis=0, keepdims=True)
        joined = d_a * gain_a + d_m * gain_m
        total[rows, :] = joined
        low[rows, :] = joined.astype(BF)
        if after is not None:
            after(rows, joined, unit)


def unit_sums(d_pre, small, width):
    for index in range(d_pre.shape[1] // width):
        piece = d_pre[:, index * width : (index + 1) * width].astype(F32)
        small[12 + index : 13 + index, :] = jnp.sum(piece, axis=0, keepdims=True)


def across_tokens(left, right, out, at=None):
    tile = min(256, left.shape[1])

    @pl.loop(0, left.shape[1] // tile)
    def _(index):
        cols = pl.ds(pl.multiple_of(index * tile, tile), tile)
        value = dot(left[:, cols], right[...], ((0,), (0,))).astype(BF)
        if at is None:
            out[cols, :] = value
        else:
            width = out.shape[2]
            for kind in range(3):
                out[kind, cols, :] = value[:, kind * width : (kind + 1) * width]


def grad_scratch(rows, full, width, units):
    shapes = [(3, full, width), (full, units), (width, full), (units, full)]
    part = full // rows
    pieces = [(3, part, width), (part, units), (width, part), (units, part)]
    return (
        [pltpu.VMEM(shape, BF) for shape in shapes] * 2
        + [pltpu.VMEM((rows,) + shape, BF) for shape in pieces]
        + [dma(4, rows)] * 4
    ), [(shape, F32) for shape in pieces]


def turning_kernel(
    rows, cols,
    back, x1_full, cot_full, vec_all, wq1, wo0, wp0, wf0, normed_a, normed_m, hidden, d_hidden, d_normed, slope0, cos, sin,
    attn_t, grad_full, d_out, d_hidden0, d_normed0, sums, small, gw_q, gw_f, gw_o, gw_p,
    inbox, d_pre, total, low, from_left, from_right, pieces,
    m0, m1, m2, m3, t0, t1, t2, t3, i0, i1, i2, i3, gh, ghr, gs, gr,
    back_s, back_r, rs_a, rs_b, rs_c, rs_d, ag_a, ag_b, ag_c, as_, ar, local,
):
    place = Place(rows, cols)
    c = place.c
    tokens, full = x1_full.shape
    width = full // cols
    place.greet(rows=True, cols=True, partner=True)

    def token_cols(ref):
        return lambda block: ref.at[:, pl.ds(pl.multiple_of(block * tokens, tokens), tokens)]

    returning = RowExchange(
        place, token_cols(back), lambda source: inbox.at[source], back_s, back_r, local.at[0]
    )
    returning.start()
    grads = GradExchange(
        place, 1, (m0, m1, m2, m3), (t0, t1, t2, t3), (i0, i1, i2, i3), gh, ghr, gs, gr
    )
    own = pl.ds(pl.multiple_of(c * width, width), width)
    small[...] = jnp.zeros_like(small)
    small[11:12, :] = jnp.sum(cot_full[:, own].astype(F32), axis=0, keepdims=True)
    unit_sums(d_hidden, small, width)
    across_tokens(hidden, cot_full, m3)
    grads.hand(3)
    returning.arrive()
    for head in range(rows):
        attn_t[head * HEAD_DIM : (head + 1) * HEAD_DIM, :] = inbox[head, :HEAD_DIM, :]
    d_projection(inbox, HEAD_DIM, cos, sin, rows, d_pre, small)
    d_norms(
        x1_full, d_pre, wq1, d_normed, vec_all[1, 0:1, :], vec_all[1, 1:2, :], total, low, sums
    )

    def produce(summed, mine):
        unit, rstd = unit_rows(x1_full[mine, :].astype(F32))
        moved = (
            summed
            - jnp.mean(summed, axis=1, keepdims=True)
            - unit * jnp.mean(summed * unit, axis=1, keepdims=True)
        )
        return (cot_full[mine, :].astype(F32) + rstd * moved).astype(BF)

    def work(time):
        if time == 0:
            across_tokens(normed_m, d_hidden, m1)
            grads.hand(1)
        if time == 1:
            grads.merge(3)
            across_tokens(normed_a, d_pre, m0, at=0)
            grads.hand(0)
        if time == 2:
            for at in range(0, full, 256):
                m2[:, at : at + 256] = dot(attn_t[...], cot_full[:, at : at + 256]).astype(BF)
            grads.hand(2)
        if time == 3:
            grads.merge(1)
        if time == 4:
            grads.merge(0)
            grads.merge(2)

    line_sum(
        place, total, low, from_left, from_right, grad_full, (rs_a, rs_b, rs_c, rs_d),
        (ag_a, ag_b, ag_c), PARTS, produce, work,
    )
    flipped = dot(grad_full[...], wo0[...], ((1,), (1,))).T
    for head in range(rows):
        pieces[head] = flipped[head * HEAD_DIM : (head + 1) * HEAD_DIM].astype(BF)
    exchange = RowExchange(
        place, lambda target: pieces.at[target], token_cols(d_out), as_, ar, local.at[1]
    )
    exchange.start()

    def times_slope(value, where):
        return (value * slope0[:, where]).astype(BF)

    times_tiles(grad_full, wp0, d_hidden0, times_slope, ((1,), (1,)))
    times_tiles(d_hidden0, wf0, d_normed0, None, ((1,), (1,)))
    exchange.arrive()
    exchange.finish()
    returning.finish()
    for kind, out in ((3, gw_p), (1, gw_f), (0, gw_q), (2, gw_o)):
        grads.take(kind, out)
    for kind in range(4):
        grads.finish(kind)


def turning(
    rows, cols, back, x1_full, cot_full, vec_all, wq1, wo0, wp0, wf0, normed_a, normed_m, hidden, d_hidden, d_normed, slope0, cos, sin
):
    tokens, full = x1_full.shape
    width, units = full // cols, wf0.shape[1]
    grad_refs, grad_outs = grad_scratch(rows, full, width, units)
    outs = [
        ((width, tokens), BF),
        ((tokens, full), BF),
        ((HEAD_DIM, rows * tokens), BF),
        ((tokens, units), BF),
        ((tokens, full), F32),
        ((8, full), F32),
        ((16, width), F32),
    ] + grad_outs
    scratch = (
        [
            pltpu.VMEM((rows, 4 * HEAD_DIM, tokens), BF),
            pltpu.VMEM((tokens, 3 * width), BF),
            pltpu.VMEM((tokens, full), F32),
            pltpu.VMEM((tokens, full), BF),
            pltpu.VMEM((tokens, full), BF),
            pltpu.VMEM((tokens, full), BF),
            pltpu.VMEM((rows, HEAD_DIM, tokens), BF),
        ]
        + grad_refs
        + [dma(rows)] * 2
        + [dma(PARTS, cols)] * 7
        + [dma(rows)] * 2
        + [dma(2)]
    )
    return kernel_call(
        partial(turning_kernel, rows, cols), 3, outs, scratch,
        back, x1_full, cot_full, vec_all, wq1, wo0, wp0, wf0, normed_a, normed_m, hidden, d_hidden, d_normed, slope0, cos, sin,
    )


def closing_kernel(
    rows, cols,
    back, x_full, x1_full, grad_full, vec_all, wq0, wo1, attn_t0, attn_t1, normed_a, normed_m, hidden, d_hidden, d_normed, branch1, sums1, small1, g1_q, g1_f, g1_o, g1_p, cos, sin,
    out_rows, grad_rows, small_out, gw_q, gw_f, gw_o, gw_p,
    inbox, d_pre, total, low, from_left, from_right, o_total, o_low, o_left, o_right, sums, small, line_sums, line_in, col_in, row_in, o_own, g_own,
    m0, m1, m2, m3, t0, t1, t2, t3, i0, i1, i2, i3, gh, ghr, gs, gr,
    back_s, back_r, rs_a, rs_b, rs_c, rs_d, os_a, os_b, os_c, os_d, ls_s, ls_r, cs_s, cs_r, rw_s, rw_r, sw_s, sw_r, local,
):
    place = Place(rows, cols)
    s, r, c = place.s, place.r, place.c
    tokens, full = x_full.shape
    width = full // cols
    place.greet(rows=True, cols=True, partner=True, cross_rows=True)
    own = pl.ds(pl.multiple_of(c * width, width), width)

    def features(owner):
        return (slice(None), pl.ds(pl.multiple_of(owner * width, width), width))

    returning = RowExchange(
        place,
        lambda target: back.at[:, pl.ds(pl.multiple_of(target * tokens, tokens), tokens)],
        lambda source: inbox.at[source],
        back_s, back_r, local.at[0],
    )
    returning.start()
    attn_rows = attn_t1[...].astype(F32).T.astype(BF)
    tile = min(256, full)
    for at in range(0, full, tile):
        value = branch1[:, at : at + tile] + dot(attn_rows, wo1[:, at : at + tile])
        o_total[:, at : at + tile] = value
        o_low[:, at : at + tile] = value.astype(BF)
    out_sum = LineReduce(
        place, o_total, o_low, o_left, o_right, features, (os_a, os_b, os_c, os_d)
    )
    grad_sum = LineReduce(
        place, total, low, from_left, from_right, features, (rs_a, rs_b, rs_c, rs_d)
    )
    grads = GradExchange(
        place, 0, (m0, m1, m2, m3), (t0, t1, t2, t3), (i0, i1, i2, i3), gh, ghr, gs, gr
    )
    out_sum.step(0)
    across_tokens(hidden, grad_full, m3)
    grads.hand(3)
    small[...] = jnp.zeros_like(small)
    small[1] = small1[...]
    small[0, 11:12, :] = jnp.sum(grad_full[:, own].astype(F32), axis=0, keepdims=True)
    unit_sums(d_hidden, small.at[0], width)
    returning.arrive()
    d_projection(inbox, 0, cos, sin, rows, d_pre, small.at[0])
    lane = lax.broadcasted_iota(jnp.int32, (min(128, tokens), 128), 1)

    def row_sums(where, joined, unit):
        first = jnp.sum(joined, axis=1, keepdims=True)
        second = jnp.sum(joined * unit, axis=1, keepdims=True)
        both = jnp.where(lane == 0, first, jnp.where(lane == 1, second, 0.0))
        line_sums[:, where] = both.T[:8]

    d_norms(
        x_full, d_pre, wq0, d_normed, vec_all[0, 0:1, :], vec_all[0, 1:2, :], total, low,
        sums.at[0], row_sums,
    )
    sums[1] = sums1[...]

    def line_copy(step):
        return rcopy(
            line_sums, line_in.at[step], ls_s.at[step], ls_r.at[step], col=place.col_to(step)
        )

    def col_copy(step):
        target = place.col_to(step)
        piece = sums.at[:, :, pl.ds(pl.multiple_of(target * width, width), width)]
        return rcopy(piece, col_in.at[step], cs_s.at[step], cs_r.at[step], col=target)

    def row_copy(ds, step):
        index = ds * rows + step
        layer = lax.rem(s + ds, 2)
        return rcopy(
            small.at[layer], row_in.at[index], rw_s.at[index], rw_r.at[index],
            section=layer, row=place.row_to(step),
        )

    for step in range(1, cols):
        line_copy(step).start()
        col_copy(step).start()
    grad_sum.step(0)
    out_sum.step(1)
    across_tokens(normed_m, d_hidden, m1)
    grads.hand(1)
    grads.merge(3)
    across_tokens(normed_a, d_pre, m0, at=0)
    grads.hand(0)
    out_sum.step(2)
    grad_sum.step(1)
    for at in range(0, full, tile):
        m2[:, at : at + tile] = dot(attn_t0[...], grad_full[:, at : at + tile]).astype(BF)
    grads.hand(2)
    grads.merge(1)
    for step in range(1, cols):
        col_copy(step).wait_recv()
    head = sums[:, :, own]
    for step in range(1, cols):
        head = head + col_in[step]
    small[:, :8, :] = head
    others = [(ds, step) for ds in range(2) for step in range(rows) if ds or step]
    for ds, step in others:
        row_copy(ds, step).start()
    out_own = x1_full[:, own].astype(F32) + out_sum.own() + vec_all[1, 7:8, own]
    o_own[1] = out_own.astype(BF)
    o_own[0] = x1_full[:, own]
    grads.merge(0)
    grads.merge(2)

    def swap_copy(index, source, target):
        return rcopy(
            source.at[1 - s], target.at[s], sw_s.at[index], sw_r.at[index], section=1 - s
        )

    out_swap = swap_copy(0, o_own, out_rows)
    grad_swap = swap_copy(1, g_own, grad_rows)
    out_swap.start()
    out_keep = pltpu.make_async_copy(o_own.at[s], out_rows.at[s], local.at[1])
    out_keep.start()
    grad_sum.step(2)
    joined = line_sums[...]
    for step in range(1, cols):
        line_copy(step).wait_recv()
        joined = joined + line_in[step]
    wide = jnp.concatenate([joined, jnp.zeros((120, tokens), F32)], axis=0).T
    unit, rstd = unit_rows(x_full[...].astype(F32))
    o_total[...] = unit
    moved = (
        grad_sum.own() - wide[:, 0:1] / full - o_total[:, own] * (wide[:, 1:2] / full)
    )
    g_own[0] = (grad_full[:, own].astype(F32) + rstd * moved).astype(BF)
    g_own[1] = grad_full[:, own]
    grad_swap.start()
    grad_keep = pltpu.make_async_copy(g_own.at[s], grad_rows.at[s], local.at[2])
    grad_keep.start()
    mine = small[s]
    for ds, step in others:
        row_copy(ds, step).wait_recv()
        mine = mine + row_in[ds * rows + step]
    small_out[...] = mine
    for kind, out, later in ((3, gw_p, g1_p), (1, gw_f, g1_f), (0, gw_q, g1_q), (2, gw_o, g1_o)):

        @pl.when(s == 1)
        def _():
            out[...] = later[...]

        grads.take(kind, out)
    out_keep.wait()
    grad_keep.wait()
    out_swap.wait()
    grad_swap.wait()
    returning.finish()
    out_sum.finish()
    grad_sum.finish()
    for step in range(1, cols):
        line_copy(step).wait_send()
        col_copy(step).wait_send()
    for ds, step in others:
        row_copy(ds, step).wait_send()
    for kind in range(4):
        grads.finish(kind)


def closing(
    rows, cols, back, x_full, x1_full, grad_full, vec_all, wq0, wo1, attn_t0, attn_t1, normed_a, normed_m, hidden, d_hidden, d_normed, branch1, sums1, small1, later, cos, sin
):
    tokens, full = x_full.shape
    width, units = full // cols, hidden.shape[1]
    grad_refs, grad_outs = grad_scratch(rows, full, width, units)
    outs = [
        ((2, tokens, width), BF),
        ((2, tokens, width), BF),
        ((16, width), F32),
    ] + grad_outs
    wide = [
        pltpu.VMEM((tokens, full), F32),
        pltpu.VMEM((tokens, full), BF),
        pltpu.VMEM((tokens, full), BF),
        pltpu.VMEM((tokens, full), BF),
    ]
    scratch = (
        [pltpu.VMEM((rows, 3 * HEAD_DIM, tokens), BF), pltpu.VMEM((tokens, 3 * width), BF)]
        + wide
        + wide
        + [
            pltpu.VMEM((2, 8, full), F32),
            pltpu.VMEM((2, 16, width), F32),
            pltpu.VMEM((8, tokens), F32),
            pltpu.VMEM((cols, 8, tokens), F32),
            pltpu.VMEM((cols, 2, 8, width), F32),
            pltpu.VMEM((2 * rows, 16, width), F32),
            pltpu.VMEM((2, tokens, width), BF),
            pltpu.VMEM((2, tokens, width), BF),
        ]
        + grad_refs
        + [dma(rows)] * 2
        + [dma(1, cols)] * 8
        + [dma(cols)] * 4
        + [dma(2 * rows)] * 2
        + [dma(2)] * 2
        + [dma(3)]
    )
    return kernel_call(
        partial(closing_kernel, rows, cols), 4, outs, scratch,
        back, x_full, x1_full, grad_full, vec_all, wq0, wo1, attn_t0, attn_t1, normed_a, normed_m, hidden, d_hidden, d_normed, branch1, sums1, small1, *later, cos, sin,
    )


def relay_body(
    hidden_in,
    cotangent,
    lengths,
    norm_gains,
    norm_biases,
    w_qkv,
    b_qkv,
    w_out,
    w_fc,
    b_fc,
    w_proj,
    b_out,
):
    rows, cols = lax.axis_size("row"), lax.axis_size("col")
    tokens, width = hidden_in.shape[1:]
    section = lax.axis_index("section")
    lengths_row = lax.dynamic_index_in_dim(lengths, section, 0, keepdims=False)
    all_tokens = jnp.arange(tokens * rows, dtype=jnp.int32)
    my_tokens = lax.axis_index("row") * tokens + jnp.arange(tokens, dtype=jnp.int32)
    starts, segment, position = token_layout(lengths_row, my_tokens)
    cos, sin = rotary_tables(position, ROT)
    cos, sin = cos.T, sin.T
    segments = segment_of(all_tokens, starts)
    labels = jnp.arange(1, lengths_row.shape[0], dtype=jnp.int32)
    first = jnp.sum(
        jnp.where(segments[:, None] == labels[None, :], starts[None, 1:], 0), axis=1
    )[None]
    prompt = lengths_row[:1]
    vectors = jnp.concatenate(
        [norm_gains[0], norm_biases[0], b_qkv[0], b_out, b_fc[0].reshape(-1, width)], axis=0
    )
    vectors = jnp.pad(vectors, ((0, 16 - vectors.shape[0]), (0, 0)))
    blocks = (w_qkv[0], w_fc[0], w_out[0], w_proj[0])
    (
        x_full, cot_full, vec_all, wq0, wf0, wo0, wp0, normed_a0, normed_m0, qkv0, hidden0, slope0, branch0,
    ) = opening(rows, cols, hidden_in, cotangent, vectors, *blocks, cos, sin)
    out0, low0, log0 = attention_forward(prompt, first, qkv0)
    (
        attn_t0, x1_full, wq1, wf1, wo1, wp1, normed_a1, normed_m1, qkvd1, hidden1, d_hidden1, branch1, d_normed1,
    ) = middle(
        rows, cols, low0, wo0, branch0, x_full, vec_all, *blocks, cot_full, cos, sin
    )
    back1 = attention_both(prompt, first, qkvd1)
    attn_t1, grad_full, d_out0, d_hidden0, d_normed0, sums1, small1, *later = turning(
        rows, cols, back1, x1_full, cot_full, vec_all, wq1, wo0, wp0, wf0, normed_a1, normed_m1,
        hidden1, d_hidden1, d_normed1, slope0, cos, sin,
    )
    back0 = attention_backward(prompt, first, qkv0, d_out0, out0, log0)
    out_rows, grad_rows, small, gw_q, gw_f, gw_o, gw_p = closing(
        rows, cols, back0, x_full, x1_full, grad_full, vec_all, wq0, wo1, attn_t0, attn_t1,
        normed_a0, normed_m0, hidden0, d_hidden0, d_normed0, branch1, sums1, small1, later, cos, sin,
    )
    return (
        out_rows[None],
        grad_rows[None],
        small[None, 0:2],
        small[None, 2:4],
        gw_q[None],
        small[None, 8:11],
        gw_o[None],
        gw_f[None],
        small[12 : 12 + b_fc.shape[1] // width].reshape(1, -1),
        gw_p[None],
        small[11:12],
    )


def fits(mesh):
    rows, cols = mesh.shape["row"], mesh.shape["col"]
    return rows == cols and MODEL_WIDTH == rows * cols * HEAD_DIM


def solution(mesh):
    return jax.shard_map(
        relay_body if fits(mesh) else body,
        mesh=mesh,
        in_specs=(
            P(None, "row", "col"),
            P(None, "row", "col"),
            P(),
            P("section", None, "col"),
            P("section", None, "col"),
            P("section", None, "row", "col"),
            P("section", None, "col"),
            P("section", "col", "row"),
            P("section", "row", "col"),
            P("section", "col"),
            P("section", "col", "row"),
            P("section", "col"),
        ),
        out_specs=(
            P("section", None, "row", "col"),
            P("section", None, "row", "col"),
            P("section", None, "col"),
            P("section", None, "col"),
            P("section", None, "row", "col"),
            P("section", None, "col"),
            P("section", "col", "row"),
            P("section", "row", "col"),
            P("section", "col"),
            P("section", "col", "row"),
            P("section", "col"),
        ),
        check_vma=False,
    )
```

```python
from functools import partial
import math

import jax
import jax.numpy as jnp
from jax import lax
from jax.experimental import pallas as pl
from jax.experimental.pallas import tpu as pltpu
from jax.sharding import PartitionSpec as P

MODEL_WIDTH = 1024
HEAD_DIM = 64
ROT = 16
SECTION, ROW, COL = "section", "row", "col"


EPS = 1e-05
NEG = -1e30


def from_partner(value, axis, apart):
    mask = 2**apart
    pairs = [(source, source ^ mask) for source in range(lax.axis_size(axis))]
    return lax.ppermute(value, axis, pairs)


def segment_of(token_ids, starts):
    return jnp.sum((token_ids[:, None] >= starts[None, 1:]).astype(jnp.int32), axis=1)


def token_layout(lengths_row, token_ids):
    starts = jnp.cumsum(lengths_row) - lengths_row
    segment = segment_of(token_ids, starts)
    labels = jnp.arange(1, lengths_row.shape[0], dtype=jnp.int32)
    seg_begin = jnp.sum(jnp.where(segment[:, None] == labels[None, :], starts[None, 1:], 0), axis=1)
    position = jnp.where(segment == 0, token_ids, lengths_row[0] + token_ids - seg_begin)
    return (starts, segment, position)


def rotary_tables(position, turned):
    half_rot = turned // 2
    freqs = 10000.0 ** (-(2.0 * jnp.arange(half_rot, dtype=jnp.float32)) / turned)
    angles = position.astype(jnp.float32)[:, None] * freqs[None, :]
    return (jnp.cos(angles), jnp.sin(angles))


def rotate(values, cos_table, sin_table, direction):
    half_rot = cos_table.shape[-1]
    lower = values[..., :half_rot]
    upper = values[..., half_rot : 2 * half_rot]
    cos_cast = cos_table[:, None, :]
    sin_cast = direction * sin_table[:, None, :]
    return jnp.concatenate(
        [
            lower * cos_cast - upper * sin_cast,
            upper * cos_cast + lower * sin_cast,
            values[..., 2 * half_rot :],
        ],
        axis=-1,
    )


def permitted(query_seg, query_tok, key_seg, key_tok):
    from_prompt = (key_seg[None, :] == 0) & (query_seg[:, None] > 0)
    same_causal = (key_seg[None, :] == query_seg[:, None]) & (
        key_tok[None, :] <= query_tok[:, None]
    )
    return from_prompt | same_causal


def attend(running, key_piece, value_piece, query3, layout):
    run_max, run_sum, totals = running
    piece_len = key_piece.shape[0]
    key3 = key_piece.reshape(piece_len, query3.shape[1], query3.shape[2])
    value3 = value_piece.reshape(piece_len, query3.shape[1], query3.shape[2])
    key_tok = jnp.arange(piece_len, dtype=jnp.int32)
    key_seg = segment_of(key_tok, layout["starts"])
    allowed = permitted(layout["segment"], layout["tokens"], key_seg, key_tok)[None]
    scores = jnp.einsum("qhd,khd->hqk", query3, key3, preferred_element_type=jnp.float32) * (
        1.0 / math.sqrt(query3.shape[2])
    )
    masked = jnp.where(allowed, scores, NEG)
    new_max = jnp.maximum(run_max, jnp.max(masked, axis=-1))
    weights = jnp.where(allowed, jnp.exp(masked - new_max[..., None]), 0.0)
    run_sum = jnp.sum(weights, axis=-1)
    totals = jnp.einsum(
        "hqk,khd->hqd", weights.astype(jnp.bfloat16), value3, preferred_element_type=jnp.float32
    )
    return (new_max, run_sum, totals)


def layer_forward(x, full, weights, layout, complete_gains, complete_shifts):
    w_query, b_query, w_output, w_hidden, b_hidden, w_project, b_output = weights
    row_tokens, local_width = x.shape
    heads_local = local_width // HEAD_DIM
    shaped = (row_tokens, heads_local, HEAD_DIM)
    as_float = full.astype(jnp.float32)
    row_mean = jnp.mean(as_float, axis=1, keepdims=True)
    centred = as_float - row_mean
    rstd = lax.rsqrt(jnp.mean(centred * centred, axis=1, keepdims=True) + EPS)
    unit = centred * rstd
    normed_a = (unit * complete_gains[0] + complete_shifts[0]).astype(jnp.bfloat16)
    normed_m = (unit * complete_gains[1] + complete_shifts[1]).astype(jnp.bfloat16)
    projected = (
        jnp.einsum("td,cde->cte", normed_a, w_query, preferred_element_type=jnp.float32)
        + b_query[:, None, :]
    )
    cos_table, sin_table = layout["cos_table"], layout["sin_table"]
    query3 = rotate(projected[0].reshape(shaped), cos_table, sin_table, 1.0).astype(jnp.bfloat16)
    key_flat = (
        rotate(projected[1].reshape(shaped), cos_table, sin_table, 1.0)
        .reshape(row_tokens, local_width)
        .astype(jnp.bfloat16)
    )
    value_flat = projected[2].astype(jnp.bfloat16)
    key_full = lax.all_gather(key_flat, ROW, axis=0, tiled=True)
    value_full = lax.all_gather(value_flat, ROW, axis=0, tiled=True)
    initial = (
        jnp.full((heads_local, row_tokens), NEG, jnp.float32),
        jnp.zeros((heads_local, row_tokens), jnp.float32),
        jnp.zeros((heads_local, row_tokens, HEAD_DIM), jnp.float32),
    )
    run_max, run_sum, totals = attend(initial, key_full, value_full, query3, layout)
    out_exact = totals / run_sum[..., None]
    log_sum = run_max + jnp.log(run_sum)
    attn_flat = (
        jnp.transpose(out_exact, (1, 0, 2)).reshape(row_tokens, local_width).astype(jnp.bfloat16)
    )
    hidden_pre = jnp.dot(normed_m, w_hidden, preferred_element_type=jnp.float32) + b_hidden
    hidden = jax.nn.gelu(hidden_pre, approximate=False).astype(jnp.bfloat16)
    branch = jnp.dot(attn_flat, w_output, preferred_element_type=jnp.float32) + jnp.dot(
        hidden, w_project, preferred_element_type=jnp.float32
    )
    summed = lax.psum_scatter(
        branch.astype(jnp.bfloat16), COL, scatter_dimension=1, tiled=True
    ).astype(jnp.float32)
    output = (x.astype(jnp.float32) + summed + b_output).astype(jnp.bfloat16)
    state = dict(
        unit=unit, rstd=rstd, normed_a=normed_a, normed_m=normed_m, query3=query3,
        key_full=key_full, value_full=value_full, attn_flat=attn_flat, out_exact=out_exact,
        log_sum=log_sum, hidden_pre=hidden_pre, hidden=hidden,
    )
    return output, state


def layer_backward(state, grad_in, grad_full, weights, layout, complete_gains, scatter_tokens):
    w_query, b_query, w_output, w_hidden, b_hidden, w_project, b_output = weights
    row_tokens = state["normed_a"].shape[0]
    local_width = w_output.shape[0]
    heads_local = local_width // HEAD_DIM
    shaped = (row_tokens, heads_local, HEAD_DIM)
    score_scale = 1.0 / math.sqrt(HEAD_DIM)
    total_tokens = state["key_full"].shape[0]
    key_block = min(512, total_tokens)
    grad_wout = jnp.einsum(
        "te,td->ed", state["attn_flat"], grad_full, preferred_element_type=jnp.float32
    )
    grad_wproj = jnp.einsum(
        "tf,td->fd", state["hidden"], grad_full, preferred_element_type=jnp.float32
    )
    grad_bout = jnp.sum(grad_in.astype(jnp.float32), axis=0)
    grad_attn = jnp.einsum(
        "td,ed->te", grad_full, w_output, preferred_element_type=jnp.float32
    ).astype(jnp.bfloat16)
    grad_hidden = jnp.einsum("td,fd->tf", grad_full, w_project, preferred_element_type=jnp.float32)
    gelu_value, gelu_back = jax.vjp(partial(jax.nn.gelu, approximate=False), state["hidden_pre"])
    grad_hpre = gelu_back(grad_hidden)[0].astype(jnp.bfloat16)
    grad_wfc = jnp.einsum(
        "td,tf->df", state["normed_m"], grad_hpre, preferred_element_type=jnp.float32
    )
    grad_bfc = jnp.sum(grad_hpre.astype(jnp.float32), axis=0)
    grad_normed_m = jnp.einsum("tf,df->td", grad_hpre, w_hidden, preferred_element_type=jnp.float32)
    grad_out3 = grad_attn.reshape(shaped)
    query3 = state["query3"]
    delta = jnp.sum(
        jnp.transpose(grad_out3.astype(jnp.float32), (1, 0, 2)) * state["out_exact"], axis=-1
    )
    grad_query = jnp.zeros(shaped, jnp.float32)
    key_terms = []
    value_terms = []
    for block_no in range(total_tokens // key_block):
        begin_at = block_no * key_block
        key_part = state["key_full"][begin_at : begin_at + key_block].reshape(
            key_block, heads_local, HEAD_DIM
        )
        value_part = state["value_full"][begin_at : begin_at + key_block].reshape(
            key_block, heads_local, HEAD_DIM
        )
        key_tok = begin_at + jnp.arange(key_block, dtype=jnp.int32)
        key_seg = segment_of(key_tok, layout["starts"])
        allowed = permitted(layout["segment"], layout["tokens"], key_seg, key_tok)[None]
        scores = (
            jnp.einsum("qhd,khd->hqk", query3, key_part, preferred_element_type=jnp.float32)
            * score_scale
        )
        probs = jnp.where(
            allowed,
            jnp.exp(jnp.where(allowed, scores, NEG) - state["log_sum"][..., None]),
            0.0,
        )
        grad_probs = jnp.einsum(
            "qhd,khd->hqk", grad_out3, value_part, preferred_element_type=jnp.float32
        )
        grad_scores = (probs * (grad_probs - delta[..., None])).astype(jnp.bfloat16)
        grad_query = grad_query + jnp.einsum(
            "hqk,khd->qhd", grad_scores, key_part, preferred_element_type=jnp.float32
        )
        key_terms.append(
            jnp.einsum(
                "hqk,qhd->khd", grad_scores, query3, preferred_element_type=jnp.float32
            ).reshape(key_block, local_width)
            * score_scale
        )
        value_terms.append(
            jnp.einsum(
                "hqk,qhd->khd",
                probs.astype(jnp.bfloat16),
                grad_out3,
                preferred_element_type=jnp.float32,
            ).reshape(key_block, local_width)
        )
    grad_query = grad_query * score_scale
    kv_terms = jnp.concatenate(
        [jnp.concatenate(key_terms, axis=0), jnp.concatenate(value_terms, axis=0)], axis=1
    )
    kv_grads = lax.psum_scatter(
        kv_terms.astype(jnp.bfloat16), ROW, scatter_dimension=0, tiled=True
    ).astype(jnp.float32)
    grad_key = kv_grads[:, :local_width].reshape(shaped)
    grad_value = kv_grads[:, local_width:]
    cos_table, sin_table = layout["cos_table"], layout["sin_table"]
    grad_pre = jnp.stack(
        [
            rotate(grad_query, cos_table, sin_table, -1.0).reshape(row_tokens, local_width),
            rotate(grad_key, cos_table, sin_table, -1.0).reshape(row_tokens, local_width),
            grad_value,
        ]
    ).astype(jnp.bfloat16)
    grad_wqkv = jnp.einsum(
        "td,cte->cde", state["normed_a"], grad_pre, preferred_element_type=jnp.float32
    )
    grad_bqkv = jnp.sum(grad_pre.astype(jnp.float32), axis=1)
    grad_normed_a = jnp.einsum("cte,cde->td", grad_pre, w_query, preferred_element_type=jnp.float32)
    unit = state["unit"]
    grad_gains = jnp.stack(
        [jnp.sum(grad_normed_a * unit, axis=0), jnp.sum(grad_normed_m * unit, axis=0)]
    )
    grad_shifts = jnp.stack([jnp.sum(grad_normed_a, axis=0), jnp.sum(grad_normed_m, axis=0)])
    grad_unit = grad_normed_a * complete_gains[0] + grad_normed_m * complete_gains[1]
    big = (grad_wqkv, grad_wout, grad_wfc, grad_wproj)
    big = tuple(member.astype(jnp.bfloat16) for member in big)
    shared = (grad_gains, grad_shifts)
    local = (grad_bqkv, grad_bfc, grad_bout)
    if scatter_tokens:
        piece = lax.psum_scatter(
            grad_unit.astype(jnp.bfloat16), COL, scatter_dimension=0, tiled=True
        ).astype(jnp.float32)
        rows = piece.shape[0]
        start = lax.axis_index(COL) * rows
        unit_part = lax.dynamic_slice_in_dim(unit, start, rows, 0)
        rstd_part = lax.dynamic_slice_in_dim(state["rstd"], start, rows, 0)
        grad_part = lax.dynamic_slice_in_dim(grad_full, start, rows, 0).astype(jnp.float32)
        moved = (
            piece
            - jnp.mean(piece, axis=1, keepdims=True)
            - unit_part * jnp.mean(piece * unit_part, axis=1, keepdims=True)
        )
        grad_input = (grad_part + rstd_part * moved).astype(jnp.bfloat16)
    else:
        sums = lax.psum(
            jnp.stack([jnp.sum(grad_unit, axis=1), jnp.sum(grad_unit * unit, axis=1)]), COL
        )
        piece = lax.psum_scatter(
            grad_unit.astype(jnp.bfloat16), COL, scatter_dimension=1, tiled=True
        ).astype(jnp.float32)
        width = piece.shape[1]
        unit_part = lax.dynamic_slice_in_dim(unit, lax.axis_index(COL) * width, width, 1)
        moved = (
            piece
            - sums[0][:, None] / MODEL_WIDTH
            - unit_part * (sums[1][:, None] / MODEL_WIDTH)
        )
        grad_input = (grad_in.astype(jnp.float32) + state["rstd"] * moved).astype(jnp.bfloat16)
    return grad_input, big, shared, local


def body(
    hidden_in,
    cotangent,
    lengths,
    norm_gains,
    norm_biases,
    w_qkv,
    b_qkv,
    w_out,
    w_fc,
    b_fc,
    w_proj,
    b_out,
):
    row_tokens = hidden_in.shape[1]
    local_width = hidden_in.shape[2]
    section = lax.axis_index(SECTION)
    is_first = section == 0
    my_tokens = lax.axis_index(ROW) * row_tokens + jnp.arange(row_tokens, dtype=jnp.int32)
    x0 = lax.dynamic_index_in_dim(hidden_in, section, 0, keepdims=False)
    cot = lax.dynamic_index_in_dim(cotangent, section, 0, keepdims=False)
    lengths_row = lax.dynamic_index_in_dim(lengths, section, 0, keepdims=False)
    starts, segment, position = token_layout(lengths_row, my_tokens)
    cos_table, sin_table = rotary_tables(position, ROT)
    layout = {
        "starts": starts,
        "segment": segment,
        "tokens": my_tokens,
        "cos_table": cos_table,
        "sin_table": sin_table,
    }
    both = (SECTION, ROW)
    gains = lax.all_gather(norm_gains[0], (SECTION, COL), axis=0)
    shifts = lax.all_gather(norm_biases[0], (SECTION, COL), axis=0)
    cols = lax.axis_size(COL)

    def whole(vectors):
        split = vectors.reshape(2, cols, 2, local_width)
        return jnp.transpose(split, (0, 2, 1, 3)).reshape(2, 2, cols * local_width)

    gains, shifts = whole(gains), whole(shifts)
    biases = [lax.all_gather(member[0], SECTION, axis=0) for member in (b_qkv, b_fc, b_out)]
    x0_full = lax.all_gather(x0, COL, axis=1, tiled=True)
    rows = lax.axis_size(ROW)

    def unite(member, axis):
        gathered = lax.all_gather(member[0], both, axis=0)
        pieces = gathered.reshape((2, rows) + gathered.shape[1:])
        return [
            jnp.concatenate([pieces[layer, row] for row in range(rows)], axis=axis)
            for layer in range(2)
        ]

    w_query, w_hidden = unite(w_qkv, 1), unite(w_fc, 0)
    w_output, w_project = unite(w_out, 1), unite(w_proj, 1)
    weights = [
        (
            w_query[layer],
            biases[0][layer],
            w_output[layer],
            w_hidden[layer],
            biases[1][layer],
            w_project[layer],
            biases[2][layer],
        )
        for layer in range(2)
    ]
    out0, state0 = layer_forward(x0, x0_full, weights[0], layout, gains[0], shifts[0])
    x1_full = lax.all_gather(out0, COL, axis=1, tiled=True)
    cot_full = lax.all_gather(cot, COL, axis=1, tiled=True)
    out1, state1 = layer_forward(out0, x1_full, weights[1], layout, gains[1], shifts[1])
    grad1_part, big1, shared1, local1 = layer_backward(
        state1, cot, cot_full, weights[1], layout, gains[1], True
    )
    grad1_full = lax.all_gather(grad1_part, COL, axis=0, tiled=True)
    grad1 = lax.dynamic_slice_in_dim(
        grad1_full, lax.axis_index(COL) * local_width, local_width, 1
    )
    grad0, big0, shared0, local0 = layer_backward(
        state0, grad1, grad1_full, weights[0], layout, gains[0], False
    )

    def swap(first, second):
        mine = jnp.where(is_first, first, second)
        theirs = from_partner(jnp.where(is_first, second, first), SECTION, 0)
        return jnp.where(is_first, jnp.stack([mine, theirs]), jnp.stack([theirs, mine]))[None]

    out_rows = swap(out0, out1)
    grad_rows = swap(grad0, grad1)

    def scatter(first, second, axis):
        length = first.shape[axis] // rows
        pieces = jnp.stack(
            [
                lax.slice_in_dim(member, row * length, (row + 1) * length, axis=axis)
                for member in (first, second)
                for row in range(rows)
            ]
        )
        return lax.psum_scatter(pieces, both, scatter_dimension=0, tiled=True).astype(jnp.float32)

    large = [scatter(a, b, axis) for a, b, axis in zip(big0, big1, (1, 1, 0, 1))]
    shared_sums = lax.psum(
        tuple(jnp.stack([a, b]) for a, b in zip(shared0, shared1)), (SECTION, ROW, COL)
    )
    shared_mine = [
        lax.dynamic_slice(
            member,
            (section, 0, lax.axis_index(COL) * local_width),
            (1, 2, local_width),
        )
        for member in shared_sums
    ]
    local_sums = lax.psum(tuple(jnp.stack([a, b]) for a, b in zip(local0, local1)), both)
    local_mine = [lax.dynamic_index_in_dim(member, section, 0) for member in local_sums]
    return (
        out_rows,
        grad_rows,
        shared_mine[0],
        shared_mine[1],
        large[0],
        local_mine[0],
        large[1],
        large[2],
        local_mine[1],
        large[3],
        local_mine[2],
    )


BF = jnp.bfloat16
F32 = jnp.float32
BY_MESH = pl.DeviceIdType.MESH
VMEM_LIMIT = 60 * 2**20
QUERY_BLOCK = 256
KEY_BLOCK = 512
PROMPT_LEAST = 768
PARTS = 2
CHUNKS = 16
LAG = 4


def dot(a, b, contract=((1,), (0,))):
    return lax.dot_general(a, b, (contract, ((), ())), preferred_element_type=F32)


def rcopy(src, dst, ssem, rsem, **device):
    return pltpu.make_async_remote_copy(
        src_ref=src,
        dst_ref=dst,
        send_sem=ssem,
        recv_sem=rsem,
        device_id=device,
        device_id_type=BY_MESH,
    )


class Place:
    def __init__(self, rows, cols):
        self.rows, self.cols = rows, cols
        self.s = lax.axis_index(SECTION)
        self.r = lax.axis_index(ROW)
        self.c = lax.axis_index(COL)

    def row_to(self, step):
        return lax.rem(self.r + step, self.rows)

    def row_from(self, step):
        return lax.rem(self.r + self.rows - step, self.rows)

    def beside(self, way):
        if way == 0:
            return self.r + 1 - 2 * lax.rem(self.r, 2)
        return lax.rem(self.r + 2, 4)

    def across(self):
        return 3 - self.r

    def col_to(self, step):
        return lax.rem(self.c + step, self.cols)

    def col_from(self, step):
        return lax.rem(self.c + self.cols - step, self.cols)

    def greet(self, rows=False, cols=False, partner=False, cross_cols=False, cross_rows=False):
        barrier = pltpu.get_barrier_semaphore()
        count = 0

        def signal(**device):
            pl.semaphore_signal(barrier, inc=1, device_id=device, device_id_type=BY_MESH)

        if rows:
            for step in range(1, self.rows):
                signal(row=self.row_to(step))
                count += 1
        if cols:
            for step in range(1, self.cols):
                signal(col=self.col_to(step))
                count += 1
        if partner:
            signal(section=1 - self.s)
            count += 1
        if cross_cols:
            for step in range(1, self.cols):
                signal(section=1 - self.s, col=self.col_to(step))
                count += 1
        if cross_rows:
            for step in range(1, self.rows):
                signal(section=1 - self.s, row=self.row_to(step))
                count += 1
        pl.semaphore_wait(barrier, count)


class LineGather:
    def __init__(self, place, view, send_right, send_left, recv, lane=0):
        self.place, self.view, self.lane = place, view, lane
        self.send_right, self.send_left, self.recv = send_right, send_left, recv

    def right(self, block):
        return rcopy(
            self.view(block), self.view(block), self.send_right.at[self.lane, block],
            self.recv.at[self.lane, block],
            col=lax.rem(self.place.c + 1, self.place.cols),
        )

    def left(self, block):
        cols = self.place.cols
        return rcopy(
            self.view(block), self.view(block), self.send_left.at[self.lane, block],
            self.recv.at[self.lane, block],
            col=lax.rem(self.place.c + cols - 1, cols),
        )

    def hop(self, distance):
        c, cols = self.place.c, self.place.cols

        @pl.when(c >= distance)
        def _():
            block = lax.rem(c + cols - distance, cols)
            if distance:
                self.right(block).wait_recv()

            @pl.when(c < cols - 1)
            def _():
                self.right(block).start()

        @pl.when(c + distance < cols)
        def _():
            block = lax.rem(c + distance, cols)
            if distance:
                self.left(block).wait_recv()

            @pl.when(c > 0)
            def _():
                self.left(block).start()

    def finish(self):
        c, cols = self.place.c, self.place.cols
        for distance in range(cols):

            @pl.when((c >= distance) & (c < cols - 1))
            def _():
                self.right(lax.rem(c + cols - distance, cols)).wait_send()

            @pl.when((c + distance < cols) & (c > 0))
            def _():
                self.left(lax.rem(c + distance, cols)).wait_send()


class WeightGather:
    def __init__(self, place, layer, own, full, send, recv, local):
        self.place, self.layer, self.own, self.full = place, layer, own, full
        self.send, self.recv, self.local = send, recv, local

    def view(self, kind, block, half=None):
        lines = self.own[kind].shape[-2]
        length = self.own[kind].shape[-2 if kind in (0, 1) else -1]
        at, count = (0, lines) if half is None else (half * (lines // 2), lines // 2)
        if kind in (0, 1):
            piece = pl.ds(pl.multiple_of(block * length + at, count), count)
            return self.full[kind].at[:, piece, :] if kind == 0 else self.full[1].at[piece, :]
        piece = pl.ds(pl.multiple_of(block * length, length), length)
        return self.full[kind].at[at : at + count, piece]

    def direct(self, kind, way):
        place = self.place
        return rcopy(
            self.own[kind], self.view(kind, place.r), self.send.at[kind, way],
            self.recv.at[kind, way], row=place.beside(way),
        )

    def relayed(self, kind, way):
        place = self.place
        piece = self.view(kind, place.beside(way), way)
        return rcopy(
            piece, piece, self.send.at[kind, 2 + way], self.recv.at[kind, 2 + way],
            row=place.beside(1 - way),
        )

    def arriving(self, kind, way):
        block = self.view(kind, self.place.beside(way))
        return rcopy(
            block, block, self.send.at[kind, way], self.recv.at[kind, way],
            row=self.place.beside(way),
        )

    def across(self, kind, way):
        piece = self.view(kind, self.place.across(), way)
        return rcopy(
            piece, piece, self.send.at[kind, 2 + way], self.recv.at[kind, 2 + way],
            row=self.place.beside(1 - way),
        )

    def to_partner(self, kind, which):
        place = self.place
        source = (place.beside(0), place.beside(1), place.across(), place.r)[which]
        block = self.view(kind, source)
        return rcopy(
            self.own[kind] if which == 3 else block, block, self.send.at[kind, 4 + which],
            self.recv.at[kind, 4 + which], section=1 - place.s,
        )

    def keep(self, kind):
        return pltpu.make_async_copy(
            self.own[kind], self.view(kind, self.place.r), self.local.at[kind]
        )

    def start(self, kind):
        @pl.when(self.place.s == self.layer)
        def _():
            for way in range(2):
                self.direct(kind, way).start()
            self.keep(kind).start()
            self.to_partner(kind, 3).start()

    def relay(self, kind):
        @pl.when(self.place.s == self.layer)
        def _():
            for way in range(2):
                self.arriving(kind, way).wait_recv()
                self.relayed(kind, way).start()
                self.to_partner(kind, way).start()

    def forward(self, kind):
        @pl.when(self.place.s == self.layer)
        def _():
            for way in range(2):
                self.across(kind, way).wait_recv()
            self.to_partner(kind, 2).start()
            self.keep(kind).wait()

    def ready(self, kind):
        @pl.when(self.place.s != self.layer)
        def _():
            for which in range(4):
                self.to_partner(kind, which).wait_recv()

    def finish(self, kind):
        @pl.when(self.place.s == self.layer)
        def _():
            for way in range(2):
                self.direct(kind, way).wait_send()
                self.relayed(kind, way).wait_send()
            for which in range(4):
                self.to_partner(kind, which).wait_send()


class RowExchange:
    def __init__(self, place, piece_for, slot_of, send, recv, local):
        self.place, self.piece_for, self.slot_of = place, piece_for, slot_of
        self.send, self.recv, self.local = send, recv, local

    def out(self, step):
        place = self.place
        target = place.row_to(step)
        return rcopy(
            self.piece_for(target), self.slot_of(place.r), self.send.at[step], self.recv.at[step],
            row=target,
        )

    def into(self, step):
        slot = self.slot_of(self.place.row_from(step))
        return rcopy(
            slot, slot, self.send.at[step], self.recv.at[step], row=self.place.row_to(step)
        )

    def keep(self):
        return pltpu.make_async_copy(
            self.piece_for(self.place.r), self.slot_of(self.place.r), self.local
        )

    def start(self):
        for step in range(1, self.place.rows):
            self.out(step).start()
        self.keep().start()

    def arrive(self):
        for step in range(1, self.place.rows):
            self.into(step).wait_recv()
        self.keep().wait()

    def finish(self):
        for step in range(1, self.place.rows):
            self.out(step).wait_send()


def norm_rows(source, gains_a, shifts_a, gains_m, shifts_m, normed_a, normed_m, begin=0, count=None):
    count = source.shape[0] if count is None else count
    tile = min(128, count)

    @pl.loop(0, count // tile)
    def _(index):
        rows = pl.ds(pl.multiple_of(begin + index * tile, tile), tile)
        values = source[rows, :].astype(F32)
        centred = values - jnp.mean(values, axis=1, keepdims=True)
        unit = centred * lax.rsqrt(jnp.mean(centred * centred, axis=1, keepdims=True) + EPS)
        normed_a[rows, :] = (unit * gains_a + shifts_a).astype(BF)
        normed_m[rows, :] = (unit * gains_m + shifts_m).astype(BF)


def turn(block, cos, sin, direction):
    half = cos.shape[0]
    lower, upper, rest = block[:half], block[half : 2 * half], block[2 * half :]
    return jnp.concatenate(
        [
            lower * cos - upper * (direction * sin),
            upper * cos + lower * (direction * sin),
            rest,
        ],
        axis=0,
    )


def project_heads(normed_a, w_query, bias_rows, cos, sin, pieces, heads, where):
    for kind in range(3):
        flipped = (dot(normed_a[where, :], w_query[kind]) + bias_rows(kind)).T
        for head in range(heads):
            block = flipped[head * HEAD_DIM : (head + 1) * HEAD_DIM]
            if kind < 2:
                block = turn(block, cos[:, where], sin[:, where], 1.0)
            pieces[head, kind * HEAD_DIM : (kind + 1) * HEAD_DIM, where] = block.astype(BF)


def feed_forward(normed_m, w_hidden, bias_of, hidden, slope, where):
    tile = min(256, w_hidden.shape[1])

    @pl.loop(0, w_hidden.shape[1] // tile)
    def _(index):
        cols = pl.ds(pl.multiple_of(index * tile, tile), tile)
        pre = dot(normed_m[where, :], w_hidden[:, cols]) + bias_of(index)
        phi = 0.5 * (1.0 + lax.erf(pre * math.sqrt(0.5)))
        hidden[where, cols] = (pre * phi).astype(BF)
        slope[where, cols] = phi + pre * (
            jnp.exp(-0.5 * pre * pre) * (1.0 / math.sqrt(2.0 * math.pi))
        )


def times_tiles(left, right, out, convert=None, contract=((1,), (0,)), where=slice(None)):
    tile = min(256, out.shape[1])

    @pl.loop(0, out.shape[1] // tile)
    def _(index):
        cols = pl.ds(pl.multiple_of(index * tile, tile), tile)
        piece = right[:, cols] if contract[1] == (0,) else right[cols, :]
        value = dot(left[where, :], piece, contract)
        out[where, cols] = value if convert is None else convert(value, cols)


def dma(*shape):
    return pltpu.SemaphoreType.DMA(shape)


def key_mask(prompt, first, cols, key_at, query_at, keys, queries):
    in_prompt = key_at + keys <= PROMPT_LEAST
    before = key_at + keys <= query_at + 1
    if in_prompt and before:
        return None
    key = lax.broadcasted_iota(jnp.int32, (keys, queries), 0) + key_at
    allowed = None
    if not in_prompt:
        allowed = (key < prompt) | (key >= first[:, cols])
    if not before:
        causal = key <= lax.broadcasted_iota(jnp.int32, (keys, queries), 1) + query_at
        allowed = causal if allowed is None else allowed & causal
    return allowed


def rows_of_keys(qkv, at, rows):
    rows[...] = qkv[at : at + HEAD_DIM, :].astype(F32).T.astype(BF)


def key_blocks(query_at, queries):
    last = query_at + queries
    return [(at, min(KEY_BLOCK, last - at)) for at in range(0, last, KEY_BLOCK)]


def scaled_query(qkv, cols):
    return (qkv[:HEAD_DIM, cols].astype(F32) * (1.0 / math.sqrt(HEAD_DIM))).astype(BF)


def score_block(prompt, first, cols, query_at, key_at, keys, key_rows, query):
    scores = dot(key_rows[key_at : key_at + keys, :], query)
    allowed = key_mask(prompt, first, cols, key_at, query_at, keys, query.shape[1])
    return scores if allowed is None else jnp.where(allowed, scores, NEG)


def attend_block(block, size, prompt, first, qkv, key_rows, scores, keep_weights=False):
    query_at = block * size
    cols = slice(query_at, query_at + size)
    query = scaled_query(qkv, cols)
    blocks = key_blocks(query_at, size)
    top = None
    for key_at, keys in blocks:
        piece = score_block(prompt, first, cols, query_at, key_at, keys, key_rows, query)
        scores[key_at : key_at + keys, :] = piece
        highest = jnp.max(piece, axis=0, keepdims=True)
        top = highest if top is None else jnp.maximum(top, highest)
    weight, totals = None, None
    for key_at, keys in blocks:
        probs = jnp.exp(scores[key_at : key_at + keys, :] - top)
        if keep_weights:
            scores[key_at : key_at + keys, :] = probs
        part = jnp.sum(probs, axis=0, keepdims=True)
        product = dot(qkv[2 * HEAD_DIM : 3 * HEAD_DIM, key_at : key_at + keys], probs.astype(BF))
        weight = part if weight is None else weight + part
        totals = product if totals is None else totals + product
    return totals / weight, top, weight


def gradient_block(
    block, size, qkv, d_out, delta, probs_of, key_rows, value_rows, key_acc, value_acc, opening
):
    query_at = block * size
    cols = slice(query_at, query_at + size)
    query = scaled_query(qkv, cols)
    d_query = d_out[:, cols]
    d_sum = None
    for key_at, keys in key_blocks(query_at, size):
        where = slice(key_at, key_at + keys)
        probs = probs_of(key_at, keys, query)
        d_probs = dot(value_rows[where, :], d_query)
        d_scores = (probs * (d_probs - delta)).astype(BF)
        d_key = dot(query, d_scores, ((1,), (1,)))
        d_value = dot(d_query, probs.astype(BF), ((1,), (1,)))
        if opening:
            key_acc[:, where] = d_key
            value_acc[:, where] = d_value
        else:
            key_acc[:, where] += d_key
            value_acc[:, where] += d_value
        part = dot(qkv[HEAD_DIM : 2 * HEAD_DIM, where], d_scores)
        d_sum = part if d_sum is None else d_sum + part
    return d_sum * (1.0 / math.sqrt(HEAD_DIM))


class LineReduce:
    def __init__(self, place, total, low, from_left, from_right, view, sems, lane=0):
        self.place, self.total, self.low, self.view, self.lane = place, total, low, view, lane
        self.from_left, self.from_right = from_left, from_right
        self.send_right, self.send_left, self.recv_left, self.recv_right = sems

    def right(self, owner):
        return rcopy(
            self.low.at[self.view(owner)], self.from_left.at[self.view(owner)],
            self.send_right.at[self.lane, owner], self.recv_left.at[self.lane, owner],
            col=lax.rem(self.place.c + 1, self.place.cols),
        )

    def left(self, owner):
        cols = self.place.cols
        return rcopy(
            self.low.at[self.view(owner)], self.from_right.at[self.view(owner)],
            self.send_left.at[self.lane, owner], self.recv_right.at[self.lane, owner],
            col=lax.rem(self.place.c + cols - 1, cols),
        )

    def add_in(self, owner, arrived):
        view = self.view(owner)
        self.low[view] = (self.total[view] + arrived[view].astype(F32)).astype(BF)

    def step(self, time):
        c, cols = self.place.c, self.place.cols

        @pl.when(c <= time)
        def _():
            owner = cols - 1 - time + c

            @pl.when(c > 0)
            def _():
                self.right(owner).wait_recv()
                self.add_in(owner, self.from_left)

            self.right(owner).start()

        @pl.when(c >= cols - 1 - time)
        def _():
            owner = time + c - (cols - 1)

            @pl.when(c < cols - 1)
            def _():
                self.left(owner).wait_recv()
                self.add_in(owner, self.from_right)

            self.left(owner).start()

    def own(self):
        c, cols = self.place.c, self.place.cols
        view = self.view(c)

        @pl.when(c > 0)
        def _():
            self.right(c).wait_recv()

        @pl.when(c == 0)
        def _():
            self.from_left[view] = jnp.zeros_like(self.from_left[view])

        @pl.when(c < cols - 1)
        def _():
            self.left(c).wait_recv()

        @pl.when(c == cols - 1)
        def _():
            self.from_right[view] = jnp.zeros_like(self.from_right[view])

        return (
            self.total[view] + self.from_left[view].astype(F32) + self.from_right[view].astype(F32)
        )

    def finish(self):
        c, cols = self.place.c, self.place.cols
        for time in range(cols - 1):

            @pl.when(c <= time)
            def _():
                self.right(cols - 1 - time + c).wait_send()

            @pl.when(c >= cols - 1 - time)
            def _():
                self.left(time + c - (cols - 1)).wait_send()


def center_sum(place, total, low, from_outer, from_inner, full, sems, order, prepare, produce, after, work):
    c = place.c
    a_send, a_recv, b_send, b_recv, c_send, c_recv = sems
    count = len(order)
    size = total.shape[0] // count
    inner = (c == 1) | (c == 2)
    outer = (c == 0) | (c == 3)
    pair = jnp.where(c < 2, 1 - c, 5 - c)
    middle = 3 - c
    group = count // 4

    def rows(index):
        return slice(order[index] * size, (order[index] + 1) * size)

    def inward(index):
        piece = rows(index)
        return rcopy(
            low.at[piece], from_outer.at[piece], a_send.at[index], a_recv.at[index], col=pair
        )

    def exchange(index):
        piece = rows(index)
        return rcopy(
            low.at[piece], from_inner.at[piece], b_send.at[index], b_recv.at[index], col=middle
        )

    def outward(index):
        piece = rows(index)
        return rcopy(full.at[piece], full.at[piece], c_send.at[index], c_recv.at[index], col=pair)

    prepare(0)
    for time in range(count + 2 * LAG):
        if time < count:

            @pl.when(outer)
            def _():
                inward(time).start()

            @pl.when(inner)
            def _():
                piece = rows(time)
                inward(time).wait_recv()
                low[piece, :] = (total[piece, :] + from_outer[piece, :].astype(F32)).astype(BF)
                exchange(time).start()

        if LAG <= time < count + LAG:

            @pl.when(inner)
            def _():
                index = time - LAG
                piece = rows(index)
                exchange(index).wait_recv()
                summed = low[piece, :].astype(F32) + from_inner[piece, :].astype(F32)
                full[piece, :] = produce(summed, piece)
                outward(index).start()

        if time >= 2 * LAG:

            @pl.when(outer)
            def _():
                outward(time - 2 * LAG).wait_recv()

        if time + 2 < count and (time + 2) % group == 0:
            prepare((time + 2) // group)
        if time >= 2 * LAG:
            after(time - 2 * LAG)
        work(time)
    for index in range(count):

        @pl.when(outer)
        def _():
            inward(index).wait_send()

        @pl.when(inner)
        def _():
            exchange(index).wait_send()
            outward(index).wait_send()


class GradExchange:
    def __init__(self, place, layer, n, prefix):
        self.place, self.layer = place, layer
        self.mine, self.theirs, self.relay, self.inbox = (
            [getattr(n, name + kind) for kind in "qfop"]
            for name in ("mine_", "theirs_", "relay_", "inbox_")
        )
        self.send, self.recv = getattr(n, prefix + "_s"), getattr(n, prefix + "_r")

    def block(self, which):
        place = self.place
        return (place.beside(0), place.beside(1), place.across(), place.r)[which]

    def view(self, kind, block, half=None):
        shape = self.inbox[kind].shape
        length = shape[-2 if kind in (0, 1) else -1]
        lines = shape[-2]
        at, count = (0, lines) if half is None else (half * (lines // 2), lines // 2)
        if kind in (0, 1):
            piece = pl.ds(pl.multiple_of(block * length + at, count), count)
            return (slice(None), piece, slice(None)) if kind == 0 else (piece, slice(None))
        piece = pl.ds(pl.multiple_of(block * length, length), length)
        return (slice(at, at + count), piece)

    def passing(self, kind, which):
        view = self.view(kind, self.block(which))
        return rcopy(
            self.mine[kind].at[view], self.theirs[kind].at[view], self.send.at[kind, which],
            self.recv.at[kind, which], section=1 - self.place.s,
        )

    def relaying(self, kind, way):
        return rcopy(
            self.mine[kind].at[self.view(kind, self.place.across(), way)],
            self.relay[kind].at[way], self.send.at[kind, 4 + way], self.recv.at[kind, 4 + way],
            row=self.place.beside(way),
        )

    def sending(self, kind, way):
        return rcopy(
            self.mine[kind].at[self.view(kind, self.place.beside(way))],
            self.inbox[kind].at[way], self.send.at[kind, 6 + way], self.recv.at[kind, 6 + way],
            row=self.place.beside(way),
        )

    def add(self, kind, view, value):
        self.mine[kind][view] = (self.mine[kind][view].astype(F32) + value.astype(F32)).astype(BF)

    def hand(self, kind):
        @pl.when(self.place.s != self.layer)
        def _():
            for which in (2, 0, 1, 3):
                self.passing(kind, which).start()

    def merge(self, kind):
        @pl.when(self.place.s == self.layer)
        def _():
            for which in (2, 0, 1):
                self.passing(kind, which).wait_recv()
                view = self.view(kind, self.block(which))
                self.add(kind, view, self.theirs[kind][view])
                if which == 2:
                    for way in range(2):
                        self.relaying(kind, way).start()

    def pass_on(self, kind):
        @pl.when(self.place.s == self.layer)
        def _():
            for way in range(2):
                self.relaying(kind, 1 - way).wait_recv()
                view = self.view(kind, self.place.beside(way), 1 - way)
                self.add(kind, view, self.relay[kind][1 - way])
                self.sending(kind, way).start()

    def take(self, kind, out):
        @pl.when(self.place.s == self.layer)
        def _():
            self.passing(kind, 3).wait_recv()
            view = self.view(kind, self.place.r)
            total = self.mine[kind][view].astype(F32) + self.theirs[kind][view].astype(F32)
            for way in range(2):
                self.sending(kind, way).wait_recv()
                total = total + self.inbox[kind][way].astype(F32)
            out[...] = total

    def finish(self, kind):
        @pl.when(self.place.s == self.layer)
        def _():
            for way in range(2):
                self.relaying(kind, way).wait_send()
                self.sending(kind, way).wait_send()

        @pl.when(self.place.s != self.layer)
        def _():
            for which in range(4):
                self.passing(kind, which).wait_send()


def grad_shapes(rows, full, width, units):
    part = full // rows
    return (
        dict(q=(3, full, width), f=(full, units), o=(width, full), p=(units, full)),
        dict(q=(3, part, width), f=(part, units), o=(width, part), p=(units, part)),
    )


def grad_scratch(rows, full, width, units):
    wholes, pieces = grad_shapes(rows, full, width, units)
    scratch = {}
    for kind in "qfop":
        piece = pieces[kind]
        half = piece[:-2] + (piece[-2] // 2, piece[-1])
        scratch["mine_" + kind] = pltpu.VMEM(wholes[kind], BF)
        scratch["theirs_" + kind] = pltpu.VMEM(wholes[kind], BF)
        scratch["relay_" + kind] = pltpu.VMEM((2,) + half, BF)
        scratch["inbox_" + kind] = pltpu.VMEM((2,) + piece, BF)
    return scratch


class BlockExchange:
    def __init__(self, place, source, inbox, size, send, recv, local):
        self.place, self.source, self.inbox, self.size = place, source, inbox, size
        self.send, self.recv, self.local = send, recv, local

    def slot(self, head, lane):
        return self.inbox.at[head, :, lane * self.size : (lane + 1) * self.size]

    def piece(self, block):
        return self.source.at[:, block * self.size : (block + 1) * self.size]

    def away(self, block):
        return rcopy(
            self.piece(block), self.slot(self.place.r, block % PARTS), self.send.at[block],
            self.recv.at[block % PARTS, self.place.r], row=block // PARTS,
        )

    def start(self, block):
        @pl.when(self.place.r != block // PARTS)
        def _():
            self.away(block).start()

        @pl.when(self.place.r == block // PARTS)
        def _():
            pltpu.make_async_copy(
                self.piece(block), self.slot(self.place.r, block % PARTS),
                self.local.at[block % PARTS],
            ).start()

    def arrive(self, lane):
        for step in range(1, self.place.rows):
            source = self.place.row_from(step)
            slot = self.slot(source, lane)
            rcopy(
                slot, slot, self.send.at[lane], self.recv.at[lane, source],
                row=self.place.row_to(step),
            ).wait_recv()
        slot = self.slot(self.place.r, lane)
        pltpu.make_async_copy(slot, slot, self.local.at[lane]).wait()

    def finish(self):
        for block in range(self.place.rows * PARTS):

            @pl.when(self.place.r != block // PARTS)
            def _():
                self.away(block).wait_send()


def unit_rows(values):
    centred = values - jnp.mean(values, axis=1, keepdims=True)
    rstd = lax.rsqrt(jnp.mean(centred * centred, axis=1, keepdims=True) + EPS)
    return centred * rstd, rstd


def segment_begins(lengths, micro, first):
    token = lax.broadcasted_iota(jnp.int32, first.shape, 1)
    begin = jnp.zeros_like(token)
    start = lengths[micro, 0]
    for index in range(1, lengths.shape[1]):
        begin = jnp.where(token >= start, start, begin)
        start = start + lengths[micro, index]
    first[...] = begin
    return lengths[micro, 0]


class Saver:
    def __init__(self, sems):
        self.sems, self.copies = sems, []

    def copy(self, source, target):
        copy = pltpu.make_async_copy(source, target, self.sems.at[len(self.copies)])
        copy.start()
        self.copies.append(copy)
        return copy

    def finish(self):
        for copy in self.copies:
            copy.wait()


class Names:
    def joined(self, results):
        both = Names()
        for name, value in vars(self).items():
            setattr(both, name, value)
        for name, value in results.items():
            setattr(both, name[2:], value)
        return both


def named_call(body, collective_id, ins, outs, scratch):
    names = [*ins, *outs, *scratch]

    def kernel(*refs):
        held = Names()
        for name, ref in zip(names, refs):
            setattr(held, name, ref)
        body(held)

    results = pl.pallas_call(
        kernel,
        out_shape=[jax.ShapeDtypeStruct(shape, dtype) for shape, dtype, space in outs.values()],
        in_specs=[pl.BlockSpec(memory_space=space) for array, space in ins.values()],
        out_specs=[pl.BlockSpec(memory_space=space) for shape, dtype, space in outs.values()],
        scratch_shapes=list(scratch.values()),
        compiler_params=pltpu.CompilerParams(
            collective_id=collective_id,
            has_side_effects=collective_id is not None,
            vmem_limit_bytes=VMEM_LIMIT,
        ),
    )(*[array for array, space in ins.values()])
    return dict(zip(outs, results))


class VectorGather:
    def __init__(self, place, own, full, send, recv, width):
        self.place, self.own, self.full, self.width = place, own, full, width
        self.send, self.recv = send, recv
        self.others = [(ds, dc) for ds in range(2) for dc in range(place.cols) if ds or dc]

    def slot(self, section, col):
        return self.full.at[section, :, pl.ds(pl.multiple_of(col * self.width, self.width), self.width)]

    def copy(self, ds, dc, source, slot):
        index = ds * self.place.cols + dc
        return rcopy(
            source, slot, self.send.at[index], self.recv.at[index],
            section=lax.rem(self.place.s + ds, 2), col=self.place.col_to(dc),
        )

    def start(self):
        for ds, dc in self.others:
            self.copy(ds, dc, self.own, self.slot(self.place.s, self.place.c)).start()

    def arrive(self):
        for ds, dc in self.others:
            slot = self.slot(lax.rem(self.place.s + ds, 2), self.place.col_from(dc))
            self.copy(ds, dc, slot, slot).wait_recv()

    def finish(self):
        for ds, dc in self.others:
            self.copy(ds, dc, self.own, self.slot(self.place.s, self.place.c)).wait_send()


def first_kernel(rows, cols, n):
    place = Place(rows, cols)
    s, c = place.s, place.c
    tokens, full = n.x_full.shape
    width = full // cols
    length = tokens // PARTS
    own = pl.ds(pl.multiple_of(c * width, width), width)

    def lane_of(lane):
        return slice(lane * length, (lane + 1) * length)

    def block_cols(block):
        return pl.ds(pl.multiple_of(block * width, width), width)

    def token_slot(source, lane):
        return pl.ds(pl.multiple_of(source * tokens + lane * length, length), length)

    loads = Saver(n.load)
    x_own = loads.copy(n.hidden_in.at[s], n.x_full.at[:, own])
    n.vectors[0:2] = n.norm_gains[0]
    n.vectors[2:4] = n.norm_biases[0]
    n.vectors[4:7] = n.b_qkv[0]
    n.vectors[7:8] = n.b_out[...]
    for index in range(n.b_fc.shape[1] // width):
        n.vectors[8 + index : 9 + index] = n.b_fc[:, index * width : (index + 1) * width]
    n.vectors[12:16] = jnp.zeros((4, width), F32)
    v_own = loads.copy(n.vectors, n.vec_all.at[s, :, own])
    c_own = loads.copy(n.cotangent.at[s], n.cot_full.at[:, own])
    place.greet(rows=True, cols=True, partner=True, cross_cols=True)
    x_gather = [
        LineGather(
            place, lambda block, lane=lane: n.x_full.at[lane_of(lane), block_cols(block)],
            n.x_a, n.x_b, n.x_c, lane,
        )
        for lane in range(PARTS)
    ]
    c_gather = LineGather(
        place, lambda block: n.cot_full.at[:, block_cols(block)], n.c_a, n.c_b, n.c_c
    )
    vectors = VectorGather(place, n.vectors, n.vec_all, n.v_s, n.v_r, width)
    blocks = (n.wq, n.wf, n.wo, n.wp)
    weights = [
        WeightGather(place, 0, blocks, (n.wq0, n.wf0, n.wo0, n.wp0), n.w0_s, n.w0_r, n.w0_l),
        WeightGather(place, 1, blocks, (n.wq1, n.wf1, n.wo1, n.wp1), n.w1_s, n.w1_r, n.w1_l),
    ]
    QKV, FC, OUT, PROJ = range(4)
    saves = Saver(n.save)
    prompt = segment_begins(n.lengths, s, n.first)

    def row(layer, index):
        return n.vec_all[layer, index : index + 1, :]

    def bias_rows(layer):
        return lambda kind: n.vec_all[layer, 4 + kind : 5 + kind, own]

    def unit_bias(layer):
        return lambda index: n.vec_all[layer, pl.ds(8 + index, 1), own]

    def spread(pieces, slots, sends, recvs, local):
        return [
            RowExchange(
                place,
                lambda target, lane=lane: pieces(target, lane),
                lambda source, lane=lane: slots(source, lane),
                sends.at[lane], recvs.at[lane], local.at[lane],
            )
            for lane in range(PARTS)
        ]

    out0 = spread(
        lambda target, lane: n.pieces0.at[target, :, lane_of(lane)],
        lambda source, lane: n.qkv0.at[:, token_slot(source, lane)],
        n.e0_s, n.e0_r, n.e0_l,
    )
    back0 = spread(
        lambda target, lane: n.low0.at[:, token_slot(target, lane)],
        lambda source, lane: n.attn_t0.at[
            pl.ds(pl.multiple_of(source * HEAD_DIM, HEAD_DIM), HEAD_DIM), lane_of(lane)
        ],
        n.b0_s, n.b0_r, n.b0_l,
    )
    out1 = spread(
        lambda target, lane: n.pieces1.at[target, :, lane_of(lane)],
        lambda source, lane: n.qkvd1.at[:, token_slot(source, lane)],
        n.e1_s, n.e1_r, n.e1_l,
    )

    def project(layer, lane, source, normed_a, normed_m, w_query, pieces):
        norm_rows(
            source, row(layer, 0), row(layer, 2), row(layer, 1), row(layer, 3), normed_a, normed_m,
            lane * length, length,
        )
        project_heads(
            normed_a, w_query, bias_rows(layer), n.cos, n.sin, pieces, rows, lane_of(lane)
        )

    x_own.wait()
    x_gather[0].hop(0)
    vectors.start()
    weights[0].start(QKV)
    weights[0].start(FC)
    x_gather[0].hop(1)
    x_gather[1].hop(0)
    x_gather[0].hop(2)
    weights[0].relay(QKV)
    weights[0].start(PROJ)
    x_gather[1].hop(1)
    for distance in range(3, cols):
        x_gather[0].hop(distance)
    weights[0].forward(QKV)
    weights[0].relay(FC)
    vectors.arrive()
    v_own.wait()
    x_gather[1].hop(2)
    weights[0].ready(QKV)
    project(0, 0, n.x_full, n.normed_a0, n.normed_m0, n.wq0, n.pieces0)
    out0[0].start()
    weights[0].start(OUT)
    for distance in range(3, cols):
        x_gather[1].hop(distance)
    c_own.wait()
    c_gather.hop(0)
    weights[0].forward(FC)
    project(0, 1, n.x_full, n.normed_a0, n.normed_m0, n.wq0, n.pieces0)
    out0[1].start()
    weights[0].relay(PROJ)
    weights[0].relay(OUT)
    c_gather.hop(1)
    weights[0].ready(FC)
    feed_forward(n.normed_m0, n.wf0, unit_bias(0), n.hidden0, n.slope0, slice(None))
    for ref, target in (
        (n.x_full, n.o_x_full), (n.vec_all, n.o_vec_all), (n.wq0, n.o_wq0), (n.wf0, n.o_wf0),
        (n.normed_a0, n.o_normed_a0), (n.normed_m0, n.o_normed_m0), (n.hidden0, n.o_hidden0),
        (n.slope0, n.o_slope0),
    ):
        saves.copy(ref, target)
    weights[0].forward(PROJ)
    weights[0].forward(OUT)
    weights[1].start(QKV)
    weights[1].start(OUT)
    for lane in range(PARTS):
        out0[lane].arrive()
    saves.copy(n.qkv0, n.o_qkv0)

    rows_of_keys(n.qkv0, HEAD_DIM, n.key_rows)
    for lane in range(PARTS):
        for owner in range(rows):
            block = owner * PARTS + lane
            exact, top, weight = attend_block(
                block, length, prompt, n.first, n.qkv0, n.key_rows, n.scores.at[owner % 2]
            )
            cols_here = slice(block * length, (block + 1) * length)
            n.out0[:, cols_here] = exact
            n.low0[:, cols_here] = exact.astype(BF)
            n.log0[:, cols_here] = top + jnp.log(weight)
        back0[lane].start()
        if lane == 0:
            c_gather.hop(2)
            weights[1].start(FC)
            weights[1].relay(QKV)
            weights[1].relay(OUT)
    for distance in range(3, cols):
        c_gather.hop(distance)
    weights[1].start(PROJ)
    weights[1].forward(QKV)
    weights[1].forward(OUT)
    saves.copy(n.cot_full, n.o_cot_full)
    saves.copy(n.out0, n.o_out0)
    saves.copy(n.log0, n.o_log0)
    weights[0].ready(PROJ)
    weights[0].ready(OUT)
    saves.copy(n.wp0, n.o_wp0)
    saves.copy(n.wo0, n.o_wo0)

    step = 4 // PARTS
    part = tokens // 4

    def prepare(quarter):
        if quarter % step == 0:
            back0[quarter // step].arrive()
        where = slice(quarter * part, (quarter + 1) * part)
        attn_rows = n.attn_t0[:, where].astype(F32).T.astype(BF)
        tile = min(256, full)
        for at in range(0, full, tile):
            value = dot(n.hidden0[where, :], n.wp0[:, at : at + tile]) + dot(
                attn_rows, n.wo0[:, at : at + tile]
            )
            n.total[where, at : at + tile] = value
            n.low[where, at : at + tile] = value.astype(BF)

    def produce(summed, mine):
        return (n.x_full[mine, :].astype(F32) + summed + n.vec_all[0, 7:8, :]).astype(BF)

    def branches(lane):
        where = lane_of(lane)
        feed_forward(n.normed_m1, n.wf1, unit_bias(1), n.hidden1, n.slope1, where)

        def times_slope(value, cols_here):
            return (value * n.slope1[where, cols_here]).astype(BF)

        times_tiles(n.cot_full, n.wp1, n.d_hidden1, times_slope, ((1,), (1,)), where)
        times_tiles(n.hidden1, n.wp1, n.branch1, None, ((1,), (0,)), where)
        times_tiles(n.d_hidden1, n.wf1, n.d_normed1, None, ((1,), (1,)), where)

    def after(chunk):
        if (chunk + 1) % (CHUNKS // PARTS):
            return
        lane = chunk // (CHUNKS // PARTS)
        if lane == 0:
            weights[1].ready(QKV)
            weights[1].ready(OUT)
        project(1, lane, n.x1_full, n.normed_a1, n.normed_m1, n.wq1, n.pieces1)
        where = lane_of(lane)
        flipped = dot(n.cot_full[where, :], n.wo1[...], ((1,), (1,))).T
        for head in range(rows):
            n.pieces1[head, 3 * HEAD_DIM :, where] = flipped[
                head * HEAD_DIM : (head + 1) * HEAD_DIM
            ].astype(BF)
        out1[lane].start()

    def work(time):
        if time == 2:
            weights[1].relay(FC)
        if time == 6:
            weights[1].forward(FC)
            weights[1].relay(PROJ)
        if time == 10:
            weights[1].forward(PROJ)
        if time == 20:
            weights[1].ready(FC)
            weights[1].ready(PROJ)
            branches(0)

    center_sum(
        place, n.total, n.low, n.from_left, n.from_right, n.x1_full,
        (n.r_a, n.r_b, n.r_c, n.r_d, n.r_e, n.r_f), tuple(range(CHUNKS)), prepare, produce, after, work,
    )
    saves.copy(n.attn_t0, n.o_attn_t0)
    for ref, target in (
        (n.x1_full, n.o_x1_full), (n.wq1, n.o_wq1), (n.wo1, n.o_wo1),
        (n.normed_a1, n.o_normed_a1), (n.normed_m1, n.o_normed_m1),
    ):
        saves.copy(ref, target)
    for lane in range(1, PARTS):
        branches(lane)
    for ref, target in (
        (n.hidden1, n.o_hidden1), (n.d_hidden1, n.o_d_hidden1), (n.branch1, n.o_branch1),
        (n.d_normed1, n.o_d_normed1),
    ):
        saves.copy(ref, target)
    for lane in range(PARTS):
        out1[lane].arrive()
    saves.copy(n.qkvd1, n.o_qkvd1)
    for exchange in out0 + back0 + out1:
        exchange.finish()
    for gather in x_gather + [c_gather]:
        gather.finish()
    vectors.finish()
    for gather in weights:
        for kind in range(4):
            gather.finish(kind)
    saves.finish()


def first_half(rows, cols, hidden_in, cotangent, vectors, blocks, cos, sin, lengths):
    norm_gains, norm_biases, b_qkv, b_out, b_fc = vectors
    tokens, width = hidden_in.shape[1:]
    full = cols * width
    wq, wf, wo, wp = blocks
    units = wf.shape[1]
    total = rows * tokens
    hbm, vmem, smem = pl.ANY, pltpu.VMEM, pltpu.SMEM
    ins = dict(
        hidden_in=(hidden_in, hbm), cotangent=(cotangent, hbm), norm_gains=(norm_gains, vmem),
        norm_biases=(norm_biases, vmem), b_qkv=(b_qkv, vmem), b_out=(b_out, vmem), b_fc=(b_fc, vmem),
        wq=(wq, hbm), wf=(wf, hbm), wo=(wo, hbm), wp=(wp, hbm), cos=(cos, vmem), sin=(sin, vmem),
        lengths=(lengths, smem),
    )
    rows_low, rows_wide = ((tokens, full), BF), ((tokens, full), F32)
    unit_low, unit_wide = ((tokens, units), BF), ((tokens, units), F32)
    kept = dict(
        x_full=rows_low, cot_full=rows_low, vec_all=((2, 16, full), F32),
        wq0=((3, full, width), BF), wf0=((full, units), BF), wo0=((width, full), BF),
        wp0=((units, full), BF), normed_a0=rows_low, normed_m0=rows_low,
        qkv0=((3 * HEAD_DIM, total), BF), hidden0=unit_low, slope0=unit_wide,
        out0=((HEAD_DIM, total), F32), log0=((1, total), F32), attn_t0=((width, tokens), BF),
        x1_full=rows_low, wq1=((3, full, width), BF), wo1=((width, full), BF),
        normed_a1=rows_low, normed_m1=rows_low, qkvd1=((4 * HEAD_DIM, total), BF),
        hidden1=unit_low, d_hidden1=unit_low, branch1=rows_wide, d_normed1=rows_wide,
    )
    outs = {"o_" + name: shape + (hbm,) for name, shape in kept.items()}
    scratch = {name: pltpu.VMEM(*shape) for name, shape in kept.items()}
    scratch.update(
        vectors=pltpu.VMEM((16, width), F32),
        wf1=pltpu.VMEM((full, units), BF), wp1=pltpu.VMEM((units, full), BF),
        slope1=pltpu.VMEM(*unit_wide), low0=pltpu.VMEM((HEAD_DIM, total), BF),
        total=pltpu.VMEM(*rows_wide), low=pltpu.VMEM(*rows_low),
        from_left=pltpu.VMEM(*rows_low), from_right=pltpu.VMEM(*rows_low),
        pieces0=pltpu.VMEM((rows, 3 * HEAD_DIM, tokens), BF),
        pieces1=pltpu.VMEM((rows, 4 * HEAD_DIM, tokens), BF),
        first=pltpu.VMEM((1, total), jnp.int32), key_rows=pltpu.VMEM((total, HEAD_DIM), BF),
        scores=pltpu.VMEM((2, total, tokens // PARTS), F32),
        load=dma(3), save=dma(len(kept)),
        x_a=dma(PARTS, cols), x_b=dma(PARTS, cols), x_c=dma(PARTS, cols),
        c_a=dma(1, cols), c_b=dma(1, cols), c_c=dma(1, cols),
        v_s=dma(2 * cols), v_r=dma(2 * cols),
        w0_s=dma(4, 8), w0_r=dma(4, 8), w0_l=dma(4), w1_s=dma(4, 8), w1_r=dma(4, 8), w1_l=dma(4),
    )
    for name in ("e0", "b0", "e1"):
        scratch[name + "_s"] = dma(PARTS, rows)
        scratch[name + "_r"] = dma(PARTS, rows)
        scratch[name + "_l"] = dma(PARTS)
    for name in ("r_a", "r_b", "r_c", "r_d", "r_e", "r_f"):
        scratch[name] = dma(CHUNKS)
    return Names().joined(named_call(partial(first_kernel, rows, cols), 1, ins, outs, scratch))


def d_projection(inbox, at, cos, sin, rows, d_pre, small, where):
    width = rows * HEAD_DIM
    for kind in range(3):
        parts = []
        for head in range(rows):
            start = at + kind * HEAD_DIM
            block = inbox[head, start : start + HEAD_DIM, where].astype(F32)
            parts.append(turn(block, cos[:, where], sin[:, where], -1.0) if kind < 2 else block)
        values = jnp.concatenate(parts, axis=0).T.astype(BF)
        d_pre[where, kind * width : (kind + 1) * width] = values
        small[8 + kind : 9 + kind, :] += jnp.sum(values.astype(F32), axis=0, keepdims=True)


def d_norms(source, d_pre, wq, d_normed, gain_a, gain_m, total, low, sums, begin, count, also=None):
    width = wq.shape[2]
    tile = min(128, count)

    @pl.loop(0, count // tile)
    def _(index):
        rows = pl.ds(pl.multiple_of(begin + index * tile, tile), tile)
        d_a = dot(d_pre[rows, :width], wq[0], ((1,), (1,)))
        for kind in range(1, 3):
            d_a += dot(d_pre[rows, kind * width : (kind + 1) * width], wq[kind], ((1,), (1,)))
        d_m = d_normed[rows, :]
        unit, _ = unit_rows(source[rows, :].astype(F32))
        sums[0:1, :] += jnp.sum(d_a * unit, axis=0, keepdims=True)
        sums[1:2, :] += jnp.sum(d_m * unit, axis=0, keepdims=True)
        sums[2:3, :] += jnp.sum(d_a, axis=0, keepdims=True)
        sums[3:4, :] += jnp.sum(d_m, axis=0, keepdims=True)
        joined = d_a * gain_a + d_m * gain_m
        total[rows, :] = joined
        low[rows, :] = joined.astype(BF)
        if also is not None:
            also(rows, joined, unit)


def unit_sums(d_pre, small, width):
    for index in range(d_pre.shape[1] // width):
        piece = d_pre[:, index * width : (index + 1) * width].astype(F32)
        small[12 + index : 13 + index, :] = jnp.sum(piece, axis=0, keepdims=True)


def across_tokens(left, right, out, heads=False):
    tile = min(256, left.shape[1])

    @pl.loop(0, left.shape[1] // tile)
    def _(index):
        cols = pl.ds(pl.multiple_of(index * tile, tile), tile)
        value = dot(left[:, cols], right[...], ((0,), (0,))).astype(BF)
        if heads:
            width = out.shape[2]
            for kind in range(3):
                out[kind, cols, :] = value[:, kind * width : (kind + 1) * width]
        else:
            out[cols, :] = value


def out_gradient(attn_t, grad_full, out):
    tile = min(256, out.shape[1])
    for at in range(0, out.shape[1], tile):
        out[:, at : at + tile] = dot(attn_t[...], grad_full[:, at : at + tile]).astype(BF)


Q, F, O, PR = range(4)


class Loader:
    def __init__(self, n, names):
        self.entries = [
            (getattr(n, name), getattr(n, "i_" + name), n.load.at[index])
            for index, name in enumerate(names)
        ]
        self.copies = {}

    def start(self, *wanted):
        for index, (own, source, sem) in enumerate(self.entries):
            if index not in self.copies and (not wanted or any(own is ref for ref in wanted)):
                copy = pltpu.make_async_copy(source, own, sem)
                copy.start()
                self.copies[index] = copy

    def need(self, *wanted):
        for index, (own, source, sem) in enumerate(self.entries):
            if any(own is ref for ref in wanted) and self.copies[index] is not None:
                self.copies[index].wait()
                self.copies[index] = None


def turning_kernel(rows, cols, names, n):
    place = Place(rows, cols)
    c = place.c
    tokens, full = n.x1_full.shape
    width = full // cols
    length = tokens // PARTS
    size = QUERY_BLOCK
    own = pl.ds(pl.multiple_of(c * width, width), width)

    def lane_of(lane):
        return slice(lane * length, (lane + 1) * length)

    loads = Loader(n, names)
    loads.start(n.qkvd1)
    place.greet(rows=True, cols=True, partner=True)
    saves = Saver(n.save)
    grads = GradExchange(place, 1, n, "g")
    exchange = BlockExchange(place, n.result, n.inbox, size, n.b_s, n.b_r, n.b_l)
    outward = [
        RowExchange(
            place,
            lambda target, lane=lane: n.pieces.at[target, :, lane_of(lane)],
            lambda source, lane=lane: n.d_out.at[
                :, pl.ds(pl.multiple_of(source * tokens + lane * length, length), length)
            ],
            n.e_s.at[lane], n.e_r.at[lane], n.e_l.at[lane],
        )
        for lane in range(PARTS)
    ]

    loads.need(n.qkvd1)
    loads.start()
    qkvd = n.qkvd1
    rows_of_keys(qkvd, HEAD_DIM, n.key_rows)
    rows_of_keys(qkvd, 2 * HEAD_DIM, n.value_rows)
    prompt = segment_begins(n.lengths, place.s, n.first)
    count = rows * PARTS
    d_out = qkvd.at[3 * HEAD_DIM :]
    for block in reversed(range(count)):
        here = slice(block * size, (block + 1) * size)
        scores = n.scores.at[block % 2]
        exact, top, weight = attend_block(
            block, size, prompt, n.first, qkvd, n.key_rows, scores, True
        )
        delta = jnp.sum(d_out[:, here].astype(F32) * exact, axis=0, keepdims=True)
        inverse = 1.0 / weight

        def probs_of(key_at, keys, query):
            return scores[key_at : key_at + keys, :] * inverse

        d_query = gradient_block(
            block, size, qkvd, d_out, delta, probs_of, n.key_rows, n.value_rows, n.key_acc,
            n.value_acc, block == count - 1,
        )
        n.result[:HEAD_DIM, here] = exact.astype(BF)
        n.result[HEAD_DIM : 2 * HEAD_DIM, here] = d_query.astype(BF)
        n.result[2 * HEAD_DIM : 3 * HEAD_DIM, here] = n.key_acc[:, here].astype(BF)
        n.result[3 * HEAD_DIM :, here] = n.value_acc[:, here].astype(BF)
        exchange.start(block)

    n.sums1[...] = jnp.zeros_like(n.sums1)
    n.small1[...] = jnp.zeros_like(n.small1)
    loads.need(n.cot_full, n.d_hidden1, n.hidden1)
    n.small1[11:12, :] = jnp.sum(n.cot_full[:, own].astype(F32), axis=0, keepdims=True)
    unit_sums(n.d_hidden1, n.small1, width)
    across_tokens(n.hidden1, n.cot_full, n.mine_p)
    grads.hand(PR)
    loads.need(n.x1_full, n.wq1, n.d_normed1)
    gain_a, gain_m = n.vec_all[1, 0:1, :], n.vec_all[1, 1:2, :]
    quarters = (2, 3, 0, 1)
    part = tokens // 4

    def prepare(turn_no):
        if turn_no % 2 == 0:
            lane = quarters[turn_no] // 2
            exchange.arrive(lane)
            where = lane_of(lane)
            for head in range(rows):
                n.attn_t1[head * HEAD_DIM : (head + 1) * HEAD_DIM, where] = n.inbox[
                    head, :HEAD_DIM, where
                ]
            d_projection(n.inbox, HEAD_DIM, n.cos, n.sin, rows, n.d_pre, n.small1, where)
        d_norms(
            n.x1_full, n.d_pre, n.wq1, n.d_normed1, gain_a, gain_m, n.total, n.low, n.sums1,
            quarters[turn_no] * part, part,
        )

    def produce(summed, mine):
        unit, rstd = unit_rows(n.x1_full[mine, :].astype(F32))
        moved = (
            summed
            - jnp.mean(summed, axis=1, keepdims=True)
            - unit * jnp.mean(summed * unit, axis=1, keepdims=True)
        )
        return (n.cot_full[mine, :].astype(F32) + rstd * moved).astype(BF)

    def branches(lane):
        where = lane_of(lane)

        def times_slope(value, cols_here):
            return (value * n.slope0[where, cols_here]).astype(BF)

        times_tiles(n.grad_full, n.wp0, n.d_hidden0, times_slope, ((1,), (1,)), where)
        times_tiles(n.d_hidden0, n.wf0, n.d_normed0, None, ((1,), (1,)), where)

    def after(chunk):
        if (chunk + 1) % (CHUNKS // PARTS) == 0:
            lane = 1 - chunk // (CHUNKS // PARTS)
            where = lane_of(lane)
            loads.need(n.wo0)
            flipped = dot(n.grad_full[where, :], n.wo0[...], ((1,), (1,))).T
            for head in range(rows):
                n.pieces[head, :, where] = flipped[
                    head * HEAD_DIM : (head + 1) * HEAD_DIM
                ].astype(BF)
            outward[lane].start()

    def work(time):
        if time == 0:
            loads.need(n.normed_m1)
            across_tokens(n.normed_m1, n.d_hidden1, n.mine_f)
            grads.hand(F)
        if time == 3:
            grads.merge(PR)
        if time == 6:
            grads.merge(F)
        if time == 8:
            grads.pass_on(PR)
        if time == 11:
            loads.need(n.normed_a1)
            across_tokens(n.normed_a1, n.d_pre, n.mine_q, True)
            grads.hand(Q)
        if time == 12:
            out_gradient(n.attn_t1, n.cot_full, n.mine_o)
            grads.hand(O)
        if time == 13:
            grads.pass_on(F)
        if time == 15:
            grads.merge(Q)
            grads.merge(O)
        if time == 17:
            loads.need(n.wp0, n.wf0, n.slope0)
            branches(PARTS - 1)
        if time == 20:
            grads.pass_on(Q)
            grads.pass_on(O)

    chunks = tuple(range(CHUNKS // 2, CHUNKS)) + tuple(range(CHUNKS // 2))
    center_sum(
        place, n.total, n.low, n.from_left, n.from_right, n.grad_full,
        (n.r_a, n.r_b, n.r_c, n.r_d, n.r_e, n.r_f), chunks, prepare, produce, after, work,
    )
    saves.copy(n.grad_full, n.o_grad_full)
    saves.copy(n.attn_t1, n.o_attn_t1)
    saves.copy(n.sums1, n.o_sums1)
    saves.copy(n.small1, n.o_small1)
    for lane in range(PARTS - 1):
        branches(lane)
    saves.copy(n.d_hidden0, n.o_d_hidden0)
    saves.copy(n.d_normed0, n.o_d_normed0)
    for lane in range(PARTS):
        outward[lane].arrive()
    saves.copy(n.d_out, n.o_d_out)
    for kind, made, target in (
        (PR, n.gw_p, n.o_gw_p), (F, n.gw_f, n.o_gw_f), (Q, n.gw_q, n.o_gw_q), (O, n.gw_o, n.o_gw_o),
    ):
        grads.take(kind, made)
        saves.copy(made, target)
    for lane in range(PARTS):
        outward[lane].finish()
    exchange.finish()
    for kind in range(4):
        grads.finish(kind)
    saves.finish()


def turning(rows, cols, kept, cos, sin, lengths):
    tokens, full = kept.x1_full.shape
    width, units = full // cols, kept.hidden1.shape[1]
    total = rows * tokens
    hbm, vmem, smem = pl.ANY, pltpu.VMEM, pltpu.SMEM
    loaded = dict(
        qkvd1=kept.qkvd1, cot_full=kept.cot_full, d_hidden1=kept.d_hidden1, hidden1=kept.hidden1,
        x1_full=kept.x1_full, wq1=kept.wq1, d_normed1=kept.d_normed1, normed_m1=kept.normed_m1,
        normed_a1=kept.normed_a1, wo0=kept.wo0, wp0=kept.wp0, wf0=kept.wf0, slope0=kept.slope0,
    )
    ins = {"i_" + name: (value, hbm) for name, value in loaded.items()}
    ins.update(
        cos=(cos, vmem), sin=(sin, vmem), lengths=(lengths, smem),
        vec_all=(kept.vec_all, vmem),
    )
    rows_low, rows_wide = ((tokens, full), BF), ((tokens, full), F32)
    made = dict(
        grad_full=rows_low, attn_t1=((width, tokens), BF), sums1=((8, full), F32),
        small1=((16, width), F32), d_hidden0=((tokens, units), BF), d_normed0=rows_wide,
        d_out=((HEAD_DIM, total), BF),
    )
    wholes, pieces = grad_shapes(rows, full, width, units)
    made.update({"gw_" + kind: (pieces[kind], F32) for kind in "qfop"})
    outs = {"o_" + name: shape + (hbm,) for name, shape in made.items()}
    scratch = {name: pltpu.VMEM(value.shape, value.dtype) for name, value in loaded.items()}
    scratch.update({name: pltpu.VMEM(*shape) for name, shape in made.items()})
    scratch.update(grad_scratch(rows, full, width, units))
    scratch.update(
        result=pltpu.VMEM((4 * HEAD_DIM, total), BF),
        inbox=pltpu.VMEM((rows, 4 * HEAD_DIM, tokens), BF),
        pieces=pltpu.VMEM((rows, HEAD_DIM, tokens), BF),
        d_pre=pltpu.VMEM((tokens, 3 * width), BF),
        total=pltpu.VMEM(*rows_wide), low=pltpu.VMEM(*rows_low),
        from_left=pltpu.VMEM(*rows_low), from_right=pltpu.VMEM(*rows_low),
        scores=pltpu.VMEM((2, total, QUERY_BLOCK), F32),
        first=pltpu.VMEM((1, total), jnp.int32), key_rows=pltpu.VMEM((total, HEAD_DIM), BF), value_rows=pltpu.VMEM((total, HEAD_DIM), BF),
        key_acc=pltpu.VMEM((HEAD_DIM, total), F32), value_acc=pltpu.VMEM((HEAD_DIM, total), F32),
        load=dma(len(loaded)), save=dma(len(made)),
        g_s=dma(4, 8), g_r=dma(4, 8),
        b_s=dma(rows * PARTS), b_r=dma(PARTS, rows), b_l=dma(PARTS),
        e_s=dma(PARTS, rows), e_r=dma(PARTS, rows), e_l=dma(PARTS),
    )
    for name in ("r_a", "r_b", "r_c", "r_d", "r_e", "r_f"):
        scratch[name] = dma(CHUNKS)
    return kept.joined(
        named_call(partial(turning_kernel, rows, cols, tuple(loaded)), 3, ins, outs, scratch)
    )


def closing_kernel(rows, cols, names, n):
    place = Place(rows, cols)
    s, c = place.s, place.c
    tokens, full = n.x_full.shape
    width = full // cols
    length = tokens // PARTS
    size = QUERY_BLOCK
    own = pl.ds(pl.multiple_of(c * width, width), width)

    def lane_of(lane):
        return slice(lane * length, (lane + 1) * length)

    loads = Loader(n, names)
    loads.start(n.branch1, n.attn_t1, n.wo1, n.qkv0, n.d_out, n.out0, n.log0)
    place.greet(rows=True, cols=True, partner=True, cross_rows=True)
    grads = GradExchange(place, 0, n, "g")
    exchange = BlockExchange(place, n.result, n.inbox, size, n.b_s, n.b_r, n.b_l)

    def features(owner):
        return (slice(None), pl.ds(pl.multiple_of(owner * width, width), width))

    out_sum = LineReduce(
        place, n.branch1, n.o_low, n.o_left, n.o_right, features, (n.o_a, n.o_b, n.o_c, n.o_d)
    )
    grad_sums = [
        LineReduce(
            place, n.total, n.low, n.from_left, n.from_right,
            lambda owner, lane=lane: (lane_of(lane), features(owner)[1]),
            (n.r_a, n.r_b, n.r_c, n.r_d), lane,
        )
        for lane in range(PARTS)
    ]

    loads.need(n.branch1, n.attn_t1, n.wo1)
    attn_rows = n.attn_t1[...].astype(F32).T.astype(BF)
    tile = min(256, full)
    for at in range(0, full, tile):
        value = n.branch1[:, at : at + tile] + dot(attn_rows, n.wo1[:, at : at + tile])
        n.branch1[:, at : at + tile] = value
        n.o_low[:, at : at + tile] = value.astype(BF)
    out_sum.step(0)

    loads.need(n.qkv0, n.d_out, n.out0, n.log0)
    loads.start()
    rows_of_keys(n.qkv0, HEAD_DIM, n.key_rows)
    rows_of_keys(n.qkv0, 2 * HEAD_DIM, n.value_rows)
    prompt = segment_begins(n.lengths, place.s, n.first)
    count = rows * PARTS
    for block in reversed(range(count)):
        here = slice(block * size, (block + 1) * size)
        delta = jnp.sum(
            n.d_out[:, here].astype(F32) * n.out0[:, here], axis=0, keepdims=True
        )
        log_row = n.log0[:, here]

        def probs_of(key_at, keys, query):
            return jnp.exp(
                score_block(prompt, n.first, here, block * size, key_at, keys, n.key_rows, query)
                - log_row
            )

        d_query = gradient_block(
            block, size, n.qkv0, n.d_out, delta, probs_of, n.key_rows, n.value_rows, n.key_acc,
            n.value_acc, block == count - 1,
        )
        n.result[:HEAD_DIM, here] = d_query.astype(BF)
        n.result[HEAD_DIM : 2 * HEAD_DIM, here] = n.key_acc[:, here].astype(BF)
        n.result[2 * HEAD_DIM :, here] = n.value_acc[:, here].astype(BF)
        exchange.start(block)
        if block == count - 1:
            loads.need(n.hidden0, n.grad_full)
            across_tokens(n.hidden0, n.grad_full, n.mine_p)
            grads.hand(PR)
        if block == count - 2:
            out_sum.step(1)
        if block == count - 4:
            grads.merge(PR)
            out_sum.step(2)
    loads.need(n.normed_m0, n.d_hidden0)
    across_tokens(n.normed_m0, n.d_hidden0, n.mine_f)
    grads.hand(F)
    loads.need(n.attn_t0)
    out_gradient(n.attn_t0, n.grad_full, n.mine_o)
    grads.hand(O)
    n.small[...] = jnp.zeros_like(n.small)
    n.sums[...] = jnp.zeros_like(n.sums)
    loads.need(n.sums1, n.small1, n.x1_full)
    n.small[1] = n.small1[...]
    n.sums[1] = n.sums1[...]
    n.small[0, 11:12, :] = jnp.sum(n.grad_full[:, own].astype(F32), axis=0, keepdims=True)
    unit_sums(n.d_hidden0, n.small.at[0], width)
    out_own = n.x1_full[:, own].astype(F32) + out_sum.own() + n.vec_all[1, 7:8, own]
    n.o_own[1] = out_own.astype(BF)
    n.o_own[0] = n.x1_full[:, own]

    def swap_copy(index, source, target):
        return rcopy(
            source.at[1 - s], target.at[s], n.sw_s.at[index], n.sw_r.at[index], section=1 - s
        )

    out_swap = swap_copy(0, n.o_own, n.o_out_rows)
    out_swap.start()
    out_keep = pltpu.make_async_copy(n.o_own.at[s], n.o_out_rows.at[s], n.local.at[0])
    out_keep.start()

    loads.need(n.x_full, n.wq0, n.d_normed0)
    gain_a, gain_m = n.vec_all[0, 0:1, :], n.vec_all[0, 1:2, :]
    lane_no = lax.broadcasted_iota(jnp.int32, (min(128, length), 128), 1)

    def row_sums(where, joined, unit):
        first = jnp.sum(joined, axis=1, keepdims=True)
        second = jnp.sum(joined * unit, axis=1, keepdims=True)
        both = jnp.where(lane_no == 0, first, jnp.where(lane_no == 1, second, 0.0))
        n.line_sums[:, where] = both.T[:8]

    def prepare(lane):
        exchange.arrive(lane)
        d_projection(n.inbox, 0, n.cos, n.sin, rows, n.d_pre, n.small.at[0], lane_of(lane))
        d_norms(
            n.x_full, n.d_pre, n.wq0, n.d_normed0, gain_a, gain_m, n.total, n.low, n.sums.at[0],
            lane * length, length, row_sums,
        )

    grads.pass_on(PR)
    prepare(1)
    grad_sums[1].step(0)
    grads.merge(F)
    prepare(0)
    grad_sums[0].step(0)
    grad_sums[1].step(1)

    def line_copy(step):
        return rcopy(
            n.line_sums, n.line_in.at[step], n.ls_s.at[step], n.ls_r.at[step],
            col=place.col_to(step),
        )

    def col_copy(step):
        target = place.col_to(step)
        piece = n.sums.at[:, :, pl.ds(pl.multiple_of(target * width, width), width)]
        return rcopy(piece, n.col_in.at[step], n.cs_s.at[step], n.cs_r.at[step], col=target)

    def row_copy(ds, step):
        index = ds * rows + step
        layer = lax.rem(s + ds, 2)
        return rcopy(
            n.small.at[layer], n.row_in.at[index], n.rw_s.at[index], n.rw_r.at[index],
            section=layer, row=place.row_to(step),
        )

    for step in range(1, cols):
        line_copy(step).start()
        col_copy(step).start()
    loads.need(n.normed_a0)
    across_tokens(n.normed_a0, n.d_pre, n.mine_q, True)
    grads.hand(Q)
    grad_sums[1].step(2)
    grad_sums[0].step(1)
    grads.merge(O)
    grads.pass_on(F)
    for step in range(1, cols):
        col_copy(step).wait_recv()
    head = n.sums[:, :, own]
    for step in range(1, cols):
        head = head + n.col_in[step]
    n.small[:, :8, :] = head
    others = [(ds, step) for ds in range(2) for step in range(rows) if ds or step]
    for ds, step in others:
        row_copy(ds, step).start()
    grads.merge(Q)
    grad_sums[0].step(2)
    joined = n.line_sums[...]
    for step in range(1, cols):
        line_copy(step).wait_recv()
        joined = joined + n.line_in[step]
    wide = jnp.concatenate([joined, jnp.zeros((120, tokens), F32)], axis=0).T
    unit, rstd = unit_rows(n.x_full[...].astype(F32))
    n.unit[...] = unit
    grads.pass_on(O)
    grads.pass_on(Q)
    for lane in reversed(range(PARTS)):
        where = lane_of(lane)
        moved = (
            grad_sums[lane].own()
            - wide[where, 0:1] / full
            - n.unit[where, own] * (wide[where, 1:2] / full)
        )
        n.g_own[0, where] = (
            n.grad_full[where, own].astype(F32) + rstd[where] * moved
        ).astype(BF)
    n.g_own[1] = n.grad_full[:, own]
    grad_swap = swap_copy(1, n.g_own, n.o_grad_rows)
    grad_swap.start()
    grad_keep = pltpu.make_async_copy(n.g_own.at[s], n.o_grad_rows.at[s], n.local.at[1])
    grad_keep.start()
    mine = n.small[s]
    for ds, step in others:
        row_copy(ds, step).wait_recv()
        mine = mine + n.row_in[ds * rows + step]
    n.o_small[...] = mine
    loads.need(n.gw_p, n.gw_f, n.gw_q, n.gw_o)
    saves = Saver(n.save)
    for kind, made, target in (
        (PR, n.gw_p, n.o_gw_p), (F, n.gw_f, n.o_gw_f), (O, n.gw_o, n.o_gw_o), (Q, n.gw_q, n.o_gw_q),
    ):
        grads.take(kind, made)
        saves.copy(made, target)
    out_keep.wait()
    grad_keep.wait()
    out_swap.wait()
    grad_swap.wait()
    exchange.finish()
    out_sum.finish()
    for reduce in grad_sums:
        reduce.finish()
    for step in range(1, cols):
        line_copy(step).wait_send()
        col_copy(step).wait_send()
    for ds, step in others:
        row_copy(ds, step).wait_send()
    for kind in range(4):
        grads.finish(kind)
    saves.finish()


def closing(rows, cols, kept, cos, sin, lengths):
    tokens, full = kept.x_full.shape
    width, units = full // cols, kept.hidden0.shape[1]
    total = rows * tokens
    hbm, vmem, smem = pl.ANY, pltpu.VMEM, pltpu.SMEM
    loaded = dict(
        qkv0=kept.qkv0, d_out=kept.d_out, out0=kept.out0, log0=kept.log0, hidden0=kept.hidden0,
        grad_full=kept.grad_full, normed_m0=kept.normed_m0, d_hidden0=kept.d_hidden0,
        attn_t0=kept.attn_t0, branch1=kept.branch1, attn_t1=kept.attn_t1, wo1=kept.wo1,
        x_full=kept.x_full, wq0=kept.wq0, d_normed0=kept.d_normed0, normed_a0=kept.normed_a0,
        x1_full=kept.x1_full, sums1=kept.sums1, small1=kept.small1, gw_p=kept.gw_p,
        gw_f=kept.gw_f, gw_q=kept.gw_q, gw_o=kept.gw_o,
    )
    ins = {"i_" + name: (value, hbm) for name, value in loaded.items()}
    ins.update(
        cos=(cos, vmem), sin=(sin, vmem), lengths=(lengths, smem),
        vec_all=(kept.vec_all, vmem),
    )
    rows_low, rows_wide = ((tokens, full), BF), ((tokens, full), F32)
    wholes, pieces = grad_shapes(rows, full, width, units)
    outs = dict(
        o_out_rows=((2, tokens, width), BF, vmem),
        o_grad_rows=((2, tokens, width), BF, vmem), o_small=((16, width), F32, vmem),
    )
    outs.update({"o_gw_" + kind: (pieces[kind], F32, hbm) for kind in "qfop"})
    scratch = {name: pltpu.VMEM(value.shape, value.dtype) for name, value in loaded.items()}
    scratch.update(grad_scratch(rows, full, width, units))
    scratch.update(
        result=pltpu.VMEM((3 * HEAD_DIM, total), BF),
        inbox=pltpu.VMEM((rows, 3 * HEAD_DIM, tokens), BF),
        d_pre=pltpu.VMEM((tokens, 3 * width), BF),
        total=pltpu.VMEM(*rows_wide), low=pltpu.VMEM(*rows_low),
        from_left=pltpu.VMEM(*rows_low), from_right=pltpu.VMEM(*rows_low),
        o_low=pltpu.VMEM(*rows_low), o_left=pltpu.VMEM(*rows_low), o_right=pltpu.VMEM(*rows_low),
        unit=pltpu.VMEM(*rows_wide),
        first=pltpu.VMEM((1, total), jnp.int32), key_rows=pltpu.VMEM((total, HEAD_DIM), BF), value_rows=pltpu.VMEM((total, HEAD_DIM), BF),
        key_acc=pltpu.VMEM((HEAD_DIM, total), F32), value_acc=pltpu.VMEM((HEAD_DIM, total), F32),
        sums=pltpu.VMEM((2, 8, full), F32), small=pltpu.VMEM((2, 16, width), F32),
        line_sums=pltpu.VMEM((8, tokens), F32), line_in=pltpu.VMEM((cols, 8, tokens), F32),
        col_in=pltpu.VMEM((cols, 2, 8, width), F32),
        row_in=pltpu.VMEM((2 * rows, 16, width), F32),
        o_own=pltpu.VMEM((2, tokens, width), BF), g_own=pltpu.VMEM((2, tokens, width), BF),
        load=dma(len(loaded)), save=dma(4), local=dma(2),
        g_s=dma(4, 8), g_r=dma(4, 8),
        b_s=dma(rows * PARTS), b_r=dma(PARTS, rows), b_l=dma(PARTS),
        ls_s=dma(cols), ls_r=dma(cols), cs_s=dma(cols), cs_r=dma(cols),
        rw_s=dma(2 * rows), rw_r=dma(2 * rows), sw_s=dma(2), sw_r=dma(2),
    )
    for name in ("r_a", "r_b", "r_c", "r_d"):
        scratch[name] = dma(PARTS, cols)
    for name in ("o_a", "o_b", "o_c", "o_d"):
        scratch[name] = dma(1, cols)
    return Names().joined(
        named_call(partial(closing_kernel, rows, cols, tuple(loaded)), 4, ins, outs, scratch)
    )


def finishing_kernel(n):
    for source, target in (
        (n.i_out_rows, n.out_rows), (n.i_grad_rows, n.grad_rows), (n.i_gw_q, n.gw_q),
        (n.i_gw_f, n.gw_f), (n.i_gw_o, n.gw_o), (n.i_gw_p, n.gw_p),
    ):
        target[0] = source[...]
    width = n.small.shape[1]
    n.gains[0] = n.small[0:2]
    n.shifts[0] = n.small[2:4]
    n.g_qkv[0] = n.small[8:11]
    n.g_out[...] = n.small[11:12]
    for index in range(n.g_fc.shape[1] // width):
        n.g_fc[:, index * width : (index + 1) * width] = n.small[12 + index : 13 + index]


def finishing(k):
    vmem = pltpu.VMEM
    made = dict(
        out_rows=k.out_rows, grad_rows=k.grad_rows, gw_q=k.gw_q, gw_f=k.gw_f, gw_o=k.gw_o,
        gw_p=k.gw_p,
    )
    ins = {"i_" + name: (value, vmem) for name, value in made.items()}
    ins.update(small=(k.small, vmem))
    width, units = k.small.shape[1], k.gw_f.shape[1]
    large = {name: ((1,) + value.shape, value.dtype, vmem) for name, value in made.items()}
    outs = dict(
        out_rows=None, grad_rows=None, gains=((1, 2, width), F32, vmem),
        shifts=((1, 2, width), F32, vmem), gw_q=None, g_qkv=((1, 3, width), F32, vmem), gw_o=None,
        gw_f=None, g_fc=((1, units), F32, vmem), gw_p=None, g_out=((1, width), F32, vmem),
    )
    outs.update(large)
    return tuple(named_call(finishing_kernel, None, ins, outs, {}).values())


def relay_body(
    hidden_in,
    cotangent,
    lengths,
    norm_gains,
    norm_biases,
    w_qkv,
    b_qkv,
    w_out,
    w_fc,
    b_fc,
    w_proj,
    b_out,
):
    rows, cols = lax.axis_size(ROW), lax.axis_size(COL)
    tokens, width = hidden_in.shape[1:]
    section = lax.axis_index(SECTION)
    lengths_row = lax.dynamic_index_in_dim(lengths, section, 0, keepdims=False)

    def begin_of(token_ids):
        begin = jnp.zeros_like(token_ids)
        start = lengths_row[0]
        for index in range(1, lengths_row.shape[0]):
            begin = jnp.where(token_ids >= start, start, begin)
            start = start + lengths_row[index]
        return begin

    my_tokens = (
        lax.axis_index(ROW) * tokens + lax.broadcasted_iota(jnp.int32, (ROT // 2, tokens), 1)
    )
    my_first = begin_of(my_tokens)
    position = jnp.where(my_first == 0, my_tokens, lengths_row[0] + my_tokens - my_first)
    freqs = 10000.0 ** (-(2.0 * jnp.arange(ROT // 2, dtype=jnp.float32)) / ROT)
    angles = position.astype(F32) * freqs[:, None]
    cos, sin = jnp.cos(angles), jnp.sin(angles)
    blocks = (w_qkv[0], w_fc[0], w_out[0], w_proj[0])
    vectors = (norm_gains, norm_biases, b_qkv, b_out, b_fc)
    k = first_half(rows, cols, hidden_in, cotangent, vectors, blocks, cos, sin, lengths)
    k = turning(rows, cols, k, cos, sin, lengths)
    return finishing(closing(rows, cols, k, cos, sin, lengths))


def fits(mesh):
    rows, cols = mesh.shape[ROW], mesh.shape[COL]
    return rows == cols == 4 and MODEL_WIDTH == rows * cols * HEAD_DIM


def solution(mesh):
    return jax.shard_map(
        relay_body if fits(mesh) else body,
        mesh=mesh,
        in_specs=(
            P(None, ROW, COL),
            P(None, ROW, COL),
            P(),
            P(SECTION, None, COL),
            P(SECTION, None, COL),
            P(SECTION, None, ROW, COL),
            P(SECTION, None, COL),
            P(SECTION, COL, ROW),
            P(SECTION, ROW, COL),
            P(SECTION, COL),
            P(SECTION, COL, ROW),
            P(SECTION, COL),
        ),
        out_specs=(
            P(SECTION, None, ROW, COL),
            P(SECTION, None, ROW, COL),
            P(SECTION, None, COL),
            P(SECTION, None, COL),
            P(SECTION, None, ROW, COL),
            P(SECTION, None, COL),
            P(SECTION, COL, ROW),
            P(SECTION, ROW, COL),
            P(SECTION, COL),
            P(SECTION, COL, ROW),
            P(SECTION, COL),
        ),
        check_vma=False,
    )
```

```python
from functools import partial
import math

import jax
import jax.numpy as jnp
from jax import lax
from jax.experimental import pallas as pl
from jax.experimental.pallas import tpu as pltpu
from jax.sharding import PartitionSpec as P

MODEL_WIDTH = 1024
HEAD_DIM = 64
ROT = 16
SECTION, ROW, COL = "section", "row", "col"


EPS = 1e-05
NEG = -1e30


def from_partner(value, axis, apart):
    mask = 2**apart
    pairs = [(source, source ^ mask) for source in range(lax.axis_size(axis))]
    return lax.ppermute(value, axis, pairs)


def segment_of(token_ids, starts):
    return jnp.sum((token_ids[:, None] >= starts[None, 1:]).astype(jnp.int32), axis=1)


def token_layout(lengths_row, token_ids):
    starts = jnp.cumsum(lengths_row) - lengths_row
    segment = segment_of(token_ids, starts)
    labels = jnp.arange(1, lengths_row.shape[0], dtype=jnp.int32)
    seg_begin = jnp.sum(jnp.where(segment[:, None] == labels[None, :], starts[None, 1:], 0), axis=1)
    position = jnp.where(segment == 0, token_ids, lengths_row[0] + token_ids - seg_begin)
    return (starts, segment, position)


def rotary_tables(position, turned):
    half_rot = turned // 2
    freqs = 10000.0 ** (-(2.0 * jnp.arange(half_rot, dtype=jnp.float32)) / turned)
    angles = position.astype(jnp.float32)[:, None] * freqs[None, :]
    return (jnp.cos(angles), jnp.sin(angles))


def rotate(values, cos_table, sin_table, direction):
    half_rot = cos_table.shape[-1]
    lower = values[..., :half_rot]
    upper = values[..., half_rot : 2 * half_rot]
    cos_cast = cos_table[:, None, :]
    sin_cast = direction * sin_table[:, None, :]
    return jnp.concatenate(
        [
            lower * cos_cast - upper * sin_cast,
            upper * cos_cast + lower * sin_cast,
            values[..., 2 * half_rot :],
        ],
        axis=-1,
    )


def permitted(query_seg, query_tok, key_seg, key_tok):
    from_prompt = (key_seg[None, :] == 0) & (query_seg[:, None] > 0)
    same_causal = (key_seg[None, :] == query_seg[:, None]) & (
        key_tok[None, :] <= query_tok[:, None]
    )
    return from_prompt | same_causal


def attend(running, key_piece, value_piece, query3, layout):
    run_max, run_sum, totals = running
    piece_len = key_piece.shape[0]
    key3 = key_piece.reshape(piece_len, query3.shape[1], query3.shape[2])
    value3 = value_piece.reshape(piece_len, query3.shape[1], query3.shape[2])
    key_tok = jnp.arange(piece_len, dtype=jnp.int32)
    key_seg = segment_of(key_tok, layout["starts"])
    allowed = permitted(layout["segment"], layout["tokens"], key_seg, key_tok)[None]
    scores = jnp.einsum("qhd,khd->hqk", query3, key3, preferred_element_type=jnp.float32) * (
        1.0 / math.sqrt(query3.shape[2])
    )
    masked = jnp.where(allowed, scores, NEG)
    new_max = jnp.maximum(run_max, jnp.max(masked, axis=-1))
    weights = jnp.where(allowed, jnp.exp(masked - new_max[..., None]), 0.0)
    run_sum = jnp.sum(weights, axis=-1)
    totals = jnp.einsum(
        "hqk,khd->hqd", weights.astype(jnp.bfloat16), value3, preferred_element_type=jnp.float32
    )
    return (new_max, run_sum, totals)


def layer_forward(x, full, weights, layout, complete_gains, complete_shifts):
    w_query, b_query, w_output, w_hidden, b_hidden, w_project, b_output = weights
    row_tokens, local_width = x.shape
    heads_local = local_width // HEAD_DIM
    shaped = (row_tokens, heads_local, HEAD_DIM)
    as_float = full.astype(jnp.float32)
    row_mean = jnp.mean(as_float, axis=1, keepdims=True)
    centred = as_float - row_mean
    rstd = lax.rsqrt(jnp.mean(centred * centred, axis=1, keepdims=True) + EPS)
    unit = centred * rstd
    normed_a = (unit * complete_gains[0] + complete_shifts[0]).astype(jnp.bfloat16)
    normed_m = (unit * complete_gains[1] + complete_shifts[1]).astype(jnp.bfloat16)
    projected = (
        jnp.einsum("td,cde->cte", normed_a, w_query, preferred_element_type=jnp.float32)
        + b_query[:, None, :]
    )
    cos_table, sin_table = layout["cos_table"], layout["sin_table"]
    query3 = rotate(projected[0].reshape(shaped), cos_table, sin_table, 1.0).astype(jnp.bfloat16)
    key_flat = (
        rotate(projected[1].reshape(shaped), cos_table, sin_table, 1.0)
        .reshape(row_tokens, local_width)
        .astype(jnp.bfloat16)
    )
    value_flat = projected[2].astype(jnp.bfloat16)
    key_full = lax.all_gather(key_flat, ROW, axis=0, tiled=True)
    value_full = lax.all_gather(value_flat, ROW, axis=0, tiled=True)
    initial = (
        jnp.full((heads_local, row_tokens), NEG, jnp.float32),
        jnp.zeros((heads_local, row_tokens), jnp.float32),
        jnp.zeros((heads_local, row_tokens, HEAD_DIM), jnp.float32),
    )
    run_max, run_sum, totals = attend(initial, key_full, value_full, query3, layout)
    out_exact = totals / run_sum[..., None]
    log_sum = run_max + jnp.log(run_sum)
    attn_flat = (
        jnp.transpose(out_exact, (1, 0, 2)).reshape(row_tokens, local_width).astype(jnp.bfloat16)
    )
    hidden_pre = jnp.dot(normed_m, w_hidden, preferred_element_type=jnp.float32) + b_hidden
    hidden = jax.nn.gelu(hidden_pre, approximate=False).astype(jnp.bfloat16)
    branch = jnp.dot(attn_flat, w_output, preferred_element_type=jnp.float32) + jnp.dot(
        hidden, w_project, preferred_element_type=jnp.float32
    )
    summed = lax.psum_scatter(
        branch.astype(jnp.bfloat16), COL, scatter_dimension=1, tiled=True
    ).astype(jnp.float32)
    output = (x.astype(jnp.float32) + summed + b_output).astype(jnp.bfloat16)
    state = dict(
        unit=unit, rstd=rstd, normed_a=normed_a, normed_m=normed_m, query3=query3,
        key_full=key_full, value_full=value_full, attn_flat=attn_flat, out_exact=out_exact,
        log_sum=log_sum, hidden_pre=hidden_pre, hidden=hidden,
    )
    return output, state


def layer_backward(state, grad_in, grad_full, weights, layout, complete_gains, scatter_tokens):
    w_query, b_query, w_output, w_hidden, b_hidden, w_project, b_output = weights
    row_tokens = state["normed_a"].shape[0]
    local_width = w_output.shape[0]
    heads_local = local_width // HEAD_DIM
    shaped = (row_tokens, heads_local, HEAD_DIM)
    score_scale = 1.0 / math.sqrt(HEAD_DIM)
    total_tokens = state["key_full"].shape[0]
    key_block = min(512, total_tokens)
    grad_wout = jnp.einsum(
        "te,td->ed", state["attn_flat"], grad_full, preferred_element_type=jnp.float32
    )
    grad_wproj = jnp.einsum(
        "tf,td->fd", state["hidden"], grad_full, preferred_element_type=jnp.float32
    )
    grad_bout = jnp.sum(grad_in.astype(jnp.float32), axis=0)
    grad_attn = jnp.einsum(
        "td,ed->te", grad_full, w_output, preferred_element_type=jnp.float32
    ).astype(jnp.bfloat16)
    grad_hidden = jnp.einsum("td,fd->tf", grad_full, w_project, preferred_element_type=jnp.float32)
    gelu_value, gelu_back = jax.vjp(partial(jax.nn.gelu, approximate=False), state["hidden_pre"])
    grad_hpre = gelu_back(grad_hidden)[0].astype(jnp.bfloat16)
    grad_wfc = jnp.einsum(
        "td,tf->df", state["normed_m"], grad_hpre, preferred_element_type=jnp.float32
    )
    grad_bfc = jnp.sum(grad_hpre.astype(jnp.float32), axis=0)
    grad_normed_m = jnp.einsum("tf,df->td", grad_hpre, w_hidden, preferred_element_type=jnp.float32)
    grad_out3 = grad_attn.reshape(shaped)
    query3 = state["query3"]
    delta = jnp.sum(
        jnp.transpose(grad_out3.astype(jnp.float32), (1, 0, 2)) * state["out_exact"], axis=-1
    )
    grad_query = jnp.zeros(shaped, jnp.float32)
    key_terms = []
    value_terms = []
    for block_no in range(total_tokens // key_block):
        begin_at = block_no * key_block
        key_part = state["key_full"][begin_at : begin_at + key_block].reshape(
            key_block, heads_local, HEAD_DIM
        )
        value_part = state["value_full"][begin_at : begin_at + key_block].reshape(
            key_block, heads_local, HEAD_DIM
        )
        key_tok = begin_at + jnp.arange(key_block, dtype=jnp.int32)
        key_seg = segment_of(key_tok, layout["starts"])
        allowed = permitted(layout["segment"], layout["tokens"], key_seg, key_tok)[None]
        scores = (
            jnp.einsum("qhd,khd->hqk", query3, key_part, preferred_element_type=jnp.float32)
            * score_scale
        )
        probs = jnp.where(
            allowed,
            jnp.exp(jnp.where(allowed, scores, NEG) - state["log_sum"][..., None]),
            0.0,
        )
        grad_probs = jnp.einsum(
            "qhd,khd->hqk", grad_out3, value_part, preferred_element_type=jnp.float32
        )
        grad_scores = (probs * (grad_probs - delta[..., None])).astype(jnp.bfloat16)
        grad_query = grad_query + jnp.einsum(
            "hqk,khd->qhd", grad_scores, key_part, preferred_element_type=jnp.float32
        )
        key_terms.append(
            jnp.einsum(
                "hqk,qhd->khd", grad_scores, query3, preferred_element_type=jnp.float32
            ).reshape(key_block, local_width)
            * score_scale
        )
        value_terms.append(
            jnp.einsum(
                "hqk,qhd->khd",
                probs.astype(jnp.bfloat16),
                grad_out3,
                preferred_element_type=jnp.float32,
            ).reshape(key_block, local_width)
        )
    grad_query = grad_query * score_scale
    kv_terms = jnp.concatenate(
        [jnp.concatenate(key_terms, axis=0), jnp.concatenate(value_terms, axis=0)], axis=1
    )
    kv_grads = lax.psum_scatter(
        kv_terms.astype(jnp.bfloat16), ROW, scatter_dimension=0, tiled=True
    ).astype(jnp.float32)
    grad_key = kv_grads[:, :local_width].reshape(shaped)
    grad_value = kv_grads[:, local_width:]
    cos_table, sin_table = layout["cos_table"], layout["sin_table"]
    grad_pre = jnp.stack(
        [
            rotate(grad_query, cos_table, sin_table, -1.0).reshape(row_tokens, local_width),
            rotate(grad_key, cos_table, sin_table, -1.0).reshape(row_tokens, local_width),
            grad_value,
        ]
    ).astype(jnp.bfloat16)
    grad_wqkv = jnp.einsum(
        "td,cte->cde", state["normed_a"], grad_pre, preferred_element_type=jnp.float32
    )
    grad_bqkv = jnp.sum(grad_pre.astype(jnp.float32), axis=1)
    grad_normed_a = jnp.einsum("cte,cde->td", grad_pre, w_query, preferred_element_type=jnp.float32)
    unit = state["unit"]
    grad_gains = jnp.stack(
        [jnp.sum(grad_normed_a * unit, axis=0), jnp.sum(grad_normed_m * unit, axis=0)]
    )
    grad_shifts = jnp.stack([jnp.sum(grad_normed_a, axis=0), jnp.sum(grad_normed_m, axis=0)])
    grad_unit = grad_normed_a * complete_gains[0] + grad_normed_m * complete_gains[1]
    big = (grad_wqkv, grad_wout, grad_wfc, grad_wproj)
    big = tuple(member.astype(jnp.bfloat16) for member in big)
    shared = (grad_gains, grad_shifts)
    local = (grad_bqkv, grad_bfc, grad_bout)
    if scatter_tokens:
        piece = lax.psum_scatter(
            grad_unit.astype(jnp.bfloat16), COL, scatter_dimension=0, tiled=True
        ).astype(jnp.float32)
        rows = piece.shape[0]
        start = lax.axis_index(COL) * rows
        unit_part = lax.dynamic_slice_in_dim(unit, start, rows, 0)
        rstd_part = lax.dynamic_slice_in_dim(state["rstd"], start, rows, 0)
        grad_part = lax.dynamic_slice_in_dim(grad_full, start, rows, 0).astype(jnp.float32)
        moved = (
            piece
            - jnp.mean(piece, axis=1, keepdims=True)
            - unit_part * jnp.mean(piece * unit_part, axis=1, keepdims=True)
        )
        grad_input = (grad_part + rstd_part * moved).astype(jnp.bfloat16)
    else:
        sums = lax.psum(
            jnp.stack([jnp.sum(grad_unit, axis=1), jnp.sum(grad_unit * unit, axis=1)]), COL
        )
        piece = lax.psum_scatter(
            grad_unit.astype(jnp.bfloat16), COL, scatter_dimension=1, tiled=True
        ).astype(jnp.float32)
        width = piece.shape[1]
        unit_part = lax.dynamic_slice_in_dim(unit, lax.axis_index(COL) * width, width, 1)
        moved = (
            piece
            - sums[0][:, None] / MODEL_WIDTH
            - unit_part * (sums[1][:, None] / MODEL_WIDTH)
        )
        grad_input = (grad_in.astype(jnp.float32) + state["rstd"] * moved).astype(jnp.bfloat16)
    return grad_input, big, shared, local


def body(
    hidden_in,
    cotangent,
    lengths,
    norm_gains,
    norm_biases,
    w_qkv,
    b_qkv,
    w_out,
    w_fc,
    b_fc,
    w_proj,
    b_out,
):
    row_tokens = hidden_in.shape[1]
    local_width = hidden_in.shape[2]
    section = lax.axis_index(SECTION)
    is_first = section == 0
    my_tokens = lax.axis_index(ROW) * row_tokens + jnp.arange(row_tokens, dtype=jnp.int32)
    x0 = lax.dynamic_index_in_dim(hidden_in, section, 0, keepdims=False)
    cot = lax.dynamic_index_in_dim(cotangent, section, 0, keepdims=False)
    lengths_row = lax.dynamic_index_in_dim(lengths, section, 0, keepdims=False)
    starts, segment, position = token_layout(lengths_row, my_tokens)
    cos_table, sin_table = rotary_tables(position, ROT)
    layout = {
        "starts": starts,
        "segment": segment,
        "tokens": my_tokens,
        "cos_table": cos_table,
        "sin_table": sin_table,
    }
    both = (SECTION, ROW)
    gains = lax.all_gather(norm_gains[0], (SECTION, COL), axis=0)
    shifts = lax.all_gather(norm_biases[0], (SECTION, COL), axis=0)
    cols = lax.axis_size(COL)

    def whole(vectors):
        split = vectors.reshape(2, cols, 2, local_width)
        return jnp.transpose(split, (0, 2, 1, 3)).reshape(2, 2, cols * local_width)

    gains, shifts = whole(gains), whole(shifts)
    biases = [lax.all_gather(member[0], SECTION, axis=0) for member in (b_qkv, b_fc, b_out)]
    x0_full = lax.all_gather(x0, COL, axis=1, tiled=True)
    rows = lax.axis_size(ROW)

    def unite(member, axis):
        gathered = lax.all_gather(member[0], both, axis=0)
        pieces = gathered.reshape((2, rows) + gathered.shape[1:])
        return [
            jnp.concatenate([pieces[layer, row] for row in range(rows)], axis=axis)
            for layer in range(2)
        ]

    w_query, w_hidden = unite(w_qkv, 1), unite(w_fc, 0)
    w_output, w_project = unite(w_out, 1), unite(w_proj, 1)
    weights = [
        (
            w_query[layer],
            biases[0][layer],
            w_output[layer],
            w_hidden[layer],
            biases[1][layer],
            w_project[layer],
            biases[2][layer],
        )
        for layer in range(2)
    ]
    out0, state0 = layer_forward(x0, x0_full, weights[0], layout, gains[0], shifts[0])
    x1_full = lax.all_gather(out0, COL, axis=1, tiled=True)
    cot_full = lax.all_gather(cot, COL, axis=1, tiled=True)
    out1, state1 = layer_forward(out0, x1_full, weights[1], layout, gains[1], shifts[1])
    grad1_part, big1, shared1, local1 = layer_backward(
        state1, cot, cot_full, weights[1], layout, gains[1], True
    )
    grad1_full = lax.all_gather(grad1_part, COL, axis=0, tiled=True)
    grad1 = lax.dynamic_slice_in_dim(
        grad1_full, lax.axis_index(COL) * local_width, local_width, 1
    )
    grad0, big0, shared0, local0 = layer_backward(
        state0, grad1, grad1_full, weights[0], layout, gains[0], False
    )

    def swap(first, second):
        mine = jnp.where(is_first, first, second)
        theirs = from_partner(jnp.where(is_first, second, first), SECTION, 0)
        return jnp.where(is_first, jnp.stack([mine, theirs]), jnp.stack([theirs, mine]))[None]

    out_rows = swap(out0, out1)
    grad_rows = swap(grad0, grad1)

    def scatter(first, second, axis):
        length = first.shape[axis] // rows
        pieces = jnp.stack(
            [
                lax.slice_in_dim(member, row * length, (row + 1) * length, axis=axis)
                for member in (first, second)
                for row in range(rows)
            ]
        )
        return lax.psum_scatter(pieces, both, scatter_dimension=0, tiled=True).astype(jnp.float32)

    large = [scatter(a, b, axis) for a, b, axis in zip(big0, big1, (1, 1, 0, 1))]
    shared_sums = lax.psum(
        tuple(jnp.stack([a, b]) for a, b in zip(shared0, shared1)), (SECTION, ROW, COL)
    )
    shared_mine = [
        lax.dynamic_slice(
            member,
            (section, 0, lax.axis_index(COL) * local_width),
            (1, 2, local_width),
        )
        for member in shared_sums
    ]
    local_sums = lax.psum(tuple(jnp.stack([a, b]) for a, b in zip(local0, local1)), both)
    local_mine = [lax.dynamic_index_in_dim(member, section, 0) for member in local_sums]
    return (
        out_rows,
        grad_rows,
        shared_mine[0],
        shared_mine[1],
        large[0],
        local_mine[0],
        large[1],
        large[2],
        local_mine[1],
        large[3],
        local_mine[2],
    )


BF = jnp.bfloat16
F32 = jnp.float32
BY_MESH = pl.DeviceIdType.MESH
VMEM_LIMIT = 62 * 2**20
QUERY_BLOCK = 256
KEY_BLOCK = 512
PROMPT_LEAST = 768
PARTS = 2
CHUNKS = 16
LOADS = 24
LAG = 4


def dot(a, b, contract=((1,), (0,))):
    return lax.dot_general(a, b, (contract, ((), ())), preferred_element_type=F32)


def rcopy(src, dst, ssem, rsem, **device):
    return pltpu.make_async_remote_copy(
        src_ref=src,
        dst_ref=dst,
        send_sem=ssem,
        recv_sem=rsem,
        device_id=device,
        device_id_type=BY_MESH,
    )


class Place:
    def __init__(self, rows, cols):
        self.rows, self.cols = rows, cols
        self.s = lax.axis_index(SECTION)
        self.r = lax.axis_index(ROW)
        self.c = lax.axis_index(COL)

    def row_to(self, step):
        return lax.rem(self.r + step, self.rows)

    def row_from(self, step):
        return lax.rem(self.r + self.rows - step, self.rows)

    def beside(self, way):
        if way == 0:
            return self.r + 1 - 2 * lax.rem(self.r, 2)
        return lax.rem(self.r + 2, 4)

    def across(self):
        return 3 - self.r

    def col_to(self, step):
        return lax.rem(self.c + step, self.cols)

    def col_from(self, step):
        return lax.rem(self.c + self.cols - step, self.cols)

    def greet(self, rows=False, cols=False, partner=False, cross_cols=False, cross_rows=False):
        barrier = pltpu.get_barrier_semaphore()
        count = 0

        def signal(**device):
            pl.semaphore_signal(barrier, inc=1, device_id=device, device_id_type=BY_MESH)

        if rows:
            for step in range(1, self.rows):
                signal(row=self.row_to(step))
                count += 1
        if cols:
            for step in range(1, self.cols):
                signal(col=self.col_to(step))
                count += 1
        if partner:
            signal(section=1 - self.s)
            count += 1
        if cross_cols:
            for step in range(1, self.cols):
                signal(section=1 - self.s, col=self.col_to(step))
                count += 1
        if cross_rows:
            for step in range(1, self.rows):
                signal(section=1 - self.s, row=self.row_to(step))
                count += 1
        pl.semaphore_wait(barrier, count)


class LineGather:
    def __init__(self, place, view, send_right, send_left, recv, lane=0):
        self.place, self.view, self.lane = place, view, lane
        self.send_right, self.send_left, self.recv = send_right, send_left, recv

    def right(self, block):
        return rcopy(
            self.view(block), self.view(block), self.send_right.at[self.lane, block],
            self.recv.at[self.lane, block],
            col=lax.rem(self.place.c + 1, self.place.cols),
        )

    def left(self, block):
        cols = self.place.cols
        return rcopy(
            self.view(block), self.view(block), self.send_left.at[self.lane, block],
            self.recv.at[self.lane, block],
            col=lax.rem(self.place.c + cols - 1, cols),
        )

    def hop(self, distance):
        c, cols = self.place.c, self.place.cols

        @pl.when(c >= distance)
        def _():
            block = lax.rem(c + cols - distance, cols)
            if distance:
                self.right(block).wait_recv()

            @pl.when(c < cols - 1)
            def _():
                self.right(block).start()

        @pl.when(c + distance < cols)
        def _():
            block = lax.rem(c + distance, cols)
            if distance:
                self.left(block).wait_recv()

            @pl.when(c > 0)
            def _():
                self.left(block).start()

    def finish(self):
        c, cols = self.place.c, self.place.cols
        for distance in range(cols):

            @pl.when((c >= distance) & (c < cols - 1))
            def _():
                self.right(lax.rem(c + cols - distance, cols)).wait_send()

            @pl.when((c + distance < cols) & (c > 0))
            def _():
                self.left(lax.rem(c + distance, cols)).wait_send()


class WeightGather:
    def __init__(self, place, layer, own, full, send, recv, local):
        self.place, self.layer, self.own, self.full = place, layer, own, full
        self.send, self.recv, self.local = send, recv, local

    def view(self, kind, block, half=None):
        lines = self.own[kind].shape[-2]
        length = self.own[kind].shape[-2 if kind in (0, 1) else -1]
        at, count = (0, lines) if half is None else (half * (lines // 2), lines // 2)
        if kind in (0, 1):
            piece = pl.ds(pl.multiple_of(block * length + at, count), count)
            return self.full[kind].at[:, piece, :] if kind == 0 else self.full[1].at[piece, :]
        piece = pl.ds(pl.multiple_of(block * length, length), length)
        return self.full[kind].at[at : at + count, piece]

    def direct(self, kind, way):
        place = self.place
        return rcopy(
            self.own[kind], self.view(kind, place.r), self.send.at[kind, way],
            self.recv.at[kind, way], row=place.beside(way),
        )

    def relayed(self, kind, way):
        place = self.place
        piece = self.view(kind, place.beside(way), way)
        return rcopy(
            piece, piece, self.send.at[kind, 2 + way], self.recv.at[kind, 2 + way],
            row=place.beside(1 - way),
        )

    def arriving(self, kind, way):
        block = self.view(kind, self.place.beside(way))
        return rcopy(
            block, block, self.send.at[kind, way], self.recv.at[kind, way],
            row=self.place.beside(way),
        )

    def across(self, kind, way):
        piece = self.view(kind, self.place.across(), way)
        return rcopy(
            piece, piece, self.send.at[kind, 2 + way], self.recv.at[kind, 2 + way],
            row=self.place.beside(1 - way),
        )

    def to_partner(self, kind, which):
        place = self.place
        source = (place.beside(0), place.beside(1), place.across(), place.r)[which]
        block = self.view(kind, source)
        return rcopy(
            self.own[kind] if which == 3 else block, block, self.send.at[kind, 4 + which],
            self.recv.at[kind, 4 + which], section=1 - place.s,
        )

    def keep(self, kind):
        return pltpu.make_async_copy(
            self.own[kind], self.view(kind, self.place.r), self.local.at[kind]
        )

    def start(self, kind):
        @pl.when(self.place.s == self.layer)
        def _():
            for way in range(2):
                self.direct(kind, way).start()
            self.keep(kind).start()
            self.to_partner(kind, 3).start()

    def relay(self, kind):
        @pl.when(self.place.s == self.layer)
        def _():
            for way in range(2):
                self.arriving(kind, way).wait_recv()
                self.relayed(kind, way).start()
                self.to_partner(kind, way).start()

    def forward(self, kind):
        @pl.when(self.place.s == self.layer)
        def _():
            for way in range(2):
                self.across(kind, way).wait_recv()
            self.to_partner(kind, 2).start()
            self.keep(kind).wait()

    def ready(self, kind):
        @pl.when(self.place.s != self.layer)
        def _():
            for which in range(4):
                self.to_partner(kind, which).wait_recv()

    def finish(self, kind):
        @pl.when(self.place.s == self.layer)
        def _():
            for way in range(2):
                self.direct(kind, way).wait_send()
                self.relayed(kind, way).wait_send()
            for which in range(4):
                self.to_partner(kind, which).wait_send()


class RowExchange:
    def __init__(self, place, piece_for, slot_of, send, recv, local):
        self.place, self.piece_for, self.slot_of = place, piece_for, slot_of
        self.send, self.recv, self.local = send, recv, local

    def out(self, step):
        place = self.place
        target = place.row_to(step)
        return rcopy(
            self.piece_for(target), self.slot_of(place.r), self.send.at[step], self.recv.at[step],
            row=target,
        )

    def into(self, step):
        slot = self.slot_of(self.place.row_from(step))
        return rcopy(
            slot, slot, self.send.at[step], self.recv.at[step], row=self.place.row_to(step)
        )

    def keep(self):
        return pltpu.make_async_copy(
            self.piece_for(self.place.r), self.slot_of(self.place.r), self.local
        )

    def start(self):
        for step in range(1, self.place.rows):
            self.out(step).start()
        self.keep().start()

    def arrive(self):
        for step in range(1, self.place.rows):
            self.into(step).wait_recv()
        self.keep().wait()

    def finish(self):
        for step in range(1, self.place.rows):
            self.out(step).wait_send()


def norm_rows(source, gains_a, shifts_a, gains_m, shifts_m, normed_a, normed_m, begin=0, count=None):
    count = source.shape[0] if count is None else count
    tile = min(128, count)

    @pl.loop(0, count // tile)
    def _(index):
        rows = pl.ds(pl.multiple_of(begin + index * tile, tile), tile)
        values = source[rows, :].astype(F32)
        centred = values - jnp.mean(values, axis=1, keepdims=True)
        unit = centred * lax.rsqrt(jnp.mean(centred * centred, axis=1, keepdims=True) + EPS)
        normed_a[rows, :] = (unit * gains_a + shifts_a).astype(BF)
        normed_m[rows, :] = (unit * gains_m + shifts_m).astype(BF)


def turn(block, cos, sin, direction):
    half = cos.shape[0]
    lower, upper, rest = block[:half], block[half : 2 * half], block[2 * half :]
    return jnp.concatenate(
        [
            lower * cos - upper * (direction * sin),
            upper * cos + lower * (direction * sin),
            rest,
        ],
        axis=0,
    )


def project_heads(normed_a, w_query, bias_rows, cos, sin, pieces, heads, where):
    for kind in range(3):
        flipped = (dot(normed_a[where, :], w_query[kind]) + bias_rows(kind)).T
        for head in range(heads):
            block = flipped[head * HEAD_DIM : (head + 1) * HEAD_DIM]
            if kind < 2:
                block = turn(block, cos[:, where], sin[:, where], 1.0)
            pieces[head, kind * HEAD_DIM : (kind + 1) * HEAD_DIM, where] = block.astype(BF)


def feed_forward(normed_m, w_hidden, bias_of, hidden, slope, where):
    tile = min(256, w_hidden.shape[1])

    @pl.loop(0, w_hidden.shape[1] // tile)
    def _(index):
        cols = pl.ds(pl.multiple_of(index * tile, tile), tile)
        pre = dot(normed_m[where, :], w_hidden[:, cols]) + bias_of(index)
        phi = 0.5 * (1.0 + lax.erf(pre * math.sqrt(0.5)))
        hidden[where, cols] = (pre * phi).astype(BF)
        turned = phi + pre * (jnp.exp(-0.5 * pre * pre) * (1.0 / math.sqrt(2.0 * math.pi)))
        slope[where, cols] = turned.astype(slope.dtype)


def times_tiles(left, right, out, convert=None, contract=((1,), (0,)), where=slice(None)):
    tile = min(256, out.shape[1])

    @pl.loop(0, out.shape[1] // tile)
    def _(index):
        cols = pl.ds(pl.multiple_of(index * tile, tile), tile)
        piece = right[:, cols] if contract[1] == (0,) else right[cols, :]
        value = dot(left[where, :], piece, contract)
        out[where, cols] = value if convert is None else convert(value, cols)


def dma(*shape):
    return pltpu.SemaphoreType.DMA(shape)


def key_mask(prompt, first, cols, key_at, query_at, keys, queries):
    in_prompt = key_at + keys <= PROMPT_LEAST
    before = key_at + keys <= query_at + 1
    if in_prompt and before:
        return None
    key = lax.broadcasted_iota(jnp.int32, (keys, queries), 0) + key_at
    allowed = None
    if not in_prompt:
        allowed = (key < prompt) | (key >= first[:, cols])
    if not before:
        causal = key <= lax.broadcasted_iota(jnp.int32, (keys, queries), 1) + query_at
        allowed = causal if allowed is None else allowed & causal
    return allowed


def rows_of_keys(qkv, at, rows):
    rows[...] = qkv[at : at + HEAD_DIM, :].astype(F32).T.astype(BF)


def key_blocks(query_at, queries):
    last = query_at + queries
    return [(at, min(KEY_BLOCK, last - at)) for at in range(0, last, KEY_BLOCK)]


def scaled_query(qkv, cols):
    return (qkv[:HEAD_DIM, cols].astype(F32) * (1.0 / math.sqrt(HEAD_DIM))).astype(BF)


def score_block(prompt, first, cols, query_at, key_at, keys, key_rows, query):
    scores = dot(key_rows[key_at : key_at + keys, :], query)
    allowed = key_mask(prompt, first, cols, key_at, query_at, keys, query.shape[1])
    return scores if allowed is None else jnp.where(allowed, scores, NEG)


def attend_block(block, size, prompt, first, qkv, key_rows, scores, spot, keep_weights=False):
    query_at = block * size
    cols = slice(query_at, query_at + size)
    query = scaled_query(qkv, cols)
    blocks = key_blocks(query_at, size)
    top = None
    for key_at, keys in blocks:
        piece = score_block(prompt, first, cols, query_at, key_at, keys, key_rows, query)
        scores[spot(key_at, keys)] = piece
        highest = jnp.max(piece, axis=0, keepdims=True)
        top = highest if top is None else jnp.maximum(top, highest)
    weight, totals = None, None
    for key_at, keys in blocks:
        probs = jnp.exp(scores[spot(key_at, keys)] - top)
        if keep_weights:
            scores[spot(key_at, keys)] = probs
        part = jnp.sum(probs, axis=0, keepdims=True)
        product = dot(qkv[2 * HEAD_DIM : 3 * HEAD_DIM, key_at : key_at + keys], probs.astype(BF))
        weight = part if weight is None else weight + part
        totals = product if totals is None else totals + product
    return totals / weight, top, weight


def gradient_block(
    block, size, qkv, d_out, delta, probs_of, key_rows, value_rows, key_acc, value_acc, opening
):
    query_at = block * size
    cols = slice(query_at, query_at + size)
    query = scaled_query(qkv, cols)
    d_query = d_out[:, cols]
    d_sum = None
    for key_at, keys in key_blocks(query_at, size):
        where = slice(key_at, key_at + keys)
        probs = probs_of(key_at, keys, query)
        d_probs = dot(value_rows[where, :], d_query)
        d_scores = (probs * (d_probs - delta)).astype(BF)
        d_key = dot(query, d_scores, ((1,), (1,)))
        d_value = dot(d_query, probs.astype(BF), ((1,), (1,)))
        if opening:
            key_acc[:, where] = d_key
            value_acc[:, where] = d_value
        else:
            key_acc[:, where] += d_key
            value_acc[:, where] += d_value
        part = dot(qkv[HEAD_DIM : 2 * HEAD_DIM, where], d_scores)
        d_sum = part if d_sum is None else d_sum + part
    return d_sum * (1.0 / math.sqrt(HEAD_DIM))


class LineReduce:
    def __init__(self, place, total, low, from_left, from_right, view, sems, lane=0):
        self.place, self.total, self.low, self.view, self.lane = place, total, low, view, lane
        self.from_left, self.from_right = from_left, from_right
        self.send_right, self.send_left, self.recv_left, self.recv_right = sems

    def right(self, owner):
        return rcopy(
            self.low.at[self.view(owner)], self.from_left.at[self.view(owner)],
            self.send_right.at[self.lane, owner], self.recv_left.at[self.lane, owner],
            col=lax.rem(self.place.c + 1, self.place.cols),
        )

    def left(self, owner):
        cols = self.place.cols
        return rcopy(
            self.low.at[self.view(owner)], self.from_right.at[self.view(owner)],
            self.send_left.at[self.lane, owner], self.recv_right.at[self.lane, owner],
            col=lax.rem(self.place.c + cols - 1, cols),
        )

    def add_in(self, owner, arrived):
        view = self.view(owner)
        self.low[view] = (self.total[view] + arrived[view].astype(F32)).astype(BF)

    def step(self, time):
        c, cols = self.place.c, self.place.cols

        @pl.when(c <= time)
        def _():
            owner = cols - 1 - time + c

            @pl.when(c > 0)
            def _():
                self.right(owner).wait_recv()
                self.add_in(owner, self.from_left)

            self.right(owner).start()

        @pl.when(c >= cols - 1 - time)
        def _():
            owner = time + c - (cols - 1)

            @pl.when(c < cols - 1)
            def _():
                self.left(owner).wait_recv()
                self.add_in(owner, self.from_right)

            self.left(owner).start()

    def own(self):
        c, cols = self.place.c, self.place.cols
        view = self.view(c)

        @pl.when(c > 0)
        def _():
            self.right(c).wait_recv()

        @pl.when(c == 0)
        def _():
            self.from_left[view] = jnp.zeros_like(self.from_left[view])

        @pl.when(c < cols - 1)
        def _():
            self.left(c).wait_recv()

        @pl.when(c == cols - 1)
        def _():
            self.from_right[view] = jnp.zeros_like(self.from_right[view])

        return (
            self.total[view] + self.from_left[view].astype(F32) + self.from_right[view].astype(F32)
        )

    def finish(self):
        c, cols = self.place.c, self.place.cols
        for time in range(cols - 1):

            @pl.when(c <= time)
            def _():
                self.right(cols - 1 - time + c).wait_send()

            @pl.when(c >= cols - 1 - time)
            def _():
                self.left(time + c - (cols - 1)).wait_send()


def center_sum(place, total, low, from_outer, from_inner, full, sems, order, prepare, produce, after, work):
    c = place.c
    a_send, a_recv, b_send, b_recv, c_send, c_recv = sems
    count = len(order)
    size = total.shape[0] // count
    inner = (c == 1) | (c == 2)
    outer = (c == 0) | (c == 3)
    pair = jnp.where(c < 2, 1 - c, 5 - c)
    middle = 3 - c
    group = count // 4

    def rows(index):
        return slice(order[index] * size, (order[index] + 1) * size)

    def inward(index):
        piece = rows(index)
        return rcopy(
            low.at[piece], from_outer.at[piece], a_send.at[index], a_recv.at[index], col=pair
        )

    def exchange(index):
        piece = rows(index)
        return rcopy(
            low.at[piece], from_inner.at[piece], b_send.at[index], b_recv.at[index], col=middle
        )

    def outward(index):
        piece = rows(index)
        return rcopy(full.at[piece], full.at[piece], c_send.at[index], c_recv.at[index], col=pair)

    prepare(0)
    for time in range(count + 2 * LAG):
        if time < count:

            @pl.when(outer)
            def _():
                inward(time).start()

            @pl.when(inner)
            def _():
                piece = rows(time)
                inward(time).wait_recv()
                low[piece, :] = (total[piece, :] + from_outer[piece, :].astype(F32)).astype(BF)
                exchange(time).start()

        if LAG <= time < count + LAG:

            @pl.when(inner)
            def _():
                index = time - LAG
                piece = rows(index)
                exchange(index).wait_recv()
                summed = low[piece, :].astype(F32) + from_inner[piece, :].astype(F32)
                full[piece, :] = produce(summed, piece)
                outward(index).start()

        if time >= 2 * LAG:

            @pl.when(outer)
            def _():
                outward(time - 2 * LAG).wait_recv()

        if time + 2 < count and (time + 2) % group == 0:
            prepare((time + 2) // group)
        if time >= 2 * LAG:
            after(time - 2 * LAG)
        work(time)
    for index in range(count):

        @pl.when(outer)
        def _():
            inward(index).wait_send()

        @pl.when(inner)
        def _():
            exchange(index).wait_send()
            outward(index).wait_send()


class GradExchange:
    def __init__(self, place, layer, n, send, recv):
        self.place, self.layer = place, layer
        self.mine, self.theirs, self.relay, self.inbox = (
            [getattr(n, name + kind) for kind in "qfop"]
            for name in ("mine_", "theirs_", "relay_", "inbox_")
        )
        self.send, self.recv = send, recv

    def block(self, which):
        place = self.place
        return (place.beside(0), place.beside(1), place.across(), place.r)[which]

    def view(self, kind, block, half=None):
        shape = self.inbox[kind].shape
        length = shape[-2 if kind in (0, 1) else -1]
        lines = shape[-2]
        at, count = (0, lines) if half is None else (half * (lines // 2), lines // 2)
        if kind in (0, 1):
            piece = pl.ds(pl.multiple_of(block * length + at, count), count)
            return (slice(None), piece, slice(None)) if kind == 0 else (piece, slice(None))
        piece = pl.ds(pl.multiple_of(block * length, length), length)
        return (slice(at, at + count), piece)

    def passing(self, kind, which):
        view = self.view(kind, self.block(which))
        return rcopy(
            self.mine[kind].at[view], self.theirs[kind].at[view], self.send.at[kind, which],
            self.recv.at[kind, which], section=1 - self.place.s,
        )

    def relaying(self, kind, way):
        return rcopy(
            self.mine[kind].at[self.view(kind, self.place.across(), way)],
            self.relay[kind].at[way], self.send.at[kind, 4 + way], self.recv.at[kind, 4 + way],
            row=self.place.beside(way),
        )

    def sending(self, kind, way):
        return rcopy(
            self.mine[kind].at[self.view(kind, self.place.beside(way))],
            self.inbox[kind].at[way], self.send.at[kind, 6 + way], self.recv.at[kind, 6 + way],
            row=self.place.beside(way),
        )

    def add(self, kind, view, value):
        self.mine[kind][view] = (self.mine[kind][view].astype(F32) + value.astype(F32)).astype(BF)

    def hand(self, kind):
        @pl.when(self.place.s != self.layer)
        def _():
            for which in (2, 0, 1, 3):
                self.passing(kind, which).start()

    def merge(self, kind):
        @pl.when(self.place.s == self.layer)
        def _():
            for which in (2, 0, 1):
                self.passing(kind, which).wait_recv()
                view = self.view(kind, self.block(which))
                self.add(kind, view, self.theirs[kind][view])
                if which == 2:
                    for way in range(2):
                        self.relaying(kind, way).start()

    def pass_on(self, kind):
        @pl.when(self.place.s == self.layer)
        def _():
            for way in range(2):
                self.relaying(kind, 1 - way).wait_recv()
                view = self.view(kind, self.place.beside(way), 1 - way)
                self.add(kind, view, self.relay[kind][1 - way])
                self.sending(kind, way).start()

    def take(self, kind, out):
        @pl.when(self.place.s == self.layer)
        def _():
            self.passing(kind, 3).wait_recv()
            view = self.view(kind, self.place.r)
            total = self.mine[kind][view].astype(F32) + self.theirs[kind][view].astype(F32)
            for way in range(2):
                self.sending(kind, way).wait_recv()
                total = total + self.inbox[kind][way].astype(F32)
            out[...] = total

    def finish(self, kind):
        @pl.when(self.place.s == self.layer)
        def _():
            for way in range(2):
                self.relaying(kind, way).wait_send()
                self.sending(kind, way).wait_send()

        @pl.when(self.place.s != self.layer)
        def _():
            for which in range(4):
                self.passing(kind, which).wait_send()


def grad_shapes(rows, full, width, units):
    part = full // rows
    return (
        dict(q=(3, full, width), f=(full, units), o=(width, full), p=(units, full)),
        dict(q=(3, part, width), f=(part, units), o=(width, part), p=(units, part)),
    )


def grad_scratch(rows, full, width, units):
    wholes, pieces = grad_shapes(rows, full, width, units)
    scratch = {}
    for kind in "qfop":
        piece = pieces[kind]
        half = piece[:-2] + (piece[-2] // 2, piece[-1])
        scratch["mine_" + kind] = pltpu.VMEM(wholes[kind], BF)
        scratch["theirs_" + kind] = pltpu.VMEM(wholes[kind], BF)
        scratch["relay_" + kind] = pltpu.VMEM((2,) + half, BF)
        scratch["inbox_" + kind] = pltpu.VMEM((2,) + piece, BF)
    return scratch


class BlockExchange:
    def __init__(self, place, source, inbox, size, send, recv, local):
        self.place, self.source, self.inbox, self.size = place, source, inbox, size
        self.send, self.recv, self.local = send, recv, local

    def slot(self, head, lane):
        return self.inbox.at[head, :, lane * self.size : (lane + 1) * self.size]

    def piece(self, block):
        return self.source.at[:, block * self.size : (block + 1) * self.size]

    def away(self, block):
        return rcopy(
            self.piece(block), self.slot(self.place.r, block % PARTS), self.send.at[block],
            self.recv.at[block % PARTS, self.place.r], row=block // PARTS,
        )

    def start(self, block):
        @pl.when(self.place.r != block // PARTS)
        def _():
            self.away(block).start()

        @pl.when(self.place.r == block // PARTS)
        def _():
            pltpu.make_async_copy(
                self.piece(block), self.slot(self.place.r, block % PARTS),
                self.local.at[block % PARTS],
            ).start()

    def arrive(self, lane):
        for step in range(1, self.place.rows):
            source = self.place.row_from(step)
            slot = self.slot(source, lane)
            rcopy(
                slot, slot, self.send.at[lane], self.recv.at[lane, source],
                row=self.place.row_to(step),
            ).wait_recv()
        slot = self.slot(self.place.r, lane)
        pltpu.make_async_copy(slot, slot, self.local.at[lane]).wait()

    def finish(self):
        for block in range(self.place.rows * PARTS):

            @pl.when(self.place.r != block // PARTS)
            def _():
                self.away(block).wait_send()


def unit_rows(values):
    centred = values - jnp.mean(values, axis=1, keepdims=True)
    rstd = lax.rsqrt(jnp.mean(centred * centred, axis=1, keepdims=True) + EPS)
    return centred * rstd, rstd


def segment_begins(lengths, micro, first):
    token = lax.broadcasted_iota(jnp.int32, first.shape, 1)
    begin = jnp.zeros_like(token)
    start = lengths[micro, 0]
    for index in range(1, lengths.shape[1]):
        begin = jnp.where(token >= start, start, begin)
        start = start + lengths[micro, index]
    first[...] = begin
    return lengths[micro, 0]


class Saver:
    def __init__(self, sems):
        self.sems, self.copies = sems, []

    def copy(self, source, target):
        copy = pltpu.make_async_copy(source, target, self.sems.at[len(self.copies)])
        copy.start()
        self.copies.append(copy)
        return copy

    def finish(self):
        for copy in self.copies:
            copy.wait()


class Names:
    def joined(self, results):
        both = Names()
        for name, value in vars(self).items():
            setattr(both, name, value)
        for name, value in results.items():
            setattr(both, name[2:], value)
        return both


def named_call(body, collective_id, ins, outs, scratch):
    names = [*ins, *outs, *scratch]

    def kernel(*refs):
        held = Names()
        for name, ref in zip(names, refs):
            setattr(held, name, ref)
        body(held)

    results = pl.pallas_call(
        kernel,
        out_shape=[jax.ShapeDtypeStruct(shape, dtype) for shape, dtype, space in outs.values()],
        in_specs=[pl.BlockSpec(memory_space=space) for array, space in ins.values()],
        out_specs=[pl.BlockSpec(memory_space=space) for shape, dtype, space in outs.values()],
        scratch_shapes=list(scratch.values()),
        compiler_params=pltpu.CompilerParams(
            collective_id=collective_id,
            has_side_effects=collective_id is not None,
            vmem_limit_bytes=VMEM_LIMIT,
        ),
    )(*[array for array, space in ins.values()])
    return dict(zip(outs, results))


class VectorGather:
    def __init__(self, place, own, full, send, recv, width):
        self.place, self.own, self.full, self.width = place, own, full, width
        self.send, self.recv = send, recv
        self.others = [(ds, dc) for ds in range(2) for dc in range(place.cols) if ds or dc]

    def slot(self, section, col):
        return self.full.at[section, :, pl.ds(pl.multiple_of(col * self.width, self.width), self.width)]

    def copy(self, ds, dc, source, slot):
        index = ds * self.place.cols + dc
        return rcopy(
            source, slot, self.send.at[index], self.recv.at[index],
            section=lax.rem(self.place.s + ds, 2), col=self.place.col_to(dc),
        )

    def start(self):
        for ds, dc in self.others:
            self.copy(ds, dc, self.own, self.slot(self.place.s, self.place.c)).start()

    def arrive(self):
        for ds, dc in self.others:
            slot = self.slot(lax.rem(self.place.s + ds, 2), self.place.col_from(dc))
            self.copy(ds, dc, slot, slot).wait_recv()

    def finish(self):
        for ds, dc in self.others:
            self.copy(ds, dc, self.own, self.slot(self.place.s, self.place.c)).wait_send()


def first_kernel(rows, cols, n):
    place = Place(rows, cols)
    s, c = place.s, place.c
    tokens, full = n.x_full.shape
    width = full // cols
    length = tokens // PARTS
    own = pl.ds(pl.multiple_of(c * width, width), width)

    def lane_of(lane):
        return slice(lane * length, (lane + 1) * length)

    def block_cols(block):
        return pl.ds(pl.multiple_of(block * width, width), width)

    def token_slot(source, lane):
        return pl.ds(pl.multiple_of(source * tokens + lane * length, length), length)

    loads = Saver(n.load)
    x_own = loads.copy(n.hidden_in.at[s], n.x_full.at[:, own])
    n.vectors[0:2] = n.norm_gains[0]
    n.vectors[2:4] = n.norm_biases[0]
    n.vectors[4:7] = n.b_qkv[0]
    n.vectors[7:8] = n.b_out[...]
    for index in range(n.b_fc.shape[1] // width):
        n.vectors[8 + index : 9 + index] = n.b_fc[:, index * width : (index + 1) * width]
    n.vectors[12:16] = jnp.zeros((4, width), F32)
    v_own = loads.copy(n.vectors, n.vec_all.at[s, :, own])
    c_own = loads.copy(n.cotangent.at[s], n.cot_full.at[:, own])
    place.greet(rows=True, cols=True, partner=True, cross_cols=True)
    x_gather = [
        LineGather(
            place, lambda block, lane=lane: n.x_full.at[lane_of(lane), block_cols(block)],
            n.x_a, n.x_b, n.x_c, lane,
        )
        for lane in range(PARTS)
    ]
    c_gather = LineGather(
        place, lambda block: n.cot_full.at[:, block_cols(block)], n.c_a, n.c_b, n.c_c
    )
    vectors = VectorGather(place, n.vectors, n.vec_all, n.v_s, n.v_r, width)
    blocks = (n.wq, n.wf, n.wo, n.wp)
    weights = [
        WeightGather(place, 0, blocks, (n.wq0, n.wf0, n.wo0, n.wp0), n.w0_s, n.w0_r, n.w0_l),
        WeightGather(place, 1, blocks, (n.wq1, n.wf1, n.wo1, n.wp1), n.w1_s, n.w1_r, n.w1_l),
    ]
    QKV, FC, OUT, PROJ = range(4)
    saves = Saver(n.save)
    prompt = segment_begins(n.lengths, s, n.first)

    def row(layer, index):
        return n.vec_all[layer, index : index + 1, :]

    def bias_rows(layer):
        return lambda kind: n.vec_all[layer, 4 + kind : 5 + kind, own]

    def unit_bias(layer):
        return lambda index: n.vec_all[layer, pl.ds(8 + index, 1), own]

    def spread(pieces, slots, sends, recvs, local):
        return [
            RowExchange(
                place,
                lambda target, lane=lane: pieces(target, lane),
                lambda source, lane=lane: slots(source, lane),
                sends.at[lane], recvs.at[lane], local.at[lane],
            )
            for lane in range(PARTS)
        ]

    out0 = spread(
        lambda target, lane: n.pieces0.at[target, :, lane_of(lane)],
        lambda source, lane: n.qkv0.at[:, token_slot(source, lane)],
        n.e0_s, n.e0_r, n.e0_l,
    )
    back0 = spread(
        lambda target, lane: n.low0.at[:, token_slot(target, lane)],
        lambda source, lane: n.attn_t0.at[
            pl.ds(pl.multiple_of(source * HEAD_DIM, HEAD_DIM), HEAD_DIM), lane_of(lane)
        ],
        n.b0_s, n.b0_r, n.b0_l,
    )
    out1 = spread(
        lambda target, lane: n.pieces1.at[target, :, lane_of(lane)],
        lambda source, lane: n.qkvd1.at[:, token_slot(source, lane)],
        n.e1_s, n.e1_r, n.e1_l,
    )

    def project(layer, lane, source, normed_a, normed_m, w_query, pieces):
        norm_rows(
            source, row(layer, 0), row(layer, 2), row(layer, 1), row(layer, 3), normed_a, normed_m,
            lane * length, length,
        )
        project_heads(
            normed_a, w_query, bias_rows(layer), n.cos, n.sin, pieces, rows, lane_of(lane)
        )

    x_own.wait()
    x_gather[0].hop(0)
    vectors.start()
    weights[0].start(QKV)
    weights[0].start(FC)
    x_gather[0].hop(1)
    x_gather[1].hop(0)
    x_gather[0].hop(2)
    weights[0].relay(QKV)
    weights[0].start(PROJ)
    x_gather[1].hop(1)
    for distance in range(3, cols):
        x_gather[0].hop(distance)
    weights[0].forward(QKV)
    weights[0].relay(FC)
    vectors.arrive()
    v_own.wait()
    x_gather[1].hop(2)
    weights[0].ready(QKV)
    project(0, 0, n.x_full, n.normed_a0, n.normed_m0, n.wq0, n.pieces0)
    out0[0].start()
    weights[0].start(OUT)
    for distance in range(3, cols):
        x_gather[1].hop(distance)
    c_own.wait()
    c_gather.hop(0)
    weights[0].forward(FC)
    project(0, 1, n.x_full, n.normed_a0, n.normed_m0, n.wq0, n.pieces0)
    out0[1].start()
    weights[0].relay(PROJ)
    weights[0].relay(OUT)
    c_gather.hop(1)
    weights[0].ready(FC)
    feed_forward(n.normed_m0, n.wf0, unit_bias(0), n.hidden0, n.slope0, slice(None))
    for ref, target in (
        (n.x_full, n.o_x_full), (n.vec_all, n.o_vec_all), (n.wq0, n.o_wq0), (n.wf0, n.o_wf0),
        (n.normed_a0, n.o_normed_a0), (n.normed_m0, n.o_normed_m0), (n.hidden0, n.o_hidden0),
        (n.slope0, n.o_slope0),
    ):
        saves.copy(ref, target)
    weights[0].forward(PROJ)
    weights[0].forward(OUT)
    weights[1].start(QKV)
    weights[1].start(OUT)
    for lane in range(PARTS):
        out0[lane].arrive()
    saves.copy(n.qkv0, n.o_qkv0)

    rows_of_keys(n.qkv0, HEAD_DIM, n.key_rows)
    for lane in range(PARTS):
        for owner in range(rows):
            block = owner * PARTS + lane
            exact, top, weight = attend_block(
                block, length, prompt, n.first, n.qkv0, n.key_rows, n.scores.at[owner % 2],
                lambda key_at, keys: (slice(key_at, key_at + keys), slice(None)),
            )
            cols_here = slice(block * length, (block + 1) * length)
            n.out0[:, cols_here] = exact
            n.low0[:, cols_here] = exact.astype(BF)
            n.log0[:, cols_here] = top + jnp.log(weight)
        back0[lane].start()
        if lane == 0:
            c_gather.hop(2)
            weights[1].start(FC)
            weights[1].relay(QKV)
            weights[1].relay(OUT)
    for distance in range(3, cols):
        c_gather.hop(distance)
    weights[1].start(PROJ)
    weights[1].forward(QKV)
    weights[1].forward(OUT)
    saves.copy(n.cot_full, n.o_cot_full)
    saves.copy(n.out0, n.o_out0)
    saves.copy(n.log0, n.o_log0)
    weights[0].ready(PROJ)
    weights[0].ready(OUT)
    saves.copy(n.wp0, n.o_wp0)
    saves.copy(n.wo0, n.o_wo0)

    step = 4 // PARTS
    part = tokens // 4

    def prepare(quarter):
        if quarter % step == 0:
            back0[quarter // step].arrive()
        where = slice(quarter * part, (quarter + 1) * part)
        attn_rows = n.attn_t0[:, where].astype(F32).T.astype(BF)
        tile = min(256, full)
        for at in range(0, full, tile):
            value = dot(n.hidden0[where, :], n.wp0[:, at : at + tile]) + dot(
                attn_rows, n.wo0[:, at : at + tile]
            )
            n.total[where, at : at + tile] = value
            n.low[where, at : at + tile] = value.astype(BF)

    def produce(summed, mine):
        return (n.x_full[mine, :].astype(F32) + summed + n.vec_all[0, 7:8, :]).astype(BF)

    def branches(lane):
        where = lane_of(lane)
        feed_forward(n.normed_m1, n.wf1, unit_bias(1), n.hidden1, n.slope1, where)

        def times_slope(value, cols_here):
            return (value * n.slope1[where, cols_here]).astype(BF)

        times_tiles(n.cot_full, n.wp1, n.d_hidden1, times_slope, ((1,), (1,)), where)
        times_tiles(n.hidden1, n.wp1, n.branch1, None, ((1,), (0,)), where)
        times_tiles(n.d_hidden1, n.wf1, n.d_normed1, None, ((1,), (1,)), where)

    def after(chunk):
        if (chunk + 1) % (CHUNKS // PARTS):
            return
        lane = chunk // (CHUNKS // PARTS)
        if lane == 0:
            weights[1].ready(QKV)
            weights[1].ready(OUT)
        project(1, lane, n.x1_full, n.normed_a1, n.normed_m1, n.wq1, n.pieces1)
        where = lane_of(lane)
        flipped = dot(n.cot_full[where, :], n.wo1[...], ((1,), (1,))).T
        for head in range(rows):
            n.pieces1[head, 3 * HEAD_DIM :, where] = flipped[
                head * HEAD_DIM : (head + 1) * HEAD_DIM
            ].astype(BF)
        out1[lane].start()

    def work(time):
        if time == 2:
            weights[1].relay(FC)
        if time == 6:
            weights[1].forward(FC)
            weights[1].relay(PROJ)
        if time == 10:
            weights[1].forward(PROJ)
        if time == 20:
            weights[1].ready(FC)
            weights[1].ready(PROJ)
            branches(0)

    center_sum(
        place, n.total, n.low, n.from_left, n.from_right, n.x1_full,
        (n.r_a, n.r_b, n.r_c, n.r_d, n.r_e, n.r_f), tuple(range(CHUNKS)), prepare, produce, after, work,
    )
    saves.copy(n.attn_t0, n.o_attn_t0)
    for ref, target in (
        (n.x1_full, n.o_x1_full), (n.wq1, n.o_wq1), (n.wo1, n.o_wo1),
        (n.normed_a1, n.o_normed_a1), (n.normed_m1, n.o_normed_m1),
    ):
        saves.copy(ref, target)
    for lane in range(1, PARTS):
        branches(lane)
    for ref, target in (
        (n.hidden1, n.o_hidden1), (n.d_hidden1, n.o_d_hidden1), (n.branch1, n.o_branch1),
        (n.d_normed1, n.o_d_normed1),
    ):
        saves.copy(ref, target)
    for lane in range(PARTS):
        out1[lane].arrive()
    saves.copy(n.qkvd1, n.o_qkvd1)
    for exchange in out0 + back0 + out1:
        exchange.finish()
    for gather in x_gather + [c_gather]:
        gather.finish()
    vectors.finish()
    for gather in weights:
        for kind in range(4):
            gather.finish(kind)
    saves.finish()


def first_half(rows, cols, hidden_in, cotangent, vectors, blocks, cos, sin, lengths):
    norm_gains, norm_biases, b_qkv, b_out, b_fc = vectors
    tokens, width = hidden_in.shape[1:]
    full = cols * width
    wq, wf, wo, wp = blocks
    units = wf.shape[1]
    total = rows * tokens
    hbm, vmem, smem = pl.ANY, pltpu.VMEM, pltpu.SMEM
    ins = dict(
        hidden_in=(hidden_in, hbm), cotangent=(cotangent, hbm), norm_gains=(norm_gains, vmem),
        norm_biases=(norm_biases, vmem), b_qkv=(b_qkv, vmem), b_out=(b_out, vmem), b_fc=(b_fc, vmem),
        wq=(wq, hbm), wf=(wf, hbm), wo=(wo, hbm), wp=(wp, hbm), cos=(cos, vmem), sin=(sin, vmem),
        lengths=(lengths, smem),
    )
    rows_low, rows_wide = ((tokens, full), BF), ((tokens, full), F32)
    unit_low, unit_wide = ((tokens, units), BF), ((tokens, units), F32)
    kept = dict(
        x_full=rows_low, cot_full=rows_low, vec_all=((2, 16, full), F32),
        wq0=((3, full, width), BF), wf0=((full, units), BF), wo0=((width, full), BF),
        wp0=((units, full), BF), normed_a0=rows_low, normed_m0=rows_low,
        qkv0=((3 * HEAD_DIM, total), BF), hidden0=unit_low, slope0=unit_low,
        out0=((HEAD_DIM, total), F32), log0=((1, total), F32), attn_t0=((width, tokens), BF),
        x1_full=rows_low, wq1=((3, full, width), BF), wo1=((width, full), BF),
        normed_a1=rows_low, normed_m1=rows_low, qkvd1=((4 * HEAD_DIM, total), BF),
        hidden1=unit_low, d_hidden1=unit_low, branch1=rows_wide, d_normed1=rows_wide,
    )
    outs = {"o_" + name: shape + (hbm,) for name, shape in kept.items()}
    scratch = {name: pltpu.VMEM(*shape) for name, shape in kept.items()}
    scratch.update(
        vectors=pltpu.VMEM((16, width), F32),
        wf1=pltpu.VMEM((full, units), BF), wp1=pltpu.VMEM((units, full), BF),
        slope1=pltpu.VMEM(*unit_wide), low0=pltpu.VMEM((HEAD_DIM, total), BF),
        total=pltpu.VMEM(*rows_wide), low=pltpu.VMEM(*rows_low),
        from_left=pltpu.VMEM(*rows_low), from_right=pltpu.VMEM(*rows_low),
        pieces0=pltpu.VMEM((rows, 3 * HEAD_DIM, tokens), BF),
        pieces1=pltpu.VMEM((rows, 4 * HEAD_DIM, tokens), BF),
        first=pltpu.VMEM((1, total), jnp.int32), key_rows=pltpu.VMEM((total, HEAD_DIM), BF),
        scores=pltpu.VMEM((2, total, tokens // PARTS), F32),
        load=dma(3), save=dma(len(kept)),
        x_a=dma(PARTS, cols), x_b=dma(PARTS, cols), x_c=dma(PARTS, cols),
        c_a=dma(1, cols), c_b=dma(1, cols), c_c=dma(1, cols),
        v_s=dma(2 * cols), v_r=dma(2 * cols),
        w0_s=dma(4, 8), w0_r=dma(4, 8), w0_l=dma(4), w1_s=dma(4, 8), w1_r=dma(4, 8), w1_l=dma(4),
    )
    for name in ("e0", "b0", "e1"):
        scratch[name + "_s"] = dma(PARTS, rows)
        scratch[name + "_r"] = dma(PARTS, rows)
        scratch[name + "_l"] = dma(PARTS)
    for name in ("r_a", "r_b", "r_c", "r_d", "r_e", "r_f"):
        scratch[name] = dma(CHUNKS)
    return Names().joined(named_call(partial(first_kernel, rows, cols), 1, ins, outs, scratch))


def d_projection(inbox, at, cos, sin, rows, d_pre, small, where):
    width = rows * HEAD_DIM
    for kind in range(3):
        parts = []
        for head in range(rows):
            start = at + kind * HEAD_DIM
            block = inbox[head, start : start + HEAD_DIM, where].astype(F32)
            parts.append(turn(block, cos[:, where], sin[:, where], -1.0) if kind < 2 else block)
        values = jnp.concatenate(parts, axis=0).T.astype(BF)
        d_pre[where, kind * width : (kind + 1) * width] = values
        small[8 + kind : 9 + kind, :] += jnp.sum(values.astype(F32), axis=0, keepdims=True)


def d_norms(source, d_pre, wq, d_normed, gain_a, gain_m, total, low, sums, begin, count, also=None):
    width = wq.shape[2]
    tile = min(128, count)

    @pl.loop(0, count // tile)
    def _(index):
        rows = pl.ds(pl.multiple_of(begin + index * tile, tile), tile)
        d_a = dot(d_pre[rows, :width], wq[0], ((1,), (1,)))
        for kind in range(1, 3):
            d_a += dot(d_pre[rows, kind * width : (kind + 1) * width], wq[kind], ((1,), (1,)))
        d_m = d_normed[rows, :]
        unit, _ = unit_rows(source[rows, :].astype(F32))
        sums[0:1, :] += jnp.sum(d_a * unit, axis=0, keepdims=True)
        sums[1:2, :] += jnp.sum(d_m * unit, axis=0, keepdims=True)
        sums[2:3, :] += jnp.sum(d_a, axis=0, keepdims=True)
        sums[3:4, :] += jnp.sum(d_m, axis=0, keepdims=True)
        joined = d_a * gain_a + d_m * gain_m
        total[rows, :] = joined
        low[rows, :] = joined.astype(BF)
        if also is not None:
            also(rows, joined, unit)


def unit_sums(d_pre, small, width):
    for index in range(d_pre.shape[1] // width):
        piece = d_pre[:, index * width : (index + 1) * width].astype(F32)
        small[12 + index : 13 + index, :] = jnp.sum(piece, axis=0, keepdims=True)


def across_tokens(left, right, out, heads=False):
    tile = min(256, left.shape[1])

    @pl.loop(0, left.shape[1] // tile)
    def _(index):
        cols = pl.ds(pl.multiple_of(index * tile, tile), tile)
        value = dot(left[:, cols], right[...], ((0,), (0,))).astype(BF)
        if heads:
            width = out.shape[2]
            for kind in range(3):
                out[kind, cols, :] = value[:, kind * width : (kind + 1) * width]
        else:
            out[cols, :] = value


def out_gradient(attn_t, grad_full, out):
    tile = min(256, out.shape[1])
    for at in range(0, out.shape[1], tile):
        out[:, at : at + tile] = dot(attn_t[...], grad_full[:, at : at + tile]).astype(BF)


Q, F, O, PR = range(4)


class Load:
    def __init__(self, source, target, sem):
        self.copy, self.waiting = pltpu.make_async_copy(source, target, sem), True

    def start(self):
        self.copy.start()

    def need(self):
        if self.waiting:
            self.copy.wait()
            self.waiting = False


def second_kernel(rows, cols, n):
    place = Place(rows, cols)
    s, c = place.s, place.c
    tokens, full = n.x1_full.shape
    width = full // cols
    length = tokens // PARTS
    size = QUERY_BLOCK
    own = pl.ds(pl.multiple_of(c * width, width), width)
    count = rows * PARTS
    qkv0 = n.qkvd1.at[: 3 * HEAD_DIM]
    hidden0, normed_m0, normed_a0, wq0 = n.hidden1, n.normed_m1, n.normed_a1, n.wq1
    x_full, branch1, unit0, d_normed0 = n.d_hidden1, n.d_normed1, n.scores, n.scores
    o_low = n.cot_full
    load_no = iter(range(LOADS))

    def loading(source, target):
        return Load(source, target, n.load.at[next(load_no)])

    l_qkvd1 = loading(n.i_qkvd1, n.qkvd1)
    l_cot = loading(n.i_cot_full, n.cot_full)
    l_d_hidden1 = loading(n.i_d_hidden1, n.d_hidden1)
    l_hidden1 = loading(n.i_hidden1, n.hidden1)
    l_x1 = loading(n.i_x1_full, n.x1_full)
    l_wq1 = loading(n.i_wq1, n.wq1)
    l_d_normed1 = loading(n.i_d_normed1, n.d_normed1)
    l_normed_m1 = loading(n.i_normed_m1, n.normed_m1)
    l_normed_a1 = loading(n.i_normed_a1, n.normed_a1)
    l_wo0 = loading(n.i_wo0, n.wo0)
    l_wp0 = loading(n.i_wp0, n.wp0)
    l_wf0 = loading(n.i_wf0, n.wf0)
    l_slope0 = loading(n.i_slope0, n.slope0)
    l_wo1 = loading(n.i_wo1, n.wo1)
    l_out0 = loading(n.i_out0, n.out0)
    l_log0 = loading(n.i_log0, n.log0)
    l_attn_t0 = loading(n.i_attn_t0, n.attn_t0)
    l_qkv0 = loading(n.i_qkv0, qkv0)
    l_hidden0 = loading(n.i_hidden0, hidden0)
    l_normed_m0 = loading(n.i_normed_m0, normed_m0)
    l_normed_a0 = loading(n.i_normed_a0, normed_a0)
    l_wq0 = loading(n.i_wq0, wq0)
    l_x0 = loading(n.i_x_full, x_full)
    l_branch1 = loading(n.i_branch1, branch1)

    def lane_of(lane):
        return slice(lane * length, (lane + 1) * length)

    def features(owner):
        return (slice(None), pl.ds(pl.multiple_of(owner * width, width), width))

    l_qkvd1.start()
    place.greet(rows=True, cols=True, partner=True, cross_rows=True)
    grads1 = GradExchange(place, 1, n, n.g1_s, n.g1_r)
    grads0 = GradExchange(place, 0, n, n.g0_s, n.g0_r)
    exchange1 = BlockExchange(place, n.result, n.inbox, size, n.b1_s, n.b1_r, n.b1_l)
    exchange0 = BlockExchange(
        place, n.result.at[: 3 * HEAD_DIM], n.inbox.at[:, : 3 * HEAD_DIM], size, n.b0_s, n.b0_r,
        n.b0_l,
    )
    outward = [
        RowExchange(
            place,
            lambda target, lane=lane: n.pieces.at[target, :, lane_of(lane)],
            lambda source, lane=lane: n.d_out.at[
                :, pl.ds(pl.multiple_of(source * tokens + lane * length, length), length)
            ],
            n.e_s.at[lane], n.e_r.at[lane], n.e_l.at[lane],
        )
        for lane in range(PARTS)
    ]
    out_sum = LineReduce(
        place, branch1, o_low, n.o_left, n.o_right, features, (n.o_a, n.o_b, n.o_c, n.o_d)
    )
    grad_sums = [
        LineReduce(
            place, n.total, n.low, n.from_left, n.from_right,
            lambda owner, lane=lane: (lane_of(lane), features(owner)[1]),
            (n.s_a, n.s_b, n.s_c, n.s_d), lane,
        )
        for lane in range(PARTS)
    ]

    prompt = segment_begins(n.lengths, s, n.first)
    l_qkvd1.need()
    for load in (
        l_cot, l_d_hidden1, l_hidden1, l_x1, l_wq1, l_d_normed1, l_normed_m1, l_normed_a1, l_wo0,
        l_wp0, l_wf0, l_slope0, l_wo1, l_out0, l_log0, l_attn_t0,
    ):
        load.start()
    qkvd = n.qkvd1
    rows_of_keys(qkvd, HEAD_DIM, n.key_rows)
    rows_of_keys(qkvd, 2 * HEAD_DIM, n.value_rows)
    d_out1 = qkvd.at[3 * HEAD_DIM :]

    def spot(key_at, keys):
        at = key_at // KEY_BLOCK * size
        return (slice(0, keys), slice(at, at + size))

    for block in reversed(range(count)):
        here = slice(block * size, (block + 1) * size)
        exact, top, weight = attend_block(
            block, size, prompt, n.first, qkvd, n.key_rows, n.scores, spot, True
        )
        delta = jnp.sum(d_out1[:, here].astype(F32) * exact, axis=0, keepdims=True)
        inverse = 1.0 / weight

        def probs_of(key_at, keys, query):
            return n.scores[spot(key_at, keys)] * inverse

        d_query = gradient_block(
            block, size, qkvd, d_out1, delta, probs_of, n.key_rows, n.value_rows, n.key_acc,
            n.value_acc, block == count - 1,
        )
        n.result[:HEAD_DIM, here] = exact.astype(BF)
        n.result[HEAD_DIM : 2 * HEAD_DIM, here] = d_query.astype(BF)
        n.result[2 * HEAD_DIM : 3 * HEAD_DIM, here] = n.key_acc[:, here].astype(BF)
        n.result[3 * HEAD_DIM :, here] = n.value_acc[:, here].astype(BF)
        exchange1.start(block)

    l_qkv0.start()
    n.sums[...] = jnp.zeros_like(n.sums)
    n.small[...] = jnp.zeros_like(n.small)
    l_cot.need()
    l_d_hidden1.need()
    l_hidden1.need()
    n.small[1, 11:12, :] = jnp.sum(n.cot_full[:, own].astype(F32), axis=0, keepdims=True)
    unit_sums(n.d_hidden1, n.small.at[1], width)
    across_tokens(n.hidden1, n.cot_full, n.mine_p)
    grads1.hand(PR)
    l_hidden0.start()
    for load in (l_x1, l_wq1, l_d_normed1):
        load.need()
    quarters = (2, 3, 0, 1)
    part = tokens // 4

    def prepare(turn_no):
        if turn_no % 2 == 0:
            lane = quarters[turn_no] // 2
            exchange1.arrive(lane)
            where = lane_of(lane)
            for head in range(rows):
                n.attn_t1[head * HEAD_DIM : (head + 1) * HEAD_DIM, where] = n.inbox[
                    head, :HEAD_DIM, where
                ]
            d_projection(n.inbox, HEAD_DIM, n.cos, n.sin, rows, n.d_pre, n.small.at[1], where)
        d_norms(
            n.x1_full, n.d_pre, n.wq1, n.d_normed1, n.vec_all[1, 0:1, :], n.vec_all[1, 1:2, :],
            n.total, n.low, n.sums.at[1], quarters[turn_no] * part, part,
        )

    def produce(summed, mine):
        unit, rstd = unit_rows(n.x1_full[mine, :].astype(F32))
        moved = (
            summed
            - jnp.mean(summed, axis=1, keepdims=True)
            - unit * jnp.mean(summed * unit, axis=1, keepdims=True)
        )
        return (n.cot_full[mine, :].astype(F32) + rstd * moved).astype(BF)

    def branches(lane):
        where = lane_of(lane)

        def times_slope(value, cols_here):
            return (value * n.slope0[where, cols_here]).astype(BF)

        times_tiles(n.grad_full, n.wp0, n.d_hidden0, times_slope, ((1,), (1,)), where)
        times_tiles(n.d_hidden0, n.wf0, d_normed0, None, ((1,), (1,)), where)

    def after(chunk):
        if (chunk + 1) % (CHUNKS // PARTS) == 0:
            lane = 1 - chunk // (CHUNKS // PARTS)
            where = lane_of(lane)
            l_wo0.need()
            flipped = dot(n.grad_full[where, :], n.wo0[...], ((1,), (1,))).T
            for head in range(rows):
                n.pieces[head, :, where] = flipped[
                    head * HEAD_DIM : (head + 1) * HEAD_DIM
                ].astype(BF)
            outward[lane].start()

    def work(time):
        if time == 0:
            l_normed_m1.need()
            across_tokens(n.normed_m1, n.d_hidden1, n.mine_f)
            grads1.hand(F)
            l_normed_m0.start()
            l_x0.start()
        if time == 3:
            grads1.merge(PR)
        if time == 6:
            grads1.merge(F)
        if time == 8:
            grads1.pass_on(PR)
        if time == 11:
            l_normed_a1.need()
            across_tokens(n.normed_a1, n.d_pre, n.mine_q, True)
            grads1.hand(Q)
            l_normed_a0.start()
            l_wq0.start()
            l_branch1.start()
        if time == 12:
            out_gradient(n.attn_t1, n.cot_full, n.mine_o)
            grads1.hand(O)
        if time == 13:
            grads1.pass_on(F)
        if time == 15:
            grads1.merge(Q)
            grads1.merge(O)
        if time == 17:
            for load in (l_wp0, l_wf0, l_slope0):
                load.need()
            branches(PARTS - 1)
        if time == 20:
            grads1.pass_on(Q)
            grads1.pass_on(O)

    chunks = tuple(range(CHUNKS // 2, CHUNKS)) + tuple(range(CHUNKS // 2))
    center_sum(
        place, n.total, n.low, n.from_left, n.from_right, n.grad_full,
        (n.r_a, n.r_b, n.r_c, n.r_d, n.r_e, n.r_f), chunks, prepare, produce, after, work,
    )

    l_branch1.need()
    l_wo1.need()
    attn_rows = n.attn_t1[...].astype(F32).T.astype(BF)
    tile = min(256, full)
    for at in range(0, full, tile):
        value = branch1[:, at : at + tile] + dot(attn_rows, n.wo1[:, at : at + tile])
        branch1[:, at : at + tile] = value
        o_low[:, at : at + tile] = value.astype(BF)
    out_sum.step(0)
    for lane in range(PARTS - 1):
        branches(lane)
    exchange1.finish()
    for lane in range(PARTS):
        outward[lane].arrive()

    l_qkv0.need()
    l_out0.need()
    l_log0.need()
    rows_of_keys(qkv0, HEAD_DIM, n.key_rows)
    rows_of_keys(qkv0, 2 * HEAD_DIM, n.value_rows)
    for block in reversed(range(count)):
        here = slice(block * size, (block + 1) * size)
        delta = jnp.sum(n.d_out[:, here].astype(F32) * n.out0[:, here], axis=0, keepdims=True)
        log_row = n.log0[:, here]

        def weights_of(key_at, keys, query):
            return jnp.exp(
                score_block(prompt, n.first, here, block * size, key_at, keys, n.key_rows, query)
                - log_row
            )

        d_query = gradient_block(
            block, size, qkv0, n.d_out, delta, weights_of, n.key_rows, n.value_rows, n.key_acc,
            n.value_acc, block == count - 1,
        )
        n.result[:HEAD_DIM, here] = d_query.astype(BF)
        n.result[HEAD_DIM : 2 * HEAD_DIM, here] = n.key_acc[:, here].astype(BF)
        n.result[2 * HEAD_DIM : 3 * HEAD_DIM, here] = n.value_acc[:, here].astype(BF)
        exchange0.start(block)
        if block == count - 1:
            grads1.take(PR, n.gw_p)
            grads1.finish(PR)
            l_hidden0.need()
            across_tokens(hidden0, n.grad_full, n.mine_p)
            grads0.hand(PR)
        if block == count - 2:
            out_sum.step(1)
        if block == count - 4:
            grads0.merge(PR)
            out_sum.step(2)
    grads1.take(F, n.gw_f)
    grads1.finish(F)
    l_normed_m0.need()
    across_tokens(normed_m0, n.d_hidden0, n.mine_f)
    grads0.hand(F)
    grads1.take(O, n.gw_o)
    grads1.finish(O)
    l_attn_t0.need()
    out_gradient(n.attn_t0, n.grad_full, n.mine_o)
    grads0.hand(O)
    n.small[0, 11:12, :] = jnp.sum(n.grad_full[:, own].astype(F32), axis=0, keepdims=True)
    unit_sums(n.d_hidden0, n.small.at[0], width)
    out_own = n.x1_full[:, own].astype(F32) + out_sum.own() + n.vec_all[1, 7:8, own]
    n.o_own[1] = out_own.astype(BF)
    n.o_own[0] = n.x1_full[:, own]

    def swap_copy(index, source, target):
        return rcopy(
            source.at[1 - s], target.at[s], n.sw_s.at[index], n.sw_r.at[index], section=1 - s
        )

    out_swap = swap_copy(0, n.o_own, n.o_out_rows)
    out_swap.start()
    out_keep = pltpu.make_async_copy(n.o_own.at[s], n.o_out_rows.at[s], n.local.at[0])
    out_keep.start()

    l_x0.need()
    l_wq0.need()
    gain_a, gain_m = n.vec_all[0, 0:1, :], n.vec_all[0, 1:2, :]
    lane_no = lax.broadcasted_iota(jnp.int32, (min(128, length), 128), 1)

    def row_sums(where, joined, unit):
        first = jnp.sum(joined, axis=1, keepdims=True)
        second = jnp.sum(joined * unit, axis=1, keepdims=True)
        both = jnp.where(lane_no == 0, first, jnp.where(lane_no == 1, second, 0.0))
        n.line_sums[:, where] = both.T[:8]

    def prepare_last(lane):
        exchange0.arrive(lane)
        d_projection(n.inbox, 0, n.cos, n.sin, rows, n.d_pre, n.small.at[0], lane_of(lane))
        d_norms(
            x_full, n.d_pre, wq0, d_normed0, gain_a, gain_m, n.total, n.low, n.sums.at[0],
            lane * length, length, row_sums,
        )

    grads0.pass_on(PR)
    prepare_last(1)
    grad_sums[1].step(0)
    grads0.merge(F)
    prepare_last(0)
    grad_sums[0].step(0)
    grad_sums[1].step(1)

    def line_copy(step):
        return rcopy(
            n.line_sums, n.line_in.at[step], n.ls_s.at[step], n.ls_r.at[step],
            col=place.col_to(step),
        )

    def col_copy(step):
        target = place.col_to(step)
        piece = n.sums.at[:, :, pl.ds(pl.multiple_of(target * width, width), width)]
        return rcopy(piece, n.col_in.at[step], n.cs_s.at[step], n.cs_r.at[step], col=target)

    def row_copy(ds, step):
        index = ds * rows + step
        layer = lax.rem(s + ds, 2)
        return rcopy(
            n.small.at[layer], n.row_in.at[index], n.rw_s.at[index], n.rw_r.at[index],
            section=layer, row=place.row_to(step),
        )

    for step in range(1, cols):
        line_copy(step).start()
        col_copy(step).start()
    grads1.take(Q, n.gw_q)
    grads1.finish(Q)
    l_normed_a0.need()
    across_tokens(normed_a0, n.d_pre, n.mine_q, True)
    grads0.hand(Q)
    grad_sums[1].step(2)
    grad_sums[0].step(1)
    grads0.merge(O)
    grads0.pass_on(F)
    for step in range(1, cols):
        col_copy(step).wait_recv()
    head = n.sums[:, :, own]
    for step in range(1, cols):
        head = head + n.col_in[step]
    n.small[:, :8, :] = head
    others = [(ds, step) for ds in range(2) for step in range(rows) if ds or step]
    for ds, step in others:
        row_copy(ds, step).start()
    grads0.merge(Q)
    grad_sums[0].step(2)
    joined = n.line_sums[...]
    for step in range(1, cols):
        line_copy(step).wait_recv()
        joined = joined + n.line_in[step]
    wide = jnp.concatenate([joined, jnp.zeros((120, tokens), F32)], axis=0).T
    unit, rstd = unit_rows(x_full[...].astype(F32))
    unit0[...] = unit
    grads0.pass_on(O)
    grads0.pass_on(Q)
    out_keep.wait()
    out_swap.wait()
    for lane in reversed(range(PARTS)):
        where = lane_of(lane)
        moved = (
            grad_sums[lane].own()
            - wide[where, 0:1] / full
            - unit0[where, own] * (wide[where, 1:2] / full)
        )
        n.o_own[0, where] = (
            n.grad_full[where, own].astype(F32) + rstd[where] * moved
        ).astype(BF)
    n.o_own[1] = n.grad_full[:, own]
    grad_swap = swap_copy(1, n.o_own, n.o_grad_rows)
    grad_swap.start()
    grad_keep = pltpu.make_async_copy(n.o_own.at[s], n.o_grad_rows.at[s], n.local.at[1])
    grad_keep.start()
    mine = n.small[s]
    for ds, step in others:
        row_copy(ds, step).wait_recv()
        mine = mine + n.row_in[ds * rows + step]
    n.o_small[...] = mine
    saves = Saver(n.save)
    for kind, made, target in (
        (PR, n.gw_p, n.o_gw_p), (F, n.gw_f, n.o_gw_f), (O, n.gw_o, n.o_gw_o), (Q, n.gw_q, n.o_gw_q),
    ):
        grads0.take(kind, made)
        saves.copy(made, target)
    grad_keep.wait()
    grad_swap.wait()
    exchange0.finish()
    for exchange in outward:
        exchange.finish()
    out_sum.finish()
    for reduce in grad_sums:
        reduce.finish()
    for step in range(1, cols):
        line_copy(step).wait_send()
        col_copy(step).wait_send()
    for ds, step in others:
        row_copy(ds, step).wait_send()
    for kind in range(4):
        grads0.finish(kind)
    saves.finish()


def second_half(rows, cols, kept, cos, sin, lengths):
    tokens, full = kept.x1_full.shape
    width, units = full // cols, kept.hidden1.shape[1]
    total = rows * tokens
    hbm, vmem, smem = pl.ANY, pltpu.VMEM, pltpu.SMEM
    loaded = dict(
        qkvd1=kept.qkvd1, cot_full=kept.cot_full, d_hidden1=kept.d_hidden1, hidden1=kept.hidden1,
        x1_full=kept.x1_full, wq1=kept.wq1, d_normed1=kept.d_normed1, normed_m1=kept.normed_m1,
        normed_a1=kept.normed_a1, wo0=kept.wo0, wp0=kept.wp0, wf0=kept.wf0, slope0=kept.slope0,
        wo1=kept.wo1, out0=kept.out0, log0=kept.log0, attn_t0=kept.attn_t0,
    )
    later = dict(
        qkv0=kept.qkv0, hidden0=kept.hidden0, normed_m0=kept.normed_m0, normed_a0=kept.normed_a0,
        wq0=kept.wq0, x_full=kept.x_full, branch1=kept.branch1,
    )
    ins = {"i_" + name: (value, hbm) for name, value in {**loaded, **later}.items()}
    ins.update(
        cos=(cos, vmem), sin=(sin, vmem), lengths=(lengths, smem), vec_all=(kept.vec_all, vmem)
    )
    rows_low, rows_wide = ((tokens, full), BF), ((tokens, full), F32)
    wholes, pieces = grad_shapes(rows, full, width, units)
    outs = dict(
        o_out_rows=((2, tokens, width), BF, vmem), o_grad_rows=((2, tokens, width), BF, vmem),
        o_small=((16, width), F32, vmem),
    )
    outs.update({"o_gw_" + kind: (pieces[kind], F32, hbm) for kind in "qfop"})
    scratch = {name: pltpu.VMEM(value.shape, value.dtype) for name, value in loaded.items()}
    scratch.update(grad_scratch(rows, full, width, units))
    scratch.update({"gw_" + kind: pltpu.VMEM(pieces[kind], F32) for kind in "qfop"})
    scratch.update(
        grad_full=pltpu.VMEM(*rows_low), attn_t1=pltpu.VMEM((width, tokens), BF),
        d_hidden0=pltpu.VMEM((tokens, units), BF), d_out=pltpu.VMEM((HEAD_DIM, total), BF),
        result=pltpu.VMEM((4 * HEAD_DIM, total), BF),
        inbox=pltpu.VMEM((rows, 4 * HEAD_DIM, tokens), BF),
        pieces=pltpu.VMEM((rows, HEAD_DIM, tokens), BF),
        d_pre=pltpu.VMEM((tokens, 3 * width), BF),
        total=pltpu.VMEM(*rows_wide), low=pltpu.VMEM(*rows_low),
        from_left=pltpu.VMEM(*rows_low), from_right=pltpu.VMEM(*rows_low),
        o_left=pltpu.VMEM(*rows_low), o_right=pltpu.VMEM(*rows_low),
        scores=pltpu.VMEM((KEY_BLOCK, total // KEY_BLOCK * QUERY_BLOCK), F32),
        first=pltpu.VMEM((1, total), jnp.int32),
        key_rows=pltpu.VMEM((total, HEAD_DIM), BF), value_rows=pltpu.VMEM((total, HEAD_DIM), BF),
        key_acc=pltpu.VMEM((HEAD_DIM, total), F32), value_acc=pltpu.VMEM((HEAD_DIM, total), F32),
        sums=pltpu.VMEM((2, 8, full), F32), small=pltpu.VMEM((2, 16, width), F32),
        line_sums=pltpu.VMEM((8, tokens), F32), line_in=pltpu.VMEM((cols, 8, tokens), F32),
        col_in=pltpu.VMEM((cols, 2, 8, width), F32),
        row_in=pltpu.VMEM((2 * rows, 16, width), F32),
        o_own=pltpu.VMEM((2, tokens, width), BF),
        load=dma(LOADS), save=dma(4), local=dma(2),
        g1_s=dma(4, 8), g1_r=dma(4, 8), g0_s=dma(4, 8), g0_r=dma(4, 8),
        b1_s=dma(rows * PARTS), b1_r=dma(PARTS, rows), b1_l=dma(PARTS),
        b0_s=dma(rows * PARTS), b0_r=dma(PARTS, rows), b0_l=dma(PARTS),
        e_s=dma(PARTS, rows), e_r=dma(PARTS, rows), e_l=dma(PARTS),
        ls_s=dma(cols), ls_r=dma(cols), cs_s=dma(cols), cs_r=dma(cols),
        rw_s=dma(2 * rows), rw_r=dma(2 * rows), sw_s=dma(2), sw_r=dma(2),
    )
    for name in ("r_a", "r_b", "r_c", "r_d", "r_e", "r_f"):
        scratch[name] = dma(CHUNKS)
    for name in ("s_a", "s_b", "s_c", "s_d"):
        scratch[name] = dma(PARTS, cols)
    for name in ("o_a", "o_b", "o_c", "o_d"):
        scratch[name] = dma(1, cols)
    return Names().joined(named_call(partial(second_kernel, rows, cols), 3, ins, outs, scratch))


def finishing_kernel(n):
    for source, target in (
        (n.i_out_rows, n.out_rows), (n.i_grad_rows, n.grad_rows), (n.i_gw_q, n.gw_q),
        (n.i_gw_f, n.gw_f), (n.i_gw_o, n.gw_o), (n.i_gw_p, n.gw_p),
    ):
        target[0] = source[...]
    width = n.small.shape[1]
    n.gains[0] = n.small[0:2]
    n.shifts[0] = n.small[2:4]
    n.g_qkv[0] = n.small[8:11]
    n.g_out[...] = n.small[11:12]
    for index in range(n.g_fc.shape[1] // width):
        n.g_fc[:, index * width : (index + 1) * width] = n.small[12 + index : 13 + index]


def finishing(k):
    vmem = pltpu.VMEM
    made = dict(
        out_rows=k.out_rows, grad_rows=k.grad_rows, gw_q=k.gw_q, gw_f=k.gw_f, gw_o=k.gw_o,
        gw_p=k.gw_p,
    )
    ins = {"i_" + name: (value, vmem) for name, value in made.items()}
    ins.update(small=(k.small, vmem))
    width, units = k.small.shape[1], k.gw_f.shape[1]
    large = {name: ((1,) + value.shape, value.dtype, vmem) for name, value in made.items()}
    outs = dict(
        out_rows=None, grad_rows=None, gains=((1, 2, width), F32, vmem),
        shifts=((1, 2, width), F32, vmem), gw_q=None, g_qkv=((1, 3, width), F32, vmem), gw_o=None,
        gw_f=None, g_fc=((1, units), F32, vmem), gw_p=None, g_out=((1, width), F32, vmem),
    )
    outs.update(large)
    return tuple(named_call(finishing_kernel, None, ins, outs, {}).values())


def relay_body(
    hidden_in,
    cotangent,
    lengths,
    norm_gains,
    norm_biases,
    w_qkv,
    b_qkv,
    w_out,
    w_fc,
    b_fc,
    w_proj,
    b_out,
):
    rows, cols = lax.axis_size(ROW), lax.axis_size(COL)
    tokens, width = hidden_in.shape[1:]
    section = lax.axis_index(SECTION)
    lengths_row = lax.dynamic_index_in_dim(lengths, section, 0, keepdims=False)

    def begin_of(token_ids):
        begin = jnp.zeros_like(token_ids)
        start = lengths_row[0]
        for index in range(1, lengths_row.shape[0]):
            begin = jnp.where(token_ids >= start, start, begin)
            start = start + lengths_row[index]
        return begin

    my_tokens = (
        lax.axis_index(ROW) * tokens + lax.broadcasted_iota(jnp.int32, (ROT // 2, tokens), 1)
    )
    my_first = begin_of(my_tokens)
    position = jnp.where(my_first == 0, my_tokens, lengths_row[0] + my_tokens - my_first)
    freqs = 10000.0 ** (-(2.0 * jnp.arange(ROT // 2, dtype=jnp.float32)) / ROT)
    angles = position.astype(F32) * freqs[:, None]
    cos, sin = jnp.cos(angles), jnp.sin(angles)
    blocks = (w_qkv[0], w_fc[0], w_out[0], w_proj[0])
    vectors = (norm_gains, norm_biases, b_qkv, b_out, b_fc)
    k = first_half(rows, cols, hidden_in, cotangent, vectors, blocks, cos, sin, lengths)
    return finishing(second_half(rows, cols, k, cos, sin, lengths))


def fits(mesh):
    rows, cols = mesh.shape[ROW], mesh.shape[COL]
    return rows == cols == 4 and MODEL_WIDTH == rows * cols * HEAD_DIM


def solution(mesh):
    return jax.shard_map(
        relay_body if fits(mesh) else body,
        mesh=mesh,
        in_specs=(
            P(None, ROW, COL),
            P(None, ROW, COL),
            P(),
            P(SECTION, None, COL),
            P(SECTION, None, COL),
            P(SECTION, None, ROW, COL),
            P(SECTION, None, COL),
            P(SECTION, COL, ROW),
            P(SECTION, ROW, COL),
            P(SECTION, COL),
            P(SECTION, COL, ROW),
            P(SECTION, COL),
        ),
        out_specs=(
            P(SECTION, None, ROW, COL),
            P(SECTION, None, ROW, COL),
            P(SECTION, None, COL),
            P(SECTION, None, COL),
            P(SECTION, None, ROW, COL),
            P(SECTION, None, COL),
            P(SECTION, COL, ROW),
            P(SECTION, ROW, COL),
            P(SECTION, COL),
            P(SECTION, COL, ROW),
            P(SECTION, COL),
        ),
        check_vma=False,
    )
```

```python
from functools import partial
import math

import jax
import jax.numpy as jnp
from jax import lax
from jax.experimental import pallas as pl
from jax.experimental.pallas import tpu as pltpu
from jax.sharding import PartitionSpec as P

MODEL_WIDTH = 1024
HEAD_DIM = 64
ROT = 16
SECTION, ROW, COL = "section", "row", "col"


EPS = 1e-05
NEG = -1e30


def from_partner(value, axis, apart):
    mask = 2**apart
    pairs = [(source, source ^ mask) for source in range(lax.axis_size(axis))]
    return lax.ppermute(value, axis, pairs)


def segment_of(token_ids, starts):
    return jnp.sum((token_ids[:, None] >= starts[None, 1:]).astype(jnp.int32), axis=1)


def token_layout(lengths_row, token_ids):
    starts = jnp.cumsum(lengths_row) - lengths_row
    segment = segment_of(token_ids, starts)
    labels = jnp.arange(1, lengths_row.shape[0], dtype=jnp.int32)
    seg_begin = jnp.sum(jnp.where(segment[:, None] == labels[None, :], starts[None, 1:], 0), axis=1)
    position = jnp.where(segment == 0, token_ids, lengths_row[0] + token_ids - seg_begin)
    return (starts, segment, position)


def rotary_tables(position, turned):
    half_rot = turned // 2
    freqs = 10000.0 ** (-(2.0 * jnp.arange(half_rot, dtype=jnp.float32)) / turned)
    angles = position.astype(jnp.float32)[:, None] * freqs[None, :]
    return (jnp.cos(angles), jnp.sin(angles))


def rotate(values, cos_table, sin_table, direction):
    half_rot = cos_table.shape[-1]
    lower = values[..., :half_rot]
    upper = values[..., half_rot : 2 * half_rot]
    cos_cast = cos_table[:, None, :]
    sin_cast = direction * sin_table[:, None, :]
    return jnp.concatenate(
        [
            lower * cos_cast - upper * sin_cast,
            upper * cos_cast + lower * sin_cast,
            values[..., 2 * half_rot :],
        ],
        axis=-1,
    )


def permitted(query_seg, query_tok, key_seg, key_tok):
    from_prompt = (key_seg[None, :] == 0) & (query_seg[:, None] > 0)
    same_causal = (key_seg[None, :] == query_seg[:, None]) & (
        key_tok[None, :] <= query_tok[:, None]
    )
    return from_prompt | same_causal


def attend(running, key_piece, value_piece, query3, layout):
    run_max, run_sum, totals = running
    piece_len = key_piece.shape[0]
    key3 = key_piece.reshape(piece_len, query3.shape[1], query3.shape[2])
    value3 = value_piece.reshape(piece_len, query3.shape[1], query3.shape[2])
    key_tok = jnp.arange(piece_len, dtype=jnp.int32)
    key_seg = segment_of(key_tok, layout["starts"])
    allowed = permitted(layout["segment"], layout["tokens"], key_seg, key_tok)[None]
    scores = jnp.einsum("qhd,khd->hqk", query3, key3, preferred_element_type=jnp.float32) * (
        1.0 / math.sqrt(query3.shape[2])
    )
    masked = jnp.where(allowed, scores, NEG)
    new_max = jnp.maximum(run_max, jnp.max(masked, axis=-1))
    weights = jnp.where(allowed, jnp.exp(masked - new_max[..., None]), 0.0)
    run_sum = jnp.sum(weights, axis=-1)
    totals = jnp.einsum(
        "hqk,khd->hqd", weights.astype(jnp.bfloat16), value3, preferred_element_type=jnp.float32
    )
    return (new_max, run_sum, totals)


def layer_forward(x, full, weights, layout, complete_gains, complete_shifts):
    w_query, b_query, w_output, w_hidden, b_hidden, w_project, b_output = weights
    row_tokens, local_width = x.shape
    heads_local = local_width // HEAD_DIM
    shaped = (row_tokens, heads_local, HEAD_DIM)
    as_float = full.astype(jnp.float32)
    row_mean = jnp.mean(as_float, axis=1, keepdims=True)
    centred = as_float - row_mean
    rstd = lax.rsqrt(jnp.mean(centred * centred, axis=1, keepdims=True) + EPS)
    unit = centred * rstd
    normed_a = (unit * complete_gains[0] + complete_shifts[0]).astype(jnp.bfloat16)
    normed_m = (unit * complete_gains[1] + complete_shifts[1]).astype(jnp.bfloat16)
    projected = (
        jnp.einsum("td,cde->cte", normed_a, w_query, preferred_element_type=jnp.float32)
        + b_query[:, None, :]
    )
    cos_table, sin_table = layout["cos_table"], layout["sin_table"]
    query3 = rotate(projected[0].reshape(shaped), cos_table, sin_table, 1.0).astype(jnp.bfloat16)
    key_flat = (
        rotate(projected[1].reshape(shaped), cos_table, sin_table, 1.0)
        .reshape(row_tokens, local_width)
        .astype(jnp.bfloat16)
    )
    value_flat = projected[2].astype(jnp.bfloat16)
    key_full = lax.all_gather(key_flat, ROW, axis=0, tiled=True)
    value_full = lax.all_gather(value_flat, ROW, axis=0, tiled=True)
    initial = (
        jnp.full((heads_local, row_tokens), NEG, jnp.float32),
        jnp.zeros((heads_local, row_tokens), jnp.float32),
        jnp.zeros((heads_local, row_tokens, HEAD_DIM), jnp.float32),
    )
    run_max, run_sum, totals = attend(initial, key_full, value_full, query3, layout)
    out_exact = totals / run_sum[..., None]
    log_sum = run_max + jnp.log(run_sum)
    attn_flat = (
        jnp.transpose(out_exact, (1, 0, 2)).reshape(row_tokens, local_width).astype(jnp.bfloat16)
    )
    hidden_pre = jnp.dot(normed_m, w_hidden, preferred_element_type=jnp.float32) + b_hidden
    hidden = jax.nn.gelu(hidden_pre, approximate=False).astype(jnp.bfloat16)
    branch = jnp.dot(attn_flat, w_output, preferred_element_type=jnp.float32) + jnp.dot(
        hidden, w_project, preferred_element_type=jnp.float32
    )
    summed = lax.psum_scatter(
        branch.astype(jnp.bfloat16), COL, scatter_dimension=1, tiled=True
    ).astype(jnp.float32)
    output = (x.astype(jnp.float32) + summed + b_output).astype(jnp.bfloat16)
    state = dict(
        unit=unit, rstd=rstd, normed_a=normed_a, normed_m=normed_m, query3=query3,
        key_full=key_full, value_full=value_full, attn_flat=attn_flat, out_exact=out_exact,
        log_sum=log_sum, hidden_pre=hidden_pre, hidden=hidden,
    )
    return output, state


def layer_backward(state, grad_in, grad_full, weights, layout, complete_gains, scatter_tokens):
    w_query, b_query, w_output, w_hidden, b_hidden, w_project, b_output = weights
    row_tokens = state["normed_a"].shape[0]
    local_width = w_output.shape[0]
    heads_local = local_width // HEAD_DIM
    shaped = (row_tokens, heads_local, HEAD_DIM)
    score_scale = 1.0 / math.sqrt(HEAD_DIM)
    total_tokens = state["key_full"].shape[0]
    key_block = min(512, total_tokens)
    grad_wout = jnp.einsum(
        "te,td->ed", state["attn_flat"], grad_full, preferred_element_type=jnp.float32
    )
    grad_wproj = jnp.einsum(
        "tf,td->fd", state["hidden"], grad_full, preferred_element_type=jnp.float32
    )
    grad_bout = jnp.sum(grad_in.astype(jnp.float32), axis=0)
    grad_attn = jnp.einsum(
        "td,ed->te", grad_full, w_output, preferred_element_type=jnp.float32
    ).astype(jnp.bfloat16)
    grad_hidden = jnp.einsum("td,fd->tf", grad_full, w_project, preferred_element_type=jnp.float32)
    gelu_value, gelu_back = jax.vjp(partial(jax.nn.gelu, approximate=False), state["hidden_pre"])
    grad_hpre = gelu_back(grad_hidden)[0].astype(jnp.bfloat16)
    grad_wfc = jnp.einsum(
        "td,tf->df", state["normed_m"], grad_hpre, preferred_element_type=jnp.float32
    )
    grad_bfc = jnp.sum(grad_hpre.astype(jnp.float32), axis=0)
    grad_normed_m = jnp.einsum("tf,df->td", grad_hpre, w_hidden, preferred_element_type=jnp.float32)
    grad_out3 = grad_attn.reshape(shaped)
    query3 = state["query3"]
    delta = jnp.sum(
        jnp.transpose(grad_out3.astype(jnp.float32), (1, 0, 2)) * state["out_exact"], axis=-1
    )
    grad_query = jnp.zeros(shaped, jnp.float32)
    key_terms = []
    value_terms = []
    for block_no in range(total_tokens // key_block):
        begin_at = block_no * key_block
        key_part = state["key_full"][begin_at : begin_at + key_block].reshape(
            key_block, heads_local, HEAD_DIM
        )
        value_part = state["value_full"][begin_at : begin_at + key_block].reshape(
            key_block, heads_local, HEAD_DIM
        )
        key_tok = begin_at + jnp.arange(key_block, dtype=jnp.int32)
        key_seg = segment_of(key_tok, layout["starts"])
        allowed = permitted(layout["segment"], layout["tokens"], key_seg, key_tok)[None]
        scores = (
            jnp.einsum("qhd,khd->hqk", query3, key_part, preferred_element_type=jnp.float32)
            * score_scale
        )
        probs = jnp.where(
            allowed,
            jnp.exp(jnp.where(allowed, scores, NEG) - state["log_sum"][..., None]),
            0.0,
        )
        grad_probs = jnp.einsum(
            "qhd,khd->hqk", grad_out3, value_part, preferred_element_type=jnp.float32
        )
        grad_scores = (probs * (grad_probs - delta[..., None])).astype(jnp.bfloat16)
        grad_query = grad_query + jnp.einsum(
            "hqk,khd->qhd", grad_scores, key_part, preferred_element_type=jnp.float32
        )
        key_terms.append(
            jnp.einsum(
                "hqk,qhd->khd", grad_scores, query3, preferred_element_type=jnp.float32
            ).reshape(key_block, local_width)
            * score_scale
        )
        value_terms.append(
            jnp.einsum(
                "hqk,qhd->khd",
                probs.astype(jnp.bfloat16),
                grad_out3,
                preferred_element_type=jnp.float32,
            ).reshape(key_block, local_width)
        )
    grad_query = grad_query * score_scale
    kv_terms = jnp.concatenate(
        [jnp.concatenate(key_terms, axis=0), jnp.concatenate(value_terms, axis=0)], axis=1
    )
    kv_grads = lax.psum_scatter(
        kv_terms.astype(jnp.bfloat16), ROW, scatter_dimension=0, tiled=True
    ).astype(jnp.float32)
    grad_key = kv_grads[:, :local_width].reshape(shaped)
    grad_value = kv_grads[:, local_width:]
    cos_table, sin_table = layout["cos_table"], layout["sin_table"]
    grad_pre = jnp.stack(
        [
            rotate(grad_query, cos_table, sin_table, -1.0).reshape(row_tokens, local_width),
            rotate(grad_key, cos_table, sin_table, -1.0).reshape(row_tokens, local_width),
            grad_value,
        ]
    ).astype(jnp.bfloat16)
    grad_wqkv = jnp.einsum(
        "td,cte->cde", state["normed_a"], grad_pre, preferred_element_type=jnp.float32
    )
    grad_bqkv = jnp.sum(grad_pre.astype(jnp.float32), axis=1)
    grad_normed_a = jnp.einsum("cte,cde->td", grad_pre, w_query, preferred_element_type=jnp.float32)
    unit = state["unit"]
    grad_gains = jnp.stack(
        [jnp.sum(grad_normed_a * unit, axis=0), jnp.sum(grad_normed_m * unit, axis=0)]
    )
    grad_shifts = jnp.stack([jnp.sum(grad_normed_a, axis=0), jnp.sum(grad_normed_m, axis=0)])
    grad_unit = grad_normed_a * complete_gains[0] + grad_normed_m * complete_gains[1]
    big = (grad_wqkv, grad_wout, grad_wfc, grad_wproj)
    big = tuple(member.astype(jnp.bfloat16) for member in big)
    shared = (grad_gains, grad_shifts)
    local = (grad_bqkv, grad_bfc, grad_bout)
    if scatter_tokens:
        piece = lax.psum_scatter(
            grad_unit.astype(jnp.bfloat16), COL, scatter_dimension=0, tiled=True
        ).astype(jnp.float32)
        rows = piece.shape[0]
        start = lax.axis_index(COL) * rows
        unit_part = lax.dynamic_slice_in_dim(unit, start, rows, 0)
        rstd_part = lax.dynamic_slice_in_dim(state["rstd"], start, rows, 0)
        grad_part = lax.dynamic_slice_in_dim(grad_full, start, rows, 0).astype(jnp.float32)
        moved = (
            piece
            - jnp.mean(piece, axis=1, keepdims=True)
            - unit_part * jnp.mean(piece * unit_part, axis=1, keepdims=True)
        )
        grad_input = (grad_part + rstd_part * moved).astype(jnp.bfloat16)
    else:
        sums = lax.psum(
            jnp.stack([jnp.sum(grad_unit, axis=1), jnp.sum(grad_unit * unit, axis=1)]), COL
        )
        piece = lax.psum_scatter(
            grad_unit.astype(jnp.bfloat16), COL, scatter_dimension=1, tiled=True
        ).astype(jnp.float32)
        width = piece.shape[1]
        unit_part = lax.dynamic_slice_in_dim(unit, lax.axis_index(COL) * width, width, 1)
        moved = (
            piece
            - sums[0][:, None] / MODEL_WIDTH
            - unit_part * (sums[1][:, None] / MODEL_WIDTH)
        )
        grad_input = (grad_in.astype(jnp.float32) + state["rstd"] * moved).astype(jnp.bfloat16)
    return grad_input, big, shared, local


def body(
    hidden_in,
    cotangent,
    lengths,
    norm_gains,
    norm_biases,
    w_qkv,
    b_qkv,
    w_out,
    w_fc,
    b_fc,
    w_proj,
    b_out,
):
    row_tokens = hidden_in.shape[1]
    local_width = hidden_in.shape[2]
    section = lax.axis_index(SECTION)
    is_first = section == 0
    my_tokens = lax.axis_index(ROW) * row_tokens + jnp.arange(row_tokens, dtype=jnp.int32)
    x0 = lax.dynamic_index_in_dim(hidden_in, section, 0, keepdims=False)
    cot = lax.dynamic_index_in_dim(cotangent, section, 0, keepdims=False)
    lengths_row = lax.dynamic_index_in_dim(lengths, section, 0, keepdims=False)
    starts, segment, position = token_layout(lengths_row, my_tokens)
    cos_table, sin_table = rotary_tables(position, ROT)
    layout = {
        "starts": starts,
        "segment": segment,
        "tokens": my_tokens,
        "cos_table": cos_table,
        "sin_table": sin_table,
    }
    both = (SECTION, ROW)
    gains = lax.all_gather(norm_gains[0], (SECTION, COL), axis=0)
    shifts = lax.all_gather(norm_biases[0], (SECTION, COL), axis=0)
    cols = lax.axis_size(COL)

    def whole(vectors):
        split = vectors.reshape(2, cols, 2, local_width)
        return jnp.transpose(split, (0, 2, 1, 3)).reshape(2, 2, cols * local_width)

    gains, shifts = whole(gains), whole(shifts)
    biases = [lax.all_gather(member[0], SECTION, axis=0) for member in (b_qkv, b_fc, b_out)]
    x0_full = lax.all_gather(x0, COL, axis=1, tiled=True)
    rows = lax.axis_size(ROW)

    def unite(member, axis):
        gathered = lax.all_gather(member[0], both, axis=0)
        pieces = gathered.reshape((2, rows) + gathered.shape[1:])
        return [
            jnp.concatenate([pieces[layer, row] for row in range(rows)], axis=axis)
            for layer in range(2)
        ]

    w_query, w_hidden = unite(w_qkv, 1), unite(w_fc, 0)
    w_output, w_project = unite(w_out, 1), unite(w_proj, 1)
    weights = [
        (
            w_query[layer],
            biases[0][layer],
            w_output[layer],
            w_hidden[layer],
            biases[1][layer],
            w_project[layer],
            biases[2][layer],
        )
        for layer in range(2)
    ]
    out0, state0 = layer_forward(x0, x0_full, weights[0], layout, gains[0], shifts[0])
    x1_full = lax.all_gather(out0, COL, axis=1, tiled=True)
    cot_full = lax.all_gather(cot, COL, axis=1, tiled=True)
    out1, state1 = layer_forward(out0, x1_full, weights[1], layout, gains[1], shifts[1])
    grad1_part, big1, shared1, local1 = layer_backward(
        state1, cot, cot_full, weights[1], layout, gains[1], True
    )
    grad1_full = lax.all_gather(grad1_part, COL, axis=0, tiled=True)
    grad1 = lax.dynamic_slice_in_dim(
        grad1_full, lax.axis_index(COL) * local_width, local_width, 1
    )
    grad0, big0, shared0, local0 = layer_backward(
        state0, grad1, grad1_full, weights[0], layout, gains[0], False
    )

    def swap(first, second):
        mine = jnp.where(is_first, first, second)
        theirs = from_partner(jnp.where(is_first, second, first), SECTION, 0)
        return jnp.where(is_first, jnp.stack([mine, theirs]), jnp.stack([theirs, mine]))[None]

    out_rows = swap(out0, out1)
    grad_rows = swap(grad0, grad1)

    def scatter(first, second, axis):
        length = first.shape[axis] // rows
        pieces = jnp.stack(
            [
                lax.slice_in_dim(member, row * length, (row + 1) * length, axis=axis)
                for member in (first, second)
                for row in range(rows)
            ]
        )
        return lax.psum_scatter(pieces, both, scatter_dimension=0, tiled=True).astype(jnp.float32)

    large = [scatter(a, b, axis) for a, b, axis in zip(big0, big1, (1, 1, 0, 1))]
    shared_sums = lax.psum(
        tuple(jnp.stack([a, b]) for a, b in zip(shared0, shared1)), (SECTION, ROW, COL)
    )
    shared_mine = [
        lax.dynamic_slice(
            member,
            (section, 0, lax.axis_index(COL) * local_width),
            (1, 2, local_width),
        )
        for member in shared_sums
    ]
    local_sums = lax.psum(tuple(jnp.stack([a, b]) for a, b in zip(local0, local1)), both)
    local_mine = [lax.dynamic_index_in_dim(member, section, 0) for member in local_sums]
    return (
        out_rows,
        grad_rows,
        shared_mine[0],
        shared_mine[1],
        large[0],
        local_mine[0],
        large[1],
        large[2],
        local_mine[1],
        large[3],
        local_mine[2],
    )


BF = jnp.bfloat16
F32 = jnp.float32
BY_MESH = pl.DeviceIdType.MESH
VMEM_LIMIT = 62 * 2**20
QUERY_BLOCK = 256
KEY_BLOCK = 512
PROMPT_LEAST = 768
PARTS = 2
CHUNKS = 16
LOADS = 24
LAG = 4


def dot(a, b, contract=((1,), (0,))):
    return lax.dot_general(a, b, (contract, ((), ())), preferred_element_type=F32)


def rcopy(src, dst, ssem, rsem, **device):
    return pltpu.make_async_remote_copy(
        src_ref=src,
        dst_ref=dst,
        send_sem=ssem,
        recv_sem=rsem,
        device_id=device,
        device_id_type=BY_MESH,
    )


class Place:
    def __init__(self, rows, cols):
        self.rows, self.cols = rows, cols
        self.s = lax.axis_index(SECTION)
        self.r = lax.axis_index(ROW)
        self.c = lax.axis_index(COL)

    def row_to(self, step):
        return lax.rem(self.r + step, self.rows)

    def row_from(self, step):
        return lax.rem(self.r + self.rows - step, self.rows)

    def beside(self, way):
        if way == 0:
            return self.r + 1 - 2 * lax.rem(self.r, 2)
        return lax.rem(self.r + 2, 4)

    def across(self):
        return 3 - self.r

    def col_to(self, step):
        return lax.rem(self.c + step, self.cols)

    def col_from(self, step):
        return lax.rem(self.c + self.cols - step, self.cols)

    def greet(self, rows=False, cols=False, partner=False, cross_cols=False, cross_rows=False):
        barrier = pltpu.get_barrier_semaphore()
        count = 0

        def signal(**device):
            pl.semaphore_signal(barrier, inc=1, device_id=device, device_id_type=BY_MESH)

        if rows:
            for step in range(1, self.rows):
                signal(row=self.row_to(step))
                count += 1
        if cols:
            for step in range(1, self.cols):
                signal(col=self.col_to(step))
                count += 1
        if partner:
            signal(section=1 - self.s)
            count += 1
        if cross_cols:
            for step in range(1, self.cols):
                signal(section=1 - self.s, col=self.col_to(step))
                count += 1
        if cross_rows:
            for step in range(1, self.rows):
                signal(section=1 - self.s, row=self.row_to(step))
                count += 1
        pl.semaphore_wait(barrier, count)


class LineGather:
    def __init__(self, place, view, send_right, send_left, recv, lane=0):
        self.place, self.view, self.lane = place, view, lane
        self.send_right, self.send_left, self.recv = send_right, send_left, recv

    def right(self, block):
        return rcopy(
            self.view(block), self.view(block), self.send_right.at[self.lane, block],
            self.recv.at[self.lane, block],
            col=lax.rem(self.place.c + 1, self.place.cols),
        )

    def left(self, block):
        cols = self.place.cols
        return rcopy(
            self.view(block), self.view(block), self.send_left.at[self.lane, block],
            self.recv.at[self.lane, block],
            col=lax.rem(self.place.c + cols - 1, cols),
        )

    def hop(self, distance):
        c, cols = self.place.c, self.place.cols

        @pl.when(c >= distance)
        def _():
            block = lax.rem(c + cols - distance, cols)
            if distance:
                self.right(block).wait_recv()

            @pl.when(c < cols - 1)
            def _():
                self.right(block).start()

        @pl.when(c + distance < cols)
        def _():
            block = lax.rem(c + distance, cols)
            if distance:
                self.left(block).wait_recv()

            @pl.when(c > 0)
            def _():
                self.left(block).start()

    def finish(self):
        c, cols = self.place.c, self.place.cols
        for distance in range(cols):

            @pl.when((c >= distance) & (c < cols - 1))
            def _():
                self.right(lax.rem(c + cols - distance, cols)).wait_send()

            @pl.when((c + distance < cols) & (c > 0))
            def _():
                self.left(lax.rem(c + distance, cols)).wait_send()


class WeightGather:
    def __init__(self, place, layer, own, full, send, recv, local):
        self.place, self.layer, self.own, self.full = place, layer, own, full
        self.send, self.recv, self.local = send, recv, local

    def view(self, kind, block, half=None):
        lines = self.own[kind].shape[-2]
        length = self.own[kind].shape[-2 if kind in (0, 1) else -1]
        at, count = (0, lines) if half is None else (half * (lines // 2), lines // 2)
        if kind in (0, 1):
            piece = pl.ds(pl.multiple_of(block * length + at, count), count)
            return self.full[kind].at[:, piece, :] if kind == 0 else self.full[1].at[piece, :]
        piece = pl.ds(pl.multiple_of(block * length, length), length)
        return self.full[kind].at[at : at + count, piece]

    def direct(self, kind, way):
        place = self.place
        return rcopy(
            self.own[kind], self.view(kind, place.r), self.send.at[kind, way],
            self.recv.at[kind, way], row=place.beside(way),
        )

    def relayed(self, kind, way):
        place = self.place
        piece = self.view(kind, place.beside(way), way)
        return rcopy(
            piece, piece, self.send.at[kind, 2 + way], self.recv.at[kind, 2 + way],
            row=place.beside(1 - way),
        )

    def arriving(self, kind, way):
        block = self.view(kind, self.place.beside(way))
        return rcopy(
            block, block, self.send.at[kind, way], self.recv.at[kind, way],
            row=self.place.beside(way),
        )

    def across(self, kind, way):
        piece = self.view(kind, self.place.across(), way)
        return rcopy(
            piece, piece, self.send.at[kind, 2 + way], self.recv.at[kind, 2 + way],
            row=self.place.beside(1 - way),
        )

    def to_partner(self, kind, which):
        place = self.place
        source = (place.beside(0), place.beside(1), place.across(), place.r)[which]
        block = self.view(kind, source)
        return rcopy(
            self.own[kind] if which == 3 else block, block, self.send.at[kind, 4 + which],
            self.recv.at[kind, 4 + which], section=1 - place.s,
        )

    def keep(self, kind):
        return pltpu.make_async_copy(
            self.own[kind], self.view(kind, self.place.r), self.local.at[kind]
        )

    def start(self, kind):
        @pl.when(self.place.s == self.layer)
        def _():
            for way in range(2):
                self.direct(kind, way).start()
            self.keep(kind).start()
            self.to_partner(kind, 3).start()

    def relay(self, kind):
        @pl.when(self.place.s == self.layer)
        def _():
            for way in range(2):
                self.arriving(kind, way).wait_recv()
                self.relayed(kind, way).start()
                self.to_partner(kind, way).start()

    def forward(self, kind):
        @pl.when(self.place.s == self.layer)
        def _():
            for way in range(2):
                self.across(kind, way).wait_recv()
            self.to_partner(kind, 2).start()
            self.keep(kind).wait()

    def ready(self, kind):
        @pl.when(self.place.s != self.layer)
        def _():
            for which in range(4):
                self.to_partner(kind, which).wait_recv()

    def finish(self, kind):
        @pl.when(self.place.s == self.layer)
        def _():
            for way in range(2):
                self.direct(kind, way).wait_send()
                self.relayed(kind, way).wait_send()
            for which in range(4):
                self.to_partner(kind, which).wait_send()


class RowExchange:
    def __init__(self, place, piece_for, slot_of, send, recv, local):
        self.place, self.piece_for, self.slot_of = place, piece_for, slot_of
        self.send, self.recv, self.local = send, recv, local

    def out(self, step):
        place = self.place
        target = place.row_to(step)
        return rcopy(
            self.piece_for(target), self.slot_of(place.r), self.send.at[step], self.recv.at[step],
            row=target,
        )

    def into(self, step):
        slot = self.slot_of(self.place.row_from(step))
        return rcopy(
            slot, slot, self.send.at[step], self.recv.at[step], row=self.place.row_to(step)
        )

    def keep(self):
        return pltpu.make_async_copy(
            self.piece_for(self.place.r), self.slot_of(self.place.r), self.local
        )

    def start(self):
        for step in range(1, self.place.rows):
            self.out(step).start()
        self.keep().start()

    def arrive(self):
        for step in range(1, self.place.rows):
            self.into(step).wait_recv()
        self.keep().wait()

    def finish(self):
        for step in range(1, self.place.rows):
            self.out(step).wait_send()


def norm_rows(source, gains_a, shifts_a, gains_m, shifts_m, normed_a, normed_m, begin=0, count=None):
    count = source.shape[0] if count is None else count
    tile = min(128, count)

    @pl.loop(0, count // tile)
    def _(index):
        rows = pl.ds(pl.multiple_of(begin + index * tile, tile), tile)
        values = source[rows, :].astype(F32)
        centred = values - jnp.mean(values, axis=1, keepdims=True)
        unit = centred * lax.rsqrt(jnp.mean(centred * centred, axis=1, keepdims=True) + EPS)
        normed_a[rows, :] = (unit * gains_a + shifts_a).astype(BF)
        normed_m[rows, :] = (unit * gains_m + shifts_m).astype(BF)


def turn(block, cos, sin, direction):
    half = cos.shape[0]
    lower, upper, rest = block[:half], block[half : 2 * half], block[2 * half :]
    return jnp.concatenate(
        [
            lower * cos - upper * (direction * sin),
            upper * cos + lower * (direction * sin),
            rest,
        ],
        axis=0,
    )


def project_heads(normed_a, w_query, bias_rows, cos, sin, pieces, heads, where):
    for kind in range(3):
        flipped = (dot(normed_a[where, :], w_query[kind]) + bias_rows(kind)).T
        for head in range(heads):
            block = flipped[head * HEAD_DIM : (head + 1) * HEAD_DIM]
            if kind < 2:
                block = turn(block, cos[:, where], sin[:, where], 1.0)
            pieces[head, kind * HEAD_DIM : (kind + 1) * HEAD_DIM, where] = block.astype(BF)


def feed_forward(normed_m, w_hidden, bias_of, hidden, slope, where):
    tile = min(256, w_hidden.shape[1])

    @pl.loop(0, w_hidden.shape[1] // tile)
    def _(index):
        cols = pl.ds(pl.multiple_of(index * tile, tile), tile)
        pre = dot(normed_m[where, :], w_hidden[:, cols]) + bias_of(index)
        phi = 0.5 * (1.0 + lax.erf(pre * math.sqrt(0.5)))
        hidden[where, cols] = (pre * phi).astype(BF)
        turned = phi + pre * (jnp.exp(-0.5 * pre * pre) * (1.0 / math.sqrt(2.0 * math.pi)))
        slope[where, cols] = turned.astype(slope.dtype)


def times_tiles(left, right, out, convert=None, contract=((1,), (0,)), where=slice(None)):
    tile = min(256, out.shape[1])

    @pl.loop(0, out.shape[1] // tile)
    def _(index):
        cols = pl.ds(pl.multiple_of(index * tile, tile), tile)
        piece = right[:, cols] if contract[1] == (0,) else right[cols, :]
        value = dot(left[where, :], piece, contract)
        out[where, cols] = value if convert is None else convert(value, cols)


def dma(*shape):
    return pltpu.SemaphoreType.DMA(shape)


def key_mask(prompt, first, cols, key_at, query_at, keys, queries):
    in_prompt = key_at + keys <= PROMPT_LEAST
    before = key_at + keys <= query_at + 1
    if in_prompt and before:
        return None
    key = lax.broadcasted_iota(jnp.int32, (keys, queries), 0) + key_at
    allowed = None
    if not in_prompt:
        allowed = (key < prompt) | (key >= first[:, cols])
    if not before:
        causal = key <= lax.broadcasted_iota(jnp.int32, (keys, queries), 1) + query_at
        allowed = causal if allowed is None else allowed & causal
    return allowed


def rows_of_keys(qkv, at, rows):
    rows[...] = qkv[at : at + HEAD_DIM, :].astype(F32).T.astype(BF)


def key_blocks(query_at, queries):
    last = query_at + queries
    return [(at, min(KEY_BLOCK, last - at)) for at in range(0, last, KEY_BLOCK)]


def scaled_query(qkv, cols):
    return (qkv[:HEAD_DIM, cols].astype(F32) * (1.0 / math.sqrt(HEAD_DIM))).astype(BF)


def score_block(prompt, first, cols, query_at, key_at, keys, key_rows, query):
    scores = dot(key_rows[key_at : key_at + keys, :], query)
    allowed = key_mask(prompt, first, cols, key_at, query_at, keys, query.shape[1])
    return scores if allowed is None else jnp.where(allowed, scores, NEG)


def attend_block(block, size, prompt, first, qkv, key_rows, scores, spot, keep_weights=False):
    query_at = block * size
    cols = slice(query_at, query_at + size)
    query = scaled_query(qkv, cols)
    blocks = key_blocks(query_at, size)
    top = None
    for key_at, keys in blocks:
        piece = score_block(prompt, first, cols, query_at, key_at, keys, key_rows, query)
        scores[spot(key_at, keys)] = piece
        highest = jnp.max(piece, axis=0, keepdims=True)
        top = highest if top is None else jnp.maximum(top, highest)
    weight, totals = None, None
    for key_at, keys in blocks:
        probs = jnp.exp(scores[spot(key_at, keys)] - top)
        if keep_weights:
            scores[spot(key_at, keys)] = probs
        part = jnp.sum(probs, axis=0, keepdims=True)
        product = dot(qkv[2 * HEAD_DIM : 3 * HEAD_DIM, key_at : key_at + keys], probs.astype(BF))
        weight = part if weight is None else weight + part
        totals = product if totals is None else totals + product
    return totals / weight, top, weight


def gradient_block(
    block, size, qkv, d_out, delta, probs_of, key_rows, value_rows, key_acc, value_acc, opening
):
    query_at = block * size
    cols = slice(query_at, query_at + size)
    query = scaled_query(qkv, cols)
    d_query = d_out[:, cols]
    d_sum = None
    for key_at, keys in key_blocks(query_at, size):
        where = slice(key_at, key_at + keys)
        probs = probs_of(key_at, keys, query)
        d_probs = dot(value_rows[where, :], d_query)
        d_scores = (probs * (d_probs - delta)).astype(BF)
        d_key = dot(query, d_scores, ((1,), (1,)))
        d_value = dot(d_query, probs.astype(BF), ((1,), (1,)))
        if opening:
            key_acc[:, where] = d_key
            value_acc[:, where] = d_value
        else:
            key_acc[:, where] += d_key
            value_acc[:, where] += d_value
        part = dot(qkv[HEAD_DIM : 2 * HEAD_DIM, where], d_scores)
        d_sum = part if d_sum is None else d_sum + part
    return d_sum * (1.0 / math.sqrt(HEAD_DIM))


class LineReduce:
    def __init__(self, place, total, low, from_left, from_right, view, sems, lane=0):
        self.place, self.total, self.low, self.view, self.lane = place, total, low, view, lane
        self.from_left, self.from_right = from_left, from_right
        self.send_right, self.send_left, self.recv_left, self.recv_right = sems

    def right(self, owner):
        return rcopy(
            self.low.at[self.view(owner)], self.from_left.at[self.view(owner)],
            self.send_right.at[self.lane, owner], self.recv_left.at[self.lane, owner],
            col=lax.rem(self.place.c + 1, self.place.cols),
        )

    def left(self, owner):
        cols = self.place.cols
        return rcopy(
            self.low.at[self.view(owner)], self.from_right.at[self.view(owner)],
            self.send_left.at[self.lane, owner], self.recv_right.at[self.lane, owner],
            col=lax.rem(self.place.c + cols - 1, cols),
        )

    def add_in(self, owner, arrived):
        view = self.view(owner)
        self.low[view] = (self.total[view] + arrived[view].astype(F32)).astype(BF)

    def step(self, time):
        c, cols = self.place.c, self.place.cols

        @pl.when(c <= time)
        def _():
            owner = cols - 1 - time + c

            @pl.when(c > 0)
            def _():
                self.right(owner).wait_recv()
                self.add_in(owner, self.from_left)

            self.right(owner).start()

        @pl.when(c >= cols - 1 - time)
        def _():
            owner = time + c - (cols - 1)

            @pl.when(c < cols - 1)
            def _():
                self.left(owner).wait_recv()
                self.add_in(owner, self.from_right)

            self.left(owner).start()

    def own(self):
        c, cols = self.place.c, self.place.cols
        view = self.view(c)

        @pl.when(c > 0)
        def _():
            self.right(c).wait_recv()

        @pl.when(c == 0)
        def _():
            self.from_left[view] = jnp.zeros_like(self.from_left[view])

        @pl.when(c < cols - 1)
        def _():
            self.left(c).wait_recv()

        @pl.when(c == cols - 1)
        def _():
            self.from_right[view] = jnp.zeros_like(self.from_right[view])

        return (
            self.total[view] + self.from_left[view].astype(F32) + self.from_right[view].astype(F32)
        )

    def finish(self):
        c, cols = self.place.c, self.place.cols
        for time in range(cols - 1):

            @pl.when(c <= time)
            def _():
                self.right(cols - 1 - time + c).wait_send()

            @pl.when(c >= cols - 1 - time)
            def _():
                self.left(time + c - (cols - 1)).wait_send()


def center_sum(place, total, low, from_outer, from_inner, full, sems, order, prepare, produce, after, work):
    c = place.c
    a_send, a_recv, b_send, b_recv, c_send, c_recv = sems
    count = len(order)
    size = total.shape[0] // count
    inner = (c == 1) | (c == 2)
    outer = (c == 0) | (c == 3)
    pair = jnp.where(c < 2, 1 - c, 5 - c)
    middle = 3 - c
    group = count // 4

    def rows(index):
        return slice(order[index] * size, (order[index] + 1) * size)

    def inward(index):
        piece = rows(index)
        return rcopy(
            low.at[piece], from_outer.at[piece], a_send.at[index], a_recv.at[index], col=pair
        )

    def exchange(index):
        piece = rows(index)
        return rcopy(
            low.at[piece], from_inner.at[piece], b_send.at[index], b_recv.at[index], col=middle
        )

    def outward(index):
        piece = rows(index)
        return rcopy(full.at[piece], full.at[piece], c_send.at[index], c_recv.at[index], col=pair)

    prepare(0)
    for time in range(count + 2 * LAG):
        if time < count:

            @pl.when(outer)
            def _():
                inward(time).start()

            @pl.when(inner)
            def _():
                piece = rows(time)
                inward(time).wait_recv()
                low[piece, :] = (total[piece, :] + from_outer[piece, :].astype(F32)).astype(BF)
                exchange(time).start()

        if LAG <= time < count + LAG:

            @pl.when(inner)
            def _():
                index = time - LAG
                piece = rows(index)
                exchange(index).wait_recv()
                summed = low[piece, :].astype(F32) + from_inner[piece, :].astype(F32)
                full[piece, :] = produce(summed, piece)
                outward(index).start()

        if time >= 2 * LAG:

            @pl.when(outer)
            def _():
                outward(time - 2 * LAG).wait_recv()

        if time + 2 < count and (time + 2) % group == 0:
            prepare((time + 2) // group)
        if time >= 2 * LAG:
            after(time - 2 * LAG)
        work(time)
    for index in range(count):

        @pl.when(outer)
        def _():
            inward(index).wait_send()

        @pl.when(inner)
        def _():
            exchange(index).wait_send()
            outward(index).wait_send()


class GradExchange:
    def __init__(self, place, layer, n, send, recv):
        self.place, self.layer = place, layer
        self.mine, self.theirs, self.relay, self.inbox = (
            [getattr(n, name + kind) for kind in "qfop"]
            for name in ("mine_", "theirs_", "relay_", "inbox_")
        )
        self.send, self.recv = send, recv

    def block(self, which):
        place = self.place
        return (place.beside(0), place.beside(1), place.across(), place.r)[which]

    def view(self, kind, block, half=None):
        shape = self.inbox[kind].shape
        length = shape[-2 if kind in (0, 1) else -1]
        lines = shape[-2]
        at, count = (0, lines) if half is None else (half * (lines // 2), lines // 2)
        if kind in (0, 1):
            piece = pl.ds(pl.multiple_of(block * length + at, count), count)
            return (slice(None), piece, slice(None)) if kind == 0 else (piece, slice(None))
        piece = pl.ds(pl.multiple_of(block * length, length), length)
        return (slice(at, at + count), piece)

    def passing(self, kind, which):
        view = self.view(kind, self.block(which))
        return rcopy(
            self.mine[kind].at[view], self.theirs[kind].at[view], self.send.at[kind, which],
            self.recv.at[kind, which], section=1 - self.place.s,
        )

    def relaying(self, kind, way):
        target = self.place.across() if kind in DIRECT else self.place.beside(way)
        return rcopy(
            self.mine[kind].at[self.view(kind, self.place.across(), way)],
            self.relay[kind].at[way], self.send.at[kind, 4 + way], self.recv.at[kind, 4 + way],
            row=target,
        )

    def sending(self, kind, way):
        return rcopy(
            self.mine[kind].at[self.view(kind, self.place.beside(way))],
            self.inbox[kind].at[way], self.send.at[kind, 6 + way], self.recv.at[kind, 6 + way],
            row=self.place.beside(way),
        )

    def add(self, kind, view, value):
        self.mine[kind][view] = self.mine[kind][view] + value

    def hand(self, kind, only=(2, 0, 1, 3)):
        @pl.when(self.place.s != self.layer)
        def _():
            for which in only:
                self.passing(kind, which).start()

    def merge(self, kind):
        @pl.when(self.place.s == self.layer)
        def _():
            for which in (2, 0, 1):
                self.passing(kind, which).wait_recv()
                view = self.view(kind, self.block(which))
                self.add(kind, view, self.theirs[kind][view])
                if which == 2:
                    for way in range(2):
                        self.relaying(kind, way).start()
                elif kind in DIRECT:
                    self.sending(kind, which).start()

    def pass_on(self, kind):
        if kind in DIRECT:
            return

        @pl.when(self.place.s == self.layer)
        def _():
            for way in range(2):
                self.relaying(kind, 1 - way).wait_recv()
                view = self.view(kind, self.place.beside(way), 1 - way)
                self.add(kind, view, self.relay[kind][1 - way])
                self.sending(kind, way).start()

    def take(self, kind, out):
        @pl.when(self.place.s == self.layer)
        def _():
            self.passing(kind, 3).wait_recv()
            view = self.view(kind, self.place.r)
            total = self.mine[kind][view].astype(F32) + self.theirs[kind][view].astype(F32)
            for way in range(2):
                self.sending(kind, way).wait_recv()
                total = total + self.inbox[kind][way].astype(F32)
            out[...] = total
            if kind in DIRECT:
                for way in range(2):
                    self.relaying(kind, way).wait_recv()
                    half = self.relay[kind].shape[-2]
                    lines = slice(way * half, (way + 1) * half)
                    where = (slice(None), lines) if kind == 0 else (lines,)
                    out[where] = out[where] + self.relay[kind][way].astype(F32)

    def finish(self, kind):
        @pl.when(self.place.s == self.layer)
        def _():
            for way in range(2):
                self.relaying(kind, way).wait_send()
                self.sending(kind, way).wait_send()

        @pl.when(self.place.s != self.layer)
        def _():
            for which in range(4):
                self.passing(kind, which).wait_send()


def grad_shapes(rows, full, width, units):
    part = full // rows
    return (
        dict(q=(3, full, width), f=(full, units), o=(width, full), p=(units, full)),
        dict(q=(3, part, width), f=(part, units), o=(width, part), p=(units, part)),
    )


def grad_scratch(rows, full, width, units):
    wholes, pieces = grad_shapes(rows, full, width, units)
    scratch = {}
    for kind in "qfop":
        piece = pieces[kind]
        half = piece[:-2] + (piece[-2] // 2, piece[-1])
        scratch["mine_" + kind] = pltpu.VMEM(wholes[kind], BF)
        scratch["theirs_" + kind] = pltpu.VMEM(wholes[kind], BF)
        scratch["relay_" + kind] = pltpu.VMEM((2,) + half, BF)
        scratch["inbox_" + kind] = pltpu.VMEM((2,) + piece, BF)
    return scratch


class BlockExchange:
    def __init__(self, place, source, inbox, size, send, recv, local):
        self.place, self.source, self.inbox, self.size = place, source, inbox, size
        self.send, self.recv, self.local = send, recv, local

    def slot(self, head, lane):
        return self.inbox.at[head, :, lane * self.size : (lane + 1) * self.size]

    def piece(self, block):
        return self.source.at[:, block * self.size : (block + 1) * self.size]

    def away(self, block):
        return rcopy(
            self.piece(block), self.slot(self.place.r, block % PARTS), self.send.at[block],
            self.recv.at[block % PARTS, self.place.r], row=block // PARTS,
        )

    def start(self, block):
        @pl.when(self.place.r != block // PARTS)
        def _():
            self.away(block).start()

        @pl.when(self.place.r == block // PARTS)
        def _():
            pltpu.make_async_copy(
                self.piece(block), self.slot(self.place.r, block % PARTS),
                self.local.at[block % PARTS],
            ).start()

    def arrive(self, lane):
        for step in range(1, self.place.rows):
            source = self.place.row_from(step)
            slot = self.slot(source, lane)
            rcopy(
                slot, slot, self.send.at[lane], self.recv.at[lane, source],
                row=self.place.row_to(step),
            ).wait_recv()
        slot = self.slot(self.place.r, lane)
        pltpu.make_async_copy(slot, slot, self.local.at[lane]).wait()

    def finish(self):
        for block in range(self.place.rows * PARTS):

            @pl.when(self.place.r != block // PARTS)
            def _():
                self.away(block).wait_send()


def unit_rows(values):
    centred = values - jnp.mean(values, axis=1, keepdims=True)
    rstd = lax.rsqrt(jnp.mean(centred * centred, axis=1, keepdims=True) + EPS)
    return centred * rstd, rstd


def segment_begins(lengths, micro, first):
    token = lax.broadcasted_iota(jnp.int32, first.shape, 1)
    begin = jnp.zeros_like(token)
    start = lengths[micro, 0]
    for index in range(1, lengths.shape[1]):
        begin = jnp.where(token >= start, start, begin)
        start = start + lengths[micro, index]
    first[...] = begin
    return lengths[micro, 0]


def rotary(lengths, micro, row, cos, sin):
    half, tokens = cos.shape
    token = lax.broadcasted_iota(jnp.int32, (half, tokens), 1) + row * tokens
    begin = jnp.zeros_like(token)
    start = lengths[micro, 0]
    for index in range(1, lengths.shape[1]):
        begin = jnp.where(token >= start, start, begin)
        start = start + lengths[micro, index]
    position = jnp.where(begin == 0, token, lengths[micro, 0] + token - begin)
    which = lax.broadcasted_iota(jnp.int32, (half, tokens), 0)
    freqs = jnp.zeros((half, tokens), F32)
    for index in range(half):
        freqs = jnp.where(which == index, 10000.0 ** (-(2.0 * index) / ROT), freqs)
    angles = position.astype(F32) * freqs
    cos[...] = jnp.cos(angles)
    sin[...] = jnp.sin(angles)


class Saver:
    def __init__(self, sems):
        self.sems, self.copies = sems, []

    def copy(self, source, target):
        copy = pltpu.make_async_copy(source, target, self.sems.at[len(self.copies)])
        copy.start()
        self.copies.append(copy)
        return copy

    def finish(self):
        for copy in self.copies:
            copy.wait()


class Names:
    def joined(self, results):
        both = Names()
        for name, value in vars(self).items():
            setattr(both, name, value)
        for name, value in results.items():
            setattr(both, name[2:], value)
        return both


def named_call(body, collective_id, ins, outs, scratch):
    names = [*ins, *outs, *scratch]

    def kernel(*refs):
        held = Names()
        for name, ref in zip(names, refs):
            setattr(held, name, ref)
        body(held)

    results = pl.pallas_call(
        kernel,
        out_shape=[jax.ShapeDtypeStruct(shape, dtype) for shape, dtype, space in outs.values()],
        in_specs=[pl.BlockSpec(memory_space=space) for array, space in ins.values()],
        out_specs=[pl.BlockSpec(memory_space=space) for shape, dtype, space in outs.values()],
        scratch_shapes=list(scratch.values()),
        compiler_params=pltpu.CompilerParams(
            collective_id=collective_id,
            has_side_effects=collective_id is not None,
            vmem_limit_bytes=VMEM_LIMIT,
        ),
    )(*[array for array, space in ins.values()])
    return dict(zip(outs, results))


class VectorGather:
    def __init__(self, place, own, full, send, recv, width):
        self.place, self.own, self.full, self.width = place, own, full, width
        self.send, self.recv = send, recv
        self.others = [(ds, dc) for ds in range(2) for dc in range(place.cols) if ds or dc]

    def slot(self, section, col):
        return self.full.at[section, :, pl.ds(pl.multiple_of(col * self.width, self.width), self.width)]

    def copy(self, ds, dc, source, slot):
        index = ds * self.place.cols + dc
        return rcopy(
            source, slot, self.send.at[index], self.recv.at[index],
            section=lax.rem(self.place.s + ds, 2), col=self.place.col_to(dc),
        )

    def start(self):
        for ds, dc in self.others:
            self.copy(ds, dc, self.own, self.slot(self.place.s, self.place.c)).start()

    def arrive(self):
        for ds, dc in self.others:
            slot = self.slot(lax.rem(self.place.s + ds, 2), self.place.col_from(dc))
            self.copy(ds, dc, slot, slot).wait_recv()

    def finish(self):
        for ds, dc in self.others:
            self.copy(ds, dc, self.own, self.slot(self.place.s, self.place.c)).wait_send()


def first_kernel(rows, cols, n):
    place = Place(rows, cols)
    s, c = place.s, place.c
    tokens, full = n.x_full.shape
    width = full // cols
    length = tokens // PARTS
    own = pl.ds(pl.multiple_of(c * width, width), width)

    def lane_of(lane):
        return slice(lane * length, (lane + 1) * length)

    def block_cols(block):
        return pl.ds(pl.multiple_of(block * width, width), width)

    def token_slot(source, lane):
        return pl.ds(pl.multiple_of(source * tokens + lane * length, length), length)

    loads = Saver(n.load)
    x_own = loads.copy(n.hidden_in.at[s], n.x_full.at[:, own])
    n.vectors[0:2] = n.norm_gains[0]
    n.vectors[2:4] = n.norm_biases[0]
    for index in range(3):
        n.vectors[4 + index : 5 + index] = n.b_qkv[:, index * width : (index + 1) * width]
    n.vectors[7:8] = n.b_out[...]
    for index in range(n.b_fc.shape[1] // width):
        n.vectors[8 + index : 9 + index] = n.b_fc[:, index * width : (index + 1) * width]
    n.vectors[12:16] = jnp.zeros((4, width), F32)
    v_own = loads.copy(n.vectors, n.vec_all.at[s, :, own])
    c_own = loads.copy(n.cotangent.at[s], n.cot_full.at[:, own])
    place.greet(rows=True, cols=True, partner=True, cross_cols=True)
    x_gather = [
        LineGather(
            place, lambda block, lane=lane: n.x_full.at[lane_of(lane), block_cols(block)],
            n.x_a, n.x_b, n.x_c, lane,
        )
        for lane in range(PARTS)
    ]
    c_gather = LineGather(
        place, lambda block: n.cot_full.at[:, block_cols(block)], n.c_a, n.c_b, n.c_c
    )
    vectors = VectorGather(place, n.vectors, n.vec_all, n.v_s, n.v_r, width)
    blocks = (n.wq, n.wf, n.wo, n.wp)
    weights = [
        WeightGather(place, 0, blocks, (n.wq0, n.wf0, n.wo0, n.wp0), n.w0_s, n.w0_r, n.w0_l),
        WeightGather(place, 1, blocks, (n.wq1, n.wf1, n.wo1, n.wp1), n.w1_s, n.w1_r, n.w1_l),
    ]
    QKV, FC, OUT, PROJ = range(4)
    saves = Saver(n.save)
    def row(layer, index):
        return n.vec_all[layer, index : index + 1, :]

    def bias_rows(layer):
        return lambda kind: n.vec_all[layer, 4 + kind : 5 + kind, own]

    def unit_bias(layer):
        return lambda index: n.vec_all[layer, pl.ds(8 + index, 1), own]

    def spread(pieces, slots, sends, recvs, local):
        return [
            RowExchange(
                place,
                lambda target, lane=lane: pieces(target, lane),
                lambda source, lane=lane: slots(source, lane),
                sends.at[lane], recvs.at[lane], local.at[lane],
            )
            for lane in range(PARTS)
        ]

    out0 = spread(
        lambda target, lane: n.pieces0.at[target, :, lane_of(lane)],
        lambda source, lane: n.qkv0.at[:, token_slot(source, lane)],
        n.e0_s, n.e0_r, n.e0_l,
    )
    back0 = spread(
        lambda target, lane: n.low0.at[:, token_slot(target, lane)],
        lambda source, lane: n.attn_t0.at[
            pl.ds(pl.multiple_of(source * HEAD_DIM, HEAD_DIM), HEAD_DIM), lane_of(lane)
        ],
        n.b0_s, n.b0_r, n.b0_l,
    )
    out1 = spread(
        lambda target, lane: n.pieces1.at[target, :, lane_of(lane)],
        lambda source, lane: n.qkvd1.at[:, token_slot(source, lane)],
        n.e1_s, n.e1_r, n.e1_l,
    )

    def project(layer, lane, source, normed_a, normed_m, w_query, pieces):
        norm_rows(
            source, row(layer, 0), row(layer, 2), row(layer, 1), row(layer, 3), normed_a, normed_m,
            lane * length, length,
        )
        project_heads(
            normed_a, w_query, bias_rows(layer), n.cos, n.sin, pieces, rows, lane_of(lane)
        )

    x_own.wait()
    x_gather[0].hop(0)
    vectors.start()
    weights[0].start(QKV)
    weights[0].start(FC)
    prompt = segment_begins(n.lengths, s, n.first)
    rotary(n.lengths, s, place.r, n.cos, n.sin)
    x_gather[0].hop(1)
    x_gather[1].hop(0)
    x_gather[0].hop(2)
    weights[0].relay(QKV)
    weights[0].start(PROJ)
    x_gather[1].hop(1)
    for distance in range(3, cols):
        x_gather[0].hop(distance)
    weights[0].forward(QKV)
    weights[0].relay(FC)
    vectors.arrive()
    v_own.wait()
    x_gather[1].hop(2)
    weights[0].ready(QKV)
    project(0, 0, n.x_full, n.normed_a0, n.normed_m0, n.wq0, n.pieces0)
    out0[0].start()
    weights[0].start(OUT)
    for distance in range(3, cols):
        x_gather[1].hop(distance)
    c_own.wait()
    c_gather.hop(0)
    weights[0].forward(FC)
    project(0, 1, n.x_full, n.normed_a0, n.normed_m0, n.wq0, n.pieces0)
    out0[1].start()
    weights[0].relay(PROJ)
    weights[0].relay(OUT)
    c_gather.hop(1)
    weights[0].ready(FC)
    feed_forward(n.normed_m0, n.wf0, unit_bias(0), n.hidden0, n.slope0, slice(None))
    for ref, target in (
        (n.x_full, n.o_x_full), (n.vec_all, n.o_vec_all), (n.wq0, n.o_wq0), (n.wf0, n.o_wf0),
        (n.normed_a0, n.o_normed_a0), (n.normed_m0, n.o_normed_m0), (n.hidden0, n.o_hidden0),
        (n.slope0, n.o_slope0),
    ):
        saves.copy(ref, target)
    weights[0].forward(PROJ)
    weights[0].forward(OUT)
    weights[1].start(QKV)
    weights[1].start(OUT)
    for lane in range(PARTS):
        out0[lane].arrive()
    saves.copy(n.qkv0, n.o_qkv0)

    rows_of_keys(n.qkv0, HEAD_DIM, n.key_rows)

    def attend(lane, owner):
        block = owner * PARTS + lane
        exact, top, weight = attend_block(
            block, length, prompt, n.first, n.qkv0, n.key_rows, n.scores.at[owner % 2],
            lambda key_at, keys: (slice(key_at, key_at + keys), slice(None)),
        )
        cols_here = slice(block * length, (block + 1) * length)
        n.out0[:, cols_here] = exact
        n.low0[:, cols_here] = exact.astype(BF)
        n.log0[:, cols_here] = top + jnp.log(weight)

    for owner in range(rows):
        attend(0, owner)
    back0[0].start()
    c_gather.hop(2)
    weights[1].start(FC)
    weights[1].relay(QKV)
    weights[1].relay(OUT)
    attend(1, 0)
    attend(1, 1)
    for distance in range(3, cols):
        c_gather.hop(distance)
    weights[1].start(PROJ)
    weights[1].forward(QKV)
    weights[1].forward(OUT)
    saves.copy(n.cot_full, n.o_cot_full)
    weights[0].ready(PROJ)
    weights[0].ready(OUT)
    saves.copy(n.wp0, n.o_wp0)
    saves.copy(n.wo0, n.o_wo0)

    step = 4 // PARTS
    part = tokens // 4

    def prepare(quarter):
        if quarter % step == 0:
            back0[quarter // step].arrive()
        where = slice(quarter * part, (quarter + 1) * part)
        attn_rows = n.attn_t0[:, where].astype(F32).T.astype(BF)
        tile = min(256, full)
        for at in range(0, full, tile):
            value = dot(n.hidden0[where, :], n.wp0[:, at : at + tile]) + dot(
                attn_rows, n.wo0[:, at : at + tile]
            )
            n.total[where, at : at + tile] = value
            n.low[where, at : at + tile] = value.astype(BF)

    def produce(summed, mine):
        return (n.x_full[mine, :].astype(F32) + summed + n.vec_all[0, 7:8, :]).astype(BF)

    def branches(lane):
        where = lane_of(lane)
        feed_forward(n.normed_m1, n.wf1, unit_bias(1), n.hidden1, n.slope1, where)

        def times_slope(value, cols_here):
            return (value * n.slope1[where, cols_here]).astype(BF)

        times_tiles(n.cot_full, n.wp1, n.d_hidden1, times_slope, ((1,), (1,)), where)
        times_tiles(n.hidden1, n.wp1, n.branch1, None, ((1,), (0,)), where)
        times_tiles(n.d_hidden1, n.wf1, n.d_normed1, None, ((1,), (1,)), where)

    def after(chunk):
        if (chunk + 1) % (CHUNKS // PARTS):
            return
        lane = chunk // (CHUNKS // PARTS)
        if lane == 0:
            weights[1].ready(QKV)
            weights[1].ready(OUT)
        project(1, lane, n.x1_full, n.normed_a1, n.normed_m1, n.wq1, n.pieces1)
        where = lane_of(lane)
        flipped = dot(n.cot_full[where, :], n.wo1[...], ((1,), (1,))).T
        for head in range(rows):
            n.pieces1[head, 3 * HEAD_DIM :, where] = flipped[
                head * HEAD_DIM : (head + 1) * HEAD_DIM
            ].astype(BF)
        out1[lane].start()

    def work(time):
        if time < rows - 2:
            attend(1, 2 + time)
            if time == rows - 3:
                back0[1].start()
                saves.copy(n.out0, n.o_out0)
                saves.copy(n.log0, n.o_log0)
        if time == 2:
            weights[1].relay(FC)
        if time == 6:
            weights[1].forward(FC)
            weights[1].relay(PROJ)
        if time == 10:
            weights[1].forward(PROJ)
        if time == 20:
            weights[1].ready(FC)
            weights[1].ready(PROJ)
            branches(0)

    center_sum(
        place, n.total, n.low, n.from_left, n.from_right, n.x1_full,
        (n.r_a, n.r_b, n.r_c, n.r_d, n.r_e, n.r_f), tuple(range(CHUNKS)), prepare, produce, after, work,
    )
    saves.copy(n.attn_t0, n.o_attn_t0)
    for ref, target in (
        (n.x1_full, n.o_x1_full), (n.wq1, n.o_wq1), (n.wo1, n.o_wo1),
        (n.normed_a1, n.o_normed_a1), (n.normed_m1, n.o_normed_m1),
    ):
        saves.copy(ref, target)
    for lane in range(1, PARTS):
        branches(lane)
    for ref, target in (
        (n.hidden1, n.o_hidden1), (n.d_hidden1, n.o_d_hidden1), (n.branch1, n.o_branch1),
        (n.d_normed1, n.o_d_normed1),
    ):
        saves.copy(ref, target)
    for lane in range(PARTS):
        out1[lane].arrive()
    saves.copy(n.qkvd1, n.o_qkvd1)
    for exchange in out0 + back0 + out1:
        exchange.finish()
    for gather in x_gather + [c_gather]:
        gather.finish()
    vectors.finish()
    for gather in weights:
        for kind in range(4):
            gather.finish(kind)
    saves.finish()


def first_half(rows, cols, hidden_in, cotangent, vectors, blocks, lengths):
    norm_gains, norm_biases, b_qkv, b_out, b_fc = vectors
    tokens, width = hidden_in.shape[1:]
    full = cols * width
    wq, wf, wo, wp = blocks
    units = wf.shape[1]
    total = rows * tokens
    hbm, vmem, smem = pl.ANY, pltpu.VMEM, pltpu.SMEM
    ins = dict(
        hidden_in=(hidden_in, hbm), cotangent=(cotangent, hbm), norm_gains=(norm_gains, vmem),
        norm_biases=(norm_biases, vmem), b_qkv=(b_qkv, vmem), b_out=(b_out, vmem), b_fc=(b_fc, vmem),
        wq=(wq, hbm), wf=(wf, hbm), wo=(wo, hbm), wp=(wp, hbm),
        lengths=(lengths, smem),
    )
    rows_low, rows_wide = ((tokens, full), BF), ((tokens, full), F32)
    unit_low, unit_wide = ((tokens, units), BF), ((tokens, units), F32)
    kept = dict(
        x_full=rows_low, cot_full=rows_low, vec_all=((2, 16, full), F32),
        wq0=((3, full, width), BF), wf0=((full, units), BF), wo0=((width, full), BF),
        wp0=((units, full), BF), normed_a0=rows_low, normed_m0=rows_low,
        qkv0=((3 * HEAD_DIM, total), BF), hidden0=unit_low, slope0=unit_low,
        out0=((HEAD_DIM, total), F32), log0=((1, total), F32), attn_t0=((width, tokens), BF),
        x1_full=rows_low, wq1=((3, full, width), BF), wo1=((width, full), BF),
        normed_a1=rows_low, normed_m1=rows_low, qkvd1=((4 * HEAD_DIM, total), BF),
        hidden1=unit_low, d_hidden1=unit_low, branch1=rows_wide, d_normed1=rows_wide,
    )
    outs = {"o_" + name: shape + (hbm,) for name, shape in kept.items()}
    scratch = {name: pltpu.VMEM(*shape) for name, shape in kept.items()}
    scratch.update(
        vectors=pltpu.VMEM((16, width), F32),
        wf1=pltpu.VMEM((full, units), BF), wp1=pltpu.VMEM((units, full), BF),
        slope1=pltpu.VMEM(*unit_wide), low0=pltpu.VMEM((HEAD_DIM, total), BF),
        total=pltpu.VMEM(*rows_wide), low=pltpu.VMEM(*rows_low),
        from_left=pltpu.VMEM(*rows_low), from_right=pltpu.VMEM(*rows_low),
        pieces0=pltpu.VMEM((rows, 3 * HEAD_DIM, tokens), BF),
        pieces1=pltpu.VMEM((rows, 4 * HEAD_DIM, tokens), BF),
        first=pltpu.VMEM((1, total), jnp.int32),
        cos=pltpu.VMEM((ROT // 2, tokens), F32), sin=pltpu.VMEM((ROT // 2, tokens), F32),
        key_rows=pltpu.VMEM((total, HEAD_DIM), BF),
        scores=pltpu.VMEM((2, total, tokens // PARTS), F32),
        load=dma(3), save=dma(len(kept)),
        x_a=dma(PARTS, cols), x_b=dma(PARTS, cols), x_c=dma(PARTS, cols),
        c_a=dma(1, cols), c_b=dma(1, cols), c_c=dma(1, cols),
        v_s=dma(2 * cols), v_r=dma(2 * cols),
        w0_s=dma(4, 8), w0_r=dma(4, 8), w0_l=dma(4), w1_s=dma(4, 8), w1_r=dma(4, 8), w1_l=dma(4),
    )
    for name in ("e0", "b0", "e1"):
        scratch[name + "_s"] = dma(PARTS, rows)
        scratch[name + "_r"] = dma(PARTS, rows)
        scratch[name + "_l"] = dma(PARTS)
    for name in ("r_a", "r_b", "r_c", "r_d", "r_e", "r_f"):
        scratch[name] = dma(CHUNKS)
    return Names().joined(named_call(partial(first_kernel, rows, cols), 1, ins, outs, scratch))


def d_projection(inbox, at, cos, sin, rows, d_pre, small, where):
    width = rows * HEAD_DIM
    for kind in range(3):
        parts = []
        for head in range(rows):
            start = at + kind * HEAD_DIM
            block = inbox[head, start : start + HEAD_DIM, where].astype(F32)
            parts.append(turn(block, cos[:, where], sin[:, where], -1.0) if kind < 2 else block)
        values = jnp.concatenate(parts, axis=0).T.astype(BF)
        d_pre[where, kind * width : (kind + 1) * width] = values
        small[8 + kind : 9 + kind, :] += jnp.sum(values.astype(F32), axis=0, keepdims=True)


def d_norms(source, d_pre, wq, d_normed, gain_a, gain_m, total, low, sums, begin, count, also=None):
    width = wq.shape[2]
    tile = min(128, count)

    @pl.loop(0, count // tile)
    def _(index):
        rows = pl.ds(pl.multiple_of(begin + index * tile, tile), tile)
        d_a = dot(d_pre[rows, :width], wq[0], ((1,), (1,)))
        for kind in range(1, 3):
            d_a += dot(d_pre[rows, kind * width : (kind + 1) * width], wq[kind], ((1,), (1,)))
        d_m = d_normed[rows, :]
        unit, rstd = unit_rows(source[rows, :].astype(F32))
        sums[0:1, :] += jnp.sum(d_a * unit, axis=0, keepdims=True)
        sums[1:2, :] += jnp.sum(d_m * unit, axis=0, keepdims=True)
        sums[2:3, :] += jnp.sum(d_a, axis=0, keepdims=True)
        sums[3:4, :] += jnp.sum(d_m, axis=0, keepdims=True)
        joined = d_a * gain_a + d_m * gain_m
        total[rows, :] = joined
        low[rows, :] = joined.astype(BF)
        if also is not None:
            also(rows, joined, unit, rstd)


def unit_sums(d_pre, small, width):
    for index in range(d_pre.shape[1] // width):
        piece = d_pre[:, index * width : (index + 1) * width].astype(F32)
        small[12 + index : 13 + index, :] = jnp.sum(piece, axis=0, keepdims=True)


def across_tokens(left, right, out, heads=False, only=None):
    tile = min(256, left.shape[1])

    def at(index):
        cols = pl.ds(pl.multiple_of(index * tile, tile), tile)
        value = dot(left[:, cols], right[...], ((0,), (0,))).astype(BF)
        if heads:
            width = out.shape[2]
            for kind in range(3):
                out[kind, cols, :] = value[:, kind * width : (kind + 1) * width]
        else:
            out[cols, :] = value

    if only is None:
        pl.loop(0, left.shape[1] // tile)(at)
    else:
        at(only)


def across_blocks(grads, kind, left, right, out, heads, turns):
    for which in turns:
        across_tokens(left, right, out, heads, grads.block(which))
        grads.hand(kind, (which,))


FARTHEST_FIRST = (2, 0, 1, 3)


def out_gradient(attn_t, grad_full, out):
    tile = min(256, out.shape[1])
    for at in range(0, out.shape[1], tile):
        out[:, at : at + tile] = dot(attn_t[...], grad_full[:, at : at + tile]).astype(BF)


Q, F, O, PR = range(4)
DIRECT = (Q, O)


class Load:
    def __init__(self, source, target, sem):
        self.copy, self.waiting = pltpu.make_async_copy(source, target, sem), True

    def start(self):
        self.copy.start()

    def need(self):
        if self.waiting:
            self.copy.wait()
            self.waiting = False


def second_kernel(rows, cols, n):
    place = Place(rows, cols)
    s, c = place.s, place.c
    tokens, full = n.x1_full.shape
    width = full // cols
    length = tokens // PARTS
    size = QUERY_BLOCK
    own = pl.ds(pl.multiple_of(c * width, width), width)
    count = rows * PARTS
    qkv0 = n.qkvd1.at[: 3 * HEAD_DIM]
    hidden0, normed_m0, normed_a0, wq0 = n.hidden1, n.normed_m1, n.normed_a1, n.wq1
    x_full, branch1, unit0, d_normed0 = n.d_hidden1, n.d_normed1, n.scores, n.scores
    o_low = n.cot_full
    load_no = iter(range(LOADS))

    def loading(source, target):
        return Load(source, target, n.load.at[next(load_no)])

    l_qkvd1 = loading(n.i_qkvd1, n.qkvd1)
    l_cot = loading(n.i_cot_full, n.cot_full)
    l_d_hidden1 = loading(n.i_d_hidden1, n.d_hidden1)
    l_hidden1 = loading(n.i_hidden1, n.hidden1)
    l_x1 = loading(n.i_x1_full, n.x1_full)
    l_wq1 = loading(n.i_wq1, n.wq1)
    l_d_normed1 = loading(n.i_d_normed1, n.d_normed1)
    l_normed_m1 = loading(n.i_normed_m1, n.normed_m1)
    l_normed_a1 = loading(n.i_normed_a1, n.normed_a1)
    l_wo0 = loading(n.i_wo0, n.wo0)
    l_wp0 = loading(n.i_wp0, n.wp0)
    l_wf0 = loading(n.i_wf0, n.wf0)
    l_slope0 = loading(n.i_slope0, n.slope0)
    l_wo1 = loading(n.i_wo1, n.wo1)
    l_out0 = loading(n.i_out0, n.out0)
    l_log0 = loading(n.i_log0, n.log0)
    l_attn_t0 = loading(n.i_attn_t0, n.attn_t0)
    l_qkv0 = loading(n.i_qkv0, qkv0)
    l_hidden0 = loading(n.i_hidden0, hidden0)
    l_normed_m0 = loading(n.i_normed_m0, normed_m0)
    l_normed_a0 = loading(n.i_normed_a0, normed_a0)
    l_wq0 = loading(n.i_wq0, wq0)
    l_x0 = loading(n.i_x_full, x_full)
    l_branch1 = loading(n.i_branch1, branch1)

    def lane_of(lane):
        return slice(lane * length, (lane + 1) * length)

    def features(owner):
        return (slice(None), pl.ds(pl.multiple_of(owner * width, width), width))

    l_qkvd1.start()
    place.greet(rows=True, cols=True, partner=True, cross_rows=True)
    grads1 = GradExchange(place, 1, n, n.g1_s, n.g1_r)
    grads0 = GradExchange(place, 0, n, n.g0_s, n.g0_r)
    exchange1 = BlockExchange(place, n.result, n.inbox, size, n.b1_s, n.b1_r, n.b1_l)
    exchange0 = BlockExchange(
        place, n.result.at[: 3 * HEAD_DIM], n.inbox.at[:, : 3 * HEAD_DIM], size, n.b0_s, n.b0_r,
        n.b0_l,
    )
    outward = [
        RowExchange(
            place,
            lambda target, lane=lane: n.pieces.at[target, :, lane_of(lane)],
            lambda source, lane=lane: n.d_out.at[
                :, pl.ds(pl.multiple_of(source * tokens + lane * length, length), length)
            ],
            n.e_s.at[lane], n.e_r.at[lane], n.e_l.at[lane],
        )
        for lane in range(PARTS)
    ]
    out_sum = LineReduce(
        place, branch1, o_low, n.o_left, n.o_right, features, (n.o_a, n.o_b, n.o_c, n.o_d)
    )
    grad_sums = [
        LineReduce(
            place, n.total, n.low, n.from_left, n.from_right,
            lambda owner, lane=lane: (lane_of(lane), features(owner)[1]),
            (n.s_a, n.s_b, n.s_c, n.s_d), lane,
        )
        for lane in range(PARTS)
    ]

    prompt = segment_begins(n.lengths, s, n.first)
    rotary(n.lengths, s, place.r, n.cos, n.sin)
    l_qkvd1.need()
    for load in (
        l_cot, l_d_hidden1, l_hidden1, l_x1, l_wq1, l_d_normed1, l_normed_m1, l_normed_a1, l_wo0,
        l_wp0, l_wf0, l_slope0, l_wo1, l_out0, l_log0, l_attn_t0,
    ):
        load.start()
    qkvd = n.qkvd1
    rows_of_keys(qkvd, HEAD_DIM, n.key_rows)
    rows_of_keys(qkvd, 2 * HEAD_DIM, n.value_rows)
    d_out1 = qkvd.at[3 * HEAD_DIM :]

    def spot(key_at, keys):
        at = key_at // KEY_BLOCK * size
        return (slice(0, keys), slice(at, at + size))

    for block in reversed(range(count)):
        here = slice(block * size, (block + 1) * size)
        exact, top, weight = attend_block(
            block, size, prompt, n.first, qkvd, n.key_rows, n.scores, spot, True
        )
        delta = jnp.sum(d_out1[:, here].astype(F32) * exact, axis=0, keepdims=True)
        inverse = 1.0 / weight

        def probs_of(key_at, keys, query):
            return n.scores[spot(key_at, keys)] * inverse

        d_query = gradient_block(
            block, size, qkvd, d_out1, delta, probs_of, n.key_rows, n.value_rows, n.key_acc,
            n.value_acc, block == count - 1,
        )
        n.result[:HEAD_DIM, here] = exact.astype(BF)
        n.result[HEAD_DIM : 2 * HEAD_DIM, here] = d_query.astype(BF)
        n.result[2 * HEAD_DIM : 3 * HEAD_DIM, here] = n.key_acc[:, here].astype(BF)
        n.result[3 * HEAD_DIM :, here] = n.value_acc[:, here].astype(BF)
        exchange1.start(block)

    l_qkv0.start()
    n.sums[...] = jnp.zeros_like(n.sums)
    n.small[...] = jnp.zeros_like(n.small)
    l_cot.need()
    l_d_hidden1.need()
    l_hidden1.need()
    n.small[1, 11:12, :] = jnp.sum(n.cot_full[:, own].astype(F32), axis=0, keepdims=True)
    unit_sums(n.d_hidden1, n.small.at[1], width)
    across_tokens(n.hidden1, n.cot_full, n.mine_p)
    grads1.hand(PR)
    l_hidden0.start()
    for load in (l_x1, l_wq1, l_d_normed1):
        load.need()
    quarters = (2, 3, 0, 1)
    part = tokens // 4

    def prepare(turn_no):
        if turn_no % 2 == 0:
            lane = quarters[turn_no] // 2
            exchange1.arrive(lane)
            where = lane_of(lane)
            for head in range(rows):
                n.attn_t1[head * HEAD_DIM : (head + 1) * HEAD_DIM, where] = n.inbox[
                    head, :HEAD_DIM, where
                ]
            d_projection(n.inbox, HEAD_DIM, n.cos, n.sin, rows, n.d_pre, n.small.at[1], where)
        d_norms(
            n.x1_full, n.d_pre, n.wq1, n.d_normed1, n.vec_all[1, 0:1, :], n.vec_all[1, 1:2, :],
            n.total, n.low, n.sums.at[1], quarters[turn_no] * part, part,
        )

    def produce(summed, mine):
        unit, rstd = unit_rows(n.x1_full[mine, :].astype(F32))
        moved = (
            summed
            - jnp.mean(summed, axis=1, keepdims=True)
            - unit * jnp.mean(summed * unit, axis=1, keepdims=True)
        )
        return (n.cot_full[mine, :].astype(F32) + rstd * moved).astype(BF)

    def branches(lane):
        where = lane_of(lane)

        def times_slope(value, cols_here):
            return (value * n.slope0[where, cols_here]).astype(BF)

        times_tiles(n.grad_full, n.wp0, n.d_hidden0, times_slope, ((1,), (1,)), where)
        times_tiles(n.d_hidden0, n.wf0, d_normed0, None, ((1,), (1,)), where)

    def after(chunk):
        if (chunk + 1) % (CHUNKS // PARTS) == 0:
            lane = 1 - chunk // (CHUNKS // PARTS)
            where = lane_of(lane)
            l_wo0.need()
            flipped = dot(n.grad_full[where, :], n.wo0[...], ((1,), (1,))).T
            for head in range(rows):
                n.pieces[head, :, where] = flipped[
                    head * HEAD_DIM : (head + 1) * HEAD_DIM
                ].astype(BF)
            outward[lane].start()

    def work(time):
        if time == 0:
            l_normed_m1.need()
        if time < 4:
            across_blocks(
                grads1, F, n.normed_m1, n.d_hidden1, n.mine_f, False, FARTHEST_FIRST[time : time + 1]
            )
        if time == 3:
            l_normed_m0.start()
            l_x0.start()
        if time == 4:
            grads1.merge(PR)
        if time == 8:
            grads1.merge(F)
        if time == 9:
            grads1.pass_on(PR)
        if time == 11:
            l_normed_a1.need()
        if 11 <= time < 15:
            across_blocks(
                grads1, Q, n.normed_a1, n.d_pre, n.mine_q, True, FARTHEST_FIRST[time - 11 : time - 10]
            )
        if time == 12:
            grads1.pass_on(F)
        if time == 14:
            l_normed_a0.start()
            l_wq0.start()
            l_branch1.start()
        if time == 15:
            out_gradient(n.attn_t1, n.cot_full, n.mine_o)
            grads1.hand(O)
        if time == 17:
            grads1.merge(Q)
        if time == 22:
            grads1.merge(O)
        if time == 18:
            outward[1].arrive()
            exchange1.finish()
            l_qkv0.need()
            l_out0.need()
            l_log0.need()
            rows_of_keys(qkv0, HEAD_DIM, n.key_rows)
            rows_of_keys(qkv0, 2 * HEAD_DIM, n.value_rows)
        if 18 <= time < 18 + rows:
            attend_back((rows - 1 - (time - 18)) * PARTS + 1)

    def attend_back(block):
        here = slice(block * size, (block + 1) * size)
        delta = jnp.sum(n.d_out[:, here].astype(F32) * n.out0[:, here], axis=0, keepdims=True)
        log_row = n.log0[:, here]

        def weights_of(key_at, keys, query):
            return jnp.exp(
                score_block(prompt, n.first, here, block * size, key_at, keys, n.key_rows, query)
                - log_row
            )

        d_query = gradient_block(
            block, size, qkv0, n.d_out, delta, weights_of, n.key_rows, n.value_rows, n.key_acc,
            n.value_acc, block == count - 1,
        )
        n.result[:HEAD_DIM, here] = d_query.astype(BF)
        if block % PARTS == 0 or block == count - 1:
            for done in keys_done(block):
                there = slice(done * size, (done + 1) * size)
                n.result[HEAD_DIM : 2 * HEAD_DIM, there] = n.key_acc[:, there].astype(BF)
                n.result[2 * HEAD_DIM : 3 * HEAD_DIM, there] = n.value_acc[:, there].astype(BF)
                exchange0.start(done)

    def keys_done(block):
        return (block,) if block in (0, count - 1) else (block, block - 1)

    chunks = tuple(range(CHUNKS // 2, CHUNKS)) + tuple(range(CHUNKS // 2))
    center_sum(
        place, n.total, n.low, n.from_left, n.from_right, n.grad_full,
        (n.r_a, n.r_b, n.r_c, n.r_d, n.r_e, n.r_f), chunks, prepare, produce, after, work,
    )

    l_branch1.need()
    l_wo1.need()
    attn_rows = n.attn_t1[...].astype(F32).T.astype(BF)
    tile = min(256, full)
    for at in range(0, full, tile):
        value = branch1[:, at : at + tile] + dot(attn_rows, n.wo1[:, at : at + tile])
        branch1[:, at : at + tile] = value
        o_low[:, at : at + tile] = value.astype(BF)
    out_sum.step(0)
    grads1.take(PR, n.gw_p)
    grads1.finish(PR)
    l_hidden0.need()
    across_tokens(hidden0, n.grad_full, n.mine_p)
    grads0.hand(PR)
    outward[0].arrive()
    for block in reversed(range(0, count, PARTS)):
        attend_back(block)
        if block == count - 2:
            grads1.take(O, n.gw_o)
            grads1.finish(O)
            l_attn_t0.need()
            out_gradient(n.attn_t0, n.grad_full, n.mine_o)
            grads0.hand(O)
            out_sum.step(1)
        if block == count - 6:
            grads0.merge(PR)
    out_sum.step(2)
    for load in (l_wp0, l_wf0, l_slope0):
        load.need()
    branches(1)
    grads0.merge(O)
    grads0.pass_on(PR)
    branches(0)
    grads1.take(F, n.gw_f)
    grads1.finish(F)
    l_normed_m0.need()
    across_blocks(grads0, F, normed_m0, n.d_hidden0, n.mine_f, False, FARTHEST_FIRST)
    n.small[0, 11:12, :] = jnp.sum(n.grad_full[:, own].astype(F32), axis=0, keepdims=True)
    unit_sums(n.d_hidden0, n.small.at[0], width)
    out_own = n.x1_full[:, own].astype(F32) + out_sum.own() + n.vec_all[1, 7:8, own]
    n.o_own[1] = out_own.astype(BF)
    n.o_own[0] = n.x1_full[:, own]

    def swap_copy(index, source, target):
        return rcopy(
            source.at[1 - s], target.at[s], n.sw_s.at[index], n.sw_r.at[index], section=1 - s
        )

    out_swap = swap_copy(0, n.o_own, n.o_out_rows)
    out_swap.start()
    out_keep = pltpu.make_async_copy(n.o_own.at[s], n.o_out_rows.at[s], n.local.at[0])
    out_keep.start()

    l_x0.need()
    l_wq0.need()
    gain_a, gain_m = n.vec_all[0, 0:1, :], n.vec_all[0, 1:2, :]
    lane_no = lax.broadcasted_iota(jnp.int32, (min(128, length), 128), 1)

    def row_sums(where, joined, unit, rstd):
        first = jnp.sum(joined, axis=1, keepdims=True)
        second = jnp.sum(joined * unit, axis=1, keepdims=True)
        both = jnp.where(lane_no == 0, first, jnp.where(lane_no == 1, second, 0.0))
        n.line_sums[:, where] = both.T[:8]
        unit0[where, :] = unit
        n.rstd[where, :] = jnp.broadcast_to(rstd, (rstd.shape[0], 128))

    def prepare_last(lane):
        exchange0.arrive(lane)
        d_projection(n.inbox, 0, n.cos, n.sin, rows, n.d_pre, n.small.at[0], lane_of(lane))
        d_norms(
            x_full, n.d_pre, wq0, d_normed0, gain_a, gain_m, n.total, n.low, n.sums.at[0],
            lane * length, length, row_sums,
        )

    grads0.merge(F)
    prepare_last(1)
    grad_sums[1].step(0)
    prepare_last(0)
    grad_sums[0].step(0)
    grads0.pass_on(F)
    grad_sums[1].step(1)

    def line_copy(step):
        return rcopy(
            n.line_sums, n.line_in.at[step], n.ls_s.at[step], n.ls_r.at[step],
            col=place.col_to(step),
        )

    def col_copy(step):
        target = place.col_to(step)
        piece = n.sums.at[:, :, pl.ds(pl.multiple_of(target * width, width), width)]
        return rcopy(piece, n.col_in.at[step], n.cs_s.at[step], n.cs_r.at[step], col=target)

    def row_copy(ds, step):
        index = ds * rows + step
        layer = lax.rem(s + ds, 2)
        return rcopy(
            n.small.at[layer], n.row_in.at[index], n.rw_s.at[index], n.rw_r.at[index],
            section=layer, row=place.row_to(step),
        )

    for step in range(1, cols):
        line_copy(step).start()
        col_copy(step).start()
    grads1.take(Q, n.gw_q)
    grads1.finish(Q)
    l_normed_a0.need()
    across_blocks(grads0, Q, normed_a0, n.d_pre, n.mine_q, True, FARTHEST_FIRST)
    grad_sums[1].step(2)
    grad_sums[0].step(1)
    for step in range(1, cols):
        col_copy(step).wait_recv()
    head = n.sums[:, :, own]
    for step in range(1, cols):
        head = head + n.col_in[step]
    n.small[:, :8, :] = head
    others = [(ds, step) for ds in range(2) for step in range(rows) if ds or step]
    for ds, step in others:
        row_copy(ds, step).start()
    grads0.merge(Q)
    saves = Saver(n.save)

    def take(kind, made, target):
        grads0.take(kind, made)
        saves.copy(made, target)

    grad_sums[0].step(2)
    take(PR, n.gw_p, n.o_gw_p)
    take(O, n.gw_o, n.o_gw_o)
    joined = n.line_sums[...]
    for step in range(1, cols):
        line_copy(step).wait_recv()
        joined = joined + n.line_in[step]
    wide = jnp.concatenate([joined, jnp.zeros((120, tokens), F32)], axis=0).T
    take(F, n.gw_f, n.o_gw_f)
    out_keep.wait()
    out_swap.wait()
    for lane in reversed(range(PARTS)):
        where = lane_of(lane)
        moved = (
            grad_sums[lane].own()
            - wide[where, 0:1] / full
            - unit0[where, own] * (wide[where, 1:2] / full)
        )
        n.o_own[0, where] = (
            n.grad_full[where, own].astype(F32) + n.rstd[where, 0:1] * moved
        ).astype(BF)
    n.o_own[1] = n.grad_full[:, own]
    grad_swap = swap_copy(1, n.o_own, n.o_grad_rows)
    grad_swap.start()
    grad_keep = pltpu.make_async_copy(n.o_own.at[s], n.o_grad_rows.at[s], n.local.at[1])
    grad_keep.start()
    mine = n.small[s]
    for ds, step in others:
        row_copy(ds, step).wait_recv()
        mine = mine + n.row_in[ds * rows + step]
    n.o_small[...] = mine
    take(Q, n.gw_q, n.o_gw_q)
    grad_keep.wait()
    grad_swap.wait()
    exchange0.finish()
    for exchange in outward:
        exchange.finish()
    out_sum.finish()
    for reduce in grad_sums:
        reduce.finish()
    for step in range(1, cols):
        line_copy(step).wait_send()
        col_copy(step).wait_send()
    for ds, step in others:
        row_copy(ds, step).wait_send()
    for kind in range(4):
        grads0.finish(kind)
    saves.finish()


def second_half(rows, cols, kept, lengths):
    tokens, full = kept.x1_full.shape
    width, units = full // cols, kept.hidden1.shape[1]
    total = rows * tokens
    hbm, vmem, smem = pl.ANY, pltpu.VMEM, pltpu.SMEM
    loaded = dict(
        qkvd1=kept.qkvd1, cot_full=kept.cot_full, d_hidden1=kept.d_hidden1, hidden1=kept.hidden1,
        x1_full=kept.x1_full, wq1=kept.wq1, d_normed1=kept.d_normed1, normed_m1=kept.normed_m1,
        normed_a1=kept.normed_a1, wo0=kept.wo0, wp0=kept.wp0, wf0=kept.wf0, slope0=kept.slope0,
        wo1=kept.wo1, out0=kept.out0, log0=kept.log0, attn_t0=kept.attn_t0,
    )
    later = dict(
        qkv0=kept.qkv0, hidden0=kept.hidden0, normed_m0=kept.normed_m0, normed_a0=kept.normed_a0,
        wq0=kept.wq0, x_full=kept.x_full, branch1=kept.branch1,
    )
    ins = {"i_" + name: (value, hbm) for name, value in {**loaded, **later}.items()}
    ins.update(
        lengths=(lengths, smem), vec_all=(kept.vec_all, vmem)
    )
    rows_low, rows_wide = ((tokens, full), BF), ((tokens, full), F32)
    wholes, pieces = grad_shapes(rows, full, width, units)
    outs = dict(
        o_out_rows=((2, tokens, width), BF, vmem), o_grad_rows=((2, tokens, width), BF, vmem),
        o_small=((16, width), F32, vmem),
    )
    outs.update({"o_gw_" + kind: (pieces[kind], F32, hbm) for kind in "qfop"})
    scratch = {name: pltpu.VMEM(value.shape, value.dtype) for name, value in loaded.items()}
    scratch.update(grad_scratch(rows, full, width, units))
    scratch.update({"gw_" + kind: pltpu.VMEM(pieces[kind], F32) for kind in "qfop"})
    scratch.update(
        grad_full=pltpu.VMEM(*rows_low), attn_t1=pltpu.VMEM((width, tokens), BF),
        d_hidden0=pltpu.VMEM((tokens, units), BF), d_out=pltpu.VMEM((HEAD_DIM, total), BF),
        result=pltpu.VMEM((4 * HEAD_DIM, total), BF),
        inbox=pltpu.VMEM((rows, 4 * HEAD_DIM, tokens), BF),
        pieces=pltpu.VMEM((rows, HEAD_DIM, tokens), BF),
        d_pre=pltpu.VMEM((tokens, 3 * width), BF),
        total=pltpu.VMEM(*rows_wide), low=pltpu.VMEM(*rows_low),
        from_left=pltpu.VMEM(*rows_low), from_right=pltpu.VMEM(*rows_low),
        o_left=pltpu.VMEM(*rows_low), o_right=pltpu.VMEM(*rows_low),
        scores=pltpu.VMEM((KEY_BLOCK, total // KEY_BLOCK * QUERY_BLOCK), F32),
        first=pltpu.VMEM((1, total), jnp.int32),
        cos=pltpu.VMEM((ROT // 2, tokens), F32), sin=pltpu.VMEM((ROT // 2, tokens), F32),
        key_rows=pltpu.VMEM((total, HEAD_DIM), BF), value_rows=pltpu.VMEM((total, HEAD_DIM), BF),
        key_acc=pltpu.VMEM((HEAD_DIM, total), F32), value_acc=pltpu.VMEM((HEAD_DIM, total), F32),
        sums=pltpu.VMEM((2, 8, full), F32), small=pltpu.VMEM((2, 16, width), F32),
        rstd=pltpu.VMEM((tokens, 128), F32),
        line_sums=pltpu.VMEM((8, tokens), F32), line_in=pltpu.VMEM((cols, 8, tokens), F32),
        col_in=pltpu.VMEM((cols, 2, 8, width), F32),
        row_in=pltpu.VMEM((2 * rows, 16, width), F32),
        o_own=pltpu.VMEM((2, tokens, width), BF),
        load=dma(LOADS), save=dma(4), local=dma(2),
        g1_s=dma(4, 8), g1_r=dma(4, 8), g0_s=dma(4, 8), g0_r=dma(4, 8),
        b1_s=dma(rows * PARTS), b1_r=dma(PARTS, rows), b1_l=dma(PARTS),
        b0_s=dma(rows * PARTS), b0_r=dma(PARTS, rows), b0_l=dma(PARTS),
        e_s=dma(PARTS, rows), e_r=dma(PARTS, rows), e_l=dma(PARTS),
        ls_s=dma(cols), ls_r=dma(cols), cs_s=dma(cols), cs_r=dma(cols),
        rw_s=dma(2 * rows), rw_r=dma(2 * rows), sw_s=dma(2), sw_r=dma(2),
    )
    for name in ("r_a", "r_b", "r_c", "r_d", "r_e", "r_f"):
        scratch[name] = dma(CHUNKS)
    for name in ("s_a", "s_b", "s_c", "s_d"):
        scratch[name] = dma(PARTS, cols)
    for name in ("o_a", "o_b", "o_c", "o_d"):
        scratch[name] = dma(1, cols)
    return Names().joined(named_call(partial(second_kernel, rows, cols), 3, ins, outs, scratch))


def finishing_kernel(n):
    into, out_of = Saver(n.into), Saver(n.out_of)
    moves = [
        (into.copy(source, held), held, target)
        for source, held, target in (
            (n.i_gw_p, n.h_gw_p, n.gw_p), (n.i_gw_f, n.h_gw_f, n.gw_f), (n.i_gw_q, n.h_gw_q, n.gw_q),
            (n.i_out_rows, n.h_out_rows, n.out_rows), (n.i_grad_rows, n.h_grad_rows, n.grad_rows),
            (n.i_gw_o, n.h_gw_o, n.gw_o),
        )
    ]
    for copy, held, target in moves:
        copy.wait()
        out_of.copy(held, target.at[0])
    width = n.small.shape[1]
    n.gains[0] = n.small[0:2]
    n.shifts[0] = n.small[2:4]
    for index in range(3):
        n.g_qkv[:, index * width : (index + 1) * width] = n.small[8 + index : 9 + index]
    n.g_out[...] = n.small[11:12]
    for index in range(n.g_fc.shape[1] // width):
        n.g_fc[:, index * width : (index + 1) * width] = n.small[12 + index : 13 + index]
    out_of.finish()


def finishing(k):
    hbm, vmem = pl.ANY, pltpu.VMEM
    made = dict(
        out_rows=k.out_rows, grad_rows=k.grad_rows, gw_q=k.gw_q, gw_f=k.gw_f, gw_o=k.gw_o,
        gw_p=k.gw_p,
    )
    ins = {"i_" + name: (value, hbm) for name, value in made.items()}
    ins.update(small=(k.small, vmem))
    width, units = k.small.shape[1], k.gw_f.shape[1]
    large = {name: ((1,) + value.shape, value.dtype, hbm) for name, value in made.items()}
    outs = dict(
        out_rows=None, grad_rows=None, gains=((1, 2, width), F32, vmem),
        shifts=((1, 2, width), F32, vmem), gw_q=None, g_qkv=((1, 3 * width), F32, vmem),
        gw_o=None, gw_f=None, g_fc=((1, units), F32, vmem), gw_p=None,
        g_out=((1, width), F32, vmem),
    )
    outs.update(large)
    scratch = {"h_" + name: pltpu.VMEM(value.shape, value.dtype) for name, value in made.items()}
    scratch.update(into=dma(len(made)), out_of=dma(len(made)))
    results = named_call(finishing_kernel, None, ins, outs, scratch)
    results.update(g_qkv=results.pop("g_qkv").reshape(1, 3, width))
    return tuple(results[name] for name in outs)


def relay_body(
    hidden_in,
    cotangent,
    lengths,
    norm_gains,
    norm_biases,
    w_qkv,
    b_qkv,
    w_out,
    w_fc,
    b_fc,
    w_proj,
    b_out,
):
    rows, cols = lax.axis_size(ROW), lax.axis_size(COL)
    blocks = (w_qkv[0], w_fc[0], w_out[0], w_proj[0])
    vectors = (norm_gains, norm_biases, b_qkv.reshape(1, -1), b_out, b_fc)
    kept = first_half(rows, cols, hidden_in, cotangent, vectors, blocks, lengths)
    return finishing(second_half(rows, cols, kept, lengths))


def fits(mesh):
    rows, cols = mesh.shape[ROW], mesh.shape[COL]
    return rows == cols == 4 and MODEL_WIDTH == rows * cols * HEAD_DIM


def solution(mesh):
    return jax.shard_map(
        relay_body if fits(mesh) else body,
        mesh=mesh,
        in_specs=(
            P(None, ROW, COL),
            P(None, ROW, COL),
            P(),
            P(SECTION, None, COL),
            P(SECTION, None, COL),
            P(SECTION, None, ROW, COL),
            P(SECTION, None, COL),
            P(SECTION, COL, ROW),
            P(SECTION, ROW, COL),
            P(SECTION, COL),
            P(SECTION, COL, ROW),
            P(SECTION, COL),
        ),
        out_specs=(
            P(SECTION, None, ROW, COL),
            P(SECTION, None, ROW, COL),
            P(SECTION, None, COL),
            P(SECTION, None, COL),
            P(SECTION, None, ROW, COL),
            P(SECTION, None, COL),
            P(SECTION, COL, ROW),
            P(SECTION, ROW, COL),
            P(SECTION, COL),
            P(SECTION, COL, ROW),
            P(SECTION, COL),
        ),
        check_vma=False,
    )
```

```python
from functools import partial
import math

import jax
import jax.numpy as jnp
from jax import lax
from jax.experimental import pallas as pl
from jax.experimental.pallas import tpu as pltpu
from jax.sharding import PartitionSpec as P

MODEL_WIDTH = 1024
HEAD_DIM = 64
ROT = 16
SECTION, ROW, COL = "section", "row", "col"


EPS = 1e-05
NEG = -1e30


def from_partner(value, axis, apart):
    mask = 2**apart
    pairs = [(source, source ^ mask) for source in range(lax.axis_size(axis))]
    return lax.ppermute(value, axis, pairs)


def segment_of(token_ids, starts):
    return jnp.sum((token_ids[:, None] >= starts[None, 1:]).astype(jnp.int32), axis=1)


def token_layout(lengths_row, token_ids):
    starts = jnp.cumsum(lengths_row) - lengths_row
    segment = segment_of(token_ids, starts)
    labels = jnp.arange(1, lengths_row.shape[0], dtype=jnp.int32)
    seg_begin = jnp.sum(jnp.where(segment[:, None] == labels[None, :], starts[None, 1:], 0), axis=1)
    position = jnp.where(segment == 0, token_ids, lengths_row[0] + token_ids - seg_begin)
    return (starts, segment, position)


def rotary_tables(position, turned):
    half_rot = turned // 2
    freqs = 10000.0 ** (-(2.0 * jnp.arange(half_rot, dtype=jnp.float32)) / turned)
    angles = position.astype(jnp.float32)[:, None] * freqs[None, :]
    return (jnp.cos(angles), jnp.sin(angles))


def rotate(values, cos_table, sin_table, direction):
    half_rot = cos_table.shape[-1]
    lower = values[..., :half_rot]
    upper = values[..., half_rot : 2 * half_rot]
    cos_cast = cos_table[:, None, :]
    sin_cast = direction * sin_table[:, None, :]
    return jnp.concatenate(
        [
            lower * cos_cast - upper * sin_cast,
            upper * cos_cast + lower * sin_cast,
            values[..., 2 * half_rot :],
        ],
        axis=-1,
    )


def permitted(query_seg, query_tok, key_seg, key_tok):
    from_prompt = (key_seg[None, :] == 0) & (query_seg[:, None] > 0)
    same_causal = (key_seg[None, :] == query_seg[:, None]) & (
        key_tok[None, :] <= query_tok[:, None]
    )
    return from_prompt | same_causal


def attend(running, key_piece, value_piece, query3, layout):
    run_max, run_sum, totals = running
    piece_len = key_piece.shape[0]
    key3 = key_piece.reshape(piece_len, query3.shape[1], query3.shape[2])
    value3 = value_piece.reshape(piece_len, query3.shape[1], query3.shape[2])
    key_tok = jnp.arange(piece_len, dtype=jnp.int32)
    key_seg = segment_of(key_tok, layout["starts"])
    allowed = permitted(layout["segment"], layout["tokens"], key_seg, key_tok)[None]
    scores = jnp.einsum("qhd,khd->hqk", query3, key3, preferred_element_type=jnp.float32) * (
        1.0 / math.sqrt(query3.shape[2])
    )
    masked = jnp.where(allowed, scores, NEG)
    new_max = jnp.maximum(run_max, jnp.max(masked, axis=-1))
    weights = jnp.where(allowed, jnp.exp(masked - new_max[..., None]), 0.0)
    run_sum = jnp.sum(weights, axis=-1)
    totals = jnp.einsum(
        "hqk,khd->hqd", weights.astype(jnp.bfloat16), value3, preferred_element_type=jnp.float32
    )
    return (new_max, run_sum, totals)


def layer_forward(x, full, weights, layout, complete_gains, complete_shifts):
    w_query, b_query, w_output, w_hidden, b_hidden, w_project, b_output = weights
    row_tokens, local_width = x.shape
    heads_local = local_width // HEAD_DIM
    shaped = (row_tokens, heads_local, HEAD_DIM)
    as_float = full.astype(jnp.float32)
    row_mean = jnp.mean(as_float, axis=1, keepdims=True)
    centred = as_float - row_mean
    rstd = lax.rsqrt(jnp.mean(centred * centred, axis=1, keepdims=True) + EPS)
    unit = centred * rstd
    normed_a = (unit * complete_gains[0] + complete_shifts[0]).astype(jnp.bfloat16)
    normed_m = (unit * complete_gains[1] + complete_shifts[1]).astype(jnp.bfloat16)
    projected = (
        jnp.einsum("td,cde->cte", normed_a, w_query, preferred_element_type=jnp.float32)
        + b_query[:, None, :]
    )
    cos_table, sin_table = layout["cos_table"], layout["sin_table"]
    query3 = rotate(projected[0].reshape(shaped), cos_table, sin_table, 1.0).astype(jnp.bfloat16)
    key_flat = (
        rotate(projected[1].reshape(shaped), cos_table, sin_table, 1.0)
        .reshape(row_tokens, local_width)
        .astype(jnp.bfloat16)
    )
    value_flat = projected[2].astype(jnp.bfloat16)
    key_full = lax.all_gather(key_flat, ROW, axis=0, tiled=True)
    value_full = lax.all_gather(value_flat, ROW, axis=0, tiled=True)
    initial = (
        jnp.full((heads_local, row_tokens), NEG, jnp.float32),
        jnp.zeros((heads_local, row_tokens), jnp.float32),
        jnp.zeros((heads_local, row_tokens, HEAD_DIM), jnp.float32),
    )
    run_max, run_sum, totals = attend(initial, key_full, value_full, query3, layout)
    out_exact = totals / run_sum[..., None]
    log_sum = run_max + jnp.log(run_sum)
    attn_flat = (
        jnp.transpose(out_exact, (1, 0, 2)).reshape(row_tokens, local_width).astype(jnp.bfloat16)
    )
    hidden_pre = jnp.dot(normed_m, w_hidden, preferred_element_type=jnp.float32) + b_hidden
    hidden = jax.nn.gelu(hidden_pre, approximate=False).astype(jnp.bfloat16)
    branch = jnp.dot(attn_flat, w_output, preferred_element_type=jnp.float32) + jnp.dot(
        hidden, w_project, preferred_element_type=jnp.float32
    )
    summed = lax.psum_scatter(
        branch.astype(jnp.bfloat16), COL, scatter_dimension=1, tiled=True
    ).astype(jnp.float32)
    output = (x.astype(jnp.float32) + summed + b_output).astype(jnp.bfloat16)
    state = dict(
        unit=unit, rstd=rstd, normed_a=normed_a, normed_m=normed_m, query3=query3,
        key_full=key_full, value_full=value_full, attn_flat=attn_flat, out_exact=out_exact,
        log_sum=log_sum, hidden_pre=hidden_pre, hidden=hidden,
    )
    return output, state


def layer_backward(state, grad_in, grad_full, weights, layout, complete_gains, scatter_tokens):
    w_query, b_query, w_output, w_hidden, b_hidden, w_project, b_output = weights
    row_tokens = state["normed_a"].shape[0]
    local_width = w_output.shape[0]
    heads_local = local_width // HEAD_DIM
    shaped = (row_tokens, heads_local, HEAD_DIM)
    score_scale = 1.0 / math.sqrt(HEAD_DIM)
    total_tokens = state["key_full"].shape[0]
    key_block = min(512, total_tokens)
    grad_wout = jnp.einsum(
        "te,td->ed", state["attn_flat"], grad_full, preferred_element_type=jnp.float32
    )
    grad_wproj = jnp.einsum(
        "tf,td->fd", state["hidden"], grad_full, preferred_element_type=jnp.float32
    )
    grad_bout = jnp.sum(grad_in.astype(jnp.float32), axis=0)
    grad_attn = jnp.einsum(
        "td,ed->te", grad_full, w_output, preferred_element_type=jnp.float32
    ).astype(jnp.bfloat16)
    grad_hidden = jnp.einsum("td,fd->tf", grad_full, w_project, preferred_element_type=jnp.float32)
    gelu_value, gelu_back = jax.vjp(partial(jax.nn.gelu, approximate=False), state["hidden_pre"])
    grad_hpre = gelu_back(grad_hidden)[0].astype(jnp.bfloat16)
    grad_wfc = jnp.einsum(
        "td,tf->df", state["normed_m"], grad_hpre, preferred_element_type=jnp.float32
    )
    grad_bfc = jnp.sum(grad_hpre.astype(jnp.float32), axis=0)
    grad_normed_m = jnp.einsum("tf,df->td", grad_hpre, w_hidden, preferred_element_type=jnp.float32)
    grad_out3 = grad_attn.reshape(shaped)
    query3 = state["query3"]
    delta = jnp.sum(
        jnp.transpose(grad_out3.astype(jnp.float32), (1, 0, 2)) * state["out_exact"], axis=-1
    )
    grad_query = jnp.zeros(shaped, jnp.float32)
    key_terms = []
    value_terms = []
    for block_no in range(total_tokens // key_block):
        begin_at = block_no * key_block
        key_part = state["key_full"][begin_at : begin_at + key_block].reshape(
            key_block, heads_local, HEAD_DIM
        )
        value_part = state["value_full"][begin_at : begin_at + key_block].reshape(
            key_block, heads_local, HEAD_DIM
        )
        key_tok = begin_at + jnp.arange(key_block, dtype=jnp.int32)
        key_seg = segment_of(key_tok, layout["starts"])
        allowed = permitted(layout["segment"], layout["tokens"], key_seg, key_tok)[None]
        scores = (
            jnp.einsum("qhd,khd->hqk", query3, key_part, preferred_element_type=jnp.float32)
            * score_scale
        )
        probs = jnp.where(
            allowed,
            jnp.exp(jnp.where(allowed, scores, NEG) - state["log_sum"][..., None]),
            0.0,
        )
        grad_probs = jnp.einsum(
            "qhd,khd->hqk", grad_out3, value_part, preferred_element_type=jnp.float32
        )
        grad_scores = (probs * (grad_probs - delta[..., None])).astype(jnp.bfloat16)
        grad_query = grad_query + jnp.einsum(
            "hqk,khd->qhd", grad_scores, key_part, preferred_element_type=jnp.float32
        )
        key_terms.append(
            jnp.einsum(
                "hqk,qhd->khd", grad_scores, query3, preferred_element_type=jnp.float32
            ).reshape(key_block, local_width)
            * score_scale
        )
        value_terms.append(
            jnp.einsum(
                "hqk,qhd->khd",
                probs.astype(jnp.bfloat16),
                grad_out3,
                preferred_element_type=jnp.float32,
            ).reshape(key_block, local_width)
        )
    grad_query = grad_query * score_scale
    kv_terms = jnp.concatenate(
        [jnp.concatenate(key_terms, axis=0), jnp.concatenate(value_terms, axis=0)], axis=1
    )
    kv_grads = lax.psum_scatter(
        kv_terms.astype(jnp.bfloat16), ROW, scatter_dimension=0, tiled=True
    ).astype(jnp.float32)
    grad_key = kv_grads[:, :local_width].reshape(shaped)
    grad_value = kv_grads[:, local_width:]
    cos_table, sin_table = layout["cos_table"], layout["sin_table"]
    grad_pre = jnp.stack(
        [
            rotate(grad_query, cos_table, sin_table, -1.0).reshape(row_tokens, local_width),
            rotate(grad_key, cos_table, sin_table, -1.0).reshape(row_tokens, local_width),
            grad_value,
        ]
    ).astype(jnp.bfloat16)
    grad_wqkv = jnp.einsum(
        "td,cte->cde", state["normed_a"], grad_pre, preferred_element_type=jnp.float32
    )
    grad_bqkv = jnp.sum(grad_pre.astype(jnp.float32), axis=1)
    grad_normed_a = jnp.einsum("cte,cde->td", grad_pre, w_query, preferred_element_type=jnp.float32)
    unit = state["unit"]
    grad_gains = jnp.stack(
        [jnp.sum(grad_normed_a * unit, axis=0), jnp.sum(grad_normed_m * unit, axis=0)]
    )
    grad_shifts = jnp.stack([jnp.sum(grad_normed_a, axis=0), jnp.sum(grad_normed_m, axis=0)])
    grad_unit = grad_normed_a * complete_gains[0] + grad_normed_m * complete_gains[1]
    big = (grad_wqkv, grad_wout, grad_wfc, grad_wproj)
    big = tuple(member.astype(jnp.bfloat16) for member in big)
    shared = (grad_gains, grad_shifts)
    local = (grad_bqkv, grad_bfc, grad_bout)
    if scatter_tokens:
        piece = lax.psum_scatter(
            grad_unit.astype(jnp.bfloat16), COL, scatter_dimension=0, tiled=True
        ).astype(jnp.float32)
        rows = piece.shape[0]
        start = lax.axis_index(COL) * rows
        unit_part = lax.dynamic_slice_in_dim(unit, start, rows, 0)
        rstd_part = lax.dynamic_slice_in_dim(state["rstd"], start, rows, 0)
        grad_part = lax.dynamic_slice_in_dim(grad_full, start, rows, 0).astype(jnp.float32)
        moved = (
            piece
            - jnp.mean(piece, axis=1, keepdims=True)
            - unit_part * jnp.mean(piece * unit_part, axis=1, keepdims=True)
        )
        grad_input = (grad_part + rstd_part * moved).astype(jnp.bfloat16)
    else:
        sums = lax.psum(
            jnp.stack([jnp.sum(grad_unit, axis=1), jnp.sum(grad_unit * unit, axis=1)]), COL
        )
        piece = lax.psum_scatter(
            grad_unit.astype(jnp.bfloat16), COL, scatter_dimension=1, tiled=True
        ).astype(jnp.float32)
        width = piece.shape[1]
        unit_part = lax.dynamic_slice_in_dim(unit, lax.axis_index(COL) * width, width, 1)
        moved = (
            piece
            - sums[0][:, None] / MODEL_WIDTH
            - unit_part * (sums[1][:, None] / MODEL_WIDTH)
        )
        grad_input = (grad_in.astype(jnp.float32) + state["rstd"] * moved).astype(jnp.bfloat16)
    return grad_input, big, shared, local


def body(
    hidden_in,
    cotangent,
    lengths,
    norm_gains,
    norm_biases,
    w_qkv,
    b_qkv,
    w_out,
    w_fc,
    b_fc,
    w_proj,
    b_out,
):
    row_tokens = hidden_in.shape[1]
    local_width = hidden_in.shape[2]
    section = lax.axis_index(SECTION)
    is_first = section == 0
    my_tokens = lax.axis_index(ROW) * row_tokens + jnp.arange(row_tokens, dtype=jnp.int32)
    x0 = lax.dynamic_index_in_dim(hidden_in, section, 0, keepdims=False)
    cot = lax.dynamic_index_in_dim(cotangent, section, 0, keepdims=False)
    lengths_row = lax.dynamic_index_in_dim(lengths, section, 0, keepdims=False)
    starts, segment, position = token_layout(lengths_row, my_tokens)
    cos_table, sin_table = rotary_tables(position, ROT)
    layout = {
        "starts": starts,
        "segment": segment,
        "tokens": my_tokens,
        "cos_table": cos_table,
        "sin_table": sin_table,
    }
    both = (SECTION, ROW)
    gains = lax.all_gather(norm_gains[0], (SECTION, COL), axis=0)
    shifts = lax.all_gather(norm_biases[0], (SECTION, COL), axis=0)
    cols = lax.axis_size(COL)

    def whole(vectors):
        split = vectors.reshape(2, cols, 2, local_width)
        return jnp.transpose(split, (0, 2, 1, 3)).reshape(2, 2, cols * local_width)

    gains, shifts = whole(gains), whole(shifts)
    biases = [lax.all_gather(member[0], SECTION, axis=0) for member in (b_qkv, b_fc, b_out)]
    x0_full = lax.all_gather(x0, COL, axis=1, tiled=True)
    rows = lax.axis_size(ROW)

    def unite(member, axis):
        gathered = lax.all_gather(member[0], both, axis=0)
        pieces = gathered.reshape((2, rows) + gathered.shape[1:])
        return [
            jnp.concatenate([pieces[layer, row] for row in range(rows)], axis=axis)
            for layer in range(2)
        ]

    w_query, w_hidden = unite(w_qkv, 1), unite(w_fc, 0)
    w_output, w_project = unite(w_out, 1), unite(w_proj, 1)
    weights = [
        (
            w_query[layer],
            biases[0][layer],
            w_output[layer],
            w_hidden[layer],
            biases[1][layer],
            w_project[layer],
            biases[2][layer],
        )
        for layer in range(2)
    ]
    out0, state0 = layer_forward(x0, x0_full, weights[0], layout, gains[0], shifts[0])
    x1_full = lax.all_gather(out0, COL, axis=1, tiled=True)
    cot_full = lax.all_gather(cot, COL, axis=1, tiled=True)
    out1, state1 = layer_forward(out0, x1_full, weights[1], layout, gains[1], shifts[1])
    grad1_part, big1, shared1, local1 = layer_backward(
        state1, cot, cot_full, weights[1], layout, gains[1], True
    )
    grad1_full = lax.all_gather(grad1_part, COL, axis=0, tiled=True)
    grad1 = lax.dynamic_slice_in_dim(
        grad1_full, lax.axis_index(COL) * local_width, local_width, 1
    )
    grad0, big0, shared0, local0 = layer_backward(
        state0, grad1, grad1_full, weights[0], layout, gains[0], False
    )

    def swap(first, second):
        mine = jnp.where(is_first, first, second)
        theirs = from_partner(jnp.where(is_first, second, first), SECTION, 0)
        return jnp.where(is_first, jnp.stack([mine, theirs]), jnp.stack([theirs, mine]))[None]

    out_rows = swap(out0, out1)
    grad_rows = swap(grad0, grad1)

    def scatter(first, second, axis):
        length = first.shape[axis] // rows
        pieces = jnp.stack(
            [
                lax.slice_in_dim(member, row * length, (row + 1) * length, axis=axis)
                for member in (first, second)
                for row in range(rows)
            ]
        )
        return lax.psum_scatter(pieces, both, scatter_dimension=0, tiled=True).astype(jnp.float32)

    large = [scatter(a, b, axis) for a, b, axis in zip(big0, big1, (1, 1, 0, 1))]
    shared_sums = lax.psum(
        tuple(jnp.stack([a, b]) for a, b in zip(shared0, shared1)), (SECTION, ROW, COL)
    )
    shared_mine = [
        lax.dynamic_slice(
            member,
            (section, 0, lax.axis_index(COL) * local_width),
            (1, 2, local_width),
        )
        for member in shared_sums
    ]
    local_sums = lax.psum(tuple(jnp.stack([a, b]) for a, b in zip(local0, local1)), both)
    local_mine = [lax.dynamic_index_in_dim(member, section, 0) for member in local_sums]
    return (
        out_rows,
        grad_rows,
        shared_mine[0],
        shared_mine[1],
        large[0],
        local_mine[0],
        large[1],
        large[2],
        local_mine[1],
        large[3],
        local_mine[2],
    )


BF = jnp.bfloat16
F32 = jnp.float32
BY_MESH = pl.DeviceIdType.MESH
VMEM_LIMIT = 62 * 2**20
QUERY_BLOCK = 256
KEY_BLOCK = 512
PROMPT_LEAST = 768
PARTS = 2
CHUNKS = 16
LOADS = 24
LAG = 4


def dot(a, b, contract=((1,), (0,))):
    return lax.dot_general(a, b, (contract, ((), ())), preferred_element_type=F32)


def rcopy(src, dst, ssem, rsem, **device):
    return pltpu.make_async_remote_copy(
        src_ref=src,
        dst_ref=dst,
        send_sem=ssem,
        recv_sem=rsem,
        device_id=device,
        device_id_type=BY_MESH,
    )


class Place:
    def __init__(self, rows, cols):
        self.rows, self.cols = rows, cols
        self.s = lax.axis_index(SECTION)
        self.r = lax.axis_index(ROW)
        self.c = lax.axis_index(COL)

    def row_to(self, step):
        return lax.rem(self.r + step, self.rows)

    def row_from(self, step):
        return lax.rem(self.r + self.rows - step, self.rows)

    def beside(self, way):
        if way == 0:
            return self.r + 1 - 2 * lax.rem(self.r, 2)
        return lax.rem(self.r + 2, 4)

    def across(self):
        return 3 - self.r

    def col_to(self, step):
        return lax.rem(self.c + step, self.cols)

    def col_from(self, step):
        return lax.rem(self.c + self.cols - step, self.cols)

    def greet(self, rows=False, cols=False, partner=False, cross_cols=False, cross_rows=False):
        barrier = pltpu.get_barrier_semaphore()
        count = 0

        def signal(**device):
            pl.semaphore_signal(barrier, inc=1, device_id=device, device_id_type=BY_MESH)

        if rows:
            for step in range(1, self.rows):
                signal(row=self.row_to(step))
                count += 1
        if cols:
            for step in range(1, self.cols):
                signal(col=self.col_to(step))
                count += 1
        if partner:
            signal(section=1 - self.s)
            count += 1
        if cross_cols:
            for step in range(1, self.cols):
                signal(section=1 - self.s, col=self.col_to(step))
                count += 1
        if cross_rows:
            for step in range(1, self.rows):
                signal(section=1 - self.s, row=self.row_to(step))
                count += 1
        pl.semaphore_wait(barrier, count)


class LineGather:
    def __init__(self, place, view, send_right, send_left, recv, lane=0):
        self.place, self.view, self.lane = place, view, lane
        self.send_right, self.send_left, self.recv = send_right, send_left, recv

    def right(self, block):
        return rcopy(
            self.view(block), self.view(block), self.send_right.at[self.lane, block],
            self.recv.at[self.lane, block],
            col=lax.rem(self.place.c + 1, self.place.cols),
        )

    def left(self, block):
        cols = self.place.cols
        return rcopy(
            self.view(block), self.view(block), self.send_left.at[self.lane, block],
            self.recv.at[self.lane, block],
            col=lax.rem(self.place.c + cols - 1, cols),
        )

    def hop(self, distance):
        c, cols = self.place.c, self.place.cols

        @pl.when(c >= distance)
        def _():
            block = lax.rem(c + cols - distance, cols)
            if distance:
                self.right(block).wait_recv()

            @pl.when(c < cols - 1)
            def _():
                self.right(block).start()

        @pl.when(c + distance < cols)
        def _():
            block = lax.rem(c + distance, cols)
            if distance:
                self.left(block).wait_recv()

            @pl.when(c > 0)
            def _():
                self.left(block).start()

    def finish(self):
        c, cols = self.place.c, self.place.cols
        for distance in range(cols):

            @pl.when((c >= distance) & (c < cols - 1))
            def _():
                self.right(lax.rem(c + cols - distance, cols)).wait_send()

            @pl.when((c + distance < cols) & (c > 0))
            def _():
                self.left(lax.rem(c + distance, cols)).wait_send()


class WeightGather:
    def __init__(self, place, layer, own, full, send, recv, local):
        self.place, self.layer, self.own, self.full = place, layer, own, full
        self.send, self.recv, self.local = send, recv, local

    def view(self, kind, block, half=None):
        lines = self.own[kind].shape[-2]
        length = self.own[kind].shape[-2 if kind in (0, 1) else -1]
        at, count = (0, lines) if half is None else (half * (lines // 2), lines // 2)
        if kind in (0, 1):
            piece = pl.ds(pl.multiple_of(block * length + at, count), count)
            return self.full[kind].at[:, piece, :] if kind == 0 else self.full[1].at[piece, :]
        piece = pl.ds(pl.multiple_of(block * length, length), length)
        return self.full[kind].at[at : at + count, piece]

    def direct(self, kind, way):
        place = self.place
        return rcopy(
            self.own[kind], self.view(kind, place.r), self.send.at[kind, way],
            self.recv.at[kind, way], row=place.beside(way),
        )

    def relayed(self, kind, way):
        place = self.place
        piece = self.view(kind, place.beside(way), way)
        return rcopy(
            piece, piece, self.send.at[kind, 2 + way], self.recv.at[kind, 2 + way],
            row=place.beside(1 - way),
        )

    def arriving(self, kind, way):
        block = self.view(kind, self.place.beside(way))
        return rcopy(
            block, block, self.send.at[kind, way], self.recv.at[kind, way],
            row=self.place.beside(way),
        )

    def across(self, kind, way):
        piece = self.view(kind, self.place.across(), way)
        return rcopy(
            piece, piece, self.send.at[kind, 2 + way], self.recv.at[kind, 2 + way],
            row=self.place.beside(1 - way),
        )

    def to_partner(self, kind, which):
        place = self.place
        source = (place.beside(0), place.beside(1), place.across(), place.r)[which]
        block = self.view(kind, source)
        return rcopy(
            self.own[kind] if which == 3 else block, block, self.send.at[kind, 4 + which],
            self.recv.at[kind, 4 + which], section=1 - place.s,
        )

    def keep(self, kind):
        return pltpu.make_async_copy(
            self.own[kind], self.view(kind, self.place.r), self.local.at[kind]
        )

    def start(self, kind):
        @pl.when(self.place.s == self.layer)
        def _():
            for way in range(2):
                self.direct(kind, way).start()
            self.keep(kind).start()
            self.to_partner(kind, 3).start()

    def relay(self, kind):
        @pl.when(self.place.s == self.layer)
        def _():
            for way in range(2):
                self.arriving(kind, way).wait_recv()
                self.relayed(kind, way).start()
                self.to_partner(kind, way).start()

    def forward(self, kind):
        @pl.when(self.place.s == self.layer)
        def _():
            for way in range(2):
                self.across(kind, way).wait_recv()
            self.to_partner(kind, 2).start()
            self.keep(kind).wait()

    def ready(self, kind):
        @pl.when(self.place.s != self.layer)
        def _():
            for which in range(4):
                self.to_partner(kind, which).wait_recv()

    def finish(self, kind):
        @pl.when(self.place.s == self.layer)
        def _():
            for way in range(2):
                self.direct(kind, way).wait_send()
                self.relayed(kind, way).wait_send()
            for which in range(4):
                self.to_partner(kind, which).wait_send()


class RowExchange:
    def __init__(self, place, piece_for, slot_of, send, recv, local):
        self.place, self.piece_for, self.slot_of = place, piece_for, slot_of
        self.send, self.recv, self.local = send, recv, local

    def out(self, step):
        place = self.place
        target = place.row_to(step)
        return rcopy(
            self.piece_for(target), self.slot_of(place.r), self.send.at[step], self.recv.at[step],
            row=target,
        )

    def into(self, step):
        slot = self.slot_of(self.place.row_from(step))
        return rcopy(
            slot, slot, self.send.at[step], self.recv.at[step], row=self.place.row_to(step)
        )

    def keep(self):
        return pltpu.make_async_copy(
            self.piece_for(self.place.r), self.slot_of(self.place.r), self.local
        )

    def start(self):
        for step in range(1, self.place.rows):
            self.out(step).start()
        self.keep().start()

    def arrive(self):
        for step in range(1, self.place.rows):
            self.into(step).wait_recv()
        self.keep().wait()

    def finish(self):
        for step in range(1, self.place.rows):
            self.out(step).wait_send()


def norm_rows(source, gains_a, shifts_a, gains_m, shifts_m, normed_a, normed_m, begin=0, count=None):
    count = source.shape[0] if count is None else count
    tile = min(128, count)

    @pl.loop(0, count // tile)
    def _(index):
        rows = pl.ds(pl.multiple_of(begin + index * tile, tile), tile)
        values = source[rows, :].astype(F32)
        centred = values - jnp.mean(values, axis=1, keepdims=True)
        unit = centred * lax.rsqrt(jnp.mean(centred * centred, axis=1, keepdims=True) + EPS)
        normed_a[rows, :] = (unit * gains_a + shifts_a).astype(BF)
        normed_m[rows, :] = (unit * gains_m + shifts_m).astype(BF)


def turn(block, cos, sin, direction):
    half = cos.shape[0]
    lower, upper, rest = block[:half], block[half : 2 * half], block[2 * half :]
    return jnp.concatenate(
        [
            lower * cos - upper * (direction * sin),
            upper * cos + lower * (direction * sin),
            rest,
        ],
        axis=0,
    )


def project_heads(normed_a, w_query, bias_rows, cos, sin, pieces, heads, where):
    for kind in range(3):
        flipped = (dot(normed_a[where, :], w_query[kind]) + bias_rows(kind)).T
        for head in range(heads):
            block = flipped[head * HEAD_DIM : (head + 1) * HEAD_DIM]
            if kind < 2:
                block = turn(block, cos[:, where], sin[:, where], 1.0)
            pieces[head, kind * HEAD_DIM : (kind + 1) * HEAD_DIM, where] = block.astype(BF)


def feed_forward(normed_m, w_hidden, bias_of, hidden, slope, where):
    tile = min(256, w_hidden.shape[1])

    @pl.loop(0, w_hidden.shape[1] // tile)
    def _(index):
        cols = pl.ds(pl.multiple_of(index * tile, tile), tile)
        pre = dot(normed_m[where, :], w_hidden[:, cols]) + bias_of(index)
        phi = 0.5 * (1.0 + lax.erf(pre * math.sqrt(0.5)))
        hidden[where, cols] = (pre * phi).astype(BF)
        turned = phi + pre * (jnp.exp(-0.5 * pre * pre) * (1.0 / math.sqrt(2.0 * math.pi)))
        slope[where, cols] = turned.astype(slope.dtype)


def times_tiles(left, right, out, convert=None, contract=((1,), (0,)), where=slice(None)):
    tile = min(256, out.shape[1])

    @pl.loop(0, out.shape[1] // tile)
    def _(index):
        cols = pl.ds(pl.multiple_of(index * tile, tile), tile)
        piece = right[:, cols] if contract[1] == (0,) else right[cols, :]
        value = dot(left[where, :], piece, contract)
        out[where, cols] = value if convert is None else convert(value, cols)


def dma(*shape):
    return pltpu.SemaphoreType.DMA(shape)


def key_mask(prompt, first, cols, key_at, query_at, keys, queries):
    in_prompt = key_at + keys <= PROMPT_LEAST
    before = key_at + keys <= query_at + 1
    if in_prompt and before:
        return None
    key = lax.broadcasted_iota(jnp.int32, (keys, queries), 0) + key_at
    allowed = None
    if not in_prompt:
        allowed = (key < prompt) | (key >= first[:, cols])
    if not before:
        causal = key <= lax.broadcasted_iota(jnp.int32, (keys, queries), 1) + query_at
        allowed = causal if allowed is None else allowed & causal
    return allowed


def rows_of_keys(qkv, at, rows):
    rows[...] = qkv[at : at + HEAD_DIM, :].astype(F32).T.astype(BF)


def key_blocks(query_at, queries):
    last = query_at + queries
    return [(at, min(KEY_BLOCK, last - at)) for at in range(0, last, KEY_BLOCK)]


def scaled_query(qkv, cols):
    return (qkv[:HEAD_DIM, cols].astype(F32) * (1.0 / math.sqrt(HEAD_DIM))).astype(BF)


def score_block(prompt, first, cols, query_at, key_at, keys, key_rows, query):
    scores = dot(key_rows[key_at : key_at + keys, :], query)
    allowed = key_mask(prompt, first, cols, key_at, query_at, keys, query.shape[1])
    return scores if allowed is None else jnp.where(allowed, scores, NEG)


def attend_block(block, size, prompt, first, qkv, key_rows, scores, spot, keep_weights=False):
    query_at = block * size
    cols = slice(query_at, query_at + size)
    query = scaled_query(qkv, cols)
    blocks = key_blocks(query_at, size)
    top = None
    for key_at, keys in blocks:
        piece = score_block(prompt, first, cols, query_at, key_at, keys, key_rows, query)
        scores[spot(key_at, keys)] = piece
        highest = jnp.max(piece, axis=0, keepdims=True)
        top = highest if top is None else jnp.maximum(top, highest)
    weight, totals = None, None
    for key_at, keys in blocks:
        probs = jnp.exp(scores[spot(key_at, keys)] - top)
        if keep_weights:
            scores[spot(key_at, keys)] = probs
        part = jnp.sum(probs, axis=0, keepdims=True)
        product = dot(qkv[2 * HEAD_DIM : 3 * HEAD_DIM, key_at : key_at + keys], probs.astype(BF))
        weight = part if weight is None else weight + part
        totals = product if totals is None else totals + product
    return totals / weight, top, weight


def gradient_block(
    block, size, qkv, d_out, delta, probs_of, key_rows, value_rows, key_acc, value_acc, opening
):
    query_at = block * size
    cols = slice(query_at, query_at + size)
    query = scaled_query(qkv, cols)
    d_query = d_out[:, cols]
    d_sum = None
    for key_at, keys in key_blocks(query_at, size):
        where = slice(key_at, key_at + keys)
        probs = probs_of(key_at, keys, query)
        d_probs = dot(value_rows[where, :], d_query)
        d_scores = (probs * (d_probs - delta)).astype(BF)
        d_key = dot(query, d_scores, ((1,), (1,)))
        d_value = dot(d_query, probs.astype(BF), ((1,), (1,)))
        if opening:
            key_acc[:, where] = d_key
            value_acc[:, where] = d_value
        else:
            key_acc[:, where] += d_key
            value_acc[:, where] += d_value
        part = dot(qkv[HEAD_DIM : 2 * HEAD_DIM, where], d_scores)
        d_sum = part if d_sum is None else d_sum + part
    return d_sum * (1.0 / math.sqrt(HEAD_DIM))


class LineReduce:
    def __init__(self, place, total, low, from_left, from_right, view, sems, lane=0):
        self.place, self.total, self.low, self.view, self.lane = place, total, low, view, lane
        self.from_left, self.from_right = from_left, from_right
        self.send_right, self.send_left, self.recv_left, self.recv_right = sems

    def right(self, owner):
        return rcopy(
            self.low.at[self.view(owner)], self.from_left.at[self.view(owner)],
            self.send_right.at[self.lane, owner], self.recv_left.at[self.lane, owner],
            col=lax.rem(self.place.c + 1, self.place.cols),
        )

    def left(self, owner):
        cols = self.place.cols
        return rcopy(
            self.low.at[self.view(owner)], self.from_right.at[self.view(owner)],
            self.send_left.at[self.lane, owner], self.recv_right.at[self.lane, owner],
            col=lax.rem(self.place.c + cols - 1, cols),
        )

    def add_in(self, owner, arrived):
        view = self.view(owner)
        self.low[view] = (self.total[view] + arrived[view].astype(F32)).astype(BF)

    def step(self, time):
        c, cols = self.place.c, self.place.cols

        @pl.when(c <= time)
        def _():
            owner = cols - 1 - time + c

            @pl.when(c > 0)
            def _():
                self.right(owner).wait_recv()
                self.add_in(owner, self.from_left)

            self.right(owner).start()

        @pl.when(c >= cols - 1 - time)
        def _():
            owner = time + c - (cols - 1)

            @pl.when(c < cols - 1)
            def _():
                self.left(owner).wait_recv()
                self.add_in(owner, self.from_right)

            self.left(owner).start()

    def own(self):
        c, cols = self.place.c, self.place.cols
        view = self.view(c)

        @pl.when(c > 0)
        def _():
            self.right(c).wait_recv()

        @pl.when(c == 0)
        def _():
            self.from_left[view] = jnp.zeros_like(self.from_left[view])

        @pl.when(c < cols - 1)
        def _():
            self.left(c).wait_recv()

        @pl.when(c == cols - 1)
        def _():
            self.from_right[view] = jnp.zeros_like(self.from_right[view])

        return (
            self.total[view] + self.from_left[view].astype(F32) + self.from_right[view].astype(F32)
        )

    def finish(self):
        c, cols = self.place.c, self.place.cols
        for time in range(cols - 1):

            @pl.when(c <= time)
            def _():
                self.right(cols - 1 - time + c).wait_send()

            @pl.when(c >= cols - 1 - time)
            def _():
                self.left(time + c - (cols - 1)).wait_send()


def center_sum(place, total, low, from_outer, from_inner, full, sems, order, prepare, produce, after, work):
    c = place.c
    a_send, a_recv, b_send, b_recv, c_send, c_recv = sems
    count = len(order)
    size = total.shape[0] // count
    inner = (c == 1) | (c == 2)
    outer = (c == 0) | (c == 3)
    pair = jnp.where(c < 2, 1 - c, 5 - c)
    middle = 3 - c
    group = count // 4

    def rows(index):
        return slice(order[index] * size, (order[index] + 1) * size)

    def inward(index):
        piece = rows(index)
        return rcopy(
            low.at[piece], from_outer.at[piece], a_send.at[index], a_recv.at[index], col=pair
        )

    def exchange(index):
        piece = rows(index)
        return rcopy(
            low.at[piece], from_inner.at[piece], b_send.at[index], b_recv.at[index], col=middle
        )

    def outward(index):
        piece = rows(index)
        return rcopy(full.at[piece], full.at[piece], c_send.at[index], c_recv.at[index], col=pair)

    prepare(0)
    for time in range(count + 2 * LAG):
        if time < count:

            @pl.when(outer)
            def _():
                inward(time).start()

            @pl.when(inner)
            def _():
                piece = rows(time)
                inward(time).wait_recv()
                low[piece, :] = (total[piece, :] + from_outer[piece, :].astype(F32)).astype(BF)
                exchange(time).start()

        if LAG <= time < count + LAG:

            @pl.when(inner)
            def _():
                index = time - LAG
                piece = rows(index)
                exchange(index).wait_recv()
                summed = low[piece, :].astype(F32) + from_inner[piece, :].astype(F32)
                full[piece, :] = produce(summed, piece)
                outward(index).start()

        if time >= 2 * LAG:

            @pl.when(outer)
            def _():
                outward(time - 2 * LAG).wait_recv()

        if time + 2 < count and (time + 2) % group == 0:
            prepare((time + 2) // group)
        if time >= 2 * LAG:
            after(time - 2 * LAG)
        work(time)
    for index in range(count):

        @pl.when(outer)
        def _():
            inward(index).wait_send()

        @pl.when(inner)
        def _():
            exchange(index).wait_send()
            outward(index).wait_send()


class GradExchange:
    def __init__(self, place, layer, n, send, recv):
        self.place, self.layer = place, layer
        self.mine, self.theirs, self.relay, self.inbox = (
            [getattr(n, name + kind) for kind in "qfop"]
            for name in ("mine_", "theirs_", "relay_", "inbox_")
        )
        self.send, self.recv = send, recv

    def block(self, which):
        place = self.place
        return (place.beside(0), place.beside(1), place.across(), place.r)[which]

    def view(self, kind, block, half=None):
        shape = self.inbox[kind].shape
        length = shape[-2 if kind in (0, 1) else -1]
        lines = shape[-2]
        at, count = (0, lines) if half is None else (half * (lines // 2), lines // 2)
        if kind in (0, 1):
            piece = pl.ds(pl.multiple_of(block * length + at, count), count)
            return (slice(None), piece, slice(None)) if kind == 0 else (piece, slice(None))
        piece = pl.ds(pl.multiple_of(block * length, length), length)
        return (slice(at, at + count), piece)

    def passing(self, kind, which):
        view = self.view(kind, self.block(which))
        return rcopy(
            self.mine[kind].at[view], self.theirs[kind].at[view], self.send.at[kind, which],
            self.recv.at[kind, which], section=1 - self.place.s,
        )

    def relaying(self, kind, way):
        target = self.place.across() if kind in DIRECT else self.place.beside(way)
        return rcopy(
            self.mine[kind].at[self.view(kind, self.place.across(), way)],
            self.relay[kind].at[way], self.send.at[kind, 4 + way], self.recv.at[kind, 4 + way],
            row=target,
        )

    def sending(self, kind, way):
        return rcopy(
            self.mine[kind].at[self.view(kind, self.place.beside(way))],
            self.inbox[kind].at[way], self.send.at[kind, 6 + way], self.recv.at[kind, 6 + way],
            row=self.place.beside(way),
        )

    def add(self, kind, view, value):
        self.mine[kind][view] = self.mine[kind][view] + value

    def hand(self, kind, only=(2, 0, 1, 3)):
        @pl.when(self.place.s != self.layer)
        def _():
            for which in only:
                self.passing(kind, which).start()

    def merge(self, kind):
        @pl.when(self.place.s == self.layer)
        def _():
            for which in (2, 0, 1):
                self.passing(kind, which).wait_recv()
                view = self.view(kind, self.block(which))
                self.add(kind, view, self.theirs[kind][view])
                if which == 2:
                    for way in range(2):
                        self.relaying(kind, way).start()
                elif kind in DIRECT:
                    self.sending(kind, which).start()

    def pass_on(self, kind):
        if kind in DIRECT:
            return

        @pl.when(self.place.s == self.layer)
        def _():
            for way in range(2):
                self.relaying(kind, 1 - way).wait_recv()
                view = self.view(kind, self.place.beside(way), 1 - way)
                self.add(kind, view, self.relay[kind][1 - way])
                self.sending(kind, way).start()

    def take(self, kind, out):
        @pl.when(self.place.s == self.layer)
        def _():
            self.passing(kind, 3).wait_recv()
            view = self.view(kind, self.place.r)
            total = self.mine[kind][view].astype(F32) + self.theirs[kind][view].astype(F32)
            for way in range(2):
                self.sending(kind, way).wait_recv()
                total = total + self.inbox[kind][way].astype(F32)
            out[...] = total
            if kind in DIRECT:
                for way in range(2):
                    self.relaying(kind, way).wait_recv()
                    half = self.relay[kind].shape[-2]
                    lines = slice(way * half, (way + 1) * half)
                    where = (slice(None), lines) if kind == 0 else (lines,)
                    out[where] = out[where] + self.relay[kind][way].astype(F32)

    def finish(self, kind):
        @pl.when(self.place.s == self.layer)
        def _():
            for way in range(2):
                self.relaying(kind, way).wait_send()
                self.sending(kind, way).wait_send()

        @pl.when(self.place.s != self.layer)
        def _():
            for which in range(4):
                self.passing(kind, which).wait_send()


def grad_shapes(rows, full, width, units):
    part = full // rows
    return (
        dict(q=(3, full, width), f=(full, units), o=(width, full), p=(units, full)),
        dict(q=(3, part, width), f=(part, units), o=(width, part), p=(units, part)),
    )


def grad_scratch(rows, full, width, units):
    wholes, pieces = grad_shapes(rows, full, width, units)
    scratch = {}
    for kind in "qfop":
        piece = pieces[kind]
        half = piece[:-2] + (piece[-2] // 2, piece[-1])
        scratch["mine_" + kind] = pltpu.VMEM(wholes[kind], BF)
        scratch["theirs_" + kind] = pltpu.VMEM(wholes[kind], BF)
        scratch["relay_" + kind] = pltpu.VMEM((2,) + half, BF)
        scratch["inbox_" + kind] = pltpu.VMEM((2,) + piece, BF)
    return scratch


class BlockExchange:
    def __init__(self, place, source, inbox, size, send, recv, local):
        self.place, self.source, self.inbox, self.size = place, source, inbox, size
        self.send, self.recv, self.local = send, recv, local

    def slot(self, head, lane):
        return self.inbox.at[head, :, lane * self.size : (lane + 1) * self.size]

    def piece(self, block):
        return self.source.at[:, block * self.size : (block + 1) * self.size]

    def away(self, block):
        return rcopy(
            self.piece(block), self.slot(self.place.r, block % PARTS), self.send.at[block],
            self.recv.at[block % PARTS, self.place.r], row=block // PARTS,
        )

    def start(self, block):
        @pl.when(self.place.r != block // PARTS)
        def _():
            self.away(block).start()

        @pl.when(self.place.r == block // PARTS)
        def _():
            pltpu.make_async_copy(
                self.piece(block), self.slot(self.place.r, block % PARTS),
                self.local.at[block % PARTS],
            ).start()

    def arrive(self, lane):
        for step in range(1, self.place.rows):
            source = self.place.row_from(step)
            slot = self.slot(source, lane)
            rcopy(
                slot, slot, self.send.at[lane], self.recv.at[lane, source],
                row=self.place.row_to(step),
            ).wait_recv()
        slot = self.slot(self.place.r, lane)
        pltpu.make_async_copy(slot, slot, self.local.at[lane]).wait()

    def finish(self):
        for block in range(self.place.rows * PARTS):

            @pl.when(self.place.r != block // PARTS)
            def _():
                self.away(block).wait_send()


def unit_rows(values):
    centred = values - jnp.mean(values, axis=1, keepdims=True)
    rstd = lax.rsqrt(jnp.mean(centred * centred, axis=1, keepdims=True) + EPS)
    return centred * rstd, rstd


def segment_begins(lengths, micro, first):
    token = lax.broadcasted_iota(jnp.int32, first.shape, 1)
    begin = jnp.zeros_like(token)
    start = lengths[micro, 0]
    for index in range(1, lengths.shape[1]):
        begin = jnp.where(token >= start, start, begin)
        start = start + lengths[micro, index]
    first[...] = begin
    return lengths[micro, 0]


def rotary(lengths, micro, row, cos, sin):
    half, tokens = cos.shape
    token = lax.broadcasted_iota(jnp.int32, (half, tokens), 1) + row * tokens
    begin = jnp.zeros_like(token)
    start = lengths[micro, 0]
    for index in range(1, lengths.shape[1]):
        begin = jnp.where(token >= start, start, begin)
        start = start + lengths[micro, index]
    position = jnp.where(begin == 0, token, lengths[micro, 0] + token - begin)
    which = lax.broadcasted_iota(jnp.int32, (half, tokens), 0)
    freqs = jnp.zeros((half, tokens), F32)
    for index in range(half):
        freqs = jnp.where(which == index, 10000.0 ** (-(2.0 * index) / ROT), freqs)
    angles = position.astype(F32) * freqs
    cos[...] = jnp.cos(angles)
    sin[...] = jnp.sin(angles)


class Saver:
    def __init__(self, sems):
        self.sems, self.copies = sems, []

    def copy(self, source, target):
        copy = pltpu.make_async_copy(source, target, self.sems.at[len(self.copies)])
        copy.start()
        self.copies.append(copy)
        return copy

    def finish(self):
        for copy in self.copies:
            copy.wait()


class Names:
    def joined(self, results):
        both = Names()
        for name, value in vars(self).items():
            setattr(both, name, value)
        for name, value in results.items():
            setattr(both, name[2:], value)
        return both


def named_call(body, collective_id, ins, outs, scratch):
    names = [*ins, *outs, *scratch]

    def kernel(*refs):
        held = Names()
        for name, ref in zip(names, refs):
            setattr(held, name, ref)
        body(held)

    results = pl.pallas_call(
        kernel,
        out_shape=[jax.ShapeDtypeStruct(shape, dtype) for shape, dtype, space in outs.values()],
        in_specs=[pl.BlockSpec(memory_space=space) for array, space in ins.values()],
        out_specs=[pl.BlockSpec(memory_space=space) for shape, dtype, space in outs.values()],
        scratch_shapes=list(scratch.values()),
        compiler_params=pltpu.CompilerParams(
            collective_id=collective_id,
            has_side_effects=collective_id is not None,
            vmem_limit_bytes=VMEM_LIMIT,
        ),
    )(*[array for array, space in ins.values()])
    return dict(zip(outs, results))


class VectorGather:
    def __init__(self, place, own, full, send, recv, width):
        self.place, self.own, self.full, self.width = place, own, full, width
        self.send, self.recv = send, recv
        self.others = [(ds, dc) for ds in range(2) for dc in range(place.cols) if ds or dc]

    def slot(self, section, col):
        return self.full.at[section, :, pl.ds(pl.multiple_of(col * self.width, self.width), self.width)]

    def copy(self, ds, dc, source, slot):
        index = ds * self.place.cols + dc
        return rcopy(
            source, slot, self.send.at[index], self.recv.at[index],
            section=lax.rem(self.place.s + ds, 2), col=self.place.col_to(dc),
        )

    def start(self):
        for ds, dc in self.others:
            self.copy(ds, dc, self.own, self.slot(self.place.s, self.place.c)).start()

    def arrive(self):
        for ds, dc in self.others:
            slot = self.slot(lax.rem(self.place.s + ds, 2), self.place.col_from(dc))
            self.copy(ds, dc, slot, slot).wait_recv()

    def finish(self):
        for ds, dc in self.others:
            self.copy(ds, dc, self.own, self.slot(self.place.s, self.place.c)).wait_send()


def first_kernel(rows, cols, n):
    place = Place(rows, cols)
    s, c = place.s, place.c
    tokens, full = n.x_full.shape
    width = full // cols
    length = tokens // PARTS
    own = pl.ds(pl.multiple_of(c * width, width), width)

    def lane_of(lane):
        return slice(lane * length, (lane + 1) * length)

    def block_cols(block):
        return pl.ds(pl.multiple_of(block * width, width), width)

    def token_slot(source, lane):
        return pl.ds(pl.multiple_of(source * tokens + lane * length, length), length)

    loads = Saver(n.load)
    x_own = loads.copy(n.hidden_in.at[s], n.x_full.at[:, own])
    n.vectors[0:2] = n.norm_gains[0]
    n.vectors[2:4] = n.norm_biases[0]
    for index in range(3):
        n.vectors[4 + index : 5 + index] = n.b_qkv[:, index * width : (index + 1) * width]
    n.vectors[7:8] = n.b_out[...]
    for index in range(n.b_fc.shape[1] // width):
        n.vectors[8 + index : 9 + index] = n.b_fc[:, index * width : (index + 1) * width]
    n.vectors[12:16] = jnp.zeros((4, width), F32)
    v_own = loads.copy(n.vectors, n.vec_all.at[s, :, own])
    c_own = loads.copy(n.cotangent.at[s], n.cot_full.at[:, own])
    place.greet(rows=True, cols=True, partner=True, cross_cols=True)
    x_gather = [
        LineGather(
            place, lambda block, lane=lane: n.x_full.at[lane_of(lane), block_cols(block)],
            n.x_a, n.x_b, n.x_c, lane,
        )
        for lane in range(PARTS)
    ]
    c_gather = LineGather(
        place, lambda block: n.cot_full.at[:, block_cols(block)], n.c_a, n.c_b, n.c_c
    )
    vectors = VectorGather(place, n.vectors, n.vec_all, n.v_s, n.v_r, width)
    blocks = (n.wq, n.wf, n.wo, n.wp)
    weights = [
        WeightGather(place, 0, blocks, (n.wq0, n.wf0, n.wo0, n.wp0), n.w0_s, n.w0_r, n.w0_l),
        WeightGather(place, 1, blocks, (n.wq1, n.wf1, n.wo1, n.wp1), n.w1_s, n.w1_r, n.w1_l),
    ]
    QKV, FC, OUT, PROJ = range(4)
    saves = Saver(n.save)
    def row(layer, index):
        return n.vec_all[layer, index : index + 1, :]

    def bias_rows(layer):
        return lambda kind: n.vec_all[layer, 4 + kind : 5 + kind, own]

    def unit_bias(layer):
        return lambda index: n.vec_all[layer, pl.ds(8 + index, 1), own]

    def spread(pieces, slots, sends, recvs, local):
        return [
            RowExchange(
                place,
                lambda target, lane=lane: pieces(target, lane),
                lambda source, lane=lane: slots(source, lane),
                sends.at[lane], recvs.at[lane], local.at[lane],
            )
            for lane in range(PARTS)
        ]

    out0 = spread(
        lambda target, lane: n.pieces0.at[target, :, lane_of(lane)],
        lambda source, lane: n.qkv0.at[:, token_slot(source, lane)],
        n.e0_s, n.e0_r, n.e0_l,
    )
    back0 = spread(
        lambda target, lane: n.low0.at[:, token_slot(target, lane)],
        lambda source, lane: n.attn_t0.at[
            pl.ds(pl.multiple_of(source * HEAD_DIM, HEAD_DIM), HEAD_DIM), lane_of(lane)
        ],
        n.b0_s, n.b0_r, n.b0_l,
    )
    out1 = spread(
        lambda target, lane: n.pieces1.at[target, :, lane_of(lane)],
        lambda source, lane: n.qkvd1.at[:, token_slot(source, lane)],
        n.e1_s, n.e1_r, n.e1_l,
    )

    def project(layer, lane, source, normed_a, normed_m, w_query, pieces):
        norm_rows(
            source, row(layer, 0), row(layer, 2), row(layer, 1), row(layer, 3), normed_a, normed_m,
            lane * length, length,
        )
        project_heads(
            normed_a, w_query, bias_rows(layer), n.cos, n.sin, pieces, rows, lane_of(lane)
        )

    x_own.wait()
    x_gather[0].hop(0)
    vectors.start()
    weights[0].start(QKV)
    weights[0].start(FC)
    prompt = segment_begins(n.lengths, s, n.first)
    rotary(n.lengths, s, place.r, n.cos, n.sin)
    x_gather[0].hop(1)
    x_gather[1].hop(0)
    x_gather[0].hop(2)
    weights[0].relay(QKV)
    weights[0].start(PROJ)
    x_gather[1].hop(1)
    for distance in range(3, cols):
        x_gather[0].hop(distance)
    weights[0].forward(QKV)
    weights[0].relay(FC)
    vectors.arrive()
    v_own.wait()
    x_gather[1].hop(2)
    weights[0].ready(QKV)
    project(0, 0, n.x_full, n.normed_a0, n.normed_m0, n.wq0, n.pieces0)
    out0[0].start()
    weights[0].start(OUT)
    for distance in range(3, cols):
        x_gather[1].hop(distance)
    c_own.wait()
    c_gather.hop(0)
    weights[0].forward(FC)
    project(0, 1, n.x_full, n.normed_a0, n.normed_m0, n.wq0, n.pieces0)
    out0[1].start()
    weights[0].relay(PROJ)
    weights[0].relay(OUT)
    c_gather.hop(1)
    weights[0].ready(FC)
    feed_forward(n.normed_m0, n.wf0, unit_bias(0), n.hidden0, n.slope0, slice(None))
    for ref, target in (
        (n.x_full, n.o_x_full), (n.vec_all, n.o_vec_all), (n.wq0, n.o_wq0), (n.wf0, n.o_wf0),
        (n.normed_a0, n.o_normed_a0), (n.normed_m0, n.o_normed_m0), (n.hidden0, n.o_hidden0),
        (n.slope0, n.o_slope0),
    ):
        saves.copy(ref, target)
    weights[0].forward(PROJ)
    weights[0].forward(OUT)
    weights[1].start(QKV)
    weights[1].start(OUT)
    for lane in range(PARTS):
        out0[lane].arrive()
    saves.copy(n.qkv0, n.o_qkv0)

    rows_of_keys(n.qkv0, HEAD_DIM, n.key_rows)

    def attend(lane, owner):
        block = owner * PARTS + lane
        exact, top, weight = attend_block(
            block, length, prompt, n.first, n.qkv0, n.key_rows, n.scores.at[owner % 2],
            lambda key_at, keys: (slice(key_at, key_at + keys), slice(None)),
        )
        cols_here = slice(block * length, (block + 1) * length)
        n.out0[:, cols_here] = exact
        n.low0[:, cols_here] = exact.astype(BF)
        n.log0[:, cols_here] = top + jnp.log(weight)

    for owner in range(rows):
        attend(0, owner)
    back0[0].start()
    c_gather.hop(2)
    weights[1].start(FC)
    attend(1, 0)
    attend(1, 1)
    for distance in range(3, cols):
        c_gather.hop(distance)
    saves.copy(n.cot_full, n.o_cot_full)
    weights[0].ready(PROJ)
    weights[0].ready(OUT)
    saves.copy(n.wp0, n.o_wp0)
    saves.copy(n.wo0, n.o_wo0)

    step = 4 // PARTS
    part = tokens // 4

    def prepare(quarter):
        if quarter % step == 0:
            back0[quarter // step].arrive()
        where = slice(quarter * part, (quarter + 1) * part)
        attn_rows = n.attn_t0[:, where].astype(F32).T.astype(BF)
        tile = min(256, full)
        for at in range(0, full, tile):
            value = dot(n.hidden0[where, :], n.wp0[:, at : at + tile]) + dot(
                attn_rows, n.wo0[:, at : at + tile]
            )
            n.total[where, at : at + tile] = value
            n.low[where, at : at + tile] = value.astype(BF)

    def produce(summed, mine):
        return (n.x_full[mine, :].astype(F32) + summed + n.vec_all[0, 7:8, :]).astype(BF)

    def branches(lane):
        where = lane_of(lane)
        feed_forward(n.normed_m1, n.wf1, unit_bias(1), n.hidden1, n.slope1, where)

        def times_slope(value, cols_here):
            return (value * n.slope1[where, cols_here]).astype(BF)

        times_tiles(n.cot_full, n.wp1, n.d_hidden1, times_slope, ((1,), (1,)), where)
        times_tiles(n.hidden1, n.wp1, n.branch1, None, ((1,), (0,)), where)
        times_tiles(n.d_hidden1, n.wf1, n.d_normed1, None, ((1,), (1,)), where)

    def after(chunk):
        if (chunk + 1) % (CHUNKS // PARTS):
            return
        lane = chunk // (CHUNKS // PARTS)
        if lane == 0:
            weights[1].ready(QKV)
            weights[1].ready(OUT)
        project(1, lane, n.x1_full, n.normed_a1, n.normed_m1, n.wq1, n.pieces1)
        where = lane_of(lane)
        flipped = dot(n.cot_full[where, :], n.wo1[...], ((1,), (1,))).T
        for head in range(rows):
            n.pieces1[head, 3 * HEAD_DIM :, where] = flipped[
                head * HEAD_DIM : (head + 1) * HEAD_DIM
            ].astype(BF)
        out1[lane].start()

    def work(time):
        if time < rows - 2:
            attend(1, 2 + time)
            if time == rows - 3:
                back0[1].start()
                saves.copy(n.out0, n.o_out0)
                saves.copy(n.log0, n.o_log0)
        if time == 1:
            weights[1].relay(QKV)
            weights[1].relay(OUT)
        if time == 3:
            weights[1].forward(QKV)
            weights[1].forward(OUT)
            weights[1].start(PROJ)
        if time == 6:
            weights[1].relay(FC)
        if time == 11:
            weights[1].forward(FC)
            weights[1].relay(PROJ)
        if time == 16:
            weights[1].forward(PROJ)
        if time == 20:
            weights[1].ready(FC)
            weights[1].ready(PROJ)
            branches(0)

    center_sum(
        place, n.total, n.low, n.from_left, n.from_right, n.x1_full,
        (n.r_a, n.r_b, n.r_c, n.r_d, n.r_e, n.r_f), tuple(range(CHUNKS)), prepare, produce, after, work,
    )
    saves.copy(n.attn_t0, n.o_attn_t0)
    for ref, target in (
        (n.x1_full, n.o_x1_full), (n.wq1, n.o_wq1), (n.wo1, n.o_wo1),
        (n.normed_a1, n.o_normed_a1), (n.normed_m1, n.o_normed_m1),
    ):
        saves.copy(ref, target)
    for lane in range(1, PARTS):
        branches(lane)
    for ref, target in (
        (n.hidden1, n.o_hidden1), (n.d_hidden1, n.o_d_hidden1), (n.branch1, n.o_branch1),
        (n.d_normed1, n.o_d_normed1),
    ):
        saves.copy(ref, target)
    for lane in range(PARTS):
        out1[lane].arrive()
    saves.copy(n.qkvd1, n.o_qkvd1)
    for exchange in out0 + back0 + out1:
        exchange.finish()
    for gather in x_gather + [c_gather]:
        gather.finish()
    vectors.finish()
    for gather in weights:
        for kind in range(4):
            gather.finish(kind)
    saves.finish()


def first_half(rows, cols, hidden_in, cotangent, vectors, blocks, lengths):
    norm_gains, norm_biases, b_qkv, b_out, b_fc = vectors
    tokens, width = hidden_in.shape[1:]
    full = cols * width
    wq, wf, wo, wp = blocks
    units = wf.shape[1]
    total = rows * tokens
    hbm, vmem, smem = pl.ANY, pltpu.VMEM, pltpu.SMEM
    ins = dict(
        hidden_in=(hidden_in, hbm), cotangent=(cotangent, hbm), norm_gains=(norm_gains, vmem),
        norm_biases=(norm_biases, vmem), b_qkv=(b_qkv, vmem), b_out=(b_out, vmem), b_fc=(b_fc, vmem),
        wq=(wq, hbm), wf=(wf, hbm), wo=(wo, hbm), wp=(wp, hbm),
        lengths=(lengths, smem),
    )
    rows_low, rows_wide = ((tokens, full), BF), ((tokens, full), F32)
    unit_low, unit_wide = ((tokens, units), BF), ((tokens, units), F32)
    kept = dict(
        x_full=rows_low, cot_full=rows_low, vec_all=((2, 16, full), F32),
        wq0=((3, full, width), BF), wf0=((full, units), BF), wo0=((width, full), BF),
        wp0=((units, full), BF), normed_a0=rows_low, normed_m0=rows_low,
        qkv0=((3 * HEAD_DIM, total), BF), hidden0=unit_low, slope0=unit_low,
        out0=((HEAD_DIM, total), F32), log0=((1, total), F32), attn_t0=((width, tokens), BF),
        x1_full=rows_low, wq1=((3, full, width), BF), wo1=((width, full), BF),
        normed_a1=rows_low, normed_m1=rows_low, qkvd1=((4 * HEAD_DIM, total), BF),
        hidden1=unit_low, d_hidden1=unit_low, branch1=rows_wide, d_normed1=rows_wide,
    )
    outs = {"o_" + name: shape + (hbm,) for name, shape in kept.items()}
    scratch = {name: pltpu.VMEM(*shape) for name, shape in kept.items()}
    scratch.update(
        vectors=pltpu.VMEM((16, width), F32),
        wf1=pltpu.VMEM((full, units), BF), wp1=pltpu.VMEM((units, full), BF),
        slope1=pltpu.VMEM(*unit_wide), low0=pltpu.VMEM((HEAD_DIM, total), BF),
        total=pltpu.VMEM(*rows_wide), low=pltpu.VMEM(*rows_low),
        from_left=pltpu.VMEM(*rows_low), from_right=pltpu.VMEM(*rows_low),
        pieces0=pltpu.VMEM((rows, 3 * HEAD_DIM, tokens), BF),
        pieces1=pltpu.VMEM((rows, 4 * HEAD_DIM, tokens), BF),
        first=pltpu.VMEM((1, total), jnp.int32),
        cos=pltpu.VMEM((ROT // 2, tokens), F32), sin=pltpu.VMEM((ROT // 2, tokens), F32),
        key_rows=pltpu.VMEM((total, HEAD_DIM), BF),
        scores=pltpu.VMEM((2, total, tokens // PARTS), F32),
        load=dma(3), save=dma(len(kept)),
        x_a=dma(PARTS, cols), x_b=dma(PARTS, cols), x_c=dma(PARTS, cols),
        c_a=dma(1, cols), c_b=dma(1, cols), c_c=dma(1, cols),
        v_s=dma(2 * cols), v_r=dma(2 * cols),
        w0_s=dma(4, 8), w0_r=dma(4, 8), w0_l=dma(4), w1_s=dma(4, 8), w1_r=dma(4, 8), w1_l=dma(4),
    )
    for name in ("e0", "b0", "e1"):
        scratch[name + "_s"] = dma(PARTS, rows)
        scratch[name + "_r"] = dma(PARTS, rows)
        scratch[name + "_l"] = dma(PARTS)
    for name in ("r_a", "r_b", "r_c", "r_d", "r_e", "r_f"):
        scratch[name] = dma(CHUNKS)
    return Names().joined(named_call(partial(first_kernel, rows, cols), 1, ins, outs, scratch))


def d_projection(inbox, at, cos, sin, rows, d_pre, small, where):
    width = rows * HEAD_DIM
    for kind in range(3):
        parts = []
        for head in range(rows):
            start = at + kind * HEAD_DIM
            block = inbox[head, start : start + HEAD_DIM, where].astype(F32)
            parts.append(turn(block, cos[:, where], sin[:, where], -1.0) if kind < 2 else block)
        values = jnp.concatenate(parts, axis=0).T.astype(BF)
        d_pre[where, kind * width : (kind + 1) * width] = values
        small[8 + kind : 9 + kind, :] += jnp.sum(values.astype(F32), axis=0, keepdims=True)


def d_norms(source, d_pre, wq, d_normed, gain_a, gain_m, total, low, sums, begin, count, also=None):
    width = wq.shape[2]
    tile = min(128, count)

    @pl.loop(0, count // tile)
    def _(index):
        rows = pl.ds(pl.multiple_of(begin + index * tile, tile), tile)
        d_a = dot(d_pre[rows, :width], wq[0], ((1,), (1,)))
        for kind in range(1, 3):
            d_a += dot(d_pre[rows, kind * width : (kind + 1) * width], wq[kind], ((1,), (1,)))
        d_m = d_normed[rows, :]
        unit, rstd = unit_rows(source[rows, :].astype(F32))
        sums[0:1, :] += jnp.sum(d_a * unit, axis=0, keepdims=True)
        sums[1:2, :] += jnp.sum(d_m * unit, axis=0, keepdims=True)
        sums[2:3, :] += jnp.sum(d_a, axis=0, keepdims=True)
        sums[3:4, :] += jnp.sum(d_m, axis=0, keepdims=True)
        joined = d_a * gain_a + d_m * gain_m
        total[rows, :] = joined
        low[rows, :] = joined.astype(BF)
        if also is not None:
            also(rows, joined, unit, rstd)


def unit_sums(d_pre, small, width):
    for index in range(d_pre.shape[1] // width):
        piece = d_pre[:, index * width : (index + 1) * width].astype(F32)
        small[12 + index : 13 + index, :] = jnp.sum(piece, axis=0, keepdims=True)


def across_tokens(left, right, out, heads=False, only=None):
    tile = min(256, left.shape[1])

    def at(index):
        cols = pl.ds(pl.multiple_of(index * tile, tile), tile)
        value = dot(left[:, cols], right[...], ((0,), (0,))).astype(BF)
        if heads:
            width = out.shape[2]
            for kind in range(3):
                out[kind, cols, :] = value[:, kind * width : (kind + 1) * width]
        else:
            out[cols, :] = value

    if only is None:
        pl.loop(0, left.shape[1] // tile)(at)
    else:
        at(only)


def across_blocks(grads, kind, left, right, out, heads, turns):
    for which in turns:
        across_tokens(left, right, out, heads, grads.block(which))
        grads.hand(kind, (which,))


FARTHEST_FIRST = (2, 0, 1, 3)


def out_gradient(attn_t, grad_full, out):
    tile = min(256, out.shape[1])
    for at in range(0, out.shape[1], tile):
        out[:, at : at + tile] = dot(attn_t[...], grad_full[:, at : at + tile]).astype(BF)


Q, F, O, PR = range(4)
DIRECT = (O,)


class Load:
    def __init__(self, source, target, sem):
        self.copy, self.waiting = pltpu.make_async_copy(source, target, sem), True

    def start(self):
        self.copy.start()

    def need(self):
        if self.waiting:
            self.copy.wait()
            self.waiting = False


def second_kernel(rows, cols, n):
    place = Place(rows, cols)
    s, c = place.s, place.c
    tokens, full = n.x1_full.shape
    width = full // cols
    length = tokens // PARTS
    size = QUERY_BLOCK
    own = pl.ds(pl.multiple_of(c * width, width), width)
    count = rows * PARTS
    qkv0 = n.qkvd1.at[: 3 * HEAD_DIM]
    hidden0, normed_m0, normed_a0, wq0 = n.hidden1, n.normed_m1, n.normed_a1, n.wq1
    x_full, branch1, unit0, d_normed0 = n.d_hidden1, n.d_normed1, n.scores, n.scores
    o_low = n.cot_full
    load_no = iter(range(LOADS))

    def loading(source, target):
        return Load(source, target, n.load.at[next(load_no)])

    l_qkvd1 = loading(n.i_qkvd1, n.qkvd1)
    l_cot = loading(n.i_cot_full, n.cot_full)
    l_d_hidden1 = loading(n.i_d_hidden1, n.d_hidden1)
    l_hidden1 = loading(n.i_hidden1, n.hidden1)
    l_x1 = loading(n.i_x1_full, n.x1_full)
    l_wq1 = loading(n.i_wq1, n.wq1)
    l_d_normed1 = loading(n.i_d_normed1, n.d_normed1)
    l_normed_m1 = loading(n.i_normed_m1, n.normed_m1)
    l_normed_a1 = loading(n.i_normed_a1, n.normed_a1)
    l_wo0 = loading(n.i_wo0, n.wo0)
    l_wp0 = loading(n.i_wp0, n.wp0)
    l_wf0 = loading(n.i_wf0, n.wf0)
    l_slope0 = loading(n.i_slope0, n.slope0)
    l_wo1 = loading(n.i_wo1, n.wo1)
    l_out0 = loading(n.i_out0, n.out0)
    l_log0 = loading(n.i_log0, n.log0)
    l_attn_t0 = loading(n.i_attn_t0, n.attn_t0)
    l_qkv0 = loading(n.i_qkv0, qkv0)
    l_hidden0 = loading(n.i_hidden0, hidden0)
    l_normed_m0 = loading(n.i_normed_m0, normed_m0)
    l_normed_a0 = loading(n.i_normed_a0, normed_a0)
    l_wq0 = loading(n.i_wq0, wq0)
    l_x0 = loading(n.i_x_full, x_full)
    l_branch1 = loading(n.i_branch1, branch1)

    def lane_of(lane):
        return slice(lane * length, (lane + 1) * length)

    def features(owner):
        return (slice(None), pl.ds(pl.multiple_of(owner * width, width), width))

    l_qkvd1.start()
    place.greet(rows=True, cols=True, partner=True, cross_rows=True)
    grads1 = GradExchange(place, 1, n, n.g1_s, n.g1_r)
    grads0 = GradExchange(place, 0, n, n.g0_s, n.g0_r)
    exchange1 = BlockExchange(place, n.result, n.inbox, size, n.b1_s, n.b1_r, n.b1_l)
    exchange0 = BlockExchange(
        place, n.result.at[: 3 * HEAD_DIM], n.inbox.at[:, : 3 * HEAD_DIM], size, n.b0_s, n.b0_r,
        n.b0_l,
    )
    outward = [
        RowExchange(
            place,
            lambda target, lane=lane: n.pieces.at[target, :, lane_of(lane)],
            lambda source, lane=lane: n.d_out.at[
                :, pl.ds(pl.multiple_of(source * tokens + lane * length, length), length)
            ],
            n.e_s.at[lane], n.e_r.at[lane], n.e_l.at[lane],
        )
        for lane in range(PARTS)
    ]
    out_sum = LineReduce(
        place, branch1, o_low, n.o_left, n.o_right, features, (n.o_a, n.o_b, n.o_c, n.o_d)
    )
    grad_sums = [
        LineReduce(
            place, n.total, n.low, n.from_left, n.from_right,
            lambda owner, lane=lane: (lane_of(lane), features(owner)[1]),
            (n.s_a, n.s_b, n.s_c, n.s_d), lane,
        )
        for lane in range(PARTS)
    ]

    prompt = segment_begins(n.lengths, s, n.first)
    rotary(n.lengths, s, place.r, n.cos, n.sin)
    l_qkvd1.need()
    for load in (
        l_cot, l_d_hidden1, l_hidden1, l_x1, l_wq1, l_d_normed1, l_normed_m1, l_normed_a1, l_wo0,
        l_wp0, l_wf0, l_slope0, l_wo1, l_out0, l_log0, l_attn_t0,
    ):
        load.start()
    qkvd = n.qkvd1
    rows_of_keys(qkvd, HEAD_DIM, n.key_rows)
    rows_of_keys(qkvd, 2 * HEAD_DIM, n.value_rows)
    d_out1 = qkvd.at[3 * HEAD_DIM :]

    def spot(key_at, keys):
        at = key_at // KEY_BLOCK * size
        return (slice(0, keys), slice(at, at + size))

    for block in reversed(range(count)):
        here = slice(block * size, (block + 1) * size)
        exact, top, weight = attend_block(
            block, size, prompt, n.first, qkvd, n.key_rows, n.scores, spot, True
        )
        delta = jnp.sum(d_out1[:, here].astype(F32) * exact, axis=0, keepdims=True)
        inverse = 1.0 / weight

        def probs_of(key_at, keys, query):
            return n.scores[spot(key_at, keys)] * inverse

        d_query = gradient_block(
            block, size, qkvd, d_out1, delta, probs_of, n.key_rows, n.value_rows, n.key_acc,
            n.value_acc, block == count - 1,
        )
        n.result[:HEAD_DIM, here] = exact.astype(BF)
        n.result[HEAD_DIM : 2 * HEAD_DIM, here] = d_query.astype(BF)
        n.result[2 * HEAD_DIM : 3 * HEAD_DIM, here] = n.key_acc[:, here].astype(BF)
        n.result[3 * HEAD_DIM :, here] = n.value_acc[:, here].astype(BF)
        exchange1.start(block)

    l_qkv0.start()
    n.sums[...] = jnp.zeros_like(n.sums)
    n.small[...] = jnp.zeros_like(n.small)
    l_cot.need()
    l_d_hidden1.need()
    l_hidden1.need()
    n.small[1, 11:12, :] = jnp.sum(n.cot_full[:, own].astype(F32), axis=0, keepdims=True)
    unit_sums(n.d_hidden1, n.small.at[1], width)
    across_tokens(n.hidden1, n.cot_full, n.mine_p)
    grads1.hand(PR)
    l_hidden0.start()
    for load in (l_x1, l_wq1, l_d_normed1):
        load.need()
    quarters = (2, 3, 0, 1)
    part = tokens // 4

    def prepare(turn_no):
        if turn_no % 2 == 0:
            lane = quarters[turn_no] // 2
            exchange1.arrive(lane)
            where = lane_of(lane)
            for head in range(rows):
                n.attn_t1[head * HEAD_DIM : (head + 1) * HEAD_DIM, where] = n.inbox[
                    head, :HEAD_DIM, where
                ]
            d_projection(n.inbox, HEAD_DIM, n.cos, n.sin, rows, n.d_pre, n.small.at[1], where)
        d_norms(
            n.x1_full, n.d_pre, n.wq1, n.d_normed1, n.vec_all[1, 0:1, :], n.vec_all[1, 1:2, :],
            n.total, n.low, n.sums.at[1], quarters[turn_no] * part, part,
        )

    def produce(summed, mine):
        unit, rstd = unit_rows(n.x1_full[mine, :].astype(F32))
        moved = (
            summed
            - jnp.mean(summed, axis=1, keepdims=True)
            - unit * jnp.mean(summed * unit, axis=1, keepdims=True)
        )
        return (n.cot_full[mine, :].astype(F32) + rstd * moved).astype(BF)

    def branches(lane):
        where = lane_of(lane)

        def times_slope(value, cols_here):
            return (value * n.slope0[where, cols_here]).astype(BF)

        times_tiles(n.grad_full, n.wp0, n.d_hidden0, times_slope, ((1,), (1,)), where)
        times_tiles(n.d_hidden0, n.wf0, d_normed0, None, ((1,), (1,)), where)

    def after(chunk):
        if (chunk + 1) % (CHUNKS // PARTS) == 0:
            lane = 1 - chunk // (CHUNKS // PARTS)
            where = lane_of(lane)
            l_wo0.need()
            flipped = dot(n.grad_full[where, :], n.wo0[...], ((1,), (1,))).T
            for head in range(rows):
                n.pieces[head, :, where] = flipped[
                    head * HEAD_DIM : (head + 1) * HEAD_DIM
                ].astype(BF)
            outward[lane].start()

    def work(time):
        if time == 0:
            l_normed_m1.need()
        if time < 4:
            across_blocks(
                grads1, F, n.normed_m1, n.d_hidden1, n.mine_f, False, FARTHEST_FIRST[time : time + 1]
            )
        if time == 3:
            l_normed_m0.start()
            l_x0.start()
        if time == 4:
            grads1.merge(PR)
        if time == 8:
            grads1.merge(F)
        if time == 9:
            grads1.pass_on(PR)
        if time == 11:
            l_normed_a1.need()
        if 11 <= time < 15:
            across_blocks(
                grads1, Q, n.normed_a1, n.d_pre, n.mine_q, True, FARTHEST_FIRST[time - 11 : time - 10]
            )
        if time == 12:
            grads1.pass_on(F)
        if time == 14:
            l_normed_a0.start()
            l_wq0.start()
            l_branch1.start()
        if time == 15:
            out_gradient(n.attn_t1, n.cot_full, n.mine_o)
            grads1.hand(O)
        if time == 17:
            grads1.merge(Q)
        if time == 22:
            grads1.pass_on(Q)
            grads1.merge(O)
        if time == 18:
            outward[1].arrive()
            exchange1.finish()
            l_qkv0.need()
            l_out0.need()
            l_log0.need()
            rows_of_keys(qkv0, HEAD_DIM, n.key_rows)
            rows_of_keys(qkv0, 2 * HEAD_DIM, n.value_rows)
        if 18 <= time < 18 + rows:
            attend_back((rows - 1 - (time - 18)) * PARTS + 1)

    def attend_back(block):
        here = slice(block * size, (block + 1) * size)
        delta = jnp.sum(n.d_out[:, here].astype(F32) * n.out0[:, here], axis=0, keepdims=True)
        log_row = n.log0[:, here]

        def weights_of(key_at, keys, query):
            return jnp.exp(
                score_block(prompt, n.first, here, block * size, key_at, keys, n.key_rows, query)
                - log_row
            )

        d_query = gradient_block(
            block, size, qkv0, n.d_out, delta, weights_of, n.key_rows, n.value_rows, n.key_acc,
            n.value_acc, block == count - 1,
        )
        n.result[:HEAD_DIM, here] = d_query.astype(BF)
        if block % PARTS == 0 or block == count - 1:
            for done in keys_done(block):
                there = slice(done * size, (done + 1) * size)
                n.result[HEAD_DIM : 2 * HEAD_DIM, there] = n.key_acc[:, there].astype(BF)
                n.result[2 * HEAD_DIM : 3 * HEAD_DIM, there] = n.value_acc[:, there].astype(BF)
                exchange0.start(done)

    def keys_done(block):
        return (block,) if block in (0, count - 1) else (block, block - 1)

    chunks = tuple(range(CHUNKS // 2, CHUNKS)) + tuple(range(CHUNKS // 2))
    center_sum(
        place, n.total, n.low, n.from_left, n.from_right, n.grad_full,
        (n.r_a, n.r_b, n.r_c, n.r_d, n.r_e, n.r_f), chunks, prepare, produce, after, work,
    )

    l_branch1.need()
    l_wo1.need()
    attn_rows = n.attn_t1[...].astype(F32).T.astype(BF)
    tile = min(256, full)
    for at in range(0, full, tile):
        value = branch1[:, at : at + tile] + dot(attn_rows, n.wo1[:, at : at + tile])
        branch1[:, at : at + tile] = value
        o_low[:, at : at + tile] = value.astype(BF)
    out_sum.step(0)
    grads1.take(PR, n.gw_p)
    grads1.finish(PR)
    l_hidden0.need()
    across_tokens(hidden0, n.grad_full, n.mine_p)
    grads0.hand(PR)
    outward[0].arrive()
    for block in reversed(range(0, count, PARTS)):
        attend_back(block)
        if block == count - 2:
            grads1.take(O, n.gw_o)
            grads1.finish(O)
            l_attn_t0.need()
            out_gradient(n.attn_t0, n.grad_full, n.mine_o)
            grads0.hand(O)
            out_sum.step(1)
        if block == count - 6:
            grads0.merge(PR)
    out_sum.step(2)
    for load in (l_wp0, l_wf0, l_slope0):
        load.need()
    branches(1)
    grads0.merge(O)
    grads0.pass_on(PR)
    branches(0)
    grads1.take(F, n.gw_f)
    grads1.finish(F)
    l_normed_m0.need()
    across_blocks(grads0, F, normed_m0, n.d_hidden0, n.mine_f, False, FARTHEST_FIRST)
    n.small[0, 11:12, :] = jnp.sum(n.grad_full[:, own].astype(F32), axis=0, keepdims=True)
    unit_sums(n.d_hidden0, n.small.at[0], width)
    out_own = n.x1_full[:, own].astype(F32) + out_sum.own() + n.vec_all[1, 7:8, own]
    n.o_own[1] = out_own.astype(BF)
    n.o_own[0] = n.x1_full[:, own]

    def swap_copy(index, source, target):
        return rcopy(
            source.at[1 - s], target.at[s], n.sw_s.at[index], n.sw_r.at[index], section=1 - s
        )

    out_swap = swap_copy(0, n.o_own, n.o_out_rows)
    out_swap.start()
    out_keep = pltpu.make_async_copy(n.o_own.at[s], n.o_out_rows.at[s], n.local.at[0])
    out_keep.start()

    l_x0.need()
    l_wq0.need()
    gain_a, gain_m = n.vec_all[0, 0:1, :], n.vec_all[0, 1:2, :]
    lane_no = lax.broadcasted_iota(jnp.int32, (min(128, length), 128), 1)

    def row_sums(where, joined, unit, rstd):
        first = jnp.sum(joined, axis=1, keepdims=True)
        second = jnp.sum(joined * unit, axis=1, keepdims=True)
        both = jnp.where(lane_no == 0, first, jnp.where(lane_no == 1, second, 0.0))
        n.line_sums[:, where] = both.T[:8]
        unit0[where, :] = unit
        n.rstd[where, :] = jnp.broadcast_to(rstd, (rstd.shape[0], 128))

    def prepare_last(lane):
        exchange0.arrive(lane)
        d_projection(n.inbox, 0, n.cos, n.sin, rows, n.d_pre, n.small.at[0], lane_of(lane))
        d_norms(
            x_full, n.d_pre, wq0, d_normed0, gain_a, gain_m, n.total, n.low, n.sums.at[0],
            lane * length, length, row_sums,
        )

    grads0.merge(F)
    prepare_last(1)
    grad_sums[1].step(0)
    prepare_last(0)
    grad_sums[0].step(0)
    grad_sums[1].step(1)
    grads0.pass_on(F)

    def line_copy(step):
        return rcopy(
            n.line_sums, n.line_in.at[step], n.ls_s.at[step], n.ls_r.at[step],
            col=place.col_to(step),
        )

    def col_copy(step):
        target = place.col_to(step)
        piece = n.sums.at[:, :, pl.ds(pl.multiple_of(target * width, width), width)]
        return rcopy(piece, n.col_in.at[step], n.cs_s.at[step], n.cs_r.at[step], col=target)

    def row_copy(ds, step):
        index = ds * rows + step
        layer = lax.rem(s + ds, 2)
        return rcopy(
            n.small.at[layer], n.row_in.at[index], n.rw_s.at[index], n.rw_r.at[index],
            section=layer, row=place.row_to(step),
        )

    for step in range(1, cols):
        line_copy(step).start()
        col_copy(step).start()
    grads1.take(Q, n.gw_q)
    grads1.finish(Q)
    l_normed_a0.need()
    across_blocks(grads0, Q, normed_a0, n.d_pre, n.mine_q, True, FARTHEST_FIRST)
    grad_sums[1].step(2)
    grad_sums[0].step(1)
    for step in range(1, cols):
        col_copy(step).wait_recv()
    head = n.sums[:, :, own]
    for step in range(1, cols):
        head = head + n.col_in[step]
    n.small[:, :8, :] = head
    others = [(ds, step) for ds in range(2) for step in range(rows) if ds or step]
    for ds, step in others:
        row_copy(ds, step).start()
    grads0.merge(Q)
    saves = Saver(n.save)

    def take(kind, made, target):
        grads0.take(kind, made)
        saves.copy(made, target)

    grad_sums[0].step(2)
    grads0.pass_on(Q)
    take(PR, n.gw_p, n.o_gw_p)
    take(O, n.gw_o, n.o_gw_o)
    joined = n.line_sums[...]
    for step in range(1, cols):
        line_copy(step).wait_recv()
        joined = joined + n.line_in[step]
    wide = jnp.concatenate([joined, jnp.zeros((120, tokens), F32)], axis=0).T
    take(F, n.gw_f, n.o_gw_f)
    out_keep.wait()
    out_swap.wait()
    for lane in reversed(range(PARTS)):
        where = lane_of(lane)
        moved = (
            grad_sums[lane].own()
            - wide[where, 0:1] / full
            - unit0[where, own] * (wide[where, 1:2] / full)
        )
        n.o_own[0, where] = (
            n.grad_full[where, own].astype(F32) + n.rstd[where, 0:1] * moved
        ).astype(BF)
    n.o_own[1] = n.grad_full[:, own]
    grad_swap = swap_copy(1, n.o_own, n.o_grad_rows)
    grad_swap.start()
    grad_keep = pltpu.make_async_copy(n.o_own.at[s], n.o_grad_rows.at[s], n.local.at[1])
    grad_keep.start()
    mine = n.small[s]
    for ds, step in others:
        row_copy(ds, step).wait_recv()
        mine = mine + n.row_in[ds * rows + step]
    n.o_small[...] = mine
    take(Q, n.gw_q, n.o_gw_q)
    grad_keep.wait()
    grad_swap.wait()
    exchange0.finish()
    for exchange in outward:
        exchange.finish()
    out_sum.finish()
    for reduce in grad_sums:
        reduce.finish()
    for step in range(1, cols):
        line_copy(step).wait_send()
        col_copy(step).wait_send()
    for ds, step in others:
        row_copy(ds, step).wait_send()
    for kind in range(4):
        grads0.finish(kind)
    saves.finish()


def second_half(rows, cols, kept, lengths):
    tokens, full = kept.x1_full.shape
    width, units = full // cols, kept.hidden1.shape[1]
    total = rows * tokens
    hbm, vmem, smem = pl.ANY, pltpu.VMEM, pltpu.SMEM
    loaded = dict(
        qkvd1=kept.qkvd1, cot_full=kept.cot_full, d_hidden1=kept.d_hidden1, hidden1=kept.hidden1,
        x1_full=kept.x1_full, wq1=kept.wq1, d_normed1=kept.d_normed1, normed_m1=kept.normed_m1,
        normed_a1=kept.normed_a1, wo0=kept.wo0, wp0=kept.wp0, wf0=kept.wf0, slope0=kept.slope0,
        wo1=kept.wo1, out0=kept.out0, log0=kept.log0, attn_t0=kept.attn_t0,
    )
    later = dict(
        qkv0=kept.qkv0, hidden0=kept.hidden0, normed_m0=kept.normed_m0, normed_a0=kept.normed_a0,
        wq0=kept.wq0, x_full=kept.x_full, branch1=kept.branch1,
    )
    ins = {"i_" + name: (value, hbm) for name, value in {**loaded, **later}.items()}
    ins.update(
        lengths=(lengths, smem), vec_all=(kept.vec_all, vmem)
    )
    rows_low, rows_wide = ((tokens, full), BF), ((tokens, full), F32)
    wholes, pieces = grad_shapes(rows, full, width, units)
    outs = dict(
        o_out_rows=((2, tokens, width), BF, vmem), o_grad_rows=((2, tokens, width), BF, vmem),
        o_small=((16, width), F32, vmem),
    )
    outs.update({"o_gw_" + kind: (pieces[kind], F32, hbm) for kind in "qfop"})
    scratch = {name: pltpu.VMEM(value.shape, value.dtype) for name, value in loaded.items()}
    scratch.update(grad_scratch(rows, full, width, units))
    scratch.update({"gw_" + kind: pltpu.VMEM(pieces[kind], F32) for kind in "qfop"})
    scratch.update(
        grad_full=pltpu.VMEM(*rows_low), attn_t1=pltpu.VMEM((width, tokens), BF),
        d_hidden0=pltpu.VMEM((tokens, units), BF), d_out=pltpu.VMEM((HEAD_DIM, total), BF),
        result=pltpu.VMEM((4 * HEAD_DIM, total), BF),
        inbox=pltpu.VMEM((rows, 4 * HEAD_DIM, tokens), BF),
        pieces=pltpu.VMEM((rows, HEAD_DIM, tokens), BF),
        d_pre=pltpu.VMEM((tokens, 3 * width), BF),
        total=pltpu.VMEM(*rows_wide), low=pltpu.VMEM(*rows_low),
        from_left=pltpu.VMEM(*rows_low), from_right=pltpu.VMEM(*rows_low),
        o_left=pltpu.VMEM(*rows_low), o_right=pltpu.VMEM(*rows_low),
        scores=pltpu.VMEM((KEY_BLOCK, total // KEY_BLOCK * QUERY_BLOCK), F32),
        first=pltpu.VMEM((1, total), jnp.int32),
        cos=pltpu.VMEM((ROT // 2, tokens), F32), sin=pltpu.VMEM((ROT // 2, tokens), F32),
        key_rows=pltpu.VMEM((total, HEAD_DIM), BF), value_rows=pltpu.VMEM((total, HEAD_DIM), BF),
        key_acc=pltpu.VMEM((HEAD_DIM, total), F32), value_acc=pltpu.VMEM((HEAD_DIM, total), F32),
        sums=pltpu.VMEM((2, 8, full), F32), small=pltpu.VMEM((2, 16, width), F32),
        rstd=pltpu.VMEM((tokens, 128), F32),
        line_sums=pltpu.VMEM((8, tokens), F32), line_in=pltpu.VMEM((cols, 8, tokens), F32),
        col_in=pltpu.VMEM((cols, 2, 8, width), F32),
        row_in=pltpu.VMEM((2 * rows, 16, width), F32),
        o_own=pltpu.VMEM((2, tokens, width), BF),
        load=dma(LOADS), save=dma(4), local=dma(2),
        g1_s=dma(4, 8), g1_r=dma(4, 8), g0_s=dma(4, 8), g0_r=dma(4, 8),
        b1_s=dma(rows * PARTS), b1_r=dma(PARTS, rows), b1_l=dma(PARTS),
        b0_s=dma(rows * PARTS), b0_r=dma(PARTS, rows), b0_l=dma(PARTS),
        e_s=dma(PARTS, rows), e_r=dma(PARTS, rows), e_l=dma(PARTS),
        ls_s=dma(cols), ls_r=dma(cols), cs_s=dma(cols), cs_r=dma(cols),
        rw_s=dma(2 * rows), rw_r=dma(2 * rows), sw_s=dma(2), sw_r=dma(2),
    )
    for name in ("r_a", "r_b", "r_c", "r_d", "r_e", "r_f"):
        scratch[name] = dma(CHUNKS)
    for name in ("s_a", "s_b", "s_c", "s_d"):
        scratch[name] = dma(PARTS, cols)
    for name in ("o_a", "o_b", "o_c", "o_d"):
        scratch[name] = dma(1, cols)
    return Names().joined(named_call(partial(second_kernel, rows, cols), 3, ins, outs, scratch))


def finishing_kernel(n):
    into, out_of = Saver(n.into), Saver(n.out_of)
    moves = [
        (into.copy(source, held), held, target)
        for source, held, target in (
            (n.i_gw_p, n.h_gw_p, n.gw_p), (n.i_gw_f, n.h_gw_f, n.gw_f), (n.i_gw_q, n.h_gw_q, n.gw_q),
            (n.i_out_rows, n.h_out_rows, n.out_rows), (n.i_grad_rows, n.h_grad_rows, n.grad_rows),
            (n.i_gw_o, n.h_gw_o, n.gw_o),
        )
    ]
    for copy, held, target in moves:
        copy.wait()
        out_of.copy(held, target.at[0])
    width = n.small.shape[1]
    n.gains[0] = n.small[0:2]
    n.shifts[0] = n.small[2:4]
    for index in range(3):
        n.g_qkv[:, index * width : (index + 1) * width] = n.small[8 + index : 9 + index]
    n.g_out[...] = n.small[11:12]
    for index in range(n.g_fc.shape[1] // width):
        n.g_fc[:, index * width : (index + 1) * width] = n.small[12 + index : 13 + index]
    out_of.finish()


def finishing(k):
    hbm, vmem = pl.ANY, pltpu.VMEM
    made = dict(
        out_rows=k.out_rows, grad_rows=k.grad_rows, gw_q=k.gw_q, gw_f=k.gw_f, gw_o=k.gw_o,
        gw_p=k.gw_p,
    )
    ins = {"i_" + name: (value, hbm) for name, value in made.items()}
    ins.update(small=(k.small, vmem))
    width, units = k.small.shape[1], k.gw_f.shape[1]
    large = {name: ((1,) + value.shape, value.dtype, hbm) for name, value in made.items()}
    outs = dict(
        out_rows=None, grad_rows=None, gains=((1, 2, width), F32, vmem),
        shifts=((1, 2, width), F32, vmem), gw_q=None, g_qkv=((1, 3 * width), F32, vmem),
        gw_o=None, gw_f=None, g_fc=((1, units), F32, vmem), gw_p=None,
        g_out=((1, width), F32, vmem),
    )
    outs.update(large)
    scratch = {"h_" + name: pltpu.VMEM(value.shape, value.dtype) for name, value in made.items()}
    scratch.update(into=dma(len(made)), out_of=dma(len(made)))
    results = named_call(finishing_kernel, None, ins, outs, scratch)
    results.update(g_qkv=results.pop("g_qkv").reshape(1, 3, width))
    return tuple(results[name] for name in outs)


def relay_body(
    hidden_in,
    cotangent,
    lengths,
    norm_gains,
    norm_biases,
    w_qkv,
    b_qkv,
    w_out,
    w_fc,
    b_fc,
    w_proj,
    b_out,
):
    rows, cols = lax.axis_size(ROW), lax.axis_size(COL)
    blocks = (w_qkv[0], w_fc[0], w_out[0], w_proj[0])
    vectors = (norm_gains, norm_biases, b_qkv.reshape(1, -1), b_out, b_fc)
    kept = first_half(rows, cols, hidden_in, cotangent, vectors, blocks, lengths)
    return finishing(second_half(rows, cols, kept, lengths))


def fits(mesh):
    rows, cols = mesh.shape[ROW], mesh.shape[COL]
    return rows == cols == 4 and MODEL_WIDTH == rows * cols * HEAD_DIM


def solution(mesh):
    return jax.shard_map(
        relay_body if fits(mesh) else body,
        mesh=mesh,
        in_specs=(
            P(None, ROW, COL),
            P(None, ROW, COL),
            P(),
            P(SECTION, None, COL),
            P(SECTION, None, COL),
            P(SECTION, None, ROW, COL),
            P(SECTION, None, COL),
            P(SECTION, COL, ROW),
            P(SECTION, ROW, COL),
            P(SECTION, COL),
            P(SECTION, COL, ROW),
            P(SECTION, COL),
        ),
        out_specs=(
            P(SECTION, None, ROW, COL),
            P(SECTION, None, ROW, COL),
            P(SECTION, None, COL),
            P(SECTION, None, COL),
            P(SECTION, None, ROW, COL),
            P(SECTION, None, COL),
            P(SECTION, COL, ROW),
            P(SECTION, ROW, COL),
            P(SECTION, COL),
            P(SECTION, COL, ROW),
            P(SECTION, COL),
        ),
        check_vma=False,
    )
```

```python
from functools import partial
import math

import jax
import jax.numpy as jnp
from jax import lax
from jax.experimental import pallas as pl
from jax.experimental.pallas import tpu as pltpu
from jax.sharding import PartitionSpec as P

MODEL_WIDTH = 1024
HEAD_DIM = 64
ROT = 16
SECTION, ROW, COL = "section", "row", "col"


EPS = 1e-05
NEG = -1e30


def from_partner(value, axis, apart):
    mask = 2**apart
    pairs = [(source, source ^ mask) for source in range(lax.axis_size(axis))]
    return lax.ppermute(value, axis, pairs)


def segment_of(token_ids, starts):
    return jnp.sum((token_ids[:, None] >= starts[None, 1:]).astype(jnp.int32), axis=1)


def token_layout(lengths_row, token_ids):
    starts = jnp.cumsum(lengths_row) - lengths_row
    segment = segment_of(token_ids, starts)
    labels = jnp.arange(1, lengths_row.shape[0], dtype=jnp.int32)
    seg_begin = jnp.sum(jnp.where(segment[:, None] == labels[None, :], starts[None, 1:], 0), axis=1)
    position = jnp.where(segment == 0, token_ids, lengths_row[0] + token_ids - seg_begin)
    return (starts, segment, position)


def rotary_tables(position, turned):
    half_rot = turned // 2
    freqs = 10000.0 ** (-(2.0 * jnp.arange(half_rot, dtype=jnp.float32)) / turned)
    angles = position.astype(jnp.float32)[:, None] * freqs[None, :]
    return (jnp.cos(angles), jnp.sin(angles))


def rotate(values, cos_table, sin_table, direction):
    half_rot = cos_table.shape[-1]
    lower = values[..., :half_rot]
    upper = values[..., half_rot : 2 * half_rot]
    cos_cast = cos_table[:, None, :]
    sin_cast = direction * sin_table[:, None, :]
    return jnp.concatenate(
        [
            lower * cos_cast - upper * sin_cast,
            upper * cos_cast + lower * sin_cast,
            values[..., 2 * half_rot :],
        ],
        axis=-1,
    )


def permitted(query_seg, query_tok, key_seg, key_tok):
    from_prompt = (key_seg[None, :] == 0) & (query_seg[:, None] > 0)
    same_causal = (key_seg[None, :] == query_seg[:, None]) & (
        key_tok[None, :] <= query_tok[:, None]
    )
    return from_prompt | same_causal


def attend(running, key_piece, value_piece, query3, layout):
    run_max, run_sum, totals = running
    piece_len = key_piece.shape[0]
    key3 = key_piece.reshape(piece_len, query3.shape[1], query3.shape[2])
    value3 = value_piece.reshape(piece_len, query3.shape[1], query3.shape[2])
    key_tok = jnp.arange(piece_len, dtype=jnp.int32)
    key_seg = segment_of(key_tok, layout["starts"])
    allowed = permitted(layout["segment"], layout["tokens"], key_seg, key_tok)[None]
    scores = jnp.einsum("qhd,khd->hqk", query3, key3, preferred_element_type=jnp.float32) * (
        1.0 / math.sqrt(query3.shape[2])
    )
    masked = jnp.where(allowed, scores, NEG)
    new_max = jnp.maximum(run_max, jnp.max(masked, axis=-1))
    weights = jnp.where(allowed, jnp.exp(masked - new_max[..., None]), 0.0)
    run_sum = jnp.sum(weights, axis=-1)
    totals = jnp.einsum(
        "hqk,khd->hqd", weights.astype(jnp.bfloat16), value3, preferred_element_type=jnp.float32
    )
    return (new_max, run_sum, totals)


def layer_forward(x, full, weights, layout, complete_gains, complete_shifts):
    w_query, b_query, w_output, w_hidden, b_hidden, w_project, b_output = weights
    row_tokens, local_width = x.shape
    heads_local = local_width // HEAD_DIM
    shaped = (row_tokens, heads_local, HEAD_DIM)
    as_float = full.astype(jnp.float32)
    row_mean = jnp.mean(as_float, axis=1, keepdims=True)
    centred = as_float - row_mean
    rstd = lax.rsqrt(jnp.mean(centred * centred, axis=1, keepdims=True) + EPS)
    unit = centred * rstd
    normed_a = (unit * complete_gains[0] + complete_shifts[0]).astype(jnp.bfloat16)
    normed_m = (unit * complete_gains[1] + complete_shifts[1]).astype(jnp.bfloat16)
    projected = (
        jnp.einsum("td,cde->cte", normed_a, w_query, preferred_element_type=jnp.float32)
        + b_query[:, None, :]
    )
    cos_table, sin_table = layout["cos_table"], layout["sin_table"]
    query3 = rotate(projected[0].reshape(shaped), cos_table, sin_table, 1.0).astype(jnp.bfloat16)
    key_flat = (
        rotate(projected[1].reshape(shaped), cos_table, sin_table, 1.0)
        .reshape(row_tokens, local_width)
        .astype(jnp.bfloat16)
    )
    value_flat = projected[2].astype(jnp.bfloat16)
    key_full = lax.all_gather(key_flat, ROW, axis=0, tiled=True)
    value_full = lax.all_gather(value_flat, ROW, axis=0, tiled=True)
    initial = (
        jnp.full((heads_local, row_tokens), NEG, jnp.float32),
        jnp.zeros((heads_local, row_tokens), jnp.float32),
        jnp.zeros((heads_local, row_tokens, HEAD_DIM), jnp.float32),
    )
    run_max, run_sum, totals = attend(initial, key_full, value_full, query3, layout)
    out_exact = totals / run_sum[..., None]
    log_sum = run_max + jnp.log(run_sum)
    attn_flat = (
        jnp.transpose(out_exact, (1, 0, 2)).reshape(row_tokens, local_width).astype(jnp.bfloat16)
    )
    hidden_pre = jnp.dot(normed_m, w_hidden, preferred_element_type=jnp.float32) + b_hidden
    hidden = jax.nn.gelu(hidden_pre, approximate=False).astype(jnp.bfloat16)
    branch = jnp.dot(attn_flat, w_output, preferred_element_type=jnp.float32) + jnp.dot(
        hidden, w_project, preferred_element_type=jnp.float32
    )
    summed = lax.psum_scatter(
        branch.astype(jnp.bfloat16), COL, scatter_dimension=1, tiled=True
    ).astype(jnp.float32)
    output = (x.astype(jnp.float32) + summed + b_output).astype(jnp.bfloat16)
    state = dict(
        unit=unit, rstd=rstd, normed_a=normed_a, normed_m=normed_m, query3=query3,
        key_full=key_full, value_full=value_full, attn_flat=attn_flat, out_exact=out_exact,
        log_sum=log_sum, hidden_pre=hidden_pre, hidden=hidden,
    )
    return output, state


def layer_backward(state, grad_in, grad_full, weights, layout, complete_gains, scatter_tokens):
    w_query, b_query, w_output, w_hidden, b_hidden, w_project, b_output = weights
    row_tokens = state["normed_a"].shape[0]
    local_width = w_output.shape[0]
    heads_local = local_width // HEAD_DIM
    shaped = (row_tokens, heads_local, HEAD_DIM)
    score_scale = 1.0 / math.sqrt(HEAD_DIM)
    total_tokens = state["key_full"].shape[0]
    key_block = min(512, total_tokens)
    grad_wout = jnp.einsum(
        "te,td->ed", state["attn_flat"], grad_full, preferred_element_type=jnp.float32
    )
    grad_wproj = jnp.einsum(
        "tf,td->fd", state["hidden"], grad_full, preferred_element_type=jnp.float32
    )
    grad_bout = jnp.sum(grad_in.astype(jnp.float32), axis=0)
    grad_attn = jnp.einsum(
        "td,ed->te", grad_full, w_output, preferred_element_type=jnp.float32
    ).astype(jnp.bfloat16)
    grad_hidden = jnp.einsum("td,fd->tf", grad_full, w_project, preferred_element_type=jnp.float32)
    gelu_value, gelu_back = jax.vjp(partial(jax.nn.gelu, approximate=False), state["hidden_pre"])
    grad_hpre = gelu_back(grad_hidden)[0].astype(jnp.bfloat16)
    grad_wfc = jnp.einsum(
        "td,tf->df", state["normed_m"], grad_hpre, preferred_element_type=jnp.float32
    )
    grad_bfc = jnp.sum(grad_hpre.astype(jnp.float32), axis=0)
    grad_normed_m = jnp.einsum("tf,df->td", grad_hpre, w_hidden, preferred_element_type=jnp.float32)
    grad_out3 = grad_attn.reshape(shaped)
    query3 = state["query3"]
    delta = jnp.sum(
        jnp.transpose(grad_out3.astype(jnp.float32), (1, 0, 2)) * state["out_exact"], axis=-1
    )
    grad_query = jnp.zeros(shaped, jnp.float32)
    key_terms = []
    value_terms = []
    for block_no in range(total_tokens // key_block):
        begin_at = block_no * key_block
        key_part = state["key_full"][begin_at : begin_at + key_block].reshape(
            key_block, heads_local, HEAD_DIM
        )
        value_part = state["value_full"][begin_at : begin_at + key_block].reshape(
            key_block, heads_local, HEAD_DIM
        )
        key_tok = begin_at + jnp.arange(key_block, dtype=jnp.int32)
        key_seg = segment_of(key_tok, layout["starts"])
        allowed = permitted(layout["segment"], layout["tokens"], key_seg, key_tok)[None]
        scores = (
            jnp.einsum("qhd,khd->hqk", query3, key_part, preferred_element_type=jnp.float32)
            * score_scale
        )
        probs = jnp.where(
            allowed,
            jnp.exp(jnp.where(allowed, scores, NEG) - state["log_sum"][..., None]),
            0.0,
        )
        grad_probs = jnp.einsum(
            "qhd,khd->hqk", grad_out3, value_part, preferred_element_type=jnp.float32
        )
        grad_scores = (probs * (grad_probs - delta[..., None])).astype(jnp.bfloat16)
        grad_query = grad_query + jnp.einsum(
            "hqk,khd->qhd", grad_scores, key_part, preferred_element_type=jnp.float32
        )
        key_terms.append(
            jnp.einsum(
                "hqk,qhd->khd", grad_scores, query3, preferred_element_type=jnp.float32
            ).reshape(key_block, local_width)
            * score_scale
        )
        value_terms.append(
            jnp.einsum(
                "hqk,qhd->khd",
                probs.astype(jnp.bfloat16),
                grad_out3,
                preferred_element_type=jnp.float32,
            ).reshape(key_block, local_width)
        )
    grad_query = grad_query * score_scale
    kv_terms = jnp.concatenate(
        [jnp.concatenate(key_terms, axis=0), jnp.concatenate(value_terms, axis=0)], axis=1
    )
    kv_grads = lax.psum_scatter(
        kv_terms.astype(jnp.bfloat16), ROW, scatter_dimension=0, tiled=True
    ).astype(jnp.float32)
    grad_key = kv_grads[:, :local_width].reshape(shaped)
    grad_value = kv_grads[:, local_width:]
    cos_table, sin_table = layout["cos_table"], layout["sin_table"]
    grad_pre = jnp.stack(
        [
            rotate(grad_query, cos_table, sin_table, -1.0).reshape(row_tokens, local_width),
            rotate(grad_key, cos_table, sin_table, -1.0).reshape(row_tokens, local_width),
            grad_value,
        ]
    ).astype(jnp.bfloat16)
    grad_wqkv = jnp.einsum(
        "td,cte->cde", state["normed_a"], grad_pre, preferred_element_type=jnp.float32
    )
    grad_bqkv = jnp.sum(grad_pre.astype(jnp.float32), axis=1)
    grad_normed_a = jnp.einsum("cte,cde->td", grad_pre, w_query, preferred_element_type=jnp.float32)
    unit = state["unit"]
    grad_gains = jnp.stack(
        [jnp.sum(grad_normed_a * unit, axis=0), jnp.sum(grad_normed_m * unit, axis=0)]
    )
    grad_shifts = jnp.stack([jnp.sum(grad_normed_a, axis=0), jnp.sum(grad_normed_m, axis=0)])
    grad_unit = grad_normed_a * complete_gains[0] + grad_normed_m * complete_gains[1]
    big = (grad_wqkv, grad_wout, grad_wfc, grad_wproj)
    big = tuple(member.astype(jnp.bfloat16) for member in big)
    shared = (grad_gains, grad_shifts)
    local = (grad_bqkv, grad_bfc, grad_bout)
    if scatter_tokens:
        piece = lax.psum_scatter(
            grad_unit.astype(jnp.bfloat16), COL, scatter_dimension=0, tiled=True
        ).astype(jnp.float32)
        rows = piece.shape[0]
        start = lax.axis_index(COL) * rows
        unit_part = lax.dynamic_slice_in_dim(unit, start, rows, 0)
        rstd_part = lax.dynamic_slice_in_dim(state["rstd"], start, rows, 0)
        grad_part = lax.dynamic_slice_in_dim(grad_full, start, rows, 0).astype(jnp.float32)
        moved = (
            piece
            - jnp.mean(piece, axis=1, keepdims=True)
            - unit_part * jnp.mean(piece * unit_part, axis=1, keepdims=True)
        )
        grad_input = (grad_part + rstd_part * moved).astype(jnp.bfloat16)
    else:
        sums = lax.psum(
            jnp.stack([jnp.sum(grad_unit, axis=1), jnp.sum(grad_unit * unit, axis=1)]), COL
        )
        piece = lax.psum_scatter(
            grad_unit.astype(jnp.bfloat16), COL, scatter_dimension=1, tiled=True
        ).astype(jnp.float32)
        width = piece.shape[1]
        unit_part = lax.dynamic_slice_in_dim(unit, lax.axis_index(COL) * width, width, 1)
        moved = (
            piece
            - sums[0][:, None] / MODEL_WIDTH
            - unit_part * (sums[1][:, None] / MODEL_WIDTH)
        )
        grad_input = (grad_in.astype(jnp.float32) + state["rstd"] * moved).astype(jnp.bfloat16)
    return grad_input, big, shared, local


def body(
    hidden_in,
    cotangent,
    lengths,
    norm_gains,
    norm_biases,
    w_qkv,
    b_qkv,
    w_out,
    w_fc,
    b_fc,
    w_proj,
    b_out,
):
    row_tokens = hidden_in.shape[1]
    local_width = hidden_in.shape[2]
    section = lax.axis_index(SECTION)
    is_first = section == 0
    my_tokens = lax.axis_index(ROW) * row_tokens + jnp.arange(row_tokens, dtype=jnp.int32)
    x0 = lax.dynamic_index_in_dim(hidden_in, section, 0, keepdims=False)
    cot = lax.dynamic_index_in_dim(cotangent, section, 0, keepdims=False)
    lengths_row = lax.dynamic_index_in_dim(lengths, section, 0, keepdims=False)
    starts, segment, position = token_layout(lengths_row, my_tokens)
    cos_table, sin_table = rotary_tables(position, ROT)
    layout = {
        "starts": starts,
        "segment": segment,
        "tokens": my_tokens,
        "cos_table": cos_table,
        "sin_table": sin_table,
    }
    both = (SECTION, ROW)
    gains = lax.all_gather(norm_gains[0], (SECTION, COL), axis=0)
    shifts = lax.all_gather(norm_biases[0], (SECTION, COL), axis=0)
    cols = lax.axis_size(COL)

    def whole(vectors):
        split = vectors.reshape(2, cols, 2, local_width)
        return jnp.transpose(split, (0, 2, 1, 3)).reshape(2, 2, cols * local_width)

    gains, shifts = whole(gains), whole(shifts)
    biases = [lax.all_gather(member[0], SECTION, axis=0) for member in (b_qkv, b_fc, b_out)]
    x0_full = lax.all_gather(x0, COL, axis=1, tiled=True)
    rows = lax.axis_size(ROW)

    def unite(member, axis):
        gathered = lax.all_gather(member[0], both, axis=0)
        pieces = gathered.reshape((2, rows) + gathered.shape[1:])
        return [
            jnp.concatenate([pieces[layer, row] for row in range(rows)], axis=axis)
            for layer in range(2)
        ]

    w_query, w_hidden = unite(w_qkv, 1), unite(w_fc, 0)
    w_output, w_project = unite(w_out, 1), unite(w_proj, 1)
    weights = [
        (
            w_query[layer],
            biases[0][layer],
            w_output[layer],
            w_hidden[layer],
            biases[1][layer],
            w_project[layer],
            biases[2][layer],
        )
        for layer in range(2)
    ]
    out0, state0 = layer_forward(x0, x0_full, weights[0], layout, gains[0], shifts[0])
    x1_full = lax.all_gather(out0, COL, axis=1, tiled=True)
    cot_full = lax.all_gather(cot, COL, axis=1, tiled=True)
    out1, state1 = layer_forward(out0, x1_full, weights[1], layout, gains[1], shifts[1])
    grad1_part, big1, shared1, local1 = layer_backward(
        state1, cot, cot_full, weights[1], layout, gains[1], True
    )
    grad1_full = lax.all_gather(grad1_part, COL, axis=0, tiled=True)
    grad1 = lax.dynamic_slice_in_dim(
        grad1_full, lax.axis_index(COL) * local_width, local_width, 1
    )
    grad0, big0, shared0, local0 = layer_backward(
        state0, grad1, grad1_full, weights[0], layout, gains[0], False
    )

    def swap(first, second):
        mine = jnp.where(is_first, first, second)
        theirs = from_partner(jnp.where(is_first, second, first), SECTION, 0)
        return jnp.where(is_first, jnp.stack([mine, theirs]), jnp.stack([theirs, mine]))[None]

    out_rows = swap(out0, out1)
    grad_rows = swap(grad0, grad1)

    def scatter(first, second, axis):
        length = first.shape[axis] // rows
        pieces = jnp.stack(
            [
                lax.slice_in_dim(member, row * length, (row + 1) * length, axis=axis)
                for member in (first, second)
                for row in range(rows)
            ]
        )
        return lax.psum_scatter(pieces, both, scatter_dimension=0, tiled=True).astype(jnp.float32)

    large = [scatter(a, b, axis) for a, b, axis in zip(big0, big1, (1, 1, 0, 1))]
    shared_sums = lax.psum(
        tuple(jnp.stack([a, b]) for a, b in zip(shared0, shared1)), (SECTION, ROW, COL)
    )
    shared_mine = [
        lax.dynamic_slice(
            member,
            (section, 0, lax.axis_index(COL) * local_width),
            (1, 2, local_width),
        )
        for member in shared_sums
    ]
    local_sums = lax.psum(tuple(jnp.stack([a, b]) for a, b in zip(local0, local1)), both)
    local_mine = [lax.dynamic_index_in_dim(member, section, 0) for member in local_sums]
    return (
        out_rows,
        grad_rows,
        shared_mine[0],
        shared_mine[1],
        large[0],
        local_mine[0],
        large[1],
        large[2],
        local_mine[1],
        large[3],
        local_mine[2],
    )


BF = jnp.bfloat16
F32 = jnp.float32
BY_MESH = pl.DeviceIdType.MESH
VMEM_LIMIT = 62 * 2**20
QUERY_BLOCK = 256
KEY_BLOCK = 512
PROMPT_LEAST = 768
PARTS = 2
CHUNKS = 16
LOADS = 24
LAG = 4


def dot(a, b, contract=((1,), (0,))):
    return lax.dot_general(a, b, (contract, ((), ())), preferred_element_type=F32)


def rcopy(src, dst, ssem, rsem, **device):
    return pltpu.make_async_remote_copy(
        src_ref=src,
        dst_ref=dst,
        send_sem=ssem,
        recv_sem=rsem,
        device_id=device,
        device_id_type=BY_MESH,
    )


class Place:
    def __init__(self, rows, cols):
        self.rows, self.cols = rows, cols
        self.s = lax.axis_index(SECTION)
        self.r = lax.axis_index(ROW)
        self.c = lax.axis_index(COL)

    def row_to(self, step):
        return lax.rem(self.r + step, self.rows)

    def row_from(self, step):
        return lax.rem(self.r + self.rows - step, self.rows)

    def beside(self, way):
        if way == 0:
            return self.r + 1 - 2 * lax.rem(self.r, 2)
        return lax.rem(self.r + 2, 4)

    def across(self):
        return 3 - self.r

    def col_to(self, step):
        return lax.rem(self.c + step, self.cols)

    def col_from(self, step):
        return lax.rem(self.c + self.cols - step, self.cols)

    def greet(self, rows=False, cols=False, partner=False, cross_cols=False, cross_rows=False):
        barrier = pltpu.get_barrier_semaphore()
        count = 0

        def signal(**device):
            pl.semaphore_signal(barrier, inc=1, device_id=device, device_id_type=BY_MESH)

        if rows:
            for step in range(1, self.rows):
                signal(row=self.row_to(step))
                count += 1
        if cols:
            for step in range(1, self.cols):
                signal(col=self.col_to(step))
                count += 1
        if partner:
            signal(section=1 - self.s)
            count += 1
        if cross_cols:
            for step in range(1, self.cols):
                signal(section=1 - self.s, col=self.col_to(step))
                count += 1
        if cross_rows:
            for step in range(1, self.rows):
                signal(section=1 - self.s, row=self.row_to(step))
                count += 1
        pl.semaphore_wait(barrier, count)


class LineGather:
    def __init__(self, place, view, send_right, send_left, recv, lane=0):
        self.place, self.view, self.lane = place, view, lane
        self.send_right, self.send_left, self.recv = send_right, send_left, recv

    def right(self, block):
        return rcopy(
            self.view(block), self.view(block), self.send_right.at[self.lane, block],
            self.recv.at[self.lane, block],
            col=lax.rem(self.place.c + 1, self.place.cols),
        )

    def left(self, block):
        cols = self.place.cols
        return rcopy(
            self.view(block), self.view(block), self.send_left.at[self.lane, block],
            self.recv.at[self.lane, block],
            col=lax.rem(self.place.c + cols - 1, cols),
        )

    def hop(self, distance):
        c, cols = self.place.c, self.place.cols

        @pl.when(c >= distance)
        def _():
            block = lax.rem(c + cols - distance, cols)
            if distance:
                self.right(block).wait_recv()

            @pl.when(c < cols - 1)
            def _():
                self.right(block).start()

        @pl.when(c + distance < cols)
        def _():
            block = lax.rem(c + distance, cols)
            if distance:
                self.left(block).wait_recv()

            @pl.when(c > 0)
            def _():
                self.left(block).start()

    def finish(self):
        c, cols = self.place.c, self.place.cols
        for distance in range(cols):

            @pl.when((c >= distance) & (c < cols - 1))
            def _():
                self.right(lax.rem(c + cols - distance, cols)).wait_send()

            @pl.when((c + distance < cols) & (c > 0))
            def _():
                self.left(lax.rem(c + distance, cols)).wait_send()


class WeightGather:
    def __init__(self, place, layer, own, full, send, recv, local):
        self.place, self.layer, self.own, self.full = place, layer, own, full
        self.send, self.recv, self.local = send, recv, local

    def view(self, kind, block, half=None):
        lines = self.own[kind].shape[-2]
        length = self.own[kind].shape[-2 if kind in (0, 1) else -1]
        at, count = (0, lines) if half is None else (half * (lines // 2), lines // 2)
        if kind in (0, 1):
            piece = pl.ds(pl.multiple_of(block * length + at, count), count)
            return self.full[kind].at[:, piece, :] if kind == 0 else self.full[1].at[piece, :]
        piece = pl.ds(pl.multiple_of(block * length, length), length)
        return self.full[kind].at[at : at + count, piece]

    def direct(self, kind, way):
        place = self.place
        return rcopy(
            self.own[kind], self.view(kind, place.r), self.send.at[kind, way],
            self.recv.at[kind, way], row=place.beside(way),
        )

    def relayed(self, kind, way):
        place = self.place
        piece = self.view(kind, place.beside(way), way)
        return rcopy(
            piece, piece, self.send.at[kind, 2 + way], self.recv.at[kind, 2 + way],
            row=place.beside(1 - way),
        )

    def arriving(self, kind, way):
        block = self.view(kind, self.place.beside(way))
        return rcopy(
            block, block, self.send.at[kind, way], self.recv.at[kind, way],
            row=self.place.beside(way),
        )

    def across(self, kind, way):
        piece = self.view(kind, self.place.across(), way)
        return rcopy(
            piece, piece, self.send.at[kind, 2 + way], self.recv.at[kind, 2 + way],
            row=self.place.beside(1 - way),
        )

    def to_partner(self, kind, which):
        place = self.place
        source = (place.beside(0), place.beside(1), place.across(), place.r)[which]
        block = self.view(kind, source)
        return rcopy(
            self.own[kind] if which == 3 else block, block, self.send.at[kind, 4 + which],
            self.recv.at[kind, 4 + which], section=1 - place.s,
        )

    def keep(self, kind):
        return pltpu.make_async_copy(
            self.own[kind], self.view(kind, self.place.r), self.local.at[kind]
        )

    def start(self, kind):
        @pl.when(self.place.s == self.layer)
        def _():
            for way in range(2):
                self.direct(kind, way).start()
            self.keep(kind).start()
            self.to_partner(kind, 3).start()

    def relay(self, kind):
        @pl.when(self.place.s == self.layer)
        def _():
            for way in range(2):
                self.arriving(kind, way).wait_recv()
                self.relayed(kind, way).start()
                self.to_partner(kind, way).start()

    def forward(self, kind):
        @pl.when(self.place.s == self.layer)
        def _():
            for way in range(2):
                self.across(kind, way).wait_recv()
            self.to_partner(kind, 2).start()
            self.keep(kind).wait()

    def ready(self, kind):
        @pl.when(self.place.s != self.layer)
        def _():
            for which in range(4):
                self.to_partner(kind, which).wait_recv()

    def finish(self, kind):
        @pl.when(self.place.s == self.layer)
        def _():
            for way in range(2):
                self.direct(kind, way).wait_send()
                self.relayed(kind, way).wait_send()
            for which in range(4):
                self.to_partner(kind, which).wait_send()


class RowExchange:
    def __init__(self, place, piece_for, slot_of, send, recv, local):
        self.place, self.piece_for, self.slot_of = place, piece_for, slot_of
        self.send, self.recv, self.local = send, recv, local

    def out(self, step):
        place = self.place
        target = place.row_to(step)
        return rcopy(
            self.piece_for(target), self.slot_of(place.r), self.send.at[step], self.recv.at[step],
            row=target,
        )

    def into(self, step):
        slot = self.slot_of(self.place.row_from(step))
        return rcopy(
            slot, slot, self.send.at[step], self.recv.at[step], row=self.place.row_to(step)
        )

    def keep(self):
        return pltpu.make_async_copy(
            self.piece_for(self.place.r), self.slot_of(self.place.r), self.local
        )

    def start(self):
        for step in range(1, self.place.rows):
            self.out(step).start()
        self.keep().start()

    def arrive(self):
        for step in range(1, self.place.rows):
            self.into(step).wait_recv()
        self.keep().wait()

    def finish(self):
        for step in range(1, self.place.rows):
            self.out(step).wait_send()


def norm_rows(source, gains_a, shifts_a, gains_m, shifts_m, normed_a, normed_m, begin=0, count=None):
    count = source.shape[0] if count is None else count
    tile = min(128, count)

    @pl.loop(0, count // tile)
    def _(index):
        rows = pl.ds(pl.multiple_of(begin + index * tile, tile), tile)
        values = source[rows, :].astype(F32)
        centred = values - jnp.mean(values, axis=1, keepdims=True)
        unit = centred * lax.rsqrt(jnp.mean(centred * centred, axis=1, keepdims=True) + EPS)
        normed_a[rows, :] = (unit * gains_a + shifts_a).astype(BF)
        normed_m[rows, :] = (unit * gains_m + shifts_m).astype(BF)


def turn(block, cos, sin, direction):
    half = cos.shape[0]
    lower, upper, rest = block[:half], block[half : 2 * half], block[2 * half :]
    return jnp.concatenate(
        [
            lower * cos - upper * (direction * sin),
            upper * cos + lower * (direction * sin),
            rest,
        ],
        axis=0,
    )


def project_heads(normed_a, w_query, bias_rows, cos, sin, pieces, heads, where):
    for kind in range(3):
        flipped = (dot(normed_a[where, :], w_query[kind]) + bias_rows(kind)).T
        for head in range(heads):
            block = flipped[head * HEAD_DIM : (head + 1) * HEAD_DIM]
            if kind < 2:
                block = turn(block, cos[:, where], sin[:, where], 1.0)
            pieces[head, kind * HEAD_DIM : (kind + 1) * HEAD_DIM, where] = block.astype(BF)


def feed_forward(normed_m, w_hidden, bias_of, hidden, slope, where):
    tile = min(256, w_hidden.shape[1])

    @pl.loop(0, w_hidden.shape[1] // tile)
    def _(index):
        cols = pl.ds(pl.multiple_of(index * tile, tile), tile)
        pre = dot(normed_m[where, :], w_hidden[:, cols]) + bias_of(index)
        phi = 0.5 * (1.0 + lax.erf(pre * math.sqrt(0.5)))
        hidden[where, cols] = (pre * phi).astype(BF)
        turned = phi + pre * (jnp.exp(-0.5 * pre * pre) * (1.0 / math.sqrt(2.0 * math.pi)))
        slope[where, cols] = turned.astype(slope.dtype)


def times_tiles(left, right, out, convert=None, contract=((1,), (0,)), where=slice(None)):
    tile = min(256, out.shape[1])

    @pl.loop(0, out.shape[1] // tile)
    def _(index):
        cols = pl.ds(pl.multiple_of(index * tile, tile), tile)
        piece = right[:, cols] if contract[1] == (0,) else right[cols, :]
        value = dot(left[where, :], piece, contract)
        out[where, cols] = value if convert is None else convert(value, cols)


def dma(*shape):
    return pltpu.SemaphoreType.DMA(shape)


def key_mask(prompt, first, cols, key_at, query_at, keys, queries):
    in_prompt = key_at + keys <= PROMPT_LEAST
    before = key_at + keys <= query_at + 1
    if in_prompt and before:
        return None
    key = lax.broadcasted_iota(jnp.int32, (keys, queries), 0) + key_at
    allowed = None
    if not in_prompt:
        allowed = (key < prompt) | (key >= first[:, cols])
    if not before:
        causal = key <= lax.broadcasted_iota(jnp.int32, (keys, queries), 1) + query_at
        allowed = causal if allowed is None else allowed & causal
    return allowed


def rows_of_keys(qkv, at, rows):
    rows[...] = qkv[at : at + HEAD_DIM, :].astype(F32).T.astype(BF)


def key_blocks(query_at, queries):
    last = query_at + queries
    return [(at, min(KEY_BLOCK, last - at)) for at in range(0, last, KEY_BLOCK)]


def scaled_query(qkv, cols):
    return (qkv[:HEAD_DIM, cols].astype(F32) * (1.0 / math.sqrt(HEAD_DIM))).astype(BF)


def score_block(prompt, first, cols, query_at, key_at, keys, key_rows, query):
    scores = dot(key_rows[key_at : key_at + keys, :], query)
    allowed = key_mask(prompt, first, cols, key_at, query_at, keys, query.shape[1])
    return scores if allowed is None else jnp.where(allowed, scores, NEG)


def attend_block(block, size, prompt, first, qkv, key_rows, scores, spot, keep_weights=False):
    query_at = block * size
    cols = slice(query_at, query_at + size)
    query = scaled_query(qkv, cols)
    blocks = key_blocks(query_at, size)
    top = None
    for key_at, keys in blocks:
        piece = score_block(prompt, first, cols, query_at, key_at, keys, key_rows, query)
        scores[spot(key_at, keys)] = piece
        highest = jnp.max(piece, axis=0, keepdims=True)
        top = highest if top is None else jnp.maximum(top, highest)
    weight, totals = None, None
    for key_at, keys in blocks:
        probs = jnp.exp(scores[spot(key_at, keys)] - top)
        if keep_weights:
            scores[spot(key_at, keys)] = probs
        part = jnp.sum(probs, axis=0, keepdims=True)
        product = dot(qkv[2 * HEAD_DIM : 3 * HEAD_DIM, key_at : key_at + keys], probs.astype(BF))
        weight = part if weight is None else weight + part
        totals = product if totals is None else totals + product
    return totals / weight, top, weight


def gradient_block(
    block, size, qkv, d_out, delta, probs_of, key_rows, value_rows, key_acc, value_acc, opening
):
    query_at = block * size
    cols = slice(query_at, query_at + size)
    query = scaled_query(qkv, cols)
    d_query = d_out[:, cols]
    d_sum = None
    for key_at, keys in key_blocks(query_at, size):
        where = slice(key_at, key_at + keys)
        probs = probs_of(key_at, keys, query)
        d_probs = dot(value_rows[where, :], d_query)
        d_scores = (probs * (d_probs - delta)).astype(BF)
        d_key = dot(query, d_scores, ((1,), (1,)))
        d_value = dot(d_query, probs.astype(BF), ((1,), (1,)))
        if opening:
            key_acc[:, where] = d_key
            value_acc[:, where] = d_value
        else:
            key_acc[:, where] += d_key
            value_acc[:, where] += d_value
        part = dot(qkv[HEAD_DIM : 2 * HEAD_DIM, where], d_scores)
        d_sum = part if d_sum is None else d_sum + part
    return d_sum * (1.0 / math.sqrt(HEAD_DIM))


class LineReduce:
    def __init__(self, place, total, low, from_left, from_right, view, sems, lane=0):
        self.place, self.total, self.low, self.view, self.lane = place, total, low, view, lane
        self.from_left, self.from_right = from_left, from_right
        self.send_right, self.send_left, self.recv_left, self.recv_right = sems

    def right(self, owner):
        return rcopy(
            self.low.at[self.view(owner)], self.from_left.at[self.view(owner)],
            self.send_right.at[self.lane, owner], self.recv_left.at[self.lane, owner],
            col=lax.rem(self.place.c + 1, self.place.cols),
        )

    def left(self, owner):
        cols = self.place.cols
        return rcopy(
            self.low.at[self.view(owner)], self.from_right.at[self.view(owner)],
            self.send_left.at[self.lane, owner], self.recv_right.at[self.lane, owner],
            col=lax.rem(self.place.c + cols - 1, cols),
        )

    def add_in(self, owner, arrived):
        view = self.view(owner)
        self.low[view] = (self.total[view] + arrived[view].astype(F32)).astype(BF)

    def step(self, time):
        c, cols = self.place.c, self.place.cols

        @pl.when(c <= time)
        def _():
            owner = cols - 1 - time + c

            @pl.when(c > 0)
            def _():
                self.right(owner).wait_recv()
                self.add_in(owner, self.from_left)

            self.right(owner).start()

        @pl.when(c >= cols - 1 - time)
        def _():
            owner = time + c - (cols - 1)

            @pl.when(c < cols - 1)
            def _():
                self.left(owner).wait_recv()
                self.add_in(owner, self.from_right)

            self.left(owner).start()

    def own(self):
        c, cols = self.place.c, self.place.cols
        view = self.view(c)

        @pl.when(c > 0)
        def _():
            self.right(c).wait_recv()

        @pl.when(c == 0)
        def _():
            self.from_left[view] = jnp.zeros_like(self.from_left[view])

        @pl.when(c < cols - 1)
        def _():
            self.left(c).wait_recv()

        @pl.when(c == cols - 1)
        def _():
            self.from_right[view] = jnp.zeros_like(self.from_right[view])

        return (
            self.total[view] + self.from_left[view].astype(F32) + self.from_right[view].astype(F32)
        )

    def finish(self):
        c, cols = self.place.c, self.place.cols
        for time in range(cols - 1):

            @pl.when(c <= time)
            def _():
                self.right(cols - 1 - time + c).wait_send()

            @pl.when(c >= cols - 1 - time)
            def _():
                self.left(time + c - (cols - 1)).wait_send()


def center_sum(place, total, low, from_outer, from_inner, full, sems, order, prepare, produce, after, work):
    c = place.c
    a_send, a_recv, b_send, b_recv, c_send, c_recv = sems
    count = len(order)
    size = total.shape[0] // count
    inner = (c == 1) | (c == 2)
    outer = (c == 0) | (c == 3)
    pair = jnp.where(c < 2, 1 - c, 5 - c)
    middle = 3 - c
    group = count // 4

    def rows(index):
        return slice(order[index] * size, (order[index] + 1) * size)

    def inward(index):
        piece = rows(index)
        return rcopy(
            low.at[piece], from_outer.at[piece], a_send.at[index], a_recv.at[index], col=pair
        )

    def exchange(index):
        piece = rows(index)
        return rcopy(
            low.at[piece], from_inner.at[piece], b_send.at[index], b_recv.at[index], col=middle
        )

    def outward(index):
        piece = rows(index)
        return rcopy(full.at[piece], full.at[piece], c_send.at[index], c_recv.at[index], col=pair)

    prepare(0)
    for time in range(count + 2 * LAG):
        if time < count:

            @pl.when(outer)
            def _():
                inward(time).start()

            @pl.when(inner)
            def _():
                piece = rows(time)
                inward(time).wait_recv()
                low[piece, :] = (total[piece, :] + from_outer[piece, :].astype(F32)).astype(BF)
                exchange(time).start()

        if LAG <= time < count + LAG:

            @pl.when(inner)
            def _():
                index = time - LAG
                piece = rows(index)
                exchange(index).wait_recv()
                summed = low[piece, :].astype(F32) + from_inner[piece, :].astype(F32)
                full[piece, :] = produce(summed, piece)
                outward(index).start()

        if time >= 2 * LAG:

            @pl.when(outer)
            def _():
                outward(time - 2 * LAG).wait_recv()

        if time + 2 < count and (time + 2) % group == 0:
            prepare((time + 2) // group)
        if time >= 2 * LAG:
            after(time - 2 * LAG)
        work(time)
    for index in range(count):

        @pl.when(outer)
        def _():
            inward(index).wait_send()

        @pl.when(inner)
        def _():
            exchange(index).wait_send()
            outward(index).wait_send()


class GradExchange:
    def __init__(self, place, layer, n, send, recv):
        self.place, self.layer = place, layer
        self.mine, self.theirs, self.relay, self.inbox = (
            [getattr(n, name + kind) for kind in "qfop"]
            for name in ("mine_", "theirs_", "relay_", "inbox_")
        )
        self.send, self.recv = send, recv

    def block(self, which):
        place = self.place
        return (place.beside(0), place.beside(1), place.across(), place.r)[which]

    def view(self, kind, block, half=None):
        shape = self.inbox[kind].shape
        length = shape[-2 if kind in (0, 1) else -1]
        lines = shape[-2]
        at, count = (0, lines) if half is None else (half * (lines // 2), lines // 2)
        if kind in (0, 1):
            piece = pl.ds(pl.multiple_of(block * length + at, count), count)
            return (slice(None), piece, slice(None)) if kind == 0 else (piece, slice(None))
        piece = pl.ds(pl.multiple_of(block * length, length), length)
        return (slice(at, at + count), piece)

    def passing(self, kind, which):
        view = self.view(kind, self.block(which))
        return rcopy(
            self.mine[kind].at[view], self.theirs[kind].at[view], self.send.at[kind, which],
            self.recv.at[kind, which], section=1 - self.place.s,
        )

    def relaying(self, kind, way):
        target = self.place.across() if kind in DIRECT else self.place.beside(way)
        return rcopy(
            self.mine[kind].at[self.view(kind, self.place.across(), way)],
            self.relay[kind].at[way], self.send.at[kind, 4 + way], self.recv.at[kind, 4 + way],
            row=target,
        )

    def sending(self, kind, way):
        return rcopy(
            self.mine[kind].at[self.view(kind, self.place.beside(way))],
            self.inbox[kind].at[way], self.send.at[kind, 6 + way], self.recv.at[kind, 6 + way],
            row=self.place.beside(way),
        )

    def add(self, kind, view, value):
        self.mine[kind][view] = self.mine[kind][view] + value

    def hand(self, kind, only=(2, 0, 1, 3)):
        @pl.when(self.place.s != self.layer)
        def _():
            for which in only:
                self.passing(kind, which).start()

    def merge(self, kind):
        @pl.when(self.place.s == self.layer)
        def _():
            for which in (2, 0, 1):
                self.passing(kind, which).wait_recv()
                view = self.view(kind, self.block(which))
                self.add(kind, view, self.theirs[kind][view])
                if which == 2:
                    for way in range(2):
                        self.relaying(kind, way).start()
                elif kind in DIRECT:
                    self.sending(kind, which).start()

    def pass_on(self, kind):
        if kind in DIRECT:
            return

        @pl.when(self.place.s == self.layer)
        def _():
            for way in range(2):
                self.relaying(kind, 1 - way).wait_recv()
                view = self.view(kind, self.place.beside(way), 1 - way)
                self.add(kind, view, self.relay[kind][1 - way])
                self.sending(kind, way).start()

    def take(self, kind, out):
        @pl.when(self.place.s == self.layer)
        def _():
            self.passing(kind, 3).wait_recv()
            view = self.view(kind, self.place.r)
            total = self.mine[kind][view].astype(F32) + self.theirs[kind][view].astype(F32)
            for way in range(2):
                self.sending(kind, way).wait_recv()
                total = total + self.inbox[kind][way].astype(F32)
            out[...] = total
            if kind in DIRECT:
                for way in range(2):
                    self.relaying(kind, way).wait_recv()
                    half = self.relay[kind].shape[-2]
                    lines = slice(way * half, (way + 1) * half)
                    where = (slice(None), lines) if kind == 0 else (lines,)
                    out[where] = out[where] + self.relay[kind][way].astype(F32)

    def finish(self, kind):
        @pl.when(self.place.s == self.layer)
        def _():
            for way in range(2):
                self.relaying(kind, way).wait_send()
                self.sending(kind, way).wait_send()

        @pl.when(self.place.s != self.layer)
        def _():
            for which in range(4):
                self.passing(kind, which).wait_send()


def grad_shapes(rows, full, width, units):
    part = full // rows
    return (
        dict(q=(3, full, width), f=(full, units), o=(width, full), p=(units, full)),
        dict(q=(3, part, width), f=(part, units), o=(width, part), p=(units, part)),
    )


def grad_scratch(rows, full, width, units):
    wholes, pieces = grad_shapes(rows, full, width, units)
    scratch = {}
    for kind in "qfop":
        piece = pieces[kind]
        half = piece[:-2] + (piece[-2] // 2, piece[-1])
        scratch["mine_" + kind] = pltpu.VMEM(wholes[kind], BF)
        scratch["theirs_" + kind] = pltpu.VMEM(wholes[kind], BF)
        scratch["relay_" + kind] = pltpu.VMEM((2,) + half, BF)
        scratch["inbox_" + kind] = pltpu.VMEM((2,) + piece, BF)
    return scratch


class BlockExchange:
    def __init__(self, place, source, inbox, size, send, recv, local):
        self.place, self.source, self.inbox, self.size = place, source, inbox, size
        self.send, self.recv, self.local = send, recv, local

    def slot(self, head, lane):
        return self.inbox.at[head, :, lane * self.size : (lane + 1) * self.size]

    def piece(self, block):
        return self.source.at[:, block * self.size : (block + 1) * self.size]

    def away(self, block):
        return rcopy(
            self.piece(block), self.slot(self.place.r, block % PARTS), self.send.at[block],
            self.recv.at[block % PARTS, self.place.r], row=block // PARTS,
        )

    def start(self, block):
        @pl.when(self.place.r != block // PARTS)
        def _():
            self.away(block).start()

        @pl.when(self.place.r == block // PARTS)
        def _():
            pltpu.make_async_copy(
                self.piece(block), self.slot(self.place.r, block % PARTS),
                self.local.at[block % PARTS],
            ).start()

    def arrive(self, lane):
        for step in range(1, self.place.rows):
            source = self.place.row_from(step)
            slot = self.slot(source, lane)
            rcopy(
                slot, slot, self.send.at[lane], self.recv.at[lane, source],
                row=self.place.row_to(step),
            ).wait_recv()
        slot = self.slot(self.place.r, lane)
        pltpu.make_async_copy(slot, slot, self.local.at[lane]).wait()

    def finish(self):
        for block in range(self.place.rows * PARTS):

            @pl.when(self.place.r != block // PARTS)
            def _():
                self.away(block).wait_send()


def unit_rows(values):
    centred = values - jnp.mean(values, axis=1, keepdims=True)
    rstd = lax.rsqrt(jnp.mean(centred * centred, axis=1, keepdims=True) + EPS)
    return centred * rstd, rstd


def segment_begins(lengths, micro, first):
    token = lax.broadcasted_iota(jnp.int32, first.shape, 1)
    begin = jnp.zeros_like(token)
    start = lengths[micro, 0]
    for index in range(1, lengths.shape[1]):
        begin = jnp.where(token >= start, start, begin)
        start = start + lengths[micro, index]
    first[...] = begin
    return lengths[micro, 0]


def rotary(lengths, micro, row, cos, sin):
    half, tokens = cos.shape
    token = lax.broadcasted_iota(jnp.int32, (half, tokens), 1) + row * tokens
    begin = jnp.zeros_like(token)
    start = lengths[micro, 0]
    for index in range(1, lengths.shape[1]):
        begin = jnp.where(token >= start, start, begin)
        start = start + lengths[micro, index]
    position = jnp.where(begin == 0, token, lengths[micro, 0] + token - begin)
    which = lax.broadcasted_iota(jnp.int32, (half, tokens), 0)
    freqs = jnp.zeros((half, tokens), F32)
    for index in range(half):
        freqs = jnp.where(which == index, 10000.0 ** (-(2.0 * index) / ROT), freqs)
    angles = position.astype(F32) * freqs
    cos[...] = jnp.cos(angles)
    sin[...] = jnp.sin(angles)


class Saver:
    def __init__(self, sems):
        self.sems, self.copies = sems, []

    def copy(self, source, target):
        copy = pltpu.make_async_copy(source, target, self.sems.at[len(self.copies)])
        copy.start()
        self.copies.append(copy)
        return copy

    def finish(self):
        for copy in self.copies:
            copy.wait()


class Names:
    def joined(self, results):
        both = Names()
        for name, value in vars(self).items():
            setattr(both, name, value)
        for name, value in results.items():
            setattr(both, name[2:], value)
        return both


def named_call(body, collective_id, ins, outs, scratch):
    names = [*ins, *outs, *scratch]

    def kernel(*refs):
        held = Names()
        for name, ref in zip(names, refs):
            setattr(held, name, ref)
        body(held)

    results = pl.pallas_call(
        kernel,
        out_shape=[jax.ShapeDtypeStruct(shape, dtype) for shape, dtype, space in outs.values()],
        in_specs=[pl.BlockSpec(memory_space=space) for array, space in ins.values()],
        out_specs=[pl.BlockSpec(memory_space=space) for shape, dtype, space in outs.values()],
        scratch_shapes=list(scratch.values()),
        compiler_params=pltpu.CompilerParams(
            collective_id=collective_id,
            has_side_effects=collective_id is not None,
            vmem_limit_bytes=VMEM_LIMIT,
        ),
    )(*[array for array, space in ins.values()])
    return dict(zip(outs, results))


class VectorGather:
    def __init__(self, place, own, full, send, recv, width):
        self.place, self.own, self.full, self.width = place, own, full, width
        self.send, self.recv = send, recv
        self.others = [(ds, dc) for ds in range(2) for dc in range(place.cols) if ds or dc]

    def slot(self, section, col):
        return self.full.at[section, :, pl.ds(pl.multiple_of(col * self.width, self.width), self.width)]

    def copy(self, ds, dc, source, slot):
        index = ds * self.place.cols + dc
        return rcopy(
            source, slot, self.send.at[index], self.recv.at[index],
            section=lax.rem(self.place.s + ds, 2), col=self.place.col_to(dc),
        )

    def start(self):
        for ds, dc in self.others:
            self.copy(ds, dc, self.own, self.slot(self.place.s, self.place.c)).start()

    def arrive(self):
        for ds, dc in self.others:
            slot = self.slot(lax.rem(self.place.s + ds, 2), self.place.col_from(dc))
            self.copy(ds, dc, slot, slot).wait_recv()

    def finish(self):
        for ds, dc in self.others:
            self.copy(ds, dc, self.own, self.slot(self.place.s, self.place.c)).wait_send()


def first_kernel(rows, cols, n):
    place = Place(rows, cols)
    s, c = place.s, place.c
    tokens, full = n.x_full.shape
    width = full // cols
    length = tokens // PARTS
    own = pl.ds(pl.multiple_of(c * width, width), width)

    def lane_of(lane):
        return slice(lane * length, (lane + 1) * length)

    def block_cols(block):
        return pl.ds(pl.multiple_of(block * width, width), width)

    def token_slot(source, lane):
        return pl.ds(pl.multiple_of(source * tokens + lane * length, length), length)

    loads = Saver(n.load)
    x_own = loads.copy(n.hidden_in.at[s], n.x_full.at[:, own])
    n.vectors[0:2] = n.norm_gains[0]
    n.vectors[2:4] = n.norm_biases[0]
    for index in range(3):
        n.vectors[4 + index : 5 + index] = n.b_qkv[:, index * width : (index + 1) * width]
    n.vectors[7:8] = n.b_out[...]
    for index in range(n.b_fc.shape[1] // width):
        n.vectors[8 + index : 9 + index] = n.b_fc[:, index * width : (index + 1) * width]
    n.vectors[12:16] = jnp.zeros((4, width), F32)
    v_own = loads.copy(n.vectors, n.vec_all.at[s, :, own])
    c_own = loads.copy(n.cotangent.at[s], n.cot_full.at[:, own])
    place.greet(rows=True, cols=True, partner=True, cross_cols=True)
    x_gather = [
        LineGather(
            place, lambda block, lane=lane: n.x_full.at[lane_of(lane), block_cols(block)],
            n.x_a, n.x_b, n.x_c, lane,
        )
        for lane in range(PARTS)
    ]
    c_gather = LineGather(
        place, lambda block: n.cot_full.at[:, block_cols(block)], n.c_a, n.c_b, n.c_c
    )
    vectors = VectorGather(place, n.vectors, n.vec_all, n.v_s, n.v_r, width)
    blocks = (n.wq, n.wf, n.wo, n.wp)
    weights = [
        WeightGather(place, 0, blocks, (n.wq0, n.wf0, n.wo0, n.wp0), n.w0_s, n.w0_r, n.w0_l),
        WeightGather(place, 1, blocks, (n.wq1, n.wf1, n.wo1, n.wp1), n.w1_s, n.w1_r, n.w1_l),
    ]
    QKV, FC, OUT, PROJ = range(4)
    saves = Saver(n.save)
    def row(layer, index):
        return n.vec_all[layer, index : index + 1, :]

    def bias_rows(layer):
        return lambda kind: n.vec_all[layer, 4 + kind : 5 + kind, own]

    def unit_bias(layer):
        return lambda index: n.vec_all[layer, pl.ds(8 + index, 1), own]

    def spread(pieces, slots, sends, recvs, local):
        return [
            RowExchange(
                place,
                lambda target, lane=lane: pieces(target, lane),
                lambda source, lane=lane: slots(source, lane),
                sends.at[lane], recvs.at[lane], local.at[lane],
            )
            for lane in range(PARTS)
        ]

    out0 = spread(
        lambda target, lane: n.pieces0.at[target, :, lane_of(lane)],
        lambda source, lane: n.qkv0.at[:, token_slot(source, lane)],
        n.e0_s, n.e0_r, n.e0_l,
    )
    back0 = spread(
        lambda target, lane: n.low0.at[:, token_slot(target, lane)],
        lambda source, lane: n.attn_t0.at[
            pl.ds(pl.multiple_of(source * HEAD_DIM, HEAD_DIM), HEAD_DIM), lane_of(lane)
        ],
        n.b0_s, n.b0_r, n.b0_l,
    )
    out1 = spread(
        lambda target, lane: n.pieces1.at[target, :, lane_of(lane)],
        lambda source, lane: n.qkvd1.at[:, token_slot(source, lane)],
        n.e1_s, n.e1_r, n.e1_l,
    )

    def project(layer, lane, source, normed_a, normed_m, w_query, pieces):
        norm_rows(
            source, row(layer, 0), row(layer, 2), row(layer, 1), row(layer, 3), normed_a, normed_m,
            lane * length, length,
        )
        project_heads(
            normed_a, w_query, bias_rows(layer), n.cos, n.sin, pieces, rows, lane_of(lane)
        )

    x_own.wait()
    x_gather[0].hop(0)
    vectors.start()
    weights[0].start(QKV)
    weights[0].start(FC)
    prompt = segment_begins(n.lengths, s, n.first)
    rotary(n.lengths, s, place.r, n.cos, n.sin)
    x_gather[0].hop(1)
    x_gather[1].hop(0)
    x_gather[0].hop(2)
    weights[0].relay(QKV)
    weights[0].start(PROJ)
    x_gather[1].hop(1)
    for distance in range(3, cols):
        x_gather[0].hop(distance)
    weights[0].forward(QKV)
    weights[0].relay(FC)
    vectors.arrive()
    v_own.wait()
    x_gather[1].hop(2)
    weights[0].ready(QKV)
    project(0, 0, n.x_full, n.normed_a0, n.normed_m0, n.wq0, n.pieces0)
    out0[0].start()
    weights[0].start(OUT)
    for distance in range(3, cols):
        x_gather[1].hop(distance)
    c_own.wait()
    c_gather.hop(0)
    weights[0].forward(FC)
    project(0, 1, n.x_full, n.normed_a0, n.normed_m0, n.wq0, n.pieces0)
    out0[1].start()
    weights[0].relay(PROJ)
    weights[0].relay(OUT)
    c_gather.hop(1)
    weights[0].ready(FC)
    feed_forward(n.normed_m0, n.wf0, unit_bias(0), n.hidden0, n.slope0, slice(None))
    for ref, target in (
        (n.x_full, n.o_x_full), (n.vec_all, n.o_vec_all), (n.wq0, n.o_wq0), (n.wf0, n.o_wf0),
        (n.normed_a0, n.o_normed_a0), (n.normed_m0, n.o_normed_m0), (n.hidden0, n.o_hidden0),
        (n.slope0, n.o_slope0),
    ):
        saves.copy(ref, target)
    weights[0].forward(PROJ)
    weights[0].forward(OUT)
    weights[1].start(QKV)
    weights[1].start(OUT)
    for lane in range(PARTS):
        out0[lane].arrive()
    saves.copy(n.qkv0, n.o_qkv0)

    rows_of_keys(n.qkv0, HEAD_DIM, n.key_rows)

    def attend(lane, owner):
        block = owner * PARTS + lane
        exact, top, weight = attend_block(
            block, length, prompt, n.first, n.qkv0, n.key_rows, n.scores.at[owner % 2],
            lambda key_at, keys: (slice(key_at, key_at + keys), slice(None)),
        )
        cols_here = slice(block * length, (block + 1) * length)
        n.out0[:, cols_here] = exact
        n.low0[:, cols_here] = exact.astype(BF)
        n.log0[:, cols_here] = top + jnp.log(weight)

    for owner in range(rows):
        attend(0, owner)
    back0[0].start()
    c_gather.hop(2)
    weights[1].start(FC)
    attend(1, 0)
    attend(1, 1)
    for distance in range(3, cols):
        c_gather.hop(distance)
    saves.copy(n.cot_full, n.o_cot_full)
    weights[0].ready(PROJ)
    weights[0].ready(OUT)
    saves.copy(n.wp0, n.o_wp0)
    saves.copy(n.wo0, n.o_wo0)

    step = 4 // PARTS
    part = tokens // 4

    def prepare(quarter):
        if quarter % step == 0:
            back0[quarter // step].arrive()
        where = slice(quarter * part, (quarter + 1) * part)
        attn_rows = n.attn_t0[:, where].astype(F32).T.astype(BF)
        tile = min(256, full)
        for at in range(0, full, tile):
            value = dot(n.hidden0[where, :], n.wp0[:, at : at + tile]) + dot(
                attn_rows, n.wo0[:, at : at + tile]
            )
            n.total[where, at : at + tile] = value
            n.low[where, at : at + tile] = value.astype(BF)

    def produce(summed, mine):
        return (n.x_full[mine, :].astype(F32) + summed + n.vec_all[0, 7:8, :]).astype(BF)

    def save_rows(lane):
        where = lane_of(lane)
        for ref, target in (
            (n.hidden1, n.o_hidden1), (n.d_hidden1, n.o_d_hidden1), (n.branch1, n.o_branch1),
            (n.d_normed1, n.o_d_normed1),
        ):
            saves.copy(ref.at[where], target.at[where])

    def branches(lane):
        where = lane_of(lane)
        feed_forward(n.normed_m1, n.wf1, unit_bias(1), n.hidden1, n.slope1, where)

        def times_slope(value, cols_here):
            return (value * n.slope1[where, cols_here]).astype(BF)

        times_tiles(n.cot_full, n.wp1, n.d_hidden1, times_slope, ((1,), (1,)), where)
        times_tiles(n.hidden1, n.wp1, n.branch1, None, ((1,), (0,)), where)
        times_tiles(n.d_hidden1, n.wf1, n.d_normed1, None, ((1,), (1,)), where)

    def after(chunk):
        if chunk == CHUNKS - 1:
            advance(PARTS - 1)

    def advance(lane):
        if lane == 0:
            weights[1].ready(QKV)
            weights[1].ready(OUT)
        project(1, lane, n.x1_full, n.normed_a1, n.normed_m1, n.wq1, n.pieces1)
        where = lane_of(lane)
        flipped = dot(n.cot_full[where, :], n.wo1[...], ((1,), (1,))).T
        for head in range(rows):
            n.pieces1[head, 3 * HEAD_DIM :, where] = flipped[
                head * HEAD_DIM : (head + 1) * HEAD_DIM
            ].astype(BF)
        out1[lane].start()

    def work(time):
        if time < rows - 2:
            attend(1, 2 + time)
            if time == rows - 3:
                back0[1].start()
                saves.copy(n.out0, n.o_out0)
                saves.copy(n.log0, n.o_log0)
        if time == 1:
            weights[1].relay(QKV)
            weights[1].relay(OUT)
        if time == 3:
            weights[1].forward(QKV)
            weights[1].forward(OUT)
            weights[1].start(PROJ)
        if time == 6:
            weights[1].relay(FC)
        if time == 11:
            weights[1].forward(FC)
            weights[1].relay(PROJ)
        if time == 16:
            weights[1].forward(PROJ)
        if time == 18:
            advance(0)
        if time == 20:
            weights[1].ready(FC)
            weights[1].ready(PROJ)
            branches(0)
            save_rows(0)

    center_sum(
        place, n.total, n.low, n.from_left, n.from_right, n.x1_full,
        (n.r_a, n.r_b, n.r_c, n.r_d, n.r_e, n.r_f), tuple(range(CHUNKS)), prepare, produce, after, work,
    )
    saves.copy(n.attn_t0, n.o_attn_t0)
    for ref, target in (
        (n.x1_full, n.o_x1_full), (n.wq1, n.o_wq1), (n.wo1, n.o_wo1),
        (n.normed_a1, n.o_normed_a1), (n.normed_m1, n.o_normed_m1),
    ):
        saves.copy(ref, target)
    for lane in range(1, PARTS):
        branches(lane)
        save_rows(lane)
    for lane in range(PARTS):
        out1[lane].arrive()
    saves.copy(n.qkvd1, n.o_qkvd1)
    for exchange in out0 + back0 + out1:
        exchange.finish()
    for gather in x_gather + [c_gather]:
        gather.finish()
    vectors.finish()
    for gather in weights:
        for kind in range(4):
            gather.finish(kind)
    saves.finish()


def first_half(rows, cols, hidden_in, cotangent, vectors, blocks, lengths):
    norm_gains, norm_biases, b_qkv, b_out, b_fc = vectors
    tokens, width = hidden_in.shape[1:]
    full = cols * width
    wq, wf, wo, wp = blocks
    units = wf.shape[1]
    total = rows * tokens
    hbm, vmem, smem = pl.ANY, pltpu.VMEM, pltpu.SMEM
    ins = dict(
        hidden_in=(hidden_in, hbm), cotangent=(cotangent, hbm), norm_gains=(norm_gains, vmem),
        norm_biases=(norm_biases, vmem), b_qkv=(b_qkv, vmem), b_out=(b_out, vmem), b_fc=(b_fc, vmem),
        wq=(wq, hbm), wf=(wf, hbm), wo=(wo, hbm), wp=(wp, hbm),
        lengths=(lengths, smem),
    )
    rows_low, rows_wide = ((tokens, full), BF), ((tokens, full), F32)
    unit_low, unit_wide = ((tokens, units), BF), ((tokens, units), F32)
    kept = dict(
        x_full=rows_low, cot_full=rows_low, vec_all=((2, 16, full), F32),
        wq0=((3, full, width), BF), wf0=((full, units), BF), wo0=((width, full), BF),
        wp0=((units, full), BF), normed_a0=rows_low, normed_m0=rows_low,
        qkv0=((3 * HEAD_DIM, total), BF), hidden0=unit_low, slope0=unit_low,
        out0=((HEAD_DIM, total), F32), log0=((1, total), F32), attn_t0=((width, tokens), BF),
        x1_full=rows_low, wq1=((3, full, width), BF), wo1=((width, full), BF),
        normed_a1=rows_low, normed_m1=rows_low, qkvd1=((4 * HEAD_DIM, total), BF),
        hidden1=unit_low, d_hidden1=unit_low, branch1=rows_wide, d_normed1=rows_wide,
    )
    outs = {"o_" + name: shape + (hbm,) for name, shape in kept.items()}
    scratch = {name: pltpu.VMEM(*shape) for name, shape in kept.items()}
    scratch.update(
        vectors=pltpu.VMEM((16, width), F32),
        wf1=pltpu.VMEM((full, units), BF), wp1=pltpu.VMEM((units, full), BF),
        slope1=pltpu.VMEM(*unit_wide), low0=pltpu.VMEM((HEAD_DIM, total), BF),
        total=pltpu.VMEM(*rows_wide), low=pltpu.VMEM(*rows_low),
        from_left=pltpu.VMEM(*rows_low), from_right=pltpu.VMEM(*rows_low),
        pieces0=pltpu.VMEM((rows, 3 * HEAD_DIM, tokens), BF),
        pieces1=pltpu.VMEM((rows, 4 * HEAD_DIM, tokens), BF),
        first=pltpu.VMEM((1, total), jnp.int32),
        cos=pltpu.VMEM((ROT // 2, tokens), F32), sin=pltpu.VMEM((ROT // 2, tokens), F32),
        key_rows=pltpu.VMEM((total, HEAD_DIM), BF),
        scores=pltpu.VMEM((2, total, tokens // PARTS), F32),
        load=dma(3), save=dma(len(kept) + 4 * PARTS),
        x_a=dma(PARTS, cols), x_b=dma(PARTS, cols), x_c=dma(PARTS, cols),
        c_a=dma(1, cols), c_b=dma(1, cols), c_c=dma(1, cols),
        v_s=dma(2 * cols), v_r=dma(2 * cols),
        w0_s=dma(4, 8), w0_r=dma(4, 8), w0_l=dma(4), w1_s=dma(4, 8), w1_r=dma(4, 8), w1_l=dma(4),
    )
    for name in ("e0", "b0", "e1"):
        scratch[name + "_s"] = dma(PARTS, rows)
        scratch[name + "_r"] = dma(PARTS, rows)
        scratch[name + "_l"] = dma(PARTS)
    for name in ("r_a", "r_b", "r_c", "r_d", "r_e", "r_f"):
        scratch[name] = dma(CHUNKS)
    return Names().joined(named_call(partial(first_kernel, rows, cols), 1, ins, outs, scratch))


def d_projection(inbox, at, cos, sin, rows, d_pre, small, where):
    width = rows * HEAD_DIM
    for kind in range(3):
        parts = []
        for head in range(rows):
            start = at + kind * HEAD_DIM
            block = inbox[head, start : start + HEAD_DIM, where].astype(F32)
            parts.append(turn(block, cos[:, where], sin[:, where], -1.0) if kind < 2 else block)
        values = jnp.concatenate(parts, axis=0).T.astype(BF)
        d_pre[where, kind * width : (kind + 1) * width] = values
        small[8 + kind : 9 + kind, :] += jnp.sum(values.astype(F32), axis=0, keepdims=True)


def d_norms(source, d_pre, wq, d_normed, gain_a, gain_m, total, low, sums, begin, count, also=None):
    width = wq.shape[2]
    tile = min(128, count)

    @pl.loop(0, count // tile)
    def _(index):
        rows = pl.ds(pl.multiple_of(begin + index * tile, tile), tile)
        d_a = dot(d_pre[rows, :width], wq[0], ((1,), (1,)))
        for kind in range(1, 3):
            d_a += dot(d_pre[rows, kind * width : (kind + 1) * width], wq[kind], ((1,), (1,)))
        d_m = d_normed[rows, :]
        unit, rstd = unit_rows(source[rows, :].astype(F32))
        sums[0:1, :] += jnp.sum(d_a * unit, axis=0, keepdims=True)
        sums[1:2, :] += jnp.sum(d_m * unit, axis=0, keepdims=True)
        sums[2:3, :] += jnp.sum(d_a, axis=0, keepdims=True)
        sums[3:4, :] += jnp.sum(d_m, axis=0, keepdims=True)
        joined = d_a * gain_a + d_m * gain_m
        total[rows, :] = joined
        low[rows, :] = joined.astype(BF)
        if also is not None:
            also(rows, joined, unit, rstd)


def unit_sums(d_pre, small, width):
    for index in range(d_pre.shape[1] // width):
        piece = d_pre[:, index * width : (index + 1) * width].astype(F32)
        small[12 + index : 13 + index, :] = jnp.sum(piece, axis=0, keepdims=True)


def across_tokens(left, right, out, heads=False, only=None):
    tile = min(256, left.shape[1])

    def at(index):
        cols = pl.ds(pl.multiple_of(index * tile, tile), tile)
        value = dot(left[:, cols], right[...], ((0,), (0,))).astype(BF)
        if heads:
            width = out.shape[2]
            for kind in range(3):
                out[kind, cols, :] = value[:, kind * width : (kind + 1) * width]
        else:
            out[cols, :] = value

    if only is None:
        pl.loop(0, left.shape[1] // tile)(at)
    else:
        at(only)


def across_blocks(grads, kind, left, right, out, heads, turns):
    for which in turns:
        across_tokens(left, right, out, heads, grads.block(which))
        grads.hand(kind, (which,))


FARTHEST_FIRST = (2, 0, 1, 3)


def out_gradient(attn_t, grad_full, out):
    tile = min(256, out.shape[1])
    for at in range(0, out.shape[1], tile):
        out[:, at : at + tile] = dot(attn_t[...], grad_full[:, at : at + tile]).astype(BF)


Q, F, O, PR = range(4)
DIRECT = (O,)


class Load:
    def __init__(self, source, target, sem):
        self.copy, self.waiting = pltpu.make_async_copy(source, target, sem), True

    def start(self):
        self.copy.start()

    def need(self):
        if self.waiting:
            self.copy.wait()
            self.waiting = False


def second_kernel(rows, cols, n):
    place = Place(rows, cols)
    s, c = place.s, place.c
    tokens, full = n.x1_full.shape
    width = full // cols
    length = tokens // PARTS
    size = QUERY_BLOCK
    own = pl.ds(pl.multiple_of(c * width, width), width)
    count = rows * PARTS
    qkv0 = n.qkvd1.at[: 3 * HEAD_DIM]
    hidden0, normed_m0, normed_a0, wq0 = n.hidden1, n.normed_m1, n.normed_a1, n.wq1
    x_full, branch1, unit0, d_normed0 = n.d_hidden1, n.d_normed1, n.scores, n.scores
    o_low = n.cot_full
    load_no = iter(range(LOADS))

    def loading(source, target):
        return Load(source, target, n.load.at[next(load_no)])

    l_qkvd1 = loading(n.i_qkvd1, n.qkvd1)
    l_cot = loading(n.i_cot_full, n.cot_full)
    l_d_hidden1 = loading(n.i_d_hidden1, n.d_hidden1)
    l_hidden1 = loading(n.i_hidden1, n.hidden1)
    l_x1 = loading(n.i_x1_full, n.x1_full)
    l_wq1 = loading(n.i_wq1, n.wq1)
    l_d_normed1 = loading(n.i_d_normed1, n.d_normed1)
    l_normed_m1 = loading(n.i_normed_m1, n.normed_m1)
    l_normed_a1 = loading(n.i_normed_a1, n.normed_a1)
    l_wo0 = loading(n.i_wo0, n.wo0)
    l_wp0 = loading(n.i_wp0, n.wp0)
    l_wf0 = loading(n.i_wf0, n.wf0)
    l_slope0 = loading(n.i_slope0, n.slope0)
    l_wo1 = loading(n.i_wo1, n.wo1)
    l_out0 = loading(n.i_out0, n.out0)
    l_log0 = loading(n.i_log0, n.log0)
    l_attn_t0 = loading(n.i_attn_t0, n.attn_t0)
    l_qkv0 = loading(n.i_qkv0, qkv0)
    l_hidden0 = loading(n.i_hidden0, hidden0)
    l_normed_m0 = loading(n.i_normed_m0, normed_m0)
    l_normed_a0 = loading(n.i_normed_a0, normed_a0)
    l_wq0 = loading(n.i_wq0, wq0)
    l_x0 = loading(n.i_x_full, x_full)
    l_branch1 = loading(n.i_branch1, branch1)

    def lane_of(lane):
        return slice(lane * length, (lane + 1) * length)

    def features(owner):
        return (slice(None), pl.ds(pl.multiple_of(owner * width, width), width))

    l_qkvd1.start()
    place.greet(rows=True, cols=True, partner=True, cross_rows=True)
    grads1 = GradExchange(place, 1, n, n.g1_s, n.g1_r)
    grads0 = GradExchange(place, 0, n, n.g0_s, n.g0_r)
    exchange1 = BlockExchange(place, n.result, n.inbox, size, n.b1_s, n.b1_r, n.b1_l)
    exchange0 = BlockExchange(
        place, n.result.at[: 3 * HEAD_DIM], n.inbox.at[:, : 3 * HEAD_DIM], size, n.b0_s, n.b0_r,
        n.b0_l,
    )
    outward = [
        RowExchange(
            place,
            lambda target, lane=lane: n.pieces.at[target, :, lane_of(lane)],
            lambda source, lane=lane: n.d_out.at[
                :, pl.ds(pl.multiple_of(source * tokens + lane * length, length), length)
            ],
            n.e_s.at[lane], n.e_r.at[lane], n.e_l.at[lane],
        )
        for lane in range(PARTS)
    ]
    out_sum = LineReduce(
        place, branch1, o_low, n.o_left, n.o_right, features, (n.o_a, n.o_b, n.o_c, n.o_d)
    )
    grad_sums = [
        LineReduce(
            place, n.total, n.low, n.from_left, n.from_right,
            lambda owner, lane=lane: (lane_of(lane), features(owner)[1]),
            (n.s_a, n.s_b, n.s_c, n.s_d), lane,
        )
        for lane in range(PARTS)
    ]

    prompt = segment_begins(n.lengths, s, n.first)
    rotary(n.lengths, s, place.r, n.cos, n.sin)
    l_qkvd1.need()
    for load in (
        l_cot, l_d_hidden1, l_hidden1, l_x1, l_wq1, l_d_normed1, l_normed_m1, l_normed_a1, l_wo0,
        l_wp0, l_wf0, l_slope0, l_wo1, l_out0, l_log0, l_attn_t0,
    ):
        load.start()
    qkvd = n.qkvd1
    rows_of_keys(qkvd, HEAD_DIM, n.key_rows)
    rows_of_keys(qkvd, 2 * HEAD_DIM, n.value_rows)
    d_out1 = qkvd.at[3 * HEAD_DIM :]

    def spot(key_at, keys):
        at = key_at // KEY_BLOCK * size
        return (slice(0, keys), slice(at, at + size))

    for block in reversed(range(count)):
        here = slice(block * size, (block + 1) * size)
        scores = (n.scores, n.total)[block % 2]
        exact, top, weight = attend_block(
            block, size, prompt, n.first, qkvd, n.key_rows, scores, spot, True
        )
        delta = jnp.sum(d_out1[:, here].astype(F32) * exact, axis=0, keepdims=True)
        inverse = 1.0 / weight

        def probs_of(key_at, keys, query):
            return scores[spot(key_at, keys)] * inverse

        d_query = gradient_block(
            block, size, qkvd, d_out1, delta, probs_of, n.key_rows, n.value_rows, n.key_acc,
            n.value_acc, block == count - 1,
        )
        n.result[:HEAD_DIM, here] = exact.astype(BF)
        n.result[HEAD_DIM : 2 * HEAD_DIM, here] = d_query.astype(BF)
        n.result[2 * HEAD_DIM : 3 * HEAD_DIM, here] = n.key_acc[:, here].astype(BF)
        n.result[3 * HEAD_DIM :, here] = n.value_acc[:, here].astype(BF)
        exchange1.start(block)

    l_qkv0.start()
    n.sums[...] = jnp.zeros_like(n.sums)
    n.small[...] = jnp.zeros_like(n.small)
    l_cot.need()
    l_d_hidden1.need()
    l_hidden1.need()
    n.small[1, 11:12, :] = jnp.sum(n.cot_full[:, own].astype(F32), axis=0, keepdims=True)
    unit_sums(n.d_hidden1, n.small.at[1], width)
    across_tokens(n.hidden1, n.cot_full, n.mine_p)
    grads1.hand(PR)
    l_hidden0.start()
    for load in (l_x1, l_wq1, l_d_normed1):
        load.need()
    quarters = (2, 3, 0, 1)
    part = tokens // 4

    def prepare(turn_no):
        if turn_no % 2 == 0:
            lane = quarters[turn_no] // 2
            exchange1.arrive(lane)
            where = lane_of(lane)
            for head in range(rows):
                n.attn_t1[head * HEAD_DIM : (head + 1) * HEAD_DIM, where] = n.inbox[
                    head, :HEAD_DIM, where
                ]
            d_projection(n.inbox, HEAD_DIM, n.cos, n.sin, rows, n.d_pre, n.small.at[1], where)
        d_norms(
            n.x1_full, n.d_pre, n.wq1, n.d_normed1, n.vec_all[1, 0:1, :], n.vec_all[1, 1:2, :],
            n.total, n.low, n.sums.at[1], quarters[turn_no] * part, part,
        )

    def produce(summed, mine):
        unit, rstd = unit_rows(n.x1_full[mine, :].astype(F32))
        moved = (
            summed
            - jnp.mean(summed, axis=1, keepdims=True)
            - unit * jnp.mean(summed * unit, axis=1, keepdims=True)
        )
        return (n.cot_full[mine, :].astype(F32) + rstd * moved).astype(BF)

    def branches(lane):
        where = lane_of(lane)

        def times_slope(value, cols_here):
            return (value * n.slope0[where, cols_here]).astype(BF)

        times_tiles(n.grad_full, n.wp0, n.d_hidden0, times_slope, ((1,), (1,)), where)
        times_tiles(n.d_hidden0, n.wf0, d_normed0, None, ((1,), (1,)), where)

    def after(chunk):
        if (chunk + 1) % (CHUNKS // PARTS) == 0:
            lane = 1 - chunk // (CHUNKS // PARTS)
            where = lane_of(lane)
            l_wo0.need()
            flipped = dot(n.grad_full[where, :], n.wo0[...], ((1,), (1,))).T
            for head in range(rows):
                n.pieces[head, :, where] = flipped[
                    head * HEAD_DIM : (head + 1) * HEAD_DIM
                ].astype(BF)
            outward[lane].start()

    def work(time):
        if time == 0:
            l_normed_m1.need()
        if time < 4:
            across_blocks(
                grads1, F, n.normed_m1, n.d_hidden1, n.mine_f, False, FARTHEST_FIRST[time : time + 1]
            )
        if time == 3:
            l_normed_m0.start()
            l_x0.start()
        if time == 4:
            grads1.merge(PR)
        if time == 8:
            grads1.merge(F)
        if time == 9:
            grads1.pass_on(PR)
        if time == 11:
            l_normed_a1.need()
        if 11 <= time < 15:
            across_blocks(
                grads1, Q, n.normed_a1, n.d_pre, n.mine_q, True, FARTHEST_FIRST[time - 11 : time - 10]
            )
        if time == 12:
            grads1.pass_on(F)
        if time == 14:
            l_normed_a0.start()
            l_wq0.start()
            l_branch1.start()
        if time == 15:
            out_gradient(n.attn_t1, n.cot_full, n.mine_o)
            grads1.hand(O)
        if time == 17:
            grads1.merge(Q)
        if time == 22:
            grads1.pass_on(Q)
            grads1.merge(O)
        if time == 18:
            outward[1].arrive()
            exchange1.finish()
            l_qkv0.need()
            l_out0.need()
            l_log0.need()
            rows_of_keys(qkv0, HEAD_DIM, n.key_rows)
            rows_of_keys(qkv0, 2 * HEAD_DIM, n.value_rows)
        if 18 <= time < 18 + rows:
            attend_back((rows - 1 - (time - 18)) * PARTS + 1)

    def attend_back(block):
        here = slice(block * size, (block + 1) * size)
        delta = jnp.sum(n.d_out[:, here].astype(F32) * n.out0[:, here], axis=0, keepdims=True)
        log_row = n.log0[:, here]

        def weights_of(key_at, keys, query):
            return jnp.exp(
                score_block(prompt, n.first, here, block * size, key_at, keys, n.key_rows, query)
                - log_row
            )

        d_query = gradient_block(
            block, size, qkv0, n.d_out, delta, weights_of, n.key_rows, n.value_rows, n.key_acc,
            n.value_acc, block == count - 1,
        )
        n.result[:HEAD_DIM, here] = d_query.astype(BF)
        if block % PARTS == 0 or block == count - 1:
            for done in keys_done(block):
                there = slice(done * size, (done + 1) * size)
                n.result[HEAD_DIM : 2 * HEAD_DIM, there] = n.key_acc[:, there].astype(BF)
                n.result[2 * HEAD_DIM : 3 * HEAD_DIM, there] = n.value_acc[:, there].astype(BF)
                exchange0.start(done)

    def keys_done(block):
        return (block,) if block in (0, count - 1) else (block, block - 1)

    chunks = tuple(range(CHUNKS // 2, CHUNKS)) + tuple(range(CHUNKS // 2))
    center_sum(
        place, n.total, n.low, n.from_left, n.from_right, n.grad_full,
        (n.r_a, n.r_b, n.r_c, n.r_d, n.r_e, n.r_f), chunks, prepare, produce, after, work,
    )

    l_branch1.need()
    l_wo1.need()
    attn_rows = n.attn_t1[...].astype(F32).T.astype(BF)
    tile = min(256, full)
    for at in range(0, full, tile):
        value = branch1[:, at : at + tile] + dot(attn_rows, n.wo1[:, at : at + tile])
        branch1[:, at : at + tile] = value
        o_low[:, at : at + tile] = value.astype(BF)
    out_sum.step(0)
    grads1.take(PR, n.gw_p)
    grads1.finish(PR)
    l_hidden0.need()
    across_tokens(hidden0, n.grad_full, n.mine_p)
    grads0.hand(PR)
    outward[0].arrive()
    for block in reversed(range(0, count, PARTS)):
        attend_back(block)
        if block == count - 2:
            grads1.take(O, n.gw_o)
            grads1.finish(O)
            l_attn_t0.need()
            out_gradient(n.attn_t0, n.grad_full, n.mine_o)
            grads0.hand(O)
            out_sum.step(1)
        if block == count - 6:
            grads0.merge(PR)
    out_sum.step(2)
    for load in (l_wp0, l_wf0, l_slope0):
        load.need()
    branches(1)
    grads0.merge(O)
    grads0.pass_on(PR)
    branches(0)
    grads1.take(F, n.gw_f)
    grads1.finish(F)
    l_normed_m0.need()
    across_blocks(grads0, F, normed_m0, n.d_hidden0, n.mine_f, False, FARTHEST_FIRST)
    n.small[0, 11:12, :] = jnp.sum(n.grad_full[:, own].astype(F32), axis=0, keepdims=True)
    unit_sums(n.d_hidden0, n.small.at[0], width)
    out_own = n.x1_full[:, own].astype(F32) + out_sum.own() + n.vec_all[1, 7:8, own]
    n.o_own[1] = out_own.astype(BF)
    n.o_own[0] = n.x1_full[:, own]

    def swap_copy(index, source, target):
        return rcopy(
            source.at[1 - s], target.at[s], n.sw_s.at[index], n.sw_r.at[index], section=1 - s
        )

    out_swap = swap_copy(0, n.o_own, n.o_out_rows)
    out_swap.start()
    out_keep = pltpu.make_async_copy(n.o_own.at[s], n.o_out_rows.at[s], n.local.at[0])
    out_keep.start()

    l_x0.need()
    l_wq0.need()
    gain_a, gain_m = n.vec_all[0, 0:1, :], n.vec_all[0, 1:2, :]
    lane_no = lax.broadcasted_iota(jnp.int32, (min(128, length), 128), 1)

    def row_sums(where, joined, unit, rstd):
        first = jnp.sum(joined, axis=1, keepdims=True)
        second = jnp.sum(joined * unit, axis=1, keepdims=True)
        both = jnp.where(lane_no == 0, first, jnp.where(lane_no == 1, second, 0.0))
        n.line_sums[:, where] = both.T[:8]
        unit0[where, :] = unit
        n.rstd[where, :] = jnp.broadcast_to(rstd, (rstd.shape[0], 128))

    def prepare_last(lane):
        exchange0.arrive(lane)
        d_projection(n.inbox, 0, n.cos, n.sin, rows, n.d_pre, n.small.at[0], lane_of(lane))
        d_norms(
            x_full, n.d_pre, wq0, d_normed0, gain_a, gain_m, n.total, n.low, n.sums.at[0],
            lane * length, length, row_sums,
        )

    grads0.merge(F)
    prepare_last(1)
    grad_sums[1].step(0)
    prepare_last(0)
    grad_sums[0].step(0)
    grad_sums[1].step(1)
    grads0.pass_on(F)

    def line_copy(step):
        return rcopy(
            n.line_sums, n.line_in.at[step], n.ls_s.at[step], n.ls_r.at[step],
            col=place.col_to(step),
        )

    def col_copy(step):
        target = place.col_to(step)
        piece = n.sums.at[:, :, pl.ds(pl.multiple_of(target * width, width), width)]
        return rcopy(piece, n.col_in.at[step], n.cs_s.at[step], n.cs_r.at[step], col=target)

    def row_copy(ds, step):
        index = ds * rows + step
        layer = lax.rem(s + ds, 2)
        return rcopy(
            n.small.at[layer], n.row_in.at[index], n.rw_s.at[index], n.rw_r.at[index],
            section=layer, row=place.row_to(step),
        )

    for step in range(1, cols):
        line_copy(step).start()
        col_copy(step).start()
    grads1.take(Q, n.gw_q)
    grads1.finish(Q)
    l_normed_a0.need()
    across_blocks(grads0, Q, normed_a0, n.d_pre, n.mine_q, True, FARTHEST_FIRST)
    grad_sums[1].step(2)
    grad_sums[0].step(1)
    for step in range(1, cols):
        col_copy(step).wait_recv()
    head = n.sums[:, :, own]
    for step in range(1, cols):
        head = head + n.col_in[step]
    n.small[:, :8, :] = head
    others = [(ds, step) for ds in range(2) for step in range(rows) if ds or step]
    for ds, step in others:
        row_copy(ds, step).start()
    grads0.merge(Q)
    saves = Saver(n.save)

    def take(kind, made, target):
        grads0.take(kind, made)
        saves.copy(made, target)

    grad_sums[0].step(2)
    grads0.pass_on(Q)
    take(PR, n.gw_p, n.o_gw_p)
    take(O, n.gw_o, n.o_gw_o)
    joined = n.line_sums[...]
    for step in range(1, cols):
        line_copy(step).wait_recv()
        joined = joined + n.line_in[step]
    wide = jnp.concatenate([joined, jnp.zeros((120, tokens), F32)], axis=0).T
    take(F, n.gw_f, n.o_gw_f)
    out_keep.wait()
    out_swap.wait()
    for lane in reversed(range(PARTS)):
        where = lane_of(lane)
        moved = (
            grad_sums[lane].own()
            - wide[where, 0:1] / full
            - unit0[where, own] * (wide[where, 1:2] / full)
        )
        n.o_own[0, where] = (
            n.grad_full[where, own].astype(F32) + n.rstd[where, 0:1] * moved
        ).astype(BF)
    n.o_own[1] = n.grad_full[:, own]
    grad_swap = swap_copy(1, n.o_own, n.o_grad_rows)
    grad_swap.start()
    grad_keep = pltpu.make_async_copy(n.o_own.at[s], n.o_grad_rows.at[s], n.local.at[1])
    grad_keep.start()
    mine = n.small[s]
    for ds, step in others:
        row_copy(ds, step).wait_recv()
        mine = mine + n.row_in[ds * rows + step]
    n.o_small[...] = mine
    take(Q, n.gw_q, n.o_gw_q)
    grad_keep.wait()
    grad_swap.wait()
    exchange0.finish()
    for exchange in outward:
        exchange.finish()
    out_sum.finish()
    for reduce in grad_sums:
        reduce.finish()
    for step in range(1, cols):
        line_copy(step).wait_send()
        col_copy(step).wait_send()
    for ds, step in others:
        row_copy(ds, step).wait_send()
    for kind in range(4):
        grads0.finish(kind)
    saves.finish()


def second_half(rows, cols, kept, lengths):
    tokens, full = kept.x1_full.shape
    width, units = full // cols, kept.hidden1.shape[1]
    total = rows * tokens
    hbm, vmem, smem = pl.ANY, pltpu.VMEM, pltpu.SMEM
    loaded = dict(
        qkvd1=kept.qkvd1, cot_full=kept.cot_full, d_hidden1=kept.d_hidden1, hidden1=kept.hidden1,
        x1_full=kept.x1_full, wq1=kept.wq1, d_normed1=kept.d_normed1, normed_m1=kept.normed_m1,
        normed_a1=kept.normed_a1, wo0=kept.wo0, wp0=kept.wp0, wf0=kept.wf0, slope0=kept.slope0,
        wo1=kept.wo1, out0=kept.out0, log0=kept.log0, attn_t0=kept.attn_t0,
    )
    later = dict(
        qkv0=kept.qkv0, hidden0=kept.hidden0, normed_m0=kept.normed_m0, normed_a0=kept.normed_a0,
        wq0=kept.wq0, x_full=kept.x_full, branch1=kept.branch1,
    )
    ins = {"i_" + name: (value, hbm) for name, value in {**loaded, **later}.items()}
    ins.update(
        lengths=(lengths, smem), vec_all=(kept.vec_all, vmem)
    )
    rows_low, rows_wide = ((tokens, full), BF), ((tokens, full), F32)
    wholes, pieces = grad_shapes(rows, full, width, units)
    outs = dict(
        o_out_rows=((2, tokens, width), BF, vmem), o_grad_rows=((2, tokens, width), BF, vmem),
        o_small=((16, width), F32, vmem),
    )
    outs.update({"o_gw_" + kind: (pieces[kind], F32, hbm) for kind in "qfop"})
    scratch = {name: pltpu.VMEM(value.shape, value.dtype) for name, value in loaded.items()}
    scratch.update(grad_scratch(rows, full, width, units))
    scratch.update({"gw_" + kind: pltpu.VMEM(pieces[kind], F32) for kind in "qfop"})
    scratch.update(
        grad_full=pltpu.VMEM(*rows_low), attn_t1=pltpu.VMEM((width, tokens), BF),
        d_hidden0=pltpu.VMEM((tokens, units), BF), d_out=pltpu.VMEM((HEAD_DIM, total), BF),
        result=pltpu.VMEM((4 * HEAD_DIM, total), BF),
        inbox=pltpu.VMEM((rows, 4 * HEAD_DIM, tokens), BF),
        pieces=pltpu.VMEM((rows, HEAD_DIM, tokens), BF),
        d_pre=pltpu.VMEM((tokens, 3 * width), BF),
        total=pltpu.VMEM(*rows_wide), low=pltpu.VMEM(*rows_low),
        from_left=pltpu.VMEM(*rows_low), from_right=pltpu.VMEM(*rows_low),
        o_left=pltpu.VMEM(*rows_low), o_right=pltpu.VMEM(*rows_low),
        scores=pltpu.VMEM((KEY_BLOCK, total // KEY_BLOCK * QUERY_BLOCK), F32),
        first=pltpu.VMEM((1, total), jnp.int32),
        cos=pltpu.VMEM((ROT // 2, tokens), F32), sin=pltpu.VMEM((ROT // 2, tokens), F32),
        key_rows=pltpu.VMEM((total, HEAD_DIM), BF), value_rows=pltpu.VMEM((total, HEAD_DIM), BF),
        key_acc=pltpu.VMEM((HEAD_DIM, total), F32), value_acc=pltpu.VMEM((HEAD_DIM, total), F32),
        sums=pltpu.VMEM((2, 8, full), F32), small=pltpu.VMEM((2, 16, width), F32),
        rstd=pltpu.VMEM((tokens, 128), F32),
        line_sums=pltpu.VMEM((8, tokens), F32), line_in=pltpu.VMEM((cols, 8, tokens), F32),
        col_in=pltpu.VMEM((cols, 2, 8, width), F32),
        row_in=pltpu.VMEM((2 * rows, 16, width), F32),
        o_own=pltpu.VMEM((2, tokens, width), BF),
        load=dma(LOADS), save=dma(4), local=dma(2),
        g1_s=dma(4, 8), g1_r=dma(4, 8), g0_s=dma(4, 8), g0_r=dma(4, 8),
        b1_s=dma(rows * PARTS), b1_r=dma(PARTS, rows), b1_l=dma(PARTS),
        b0_s=dma(rows * PARTS), b0_r=dma(PARTS, rows), b0_l=dma(PARTS),
        e_s=dma(PARTS, rows), e_r=dma(PARTS, rows), e_l=dma(PARTS),
        ls_s=dma(cols), ls_r=dma(cols), cs_s=dma(cols), cs_r=dma(cols),
        rw_s=dma(2 * rows), rw_r=dma(2 * rows), sw_s=dma(2), sw_r=dma(2),
    )
    for name in ("r_a", "r_b", "r_c", "r_d", "r_e", "r_f"):
        scratch[name] = dma(CHUNKS)
    for name in ("s_a", "s_b", "s_c", "s_d"):
        scratch[name] = dma(PARTS, cols)
    for name in ("o_a", "o_b", "o_c", "o_d"):
        scratch[name] = dma(1, cols)
    return Names().joined(named_call(partial(second_kernel, rows, cols), 3, ins, outs, scratch))


def finishing_kernel(n):
    for source, target in (
        (n.i_out_rows, n.out_rows), (n.i_grad_rows, n.grad_rows), (n.i_gw_q, n.gw_q),
        (n.i_gw_f, n.gw_f), (n.i_gw_o, n.gw_o), (n.i_gw_p, n.gw_p),
    ):
        target[0] = source[...]
    width = n.small.shape[1]
    n.gains[0] = n.small[0:2]
    n.shifts[0] = n.small[2:4]
    for index in range(3):
        n.g_qkv[:, index * width : (index + 1) * width] = n.small[8 + index : 9 + index]
    n.g_out[...] = n.small[11:12]
    for index in range(n.g_fc.shape[1] // width):
        n.g_fc[:, index * width : (index + 1) * width] = n.small[12 + index : 13 + index]


def finishing(k):
    vmem = pltpu.VMEM
    made = dict(
        out_rows=k.out_rows, grad_rows=k.grad_rows, gw_q=k.gw_q, gw_f=k.gw_f, gw_o=k.gw_o,
        gw_p=k.gw_p,
    )
    ins = {"i_" + name: (value, vmem) for name, value in made.items()}
    ins.update(small=(k.small, vmem))
    width, units = k.small.shape[1], k.gw_f.shape[1]
    large = {name: ((1,) + value.shape, value.dtype, vmem) for name, value in made.items()}
    outs = dict(
        out_rows=None, grad_rows=None, gains=((1, 2, width), F32, vmem),
        shifts=((1, 2, width), F32, vmem), gw_q=None, g_qkv=((1, 3 * width), F32, vmem),
        gw_o=None, gw_f=None, g_fc=((1, units), F32, vmem), gw_p=None,
        g_out=((1, width), F32, vmem),
    )
    outs.update(large)
    results = named_call(finishing_kernel, None, ins, outs, {})
    results.update(g_qkv=results.pop("g_qkv").reshape(1, 3, width))
    return tuple(results[name] for name in outs)


def relay_body(
    hidden_in,
    cotangent,
    lengths,
    norm_gains,
    norm_biases,
    w_qkv,
    b_qkv,
    w_out,
    w_fc,
    b_fc,
    w_proj,
    b_out,
):
    rows, cols = lax.axis_size(ROW), lax.axis_size(COL)
    blocks = (w_qkv[0], w_fc[0], w_out[0], w_proj[0])
    vectors = (norm_gains, norm_biases, b_qkv.reshape(1, -1), b_out, b_fc)
    kept = first_half(rows, cols, hidden_in, cotangent, vectors, blocks, lengths)
    return finishing(second_half(rows, cols, kept, lengths))


def fits(mesh):
    rows, cols = mesh.shape[ROW], mesh.shape[COL]
    return rows == cols == 4 and MODEL_WIDTH == rows * cols * HEAD_DIM


def solution(mesh):
    return jax.shard_map(
        relay_body if fits(mesh) else body,
        mesh=mesh,
        in_specs=(
            P(None, ROW, COL),
            P(None, ROW, COL),
            P(),
            P(SECTION, None, COL),
            P(SECTION, None, COL),
            P(SECTION, None, ROW, COL),
            P(SECTION, None, COL),
            P(SECTION, COL, ROW),
            P(SECTION, ROW, COL),
            P(SECTION, COL),
            P(SECTION, COL, ROW),
            P(SECTION, COL),
        ),
        out_specs=(
            P(SECTION, None, ROW, COL),
            P(SECTION, None, ROW, COL),
            P(SECTION, None, COL),
            P(SECTION, None, COL),
            P(SECTION, None, ROW, COL),
            P(SECTION, None, COL),
            P(SECTION, COL, ROW),
            P(SECTION, ROW, COL),
            P(SECTION, COL),
            P(SECTION, COL, ROW),
            P(SECTION, COL),
        ),
        check_vma=False,
    )
```
